32 devices in a mesh: section: 2 (over x), rep: 4 (over y, core), fsdp: 4 (over z).
Axes of the slice: x: 2, y: 2, z: 4, core: 2. Of those that a mesh axis runs over, the one named last changes fastest.
Arguments:
- ends: bfloat16 [2, 2, 4, 1024, 1536], P('section', None, 'rep', 'fsdp'), may hold values from -6 to 6
- norm_gain: bfloat16 [2, 1536], P('section', 'fsdp'), may hold values from 0.5 to 1.5
- input_weight: bfloat16 [2, 1536, 6448], P('section', 'fsdp'), may hold values from -0.15625 to 0.15625
- conv_weight: bfloat16 [2, 3328, 4], P('section', 'fsdp'), may hold values from -3 to 3
- conv_bias: bfloat16 [2, 3328], P('section', 'fsdp'), may hold values from -3 to 3
- dt_bias: bfloat16 [2, 48], P('section', 'fsdp'), may hold values from -6 to -2
- a_log: bfloat16 [2, 48], P('section', 'fsdp'), may hold values from -1.5 to 0.5
- skip_gain: bfloat16 [2, 48], P('section', 'fsdp'), may hold values from 0.5 to 1.5
- gate_gain: bfloat16 [2, 3072], P('section', 'fsdp'), may hold values from 0.5 to 1.5
- output_weight: bfloat16 [2, 3072, 1536], P('section', 'fsdp'), may hold values from -0.109375 to 0.109375
Outputs:
- edges: bfloat16 [2, 2, 4, 1024, 1536], P('section', None, 'rep', 'fsdp')
- norm_gain_grad: float32 [2, 1536], P('section', 'fsdp')
- in_weight_grad: float32 [2, 1536, 6448], P('section', 'fsdp')
- conv_weight_grad: float32 [2, 3328, 4], P('section', 'fsdp')
- conv_bias_grad: float32 [2, 3328], P('section', 'fsdp')
- dt_bias_grad: float32 [2, 48], P('section', 'fsdp')
- a_log_grad: float32 [2, 48], P('section', 'fsdp')
- skip_gain_grad: float32 [2, 48], P('section', 'fsdp')
- gate_gain_grad: float32 [2, 3072], P('section', 'fsdp')
- out_weight_grad: float32 [2, 3072, 1536], P('section', 'fsdp')
The draws below stay inside these ranges and needn't reach their ends.
All inputs are finite; a program needn't handle non-finite values.
Results may differ from the reference program's by a relative error of at most 0.025.
Values may be sent and summed in bfloat16 or wider, within the bound.
No kernel may reach another device: no remote copies, remote signals or barrier semaphores. Data moves between devices by JAX's collectives and lax.ppermute only.
A program may use at most 576 MiB of HBM per device.

```python
import jax
import jax.numpy as jnp
from jax import lax

D = 1536
HEADS = 48
HEAD_DIM = 64
STATE = 128
KERNEL = 4
SEQ_LEN = 1024
MB = 2
INNER = 3072
CONV_CH = 3328
PROJ = 6448
SEQ_G = 1
SEQS = 4


def level_of(stream_key, shape, cuts, low, largest):
    def one(dim, parts):
        steps = jax.random.uniform(jax.random.fold_in(jax.random.fold_in(stream_key, 6), dim), (parts,), jnp.float32, low / len(cuts), largest / len(cuts))
        return jnp.repeat(jnp.exp(steps), shape[dim] // parts).reshape((-1,) + (1,) * (len(shape) - dim - 1))

    level = one(*cuts[0])
    for cut in cuts[1:]:
        level = level * one(*cut)
    return level


def normal_values(stream_key, dims, width, limit, cuts=(), held_as=jnp.bfloat16):
    loudness = level_of(stream_key, dims, cuts, -0.22, 0.18) if cuts else 1.0
    result = jax.random.normal(stream_key, dims, jnp.float32) * width * loudness
    return jnp.minimum(jnp.maximum(result, -limit), limit).astype(held_as)


def setup_inputs(seed: int = 0) -> dict:
    key_list = jax.random.split(jax.random.key(seed), 11)
    ends = normal_values(key_list[0], (2, MB, SEQS, SEQ_LEN, D), 1.0, 6.0, ((0, 2), (2, 4), (3, 4)))
    norm_gain = jnp.clip(1.0 + 0.1 * jax.random.normal(key_list[1], (2, D), jnp.float32), 0.5, 1.5).astype(jnp.bfloat16)
    input_weight = normal_values(key_list[2], (2, D, PROJ), D ** -0.5, 0.15625, ((0, 2), (1, 4)))
    conv_weight = normal_values(key_list[3], (2, CONV_CH, KERNEL), KERNEL ** -0.5, 3.0, ((0, 2), (1, 4)))
    conv_bias = normal_values(key_list[4], (2, CONV_CH), 0.5, 3.0, ((0, 2), (1, 4)))
    dt_bias = jnp.clip(-6.0 + 4.0 * jax.random.uniform(key_list[5], (2, HEADS), jnp.float32) ** level_of(key_list[5], (2, HEADS), ((0, 2), (1, 4)), -0.2, 0.2), -6.0, -2.0).astype(jnp.bfloat16)
    a_log = jnp.clip(-1.5 + 2.0 * jax.random.uniform(key_list[6], (2, HEADS), jnp.float32) ** level_of(key_list[6], (2, HEADS), ((0, 2), (1, 4)), -0.2, 0.2), -1.5, 0.5).astype(jnp.bfloat16)
    skip_gain = jnp.clip(0.5 + 1.0 * jax.random.uniform(key_list[7], (2, HEADS), jnp.float32) ** level_of(key_list[7], (2, HEADS), ((0, 2), (1, 4)), -0.2, 0.2), 0.5, 1.5).astype(jnp.bfloat16)
    gate_gain = jnp.clip(1.0 + 0.1 * jax.random.normal(key_list[8], (2, INNER), jnp.float32), 0.5, 1.5).astype(jnp.bfloat16)
    output_weight = normal_values(key_list[9], (2, INNER, D), INNER ** -0.5, 0.109375, ((0, 2), (1, 4)))
    return dict(ends=ends, norm_gain=norm_gain, input_weight=input_weight, conv_weight=conv_weight, conv_bias=conv_bias, dt_bias=dt_bias, a_log=a_log, skip_gain=skip_gain, gate_gain=gate_gain, output_weight=output_weight)


@jax.custom_vjp
def low(v):
    return lax.optimization_barrier(v.astype(jnp.bfloat16)).astype(jnp.float32)

@jax.custom_vjp
def low_back(v):
    return v

def low_keep(v):
    return (low(v), None)

def low_pass(kept, grad):
    return (grad,)

def back_keep(v):
    return (v, None)

def back_low(kept, grad):
    return (low(grad),)
low.defvjp(low_keep, low_pass)
low_back.defvjp(back_keep, back_low)
EPSILON = 1e-05
EXACT_MATMUL = lax.Precision.HIGHEST

def rms_scale(values, scale_gain):
    return values * lax.rsqrt(lax.optimization_barrier(jnp.mean(values * values, axis=-1, keepdims=True)) + EPSILON) * scale_gain

def block_step(carried, pieces):
    x_heads, dt_step, b_rows, c_rows, log_decay = pieces
    block_len = log_decay.shape[1]
    by_head = jnp.transpose(log_decay, (0, 2, 1))
    differ = by_head[:, :, :, None] - by_head[:, :, None, :]
    causal = jnp.arange(block_len)[:, None] >= jnp.arange(block_len)[None, :]
    mixing = jnp.where(causal, jnp.exp(jnp.where(causal, differ, 0.0)), 0.0)
    intersections = jnp.einsum('sqn,skn->sqk', c_rows, b_rows, precision=EXACT_MATMUL)
    scaled = x_heads * dt_step[..., None]
    final_result = jnp.einsum('shqk,skhd->sqhd', mixing * intersections[:, None], scaled, precision=EXACT_MATMUL)
    final_result = final_result + jnp.exp(log_decay)[..., None] * jnp.einsum('sqn,shdn->sqhd', c_rows, carried, precision=EXACT_MATMUL)
    weights = jnp.exp(log_decay[:, -1:, :] - log_decay)
    weighted = scaled * weights[..., None]
    updated = jnp.exp(log_decay[:, -1])[:, :, None, None] * carried + jnp.einsum('sqhd,sqn->shdn', weighted, b_rows, precision=EXACT_MATMUL)
    return (updated, final_result)

def mixer_layer(hidden, params):
    norm_gain, input_weight, conv_weight, conv_bias, dt_bias, a_log, skip_gain, gate_gain, output_weight = params
    seq_count, length = (hidden.shape[0], hidden.shape[1])
    normalized_rows = low(rms_scale(hidden, norm_gain))
    projected_rows = low_back(low(jnp.einsum('qkb,bu->qku', normalized_rows, input_weight, precision=EXACT_MATMUL)))
    gate_z = projected_rows[..., :INNER]
    xbc_part = projected_rows[..., INNER:INNER + CONV_CH]
    dt_raw = projected_rows[..., INNER + CONV_CH:]
    padded = jnp.pad(xbc_part, ((0, 0), (KERNEL - 1, 0), (0, 0)))
    convolved = conv_bias
    for offset in range(KERNEL):
        convolved = convolved + padded[:, offset:offset + length, :] * conv_weight[:, offset]
    activated = jax.nn.silu(convolved)
    x_heads = activated[..., :INNER].reshape(seq_count, length, HEADS, HEAD_DIM)
    b_rows = activated[..., INNER:INNER + STATE]
    c_rows = activated[..., INNER + STATE:]
    dt_step = jax.nn.softplus(dt_raw + dt_bias)
    decay_rate = -jnp.exp(a_log) * dt_step
    block_len = min(256, length)
    blocks = length // block_len

    def split_rows(values):
        return jnp.moveaxis(values.reshape((seq_count, blocks, block_len) + values.shape[2:]), 1, 0)
    log_decay = jnp.cumsum(split_rows(decay_rate), axis=2)
    start_state = jnp.zeros((seq_count, HEADS, HEAD_DIM, STATE), jnp.float32)
    _, block_out = lax.scan(jax.checkpoint(block_step), start_state, (split_rows(x_heads), split_rows(dt_step), split_rows(b_rows), split_rows(c_rows), log_decay))
    mixed_out = jnp.moveaxis(block_out, 0, 1).reshape(seq_count, length, HEADS, HEAD_DIM)
    mixed_out = (mixed_out + skip_gain[:, None] * x_heads).reshape(seq_count, length, INNER)
    gated_result = low(rms_scale(mixed_out * jax.nn.silu(gate_z), gate_gain))
    final_result = low_back(jnp.einsum('nwq,qe->nwe', gated_result, output_weight, precision=EXACT_MATMUL))
    return hidden + final_result

def reference(ends, norm_gain, input_weight, conv_weight, conv_bias, dt_bias, a_log, skip_gain, gate_gain, output_weight):
    params = tuple((member.astype(jnp.float32) for member in (norm_gain, input_weight, conv_weight, conv_bias, dt_bias, a_log, skip_gain, gate_gain, output_weight)))
    data_all = ends.astype(jnp.float32)
    inputs = data_all[0].reshape(-1, SEQ_G, SEQ_LEN, D)
    cotangent = data_all[1].reshape(-1, SEQ_G, SEQ_LEN, D)

    def network(weights, source):
        first_section = tuple((member[0] for member in weights))
        second_section = tuple((member[1] for member in weights))

        def apply_block(piece_rows):
            middle = mixer_layer(piece_rows, first_section)
            return mixer_layer(low_back(low(middle)), second_section)
        return lax.map(jax.checkpoint(apply_block), source)
    outcome, pull_back = jax.vjp(network, params, inputs)
    grad_params, grad_inputs = pull_back(cotangent)
    edges = jnp.stack([grad_inputs.reshape(data_all.shape[1:]), outcome.reshape(data_all.shape[1:])]).astype(jnp.bfloat16)
    return (edges, grad_params[0], grad_params[1], grad_params[2], grad_params[3], grad_params[4], grad_params[5], grad_params[6], grad_params[7], grad_params[8])
```

```python
import functools

import jax
import jax.numpy as jnp
from jax import lax
from jax.experimental import pallas as pl
from jax.experimental.pallas import tpu as pltpu
from jax.sharding import Mesh
from jax.sharding import PartitionSpec as P

D = 1536
HEADS = 48
HEAD_DIM = 64
STATE = 128
KERNEL = 4
INNER = 3072
CONV_CH = 3328
LANES = 128

OWN = INNER // 2
OWN_HEADS = HEADS // 2
OWN_CONV = OWN + 2 * STATE
X_AT = OWN
BC_AT = 2 * OWN
DT_AT = 2 * OWN + 2 * STATE
OWN_PROJ = DT_AT + 2 * LANES
PAIRS = OWN // LANES

EPSILON = 1e-05
EXACT_MATMUL = lax.Precision.HIGHEST
F32 = jnp.float32
BF16 = jnp.bfloat16
FORWARD_VMEM = 24
BACKWARD_VMEM = 30
JOIN_VMEM = 12


def dot(a, b):
    return lax.dot_general(a, b, (((1,), (0,)), ((), ())), preferred_element_type=F32)


def dot_nt(a, b):
    return lax.dot_general(a, b, (((1,), (1,)), ((), ())), preferred_element_type=F32)


def dot_tn(a, b):
    return lax.dot_general(a, b, (((0,), (0,)), ((), ())), preferred_element_type=F32)


def split(v, parts):
    pieces = []
    for _ in range(parts):
        piece = v.astype(BF16)
        pieces.append(piece)
        v = v - piece.astype(F32)
    return pieces


def sigmoid(v):
    return 0.5 * jnp.tanh(0.5 * v) + 0.5


def softplus(v):
    return jnp.maximum(v, 0.0) + jnp.log1p(jnp.exp(-jnp.abs(v)))


def step_sizes(dt_raw, headp):
    t = dt_raw.shape[0]
    biased = dt_raw + headp[0:1]
    dt = softplus(biased)
    rows = lax.broadcasted_iota(jnp.int32, (t, t), 0)
    cols = lax.broadcasted_iota(jnp.int32, (t, t), 1)
    tri = jnp.where(rows >= cols, 1.0, 0.0).astype(BF16)
    ld = sum(dot(tri, part) for part in split(dt * headp[1:2], 3))
    return dt, ld, biased


def at_head(v, pair):
    turned = pltpu.roll(v, lax.rem(LANES - 2 * pair, LANES), 1)
    return [jnp.broadcast_to(turned[:, i : i + 1], v.shape) for i in range(2)]


def decay_blocks(col, row, swapped):
    n = col.shape[0] // 2
    rows = lax.broadcasted_iota(jnp.int32, (n, n), 0)
    cols = lax.broadcasted_iota(jnp.int32, (n, n), 1)
    keep = rows <= cols if swapped else rows >= cols

    def block(i, j):
        down, along = col[i * n : (i + 1) * n], row[:, j * n : (j + 1) * n]
        differ = along - down if swapped else down - along
        return jnp.exp(jnp.where(keep, differ, -1e30) if i == j else differ)

    return block(0, 0), block(0, 1) if swapped else block(1, 0), block(1, 1)


def convolve(xw, sl, convp, t):
    out = convp[4:5, sl] + xw[5 : 5 + t, sl] * convp[0:1, sl]
    for k in range(1, KERNEL):
        out = out + xw[5 + k : 5 + k + t, sl] * convp[k : k + 1, sl]
    return out


def pair_loop(step):
    def two(turn, _):
        step(2 * turn)
        step(2 * turn + 1)
        return 0

    lax.fori_loop(0, PAIRS // 2, two, 0)


def aligned(value):
    return pl.multiple_of(value, LANES)


def fetch(source, target, sem):
    copy = pltpu.make_async_copy(source, target, sem)
    copy.start()
    return copy


def fetch_one_of(first, one, other, target, sem):
    @pl.when(first)
    def _():
        pltpu.make_async_copy(one, target, sem).start()

    @pl.when(jnp.logical_not(first))
    def _():
        pltpu.make_async_copy(other, target, sem).start()

    return pltpu.make_async_copy(other, target, sem)


def forward_kernel(row, sc, *refs):
    @pl.when(sc[row, VALID] == 1)
    def _():
        forward_chunk(row, sc, *refs)


def forward_chunk(
    row, sc, got_hbm, other_hbm, x_hbm, ng_ref, convp, headp, chanp, st_ref, tail_ref, win, wout, *rest
):
    p, h, st_out, tail_out = rest[-22:-18]
    h_hbm, n_hbm, pr_hbm, mx_hbm, q_hbm, st_hbm, tl_hbm = rest[-18:-11]
    normed, pr, mx, q, sti, tl, xw, ldt, ss, g_ref, sem = rest[-11:]
    t = h.shape[0]
    half = t // 2
    slot = sc[row, SLOT]
    first = sc[row, FIRST] == 1
    leading = sc[row, LEADING] == 1
    core = sc[row, CORE]

    @pl.when(leading)
    def _():
        fetch(x_hbm, h, sem.at[0]).wait()

    @pl.when(jnp.logical_not(leading))
    def _():
        mine = h.at[pl.ds(aligned(core * half), half)]
        theirs = h.at[pl.ds(aligned((1 - core) * half), half)]
        copies = fetch(got_hbm, mine, sem.at[0]), fetch(other_hbm, theirs, sem.at[1])
        for copy in copies:
            copy.wait()

    stores = [fetch(h, h_hbm.at[slot], sem.at[0])]
    hf = h[...].astype(F32)
    r = lax.rsqrt(jnp.mean(hf * hf, axis=1, keepdims=True) + EPSILON)
    normed[...] = (hf * r * ng_ref[...]).astype(BF16)
    stores.append(fetch(normed, n_hbm.at[slot], sem.at[1]))

    sti[...] = jnp.where(first, 0.0, st_ref[...])
    tl[...] = jnp.where(first, 0.0, tail_ref[...])
    stores.append(fetch(sti, st_hbm.at[slot], sem.at[2]))
    stores.append(fetch(tl, tl_hbm.at[slot], sem.at[3]))
    xw[0:8, :] = tl[...]

    for at in range(0, OWN_PROJ, 512):
        cols = slice(at, min(at + 512, OWN_PROJ))
        pr[:, cols] = dot_nt(normed[...], win[cols, :]).astype(BF16)
    stores.append(fetch(pr, pr_hbm.at[slot], sem.at[4]))
    tail_out[...] = pr[t - 8 : t, X_AT : X_AT + OWN_CONV].astype(F32)

    bc = pl.ds(OWN, 2 * STATE)
    xw[8 : 8 + t, OWN:OWN_CONV] = pr[:, BC_AT:DT_AT].astype(F32)
    conv_bc = convolve(xw, bc, convp, t)
    act = (conv_bc * sigmoid(conv_bc)).astype(BF16)
    b, c = act[:, :STATE], act[:, STATE:]
    g_ref[...] = dot_nt(c, b)
    b_turned = act[:, :STATE].astype(F32).T.astype(BF16)
    dt, ld, _ = step_sizes(pr[:, DT_AT : DT_AT + LANES].astype(F32), headp[...])
    ldt[...] = ld.T
    left = lax.broadcasted_iota(jnp.int32, (t, LANES), 1) < HEAD_DIM
    ss[...] = jnp.zeros_like(ss)

    def pair_step(pair):
        at = pl.multiple_of(pair * LANES, LANES)
        sl = pl.ds(at, LANES)
        xw[8 : 8 + t, sl] = pr[:, pl.ds(X_AT + at, LANES)].astype(F32)
        conv = convolve(xw, sl, convp, t)
        x = conv * sigmoid(conv)
        cols = at_head(ld, pair)
        u = jnp.where(left, *at_head(dt, pair)) * x
        ld_p = jnp.where(left, *cols)
        top = jnp.zeros((half, LANES), F32)
        bottom = top
        for i in range(2):
            u_i = jnp.where(left if i == 0 else jnp.logical_not(left), u, 0.0).astype(BF16)
            d00, d10, d11 = decay_blocks(cols[i], ldt[pl.ds(2 * pair + i, 1), :], False)
            m00 = (g_ref[:half, :half] * d00).astype(BF16)
            m10 = (g_ref[half:, :half] * d10).astype(BF16)
            m11 = (g_ref[half:, half:] * d11).astype(BF16)
            top = top + dot(m00, u_i[:half])
            bottom = bottom + dot(jnp.concatenate([m10, m11], axis=1), u_i)
        eld = jnp.exp(ld_p)
        st = sti[:, sl]
        y = jnp.concatenate([top, bottom], axis=0) + eld * dot(c, st.astype(BF16))
        weighted = (u * jnp.exp(ld_p[t - 1 : t] - ld_p)).astype(BF16)
        st_out[:, sl] = eld[t - 1 : t] * st + dot(b_turned, weighted)
        mixed = y + chanp[0:1, sl] * x
        mx[:, sl] = mixed
        z = pr[:, sl].astype(F32)
        gated = mixed * (z * sigmoid(z))
        ss[...] += gated * gated
        q[:, sl] = (gated * chanp[1:2, sl]).astype(BF16)

    pair_loop(pair_step)
    stores.append(fetch(mx, mx_hbm.at[slot], sem.at[5]))
    stores.append(fetch(q, q_hbm.at[slot], sem.at[6]))
    total = jnp.sum(ss[...], axis=1, keepdims=True)
    high = total.astype(BF16).astype(F32)
    lane = lax.broadcasted_iota(jnp.int32, (t, LANES), 1)
    p[:, D:] = jnp.where(lane == 0, high, jnp.where(lane == 1, total - high, 0.0)).astype(BF16)
    for at in range(0, D, 512):
        p[:, at : at + 512] = dot(q[...], wout[:, at : at + 512]).astype(BF16)
    for store in stores:
        store.wait()


def backward_kernel(row, sc, *refs):
    acc_ref, acc_out = refs[15], refs[-20]

    @pl.when(sc[row, VALID] == 1)
    def _():
        backward_chunk(row, sc, *refs)

    @pl.when(sc[row, VALID] == 0)
    def _():
        acc_out[...] = acc_ref[...]


def backward_chunk(
    row,
    sc,
    arrived_hbm,
    cot_hbm,
    h_hbm,
    pr_hbm,
    mx_hbm,
    st_hbm,
    tl_hbm,
    y_hbm,
    ri_hbm,
    convp,
    headp,
    chanp,
    dst_ref,
    dc_ref,
    val_ref,
    acc_ref,
    win,
    wout,
    *rest,
):
    gn, g_ref, h_out, dst_out, dc_out, val_out, acc_out, gp_hbm, gs_hbm = rest[-26:-17]
    pr, mx, st_ref, tl, y_ref, ri, gp, gs = rest[-17:-9]
    xw, dw, ldt, gw, gt, dgt, dci, dbi, sem = rest[-9:]
    t = g_ref.shape[0]
    half = t // 2
    slot = sc[row, SLOT]
    last = sc[row, FIRST] == 1
    g_copy = fetch_one_of(sc[row, LEADING] == 1, arrived_hbm, cot_hbm, g_ref, sem.at[0])
    y_copy = fetch(y_hbm.at[slot], y_ref, sem.at[1])
    ri_copy = fetch(ri_hbm.at[slot], ri, sem.at[2])
    pr_copy = fetch(pr_hbm.at[slot], pr, sem.at[3])
    tl_copy = fetch(tl_hbm.at[slot], tl, sem.at[4])
    mx_copy = fetch(mx_hbm.at[slot], mx, sem.at[5])
    st_copy = fetch(st_hbm.at[slot], st_ref, sem.at[6])
    h_copy = fetch(h_hbm.at[slot], h_out, sem.at[8])

    acc_out[...] = acc_ref[...]
    dw[t : t + 8, :] = jnp.where(last, 0.0, dc_ref[...])
    dgt[...] = jnp.zeros_like(dgt)
    dci[...] = jnp.zeros_like(dci)
    dbi[...] = jnp.zeros_like(dbi)
    g_copy.wait()
    for at in range(0, OWN, 512):
        gw[:, at : at + 512] = dot_nt(g_ref[...], wout[at : at + 512, :])
    y_copy.wait()
    ri_copy.wait()
    rinv = ri[:, 0:1]
    mean = jnp.sum(g_ref[...].astype(F32) * y_ref[...].astype(F32), axis=1, keepdims=True)
    lean = rinv * rinv * (mean * (1.0 / INNER))
    gs[...] = (g_ref[...].astype(F32) * rinv).astype(BF16)
    gs_store = fetch(gs, gs_hbm.at[sc[row, WRITE]], sem.at[7])
    pr_copy.wait()
    tl_copy.wait()
    xw[0:8, :] = tl[...]

    bc = pl.ds(OWN, 2 * STATE)
    xw[8 : 8 + t, OWN:OWN_CONV] = pr[:, BC_AT:DT_AT].astype(F32)
    conv_bc = convolve(xw, bc, convp, t)
    sig_bc = sigmoid(conv_bc)
    act = (conv_bc * sig_bc).astype(BF16)
    b, c = act[:, :STATE], act[:, STATE:]
    c_turned = c.astype(F32).T.astype(BF16)
    gt[...] = dot_nt(b, c)
    dt, ld, biased = step_sizes(pr[:, DT_AT : DT_AT + LANES].astype(F32), headp[...])
    ldt[...] = ld.T
    left = lax.broadcasted_iota(jnp.int32, (t, LANES), 1) < HEAD_DIM

    def add(line, sl, v):
        acc_out[line : line + 1, sl] += v

    def conv_back(dact, conv, sig, sl):
        dconv = dact * (sig * (1.0 + conv * (1.0 - sig)))
        dw[0:t, sl] = dconv
        add(4, sl, jnp.sum(dconv, axis=0, keepdims=True))
        for k in range(KERNEL):
            add(k, sl, jnp.sum(dconv * xw[5 + k : 5 + k + t, sl], axis=0, keepdims=True))
        dx = dconv * convp[KERNEL - 1 : KERNEL, sl]
        for k in range(KERNEL - 1):
            ahead = KERNEL - 1 - k
            dx = dx + dw[ahead : ahead + t, sl] * convp[k : k + 1, sl]
        return dx.astype(BF16)

    lane_head = lax.rem(lax.broadcasted_iota(jnp.int32, (2 * LANES, LANES), 0), LANES) // HEAD_DIM
    head_lane = lax.broadcasted_iota(jnp.int32, (2 * LANES, LANES), 1)
    mx_copy.wait()
    st_copy.wait()

    def pair_step(pair, carry):
        ddt, dld, dval = carry
        at = pl.multiple_of(pair * LANES, LANES)
        sl = pl.ds(at, LANES)
        xsl = pl.ds(X_AT + at, LANES)
        xw[8 : 8 + t, sl] = pr[:, xsl].astype(F32)
        conv = convolve(xw, sl, convp, t)
        sig = sigmoid(conv)
        x = conv * sig
        z = pr[:, sl].astype(F32)
        sig_z = sigmoid(z)
        s = z * sig_z
        mixed = mx[:, sl]
        gated = mixed * s
        scaled = gw[:, sl] * rinv
        add(6, sl, jnp.sum(scaled * gated, axis=0, keepdims=True))
        dgated = chanp[1:2, sl] * scaled - gated * lean
        dy = dgated * s
        gp[:, sl] = (dgated * mixed * (sig_z * (1.0 + z * (1.0 - sig_z)))).astype(BF16)
        skip = chanp[0:1, sl]
        add(5, sl, jnp.sum(dy * x, axis=0, keepdims=True))
        y = mixed - skip * x

        cols = at_head(ld, pair)
        ld_p = jnp.where(left, *cols)
        eld = jnp.exp(ld_p)
        wend = jnp.exp(ld_p[t - 1 : t] - ld_p)
        dt_p = jnp.where(left, *at_head(dt, pair))
        u = dt_p * x
        u_low = u.astype(BF16)
        dy_low = dy.astype(BF16)
        dst = jnp.where(last, 0.0, dst_ref[:, sl])
        dst_low = dst.astype(BF16)
        top = jnp.zeros((half, LANES), F32)
        bottom = top
        for i in range(2):
            side = left if i == 0 else jnp.logical_not(left)
            d00, d01, d11 = decay_blocks(cols[i], ldt[pl.ds(2 * pair + i, 1), :], True)
            m00 = (gt[:half, :half] * d00).astype(BF16)
            m01 = (gt[:half, half:] * d01).astype(BF16)
            m11 = (gt[half:, half:] * d11).astype(BF16)
            dy_i = jnp.where(side, dy, 0.0).astype(BF16)
            top = top + dot(jnp.concatenate([m00, m01], axis=1), dy_i)
            bottom = bottom + dot(m11, dy_i[half:])
            u_i = jnp.where(side, u, 0.0).astype(BF16)
            dm = dot_nt(u_i[:half], dy_low)
            dgt[:half, :half] += dm[:, :half] * d00
            dgt[:half, half:] += dm[:, half:] * d01
            dgt[half:, half:] += dot_nt(u_i[half:], dy_low[half:]) * d11
        du = jnp.concatenate([top, bottom], axis=0) + wend * dot(b, dst_low)
        st = st_ref[:, sl]
        dyl = (eld * dy).astype(BF16)
        dst_new = eld[t - 1 : t] * dst + dot(c_turned, dyl)
        dst_out[:, sl] = dst_new
        val_out[:, sl] = jnp.broadcast_to(
            jnp.sum(dst_new * st, axis=0, keepdims=True), (8, LANES)
        )
        dci[...] += dot_nt(dyl, st.astype(BF16))
        dbi[...] += dot_nt((wend * u).astype(BF16), dst_low)

        pick = jnp.where(lane_head + 2 * pair == head_lane, 1.0, 0.0).astype(BF16)


        def by_head(v):
            return dot(jnp.concatenate(split(v, 2), axis=1), pick)

        ddt = ddt + by_head(du * x)
        dld = dld + by_head(dy_low.astype(F32) * y - u_low.astype(F32) * du)
        dval = dval + by_head(jnp.where(last, 0.0, val_ref[:, sl]))
        gp[:, xsl] = conv_back(dt_p * du + skip * dy, conv, sig, sl)
        return ddt, dld, dval

    zero = jnp.zeros((t, LANES), F32)
    ddt, dld, dval = lax.fori_loop(
        0,
        PAIRS // 2,
        lambda turn, carry: pair_step(2 * turn + 1, pair_step(2 * turn, carry)),
        (zero, zero, jnp.zeros((8, LANES), F32)),
    )

    dgt_low = dgt[...].astype(BF16)
    db = dbi[...] + dot(dgt_low, c)
    dc = dci[...] + dot_tn(dgt_low, b)
    gp[:, BC_AT:DT_AT] = conv_back(jnp.concatenate([db, dc], axis=1), conv_bc, sig_bc, bc)

    rows = lax.broadcasted_iota(jnp.int32, (t, t), 0)
    cols = lax.broadcasted_iota(jnp.int32, (t, t), 1)
    upper = jnp.where(rows <= cols, 1.0, 0.0).astype(BF16)
    da = sum(dot(upper, part) for part in split(dld, 3)) + dval[0:1]
    rate = headp[1:2]
    head = pl.ds(0, LANES)
    add(8, head, jnp.sum(da * rate * dt, axis=0, keepdims=True))
    ddt_raw = (ddt + rate * da) * sigmoid(biased)
    add(7, head, jnp.sum(ddt_raw, axis=0, keepdims=True))
    gp[:, DT_AT : DT_AT + LANES] = ddt_raw.astype(BF16)
    gp[:, DT_AT + LANES :] = jnp.zeros((t, LANES), BF16)
    gp_store = fetch(gp, gp_hbm.at[sc[row, WRITE]], sem.at[0])
    dc_out[...] = dw[0:8, :]
    for at in range(0, D, 512):
        gn[:, at : at + 512] = dot(gp[...], win[:, at : at + 512]).astype(BF16)
    gp_store.wait()
    gs_store.wait()
    h_copy.wait()


def forward_join_kernel(row, sc, own_ref, other_ref, h_ref, *rest):
    out, y_hbm, ri_hbm, e_hbm, y_v, ri_v, low_v, sem = rest[-8:]
    half = out.shape[0]

    @pl.when(sc[row, VALID] == 1)
    def _():
        copies = []
        for k in range(2):
            rows = slice(k * half, (k + 1) * half)
            total = own_ref[rows].astype(F32) + other_ref[rows].astype(F32)
            square = total[:, D : D + 1] + total[:, D + 1 : D + 2]
            rinv = lax.rsqrt(square * (1.0 / INNER) + EPSILON)
            y = total[:, :D] * rinv
            y_v[rows] = y.astype(BF16)
            ri_v[rows] = jnp.broadcast_to(rinv, (half, LANES))
            low_v[rows] = (h_ref[rows].astype(F32) + y).astype(BF16)
            pieces = ((y_v, y_hbm, SLOT), (ri_v, ri_hbm, SLOT), (low_v, e_hbm, EDGE))
            for near_ref, far_ref, which in pieces:
                target = far_ref.at[sc[row, which], pl.ds(k * half, half)]
                copies.append(fetch(near_ref.at[pl.ds(k * half, half)], target, sem.at[len(copies)]))
        out[...] = low_v[pl.ds(aligned(sc[row, CORE] * half), half), :]
        for copy in copies:
            copy.wait()


def backward_join_kernel(row, sc, own_ref, other_ref, h_ref, g_ref, ng_ref, dng_ref, *rest):
    out, dng_out, e_hbm, sem = rest[-4:]
    half = out.shape[0] // 2
    dng_out[...] = dng_ref[...]

    @pl.when(sc[row, VALID] == 1)
    def _():
        copies = []
        for k in range(2):
            rows = slice(k * half, (k + 1) * half)
            gn = own_ref[rows].astype(F32) + other_ref[rows].astype(F32)
            h = h_ref[rows].astype(F32)
            r = lax.rsqrt(jnp.mean(h * h, axis=1, keepdims=True) + EPSILON)
            t = gn * ng_ref[...]
            m = jnp.mean(h * t, axis=1, keepdims=True)
            out[rows] = (g_ref[rows].astype(F32) + r * (t - h * (r * r * m))).astype(BF16)
            target = e_hbm.at[sc[row, EDGE], pl.ds(k * half, half)]
            copies.append(fetch(out.at[pl.ds(k * half, half)], target, sem.at[k]))
            dng_out[...] += jnp.sum(gn * h * r, axis=0, keepdims=True)
        for copy in copies:
            copy.wait()


def pick_kernel(first, sc, stack_hbm, out, sem):
    fetch(stack_hbm.at[first + sc[0, CORE]], out, sem.at[0]).wait()


ANY = pl.BlockSpec(memory_space=pl.ANY)
NEAR = pl.BlockSpec(memory_space=pltpu.VMEM)
SLOT, LEADING, FIRST, VALID, WRITE, EDGE, CORE = range(7)
LITTLE = pl.CostEstimate(flops=1 << 20, bytes_accessed=1 << 16, transcendentals=0)


def near(value):
    return pltpu.with_memory_space_constraint(value, pltpu.VMEM)


def away(value):
    return pltpu.with_memory_space_constraint(value, pltpu.HBM)


def chunk_call(kernel, table, free, far, close, close_outs, buffers, scratch, limit, name):
    inputs = [table, *free, *(away(v) for v in far), *(near(v) for v in close)]
    in_specs = [pl.BlockSpec(memory_space=pltpu.SMEM)]
    in_specs += [ANY] * (len(free) + len(far)) + [NEAR] * len(close)
    outs = [pltpu.VMEM(*o) for o in close_outs]
    out_specs = [NEAR] * len(close_outs)
    aliases = {}
    for held, shape, dtype in buffers:
        if held is not None:
            aliases[len(inputs)] = len(outs)
            inputs.append(away(held))
            in_specs.append(ANY)
        outs.append(pltpu.HBM(shape, dtype))
        out_specs.append(ANY)
    results = pl.pallas_call(
        kernel,
        in_specs=in_specs,
        out_specs=out_specs,
        out_shape=outs,
        scratch_shapes=scratch,
        input_output_aliases=aliases,
        compiler_params=pltpu.CompilerParams(vmem_limit_bytes=limit << 20),
        cost_estimate=LITTLE,
        name=name,
    )(*inputs)
    return tuple(results[: len(close_outs)]), tuple(results[len(close_outs) :])


def forward_call(table, row, slots, x, arrived, params, carry, held):
    t = x.shape[0]
    held = held or (None,) * 7
    kinds = (
        ((t, D), BF16),
        ((t, D), BF16),
        ((t, OWN_PROJ), BF16),
        ((t, OWN), F32),
        ((t, OWN), BF16),
        ((STATE, OWN), F32),
        ((8, OWN_CONV), F32),
    )
    gain, convp, headp, chanp, win, wout = params
    outs, held = chunk_call(
        functools.partial(forward_kernel, row),
        table,
        (*arrived, x),
        (),
        (gain, convp, headp, chanp, *carry, win, wout),
        (((t, D + LANES), BF16), kinds[0], kinds[5], kinds[6]),
        [(b, (slots,) + k, d) for b, (k, d) in zip(held, kinds)],
        [pltpu.VMEM(*k) for k in kinds[1:]]
        + [
            pltpu.VMEM((t + 8, OWN_CONV), F32),
            pltpu.VMEM((LANES, t), F32),
            pltpu.VMEM((t, LANES), F32),
            pltpu.VMEM((t, t), F32),
            pltpu.SemaphoreType.DMA((8,)),
        ],
        FORWARD_VMEM,
        "forward_chunk",
    )
    return outs[0], outs[1], outs[2:], held


def backward_call(table, row, slots, cot, arrived, saved, params, carry, held):
    t = arrived.shape[0]
    held = held or (None, None)
    _, convp, headp, chanp, win, wout = params
    wide, projected = ((t, D), BF16), ((t, OWN_PROJ), BF16)
    outs, held = chunk_call(
        functools.partial(backward_kernel, row),
        table,
        (arrived, cot),
        saved,
        (convp, headp, chanp, *carry, win, wout),
        [wide] * 3 + [(v.shape, v.dtype) for v in carry],
        [(held[0], (slots, t, OWN_PROJ), BF16), (held[1], (slots, t, D), BF16)],
        [
            pltpu.VMEM(*projected),
            pltpu.VMEM((t, OWN), F32),
            pltpu.VMEM((STATE, OWN), F32),
            pltpu.VMEM((8, OWN_CONV), F32),
            pltpu.VMEM(*wide),
            pltpu.VMEM((t, LANES), F32),
            pltpu.VMEM(*projected),
            pltpu.VMEM(*wide),
            pltpu.VMEM((t + 8, OWN_CONV), F32),
            pltpu.VMEM((t + 8, OWN_CONV), F32),
            pltpu.VMEM((LANES, t), F32),
            pltpu.VMEM((t, OWN), F32),
            pltpu.VMEM((t, t), F32),
            pltpu.VMEM((t, t), F32),
            pltpu.VMEM((t, STATE), F32),
            pltpu.VMEM((t, STATE), F32),
            pltpu.SemaphoreType.DMA((9,)),
        ],
        BACKWARD_VMEM,
        "backward_chunk",
    )
    return outs[:3], outs[3:], held


def forward_join(table, row, slots, own, other, h, held):
    t = h.shape[0]
    held = held or (None,) * 3
    wide, thin = ((t, D), BF16), ((t, LANES), F32)
    outs, held = chunk_call(
        functools.partial(forward_join_kernel, row),
        table,
        (),
        (),
        (own, other, h),
        [((t // 2, D), BF16)],
        [(b, (slots,) + k, d) for b, (k, d) in zip(held, (wide, thin, wide))],
        [pltpu.VMEM(*k) for k in (wide, thin, wide)] + [pltpu.SemaphoreType.DMA((6,))],
        JOIN_VMEM,
        "forward_join",
    )
    return outs[0], held


def backward_join(table, row, own, other, h, g, gain, dng, edge_held):
    slots = edge_held.shape[0]
    wide = (h.shape, BF16)
    outs, held = chunk_call(
        functools.partial(backward_join_kernel, row),
        table,
        (),
        (),
        (own, other, h, g, gain, dng),
        [wide, ((1, D), F32)],
        [(edge_held, (slots,) + h.shape, BF16)],
        [pltpu.SemaphoreType.DMA((2,))],
        JOIN_VMEM,
        "backward_join",
    )
    return outs[0], outs[1], held[0]


def pick(table, stack, first):
    outs, _ = chunk_call(
        functools.partial(pick_kernel, first),
        table,
        (),
        (stack,),
        (),
        [(stack.shape[1:], stack.dtype)],
        [],
        [pltpu.SemaphoreType.DMA((1,))],
        JOIN_VMEM,
        "pick",
    )
    return outs[0]


def own_of(values, core):
    lead, width = values.shape[:-1], values.shape[-1]
    blocks = values.reshape(lead + (4, 2, width // 8))
    return lax.dynamic_index_in_dim(blocks, core, len(lead) + 1, False).reshape(
        lead + (width // 2,)
    )


def woven(halves):
    width = halves.shape[-1]
    lead = halves.shape[1:-1]
    blocks = halves.reshape((2,) + lead + (4, width // 4))
    return jnp.moveaxis(blocks, 0, -2).reshape(lead + (2 * width,))


def small_params(norm_gain, conv_weight, conv_bias, dt_bias, a_log, skip_gain, gate_gain, core):
    own = functools.partial(own_of, core=core)
    taps = jnp.concatenate([conv_weight.T, conv_bias[None]], axis=0).astype(F32)
    taps = jnp.concatenate([own(taps[:, :INNER]), taps[:, INNER:]], axis=1)
    convp = jnp.pad(taps, ((0, 3), (0, 0)))
    heads = jnp.stack([own(dt_bias.astype(F32)), -jnp.exp(own(a_log.astype(F32)))])
    headp = jnp.pad(heads, ((0, 6), (0, LANES - OWN_HEADS)))
    skip = jnp.repeat(own(skip_gain.astype(F32)), HEAD_DIM)
    chanp = jnp.pad(jnp.stack([skip, own(gate_gain.astype(F32))]), ((0, 6), (0, 0)))
    return norm_gain.astype(F32)[None], convp, headp, chanp


def own_steps(weight, core):
    own = own_of(weight[INNER + CONV_CH :].T, core).T
    return jnp.pad(own, ((0, 2 * LANES - OWN_HEADS), (0, 0)))


HALF = OWN // 2
BLOCK = HALF // 2
PACKED_ROWS = HALF + HALF + 2 * STATE + 2 * BLOCK
PARTS = (
    ("in", HALF, X_AT, HALF),
    ("in", HALF, 0, HALF),
    ("in", 2 * STATE, BC_AT, 2 * STATE),
    ("out", BLOCK, 0, HALF),
    ("out", BLOCK, BLOCK, HALF),
)


def ring_place(position, count):
    back = position >= count
    return jnp.where(back, 1, 0), jnp.where(back, 2 * count - 1 - position, position)


def ring_route(count, step):
    def index(position):
        return position if position < count else count + (2 * count - 1 - position)

    size = 2 * count
    return [(index(p), index((p + step) % size)) for p in range(size)]


def pack_kernel(sc, w, steps, o, own, rest, sem):
    core, side = sc[0], sc[1]
    copies = []
    for target, y in ((own, side), (rest, 1 - side)):
        at = 0

        def put(source, rows):
            span = target.at[pl.ds(at, rows)]
            copies.append(fetch(source, span, sem.at[len(copies)]))

        for base in (INNER, 0):
            for k in range(2):
                first = aligned(base + (2 * y + k) * HALF + core * BLOCK)
                put(w.at[pl.ds(first, BLOCK)], BLOCK)
                at += BLOCK
        bc = w.at[pl.ds(2 * INNER, 2 * STATE)]
        span = target.at[pl.ds(at, 2 * STATE)]
        copies.append(fetch_one_of(y == 0, bc, steps, span, sem.at[len(copies)]))
        at += 2 * STATE
        for k in range(2):
            cols = pl.ds(aligned(y * HALF + k * BLOCK), BLOCK)
            put(o.at[pl.ds(aligned(core * BLOCK), BLOCK), cols], BLOCK)
            at += BLOCK
    for copy in copies:
        copy.wait()


def pack_weights(scalars, w, steps, o):
    return pl.pallas_call(
        pack_kernel,
        in_specs=[pl.BlockSpec(memory_space=pltpu.SMEM), ANY, ANY, ANY],
        out_specs=[NEAR, NEAR],
        out_shape=[pltpu.VMEM((PACKED_ROWS, BLOCK), BF16)] * 2,
        scratch_shapes=[pltpu.SemaphoreType.DMA((14,))],
        compiler_params=pltpu.CompilerParams(vmem_limit_bytes=4 << 20),
        cost_estimate=LITTLE,
        name="pack_weights",
    )(scalars, away(w), steps, away(o))


def place_kernel(sc, own, rest, *refs):
    (near_z, inner_2, outer_2, inner_3, outer_3), (win, wout, sem) = (
        [refs[2 * i : 2 * i + 2] for i in range(5)],
        refs[-3:],
    )
    side, place = sc[1], sc[2]
    inner = jnp.logical_and(place > 0, place < 3)
    second = jnp.where(inner, 3 - place, jnp.where(place == 0, 2, 1))
    third = jnp.where(place < 2, 3, 0)
    used = []

    def put(source, z, y, start):
        lanes = pl.ds(aligned(z * BLOCK), BLOCK)
        at = 0
        for k, (matrix, rows, first, step) in enumerate(PARTS):
            if matrix == "in":
                target = win.at[pl.ds(aligned(first + y * step), rows), lanes]
            else:
                target = wout.at[lanes, pl.ds(aligned(first + y * step), BLOCK)]
            copy = pltpu.make_async_copy(source.at[pl.ds(at, rows)], target, sem.at[start + k])
            copy.start()
            used.append(copy)
            at += rows

    put(own, place, side, 0)
    put(rest, place, 1 - side, 5)
    put(near_z[0], place + 1 - 2 * lax.rem(place, 2), side, 10)
    put(near_z[1], place + 1 - 2 * lax.rem(place, 2), 1 - side, 15)
    waits = list(used)

    @pl.when(inner)
    def _():
        put(inner_2[0], second, side, 20)
        put(inner_2[1], second, 1 - side, 25)
        put(inner_3[0], third, side, 30)
        put(inner_3[1], third, 1 - side, 35)
        for copy in used[20:]:
            copy.wait()
        del used[20:]

    @pl.when(jnp.logical_not(inner))
    def _():
        put(outer_2[0], second, side, 20)
        put(outer_2[1], second, 1 - side, 25)
        put(outer_3[0], third, side, 30)
        put(outer_3[1], third, 1 - side, 35)
        for copy in used[20:]:
            copy.wait()

    for copy in waits:
        copy.wait()


def place_weights(here, own, rest, pairs):
    inputs = [own, rest, *sum(pairs, ())]
    return pl.pallas_call(
        place_kernel,
        in_specs=[pl.BlockSpec(memory_space=pltpu.SMEM)] + [ANY] * len(inputs),
        out_specs=[NEAR, NEAR],
        out_shape=[pltpu.VMEM((OWN_PROJ, D), BF16), pltpu.VMEM((OWN, D), BF16)],
        scratch_shapes=[pltpu.SemaphoreType.DMA((40,))],
        compiler_params=pltpu.CompilerParams(vmem_limit_bytes=4 << 20),
        cost_estimate=LITTLE,
        name="place_weights",
    )(here, *inputs)


def line_gather(own, beside):
    def along(value, hops):
        route = [(y * 4 + a, y * 4 + b) for y in range(2) for a, b in hops]
        return lax.ppermute(value, ("y", "fsdp"), route)

    def across(value, places):
        route = [(y * 4 + z, (1 - y) * 4 + z) for y in range(2) for z in places]
        return lax.ppermute(value, ("y", "fsdp"), route)

    outward, middle = [(1, 0), (2, 3)], [(1, 2), (2, 1)]
    near_z = along(own, [(0, 1), (1, 0), (2, 3), (3, 2)])
    inner_2 = along(own, middle)
    near_z, inner_2, *beside = lax.optimization_barrier((near_z, inner_2, *beside))
    outer_2 = along(inner_2, outward)
    inner_3 = along(near_z, middle)
    near_y = across(near_z, range(4))
    outer_2, inner_3, near_y = lax.optimization_barrier((outer_2, inner_3, near_y))
    outer_3 = along(inner_3, outward)
    outer_2_y = across(outer_2, (0, 3))
    inner_2_y = across(inner_2, (1, 2))
    ready = near_y
    outer_3, outer_2_y, inner_2_y = lax.optimization_barrier((outer_3, outer_2_y, inner_2_y))
    outer_3_y = across(outer_3, (0, 3))
    inner_3_y = across(inner_3, (1, 2))
    return [
        (near_z, near_y),
        (inner_2, inner_2_y),
        (outer_2, outer_2_y),
        (inner_3, inner_3_y),
        (outer_3, outer_3_y),
    ], ready, beside


GROUPS = (
    (1, (HALF, X_AT, HALF), (LANES, BC_AT, 2 * STATE)),
    (-1, (HALF, 0, HALF), (LANES, BC_AT + LANES, 2 * STATE)),
)


SMALL_ROWS = 16
IN_ROWS = HALF + LANES
GROUP_ROWS = IN_ROWS + BLOCK


def block_grad_kernel(row, sc, normed_ref, q_ref, gs_ref, *refs):
    out = refs[-1]
    chunks = normed_ref.shape[0]
    at = 0
    for ref in refs[:2]:
        width = ref.shape[2]
        out[at : at + width, :] = sum(dot_tn(ref[k], normed_ref[k]) for k in range(chunks))
        at += width
    out[at:, :] = sum(dot_tn(q_ref[k], gs_ref[k]) for k in range(chunks))
    if len(refs) > 3:

        @pl.when(sc[row, 0] == 1)
        def _():
            out[HALF : HALF + SMALL_ROWS, :] = refs[2][0]


def block_grad(table, row, group, normed_held, grads_held, q_held, gs_held, small):
    slots, t, _ = normed_held.shape
    number, (_, *parts) = group, GROUPS[group]

    def block(width, index):
        return pl.BlockSpec((slots - 1, t, width), lambda i, s: (0, 0, index(s)))

    in_specs = [
        block(BLOCK, lambda s: s[row, 1]),
        block(BLOCK, lambda s: s[row, 1]),
        block(BLOCK, lambda s: 2 * s[row, 0] + number),
    ]
    for width, first, step in parts:

        def index(s, width=width, first=first, step=step):
            return first // width + s[row, 0] * (step // width)

        in_specs.append(block(width, index))
    extra = []
    if number == 1:
        extra = [small]
        in_specs.append(pl.BlockSpec((1, SMALL_ROWS, BLOCK), lambda i, s: (s[row, 1], 0, 0)))
    return pl.pallas_call(
        functools.partial(block_grad_kernel, row),
        grid_spec=pltpu.PrefetchScalarGridSpec(
            num_scalar_prefetch=1,
            grid=(1,),
            in_specs=in_specs,
            out_specs=pl.BlockSpec((GROUP_ROWS, BLOCK), lambda i, s: (0, 0)),
        ),
        out_shape=jax.ShapeDtypeStruct((GROUP_ROWS, BLOCK), F32),
        compiler_params=pltpu.CompilerParams(vmem_limit_bytes=24 << 20),
        cost_estimate=LITTLE,
        name="block_grad",
    )(
        table,
        away(normed_held),
        away(q_held),
        away(gs_held),
        *([away(grads_held)] * len(parts)),
        *extra,
    )


def grads_kernel(sc, *refs):
    in_hbm, out_hbm, small_out, in_v, out_v, sem = refs[-6:]
    core, side = sc[0], sc[1]

    def block(i, c, y, rows):
        own, across, other = refs[3 * i : 3 * i + 3]
        here = jnp.where(side == y, own[rows], across[rows])
        there = jnp.where(side == y, other[0, rows], other[1, rows])
        return jnp.where(core == c, here, there).astype(F32)

    copies = []

    def store(values, near_ref, far_ref, at):
        near_ref[at : at + values.shape[0]] = values
        span = pl.ds(at, values.shape[0])
        copies.append(fetch(near_ref.at[span], far_ref.at[span], sem.at[len(copies)]))

    for i, base in ((0, INNER), (1, 0)):
        for c in range(2):
            for y in range(2):
                for k in range(2):
                    rows = slice(k * BLOCK, (k + 1) * BLOCK)
                    store(block(i, c, y, rows), in_v, in_hbm, base + (2 * y + k) * HALF + c * BLOCK)
    rows = slice(HALF, HALF + STATE)
    for i in range(2):
        store(block(i, 0, 0, rows) + block(i, 1, 0, rows), in_v, in_hbm, 2 * INNER + i * STATE)
    steps = [block(0, c, 1, slice(HALF, HALF + 32)) for c in range(2)]
    steps = [steps[c][z * 6 : z * 6 + 6] for z in range(4) for c in range(2)]
    store(jnp.concatenate(steps, axis=0), in_v, in_hbm, INNER + CONV_CH)
    rows = slice(HALF, HALF + SMALL_ROWS)
    small_out[...] = block(1, 0, 1, rows) + block(1, 1, 1, rows)
    rows = slice(IN_ROWS, GROUP_ROWS)
    for c in range(2):
        values = [block(i, c, y, rows) for y in range(2) for i in range(2)]
        store(jnp.concatenate(values, axis=1), out_v, out_hbm, c * BLOCK)
    for copy in copies:
        copy.wait()


def join_grads(scalars, parts):
    arrays = [near(a) for part in parts for a in part]
    height = INNER + CONV_CH + HEADS
    shapes = ((height, BLOCK), F32), ((2 * BLOCK, D), F32)
    return pl.pallas_call(
        grads_kernel,
        in_specs=[pl.BlockSpec(memory_space=pltpu.SMEM)] + [NEAR] * len(arrays),
        out_specs=[ANY, ANY, NEAR],
        out_shape=[pltpu.HBM(*k) for k in shapes] + [pltpu.VMEM((SMALL_ROWS, BLOCK), F32)],
        scratch_shapes=[pltpu.VMEM(*k) for k in shapes] + [pltpu.SemaphoreType.DMA((24,))],
        compiler_params=pltpu.CompilerParams(vmem_limit_bytes=28 << 20),
        cost_estimate=LITTLE,
        name="join_grads",
    )(scalars, *arrays)


def swap(value, axis):
    return lax.ppermute(value, axis, [(0, 1), (1, 0)])


def sent_along(value, axis):
    size = lax.axis_size(axis)
    routes = [[(i, (i + k) % size) for i in range(size)] for k in range(1, size)]
    return [lax.ppermute(value, axis, path) for path in routes]


def in_order(value, others, axis):
    size, place = len(others) + 1, lax.axis_index(axis)
    ring = jnp.stack([*others[::-1], value] * 2)
    return lax.dynamic_slice_in_dim(ring, (size - 1 - place) % size, size, 0)


LAG = 2


def relay_shards(
    ends,
    norm_gain,
    input_weight,
    conv_weight,
    conv_bias,
    dt_bias,
    a_log,
    skip_gain,
    gate_gain,
    output_weight,
):
    core = lax.axis_index("core")
    place = lax.axis_index("fsdp")
    side = lax.axis_index("y")
    section = lax.axis_index("section")
    leading = (section == 0).astype(jnp.int32)
    local = ends[0][:, 0]
    t = local.shape[1]
    chunks = lax.axis_size("fsdp")
    micro = place // 2

    small = [norm_gain[0], conv_weight[0].reshape(-1), conv_bias[0], dt_bias[0], a_log[0]]
    small += [skip_gain[0], gate_gain[0]]
    packed = jnp.concatenate(small)
    others = sent_along(packed, "fsdp")
    w = input_weight[0].T
    steps = own_steps(w, core)
    here = jnp.stack([core, side, place]).astype(jnp.int32)
    own, rest = pack_weights(here, w, steps, output_weight[0])
    pairs, ready, others = line_gather(own, others)
    packed = in_order(packed, others, "fsdp")
    pieces, at = [], 0
    for member in small:
        pieces.append(packed[:, at : at + member.shape[0]].reshape(-1))
        at += member.shape[0]
    pieces[1] = pieces[1].reshape(CONV_CH, KERNEL)
    gain, convp, headp, chanp = small_params(*pieces, core)
    local, _ = lax.optimization_barrier((local, ready))

    def route(first, m):
        return [
            (c * chunks + z, (z % 2) * chunks + 2 * m + c)
            for c in range(2)
            for z in (first, first + 1)
        ]

    def bring(first):
        return [lax.ppermute(local[m], ("core", "fsdp"), route(first, m)) for m in range(2)]

    def shared(got):
        got = jnp.where(micro == 0, got[0], got[1])
        other = swap(got, "core")
        return [jnp.where(core == 0, got, other), jnp.where(core == 0, other, got)]

    def give(piece, first):
        return [
            lax.ppermute(piece, ("core", "fsdp"), [(b, a) for a, b in route(first, m)])
            for m in range(2)
        ]

    here, *got = lax.optimization_barrier((here, *bring(0), *bring(2)))
    pieces = shared(got[:2]) + shared(got[2:])
    win, wout = place_weights(here, own, rest, pairs)
    params = (gain, convp, headp, chanp, win, wout)

    def scalars(moment, lag, reverse):
        begin = jnp.where(leading == 1, lag if reverse else 0, 0 if reverse else lag)
        step = moment - begin
        valid = jnp.logical_and(step >= 0, step < chunks)
        inside = jnp.clip(step, 0, chunks - 1)
        chunk = chunks - 1 - inside if reverse else inside
        write = jnp.where(valid, chunk, chunks)
        edge_here = leading == 1 if reverse else leading == 0
        edge = jnp.where(jnp.logical_and(valid, edge_here), chunk, chunks)
        values = [chunk if reverse else write, leading, step == 0, valid, write, edge, core]
        return [jnp.asarray(v, jnp.int32) for v in values]

    moments = chunks + LAG
    table = [scalars(moment, LAG, False) for moment in range(moments)]
    table += [scalars(moment, LAG, True) for moment in range(moments)]
    table = jnp.stack(sum(table, [])).reshape(len(table), -1)

    state, tail = jnp.zeros((STATE, OWN), F32), jnp.zeros((8, OWN_CONV), F32)
    blank = jnp.zeros((t, D), BF16)
    held, joined, result = None, None, None
    moved, incoming = {}, {}
    for moment in range(moments):
        if moment > 0:
            tail, result = lax.optimization_barrier((tail, result))
            if moment - 1 < chunks:
                moved[moment - 1] = lax.ppermute(result, "section", [(0, 1)])
        arrived = incoming.get(moment - LAG, (blank[: t // 2],) * 2)
        partial, h, (state, tail), held = forward_call(
            table,
            moment,
            chunks + 1,
            pieces[min(moment, chunks - 1)],
            arrived,
            params,
            (state, tail),
            held,
        )
        if moment - 1 in moved:
            partial, got = lax.optimization_barrier((partial, moved[moment - 1]))
            incoming[moment - 1] = (got, swap(got, "core"))
        other = swap(partial, "core")
        result, joined = forward_join(table, moment, chunks + 1, partial, other, h, joined)
    h_held, normed_held, pr_held, mx_held, q_held, st_held, tl_held = held
    y_held, ri_held, edge_held = joined
    saved = (h_held, pr_held, mx_held, st_held, tl_held, y_held, ri_held)

    def tokens(buffer):
        return buffer[:chunks].reshape(chunks * t, buffer.shape[-1])

    carry = (
        jnp.zeros((STATE, OWN), F32),
        jnp.zeros((8, OWN_CONV), F32),
        jnp.zeros((8, OWN), F32),
        jnp.zeros((16, OWN_CONV), F32),
    )
    dng = jnp.zeros((1, D), F32)
    grads_held, edges_late = None, None
    incoming = {}
    for moment in range(moments):
        if moment > 0:
            *carry, acc = carry
            acc, result = lax.optimization_barrier((acc, result))
            if moment == moments - 1:
                acc, edges_late = lax.optimization_barrier((acc, edges_late))
            carry = (*carry, acc)
            if moment - 1 < chunks:
                incoming[moment - 1] = lax.ppermute(result, "section", [(1, 0)])
        arrived = incoming.get(moment - LAG, blank)
        cot = pieces[max(chunks - 1 - moment, 0)]
        (partial, g, h), carry, grads_held = backward_call(
            table, moments + moment, chunks + 1, cot, arrived, saved, params, carry, grads_held
        )
        if moment - 1 in incoming:
            partial, incoming[moment - 1] = lax.optimization_barrier(
                (partial, incoming[moment - 1])
            )
        other = swap(partial, "core")
        result, dng, edge_held = backward_join(
            table, moments + moment, partial, other, h, g, gain, dng, edge_held
        )
        if moment == LAG + 1:
            edges_late = give(pick(table, edge_held, 2), 2)

    def both(own, other, index):
        return jnp.where(index == 0, jnp.stack([own, other]), jnp.stack([other, own]))

    acc = carry[3]

    def placed(own):
        zero = jnp.zeros_like(own)
        return woven(both(own, zero, core))

    taps = jnp.concatenate([placed(acc[:5, :OWN]), acc[:5, OWN:]], axis=1)
    taps = jnp.moveaxis(taps.reshape(KERNEL + 1, chunks, -1), 1, 0)
    skip = acc[5, :OWN].reshape(OWN_HEADS, HEAD_DIM).sum(axis=1)
    vectors = [
        jnp.where(core == 0, dng[0], 0.0),
        taps,
        placed(acc[7, :OWN_HEADS]),
        placed(acc[8, :OWN_HEADS]),
        placed(skip),
        placed(acc[6, :OWN]),
    ]
    vectors = [v.reshape(chunks, -1) for v in vectors]
    small = jnp.concatenate(vectors, axis=1)
    small = jnp.pad(small, ((0, 0), (0, SMALL_ROWS * BLOCK - small.shape[1])))
    small = small.reshape(chunks, SMALL_ROWS, BLOCK)

    size = 2 * chunks
    onward, back = ring_route(chunks, 1), ring_route(chunks, -1)
    position = jnp.where(side == 0, place, size - 1 - place).astype(jnp.int32)
    owners = []
    for direction in (1, -1):
        for hop in range(size):
            owners += ring_place((position - direction * (1 + hop)) % size, chunks)
    owners = jnp.stack(owners).reshape(2 * size, 2).astype(jnp.int32)
    grads_held, gs_held = grads_held
    sums = [None] * len(GROUPS)
    for hop in range(size):
        if hop > 0:
            owners, *sums = lax.optimization_barrier((owners, *sums))
        for i, (direction, *_) in enumerate(GROUPS):
            row = hop + (0 if direction == 1 else size)
            block = block_grad(owners, row, i, normed_held, grads_held, q_held, gs_held, small)
            if hop > 0:
                path = onward if direction == 1 else back
                block = block + lax.ppermute(sums[i], ("y", "fsdp"), path).astype(F32)
            sums[i] = block.astype(BF16)
        if hop == 3:
            owners, edge_last = lax.optimization_barrier((owners, pick(table, edge_held, 0)))
    *sums, edge_last = lax.optimization_barrier((*sums, edge_last))

    edges = jnp.where(place < 2, jnp.stack(give(edge_last, 0)), jnp.stack(edges_late))
    edges = edges[None, :, None]
    parts = []
    for i, own in enumerate(sums):
        across = swap(own, "y")
        if i == 1:
            across, edges = lax.optimization_barrier((across, edges))
        parts.append((own, across, swap(jnp.stack([own, across]), "core")))
    here = jnp.stack([core, side]).astype(jnp.int32)
    in_grad, out_grad, summed = join_grads(here, parts)
    in_grad = in_grad.T
    summed = summed.reshape(-1)
    grads, at = [], 0
    for v in vectors:
        grads.append(summed[at : at + v.shape[1]][None])
        at += v.shape[1]
    taps = grads[1].reshape(KERNEL + 1, -1)
    grads[1:2] = taps[:KERNEL].T[None], taps[KERNEL:]
    return (
        edges,
        grads[0],
        in_grad[None],
        grads[1],
        grads[2],
        grads[3],
        grads[4],
        grads[5],
        grads[6],
        out_grad[None],
    )


def shifted(block, axis, distance):
    devices = range(lax.axis_size(axis))
    route = [(i - distance, i) for i in devices if i - distance in devices]
    return lax.ppermute(block, axis, route)


def prefix(value, axis, join, neutral):
    place = lax.axis_index(axis)
    gathered = jax.tree.map(
        lambda a, kind: lax.all_gather(a.astype(kind), axis), value, (jnp.bfloat16, jnp.bfloat16)
    )
    state = jax.tree.map(lambda a, e: jnp.zeros_like(a) + jnp.asarray(e, a.dtype), value, neutral)

    def one(turn, state):
        return join(
            state,
            jax.tree.map(
                lambda a, own: lax.dynamic_index_in_dim(a, turn, 0, False).astype(own.dtype),
                gathered,
                value,
            ),
        )

    return lax.fori_loop(0, place, one, state)


def prefix_2(value, axis, join, neutral):
    count = lax.axis_size(axis)
    place = lax.axis_index(axis)
    ahead = count - 1 - place
    gathered = jax.tree.map(
        lambda a, kind: lax.all_gather(a.astype(kind), axis),
        value,
        jax.tree.map(lambda a: jnp.bfloat16 if a.dtype == jnp.float32 else a.dtype, value),
    )
    state = jax.tree.map(lambda a, e: jnp.zeros_like(a) + jnp.asarray(e, a.dtype), value, neutral)

    def one(turn, state):
        source = count - 1 - turn
        return join(
            state,
            jax.tree.map(
                lambda a, own: lax.dynamic_index_in_dim(a, source, 0, False).astype(own.dtype),
                gathered,
                value,
            ),
        )

    return lax.fori_loop(0, ahead, one, state)


def rms_scale(values, scale_gain):
    return (
        values * lax.rsqrt(jnp.mean(values * values, axis=-1, keepdims=True) + EPSILON) * scale_gain
    )


def chain_rule(earlier, later_part):
    return (
        earlier[0] * later_part[0],
        later_part[1] + later_part[0][:, :, None, None] * earlier[1],
    )


def conv_features(widened, conv_weight, conv_bias, dt_raw, dt_bias, a_log):
    tap_count = conv_weight.shape[1]
    step_count = widened.shape[1] - tap_count + 1
    convolved = conv_bias
    for offset in range(tap_count):
        convolved = convolved + widened[:, offset : offset + step_count, :] * conv_weight[:, offset]
    activated = jax.nn.silu(convolved)
    x_heads = activated[..., :INNER]
    b_rows = activated[..., INNER : INNER + STATE]
    c_rows = activated[..., INNER + STATE :]
    dt_step = jax.nn.softplus(dt_raw + dt_bias)
    log_decay = jnp.cumsum(-jnp.exp(a_log) * dt_step, axis=1)
    return (x_heads, b_rows, c_rows, dt_step, log_decay)


def local_states(x_heads, b_rows, dt_step, log_decay):
    seq_count, length = (x_heads.shape[0], x_heads.shape[1])
    spread = x_heads.reshape(seq_count, length, HEADS, HEAD_DIM)
    weights = jnp.exp(log_decay[:, -1:, :] - log_decay) * dt_step
    weighted = spread * weights[..., None]
    states = jnp.einsum("sqhd,sqn->shdn", weighted, b_rows, precision=EXACT_MATMUL)
    return (jnp.exp(log_decay[:, -1]), states)


def gated_output(
    x_heads, b_rows, c_rows, dt_step, log_decay, prior_state, gate_z, skip_gain, gate_gain
):
    seq_count, length = (x_heads.shape[0], x_heads.shape[1])
    spread = x_heads.reshape(seq_count, length, HEADS, HEAD_DIM)
    scaled = spread * dt_step[..., None]
    by_head = jnp.transpose(log_decay, (0, 2, 1))
    differ = by_head[:, :, :, None] - by_head[:, :, None, :]
    causal = jnp.arange(length)[:, None] >= jnp.arange(length)[None, :]
    mixing = jnp.where(causal, jnp.exp(jnp.where(causal, differ, 0.0)), 0.0)
    intersections = jnp.einsum("sqn,skn->sqk", c_rows, b_rows, precision=EXACT_MATMUL)
    mixed_out = jnp.einsum(
        "shqk,skhd->sqhd", mixing * intersections[:, None], scaled, precision=EXACT_MATMUL
    )
    mixed_out = mixed_out + jnp.exp(log_decay)[..., None] * jnp.einsum(
        "sqn,shdn->sqhd", c_rows, prior_state, precision=EXACT_MATMUL
    )
    mixed_out = (mixed_out + skip_gain[:, None] * spread).reshape(seq_count, length, INNER)
    return rms_scale(mixed_out * jax.nn.silu(gate_z), gate_gain)


def layer_forward(hidden, weights):
    (
        norm_gain,
        input_weight,
        conv_weight,
        conv_bias,
        dt_bias,
        a_log,
        skip_gain,
        gate_gain,
        output_weight,
    ) = weights
    normalized_rows = rms_scale(hidden, norm_gain.astype(jnp.float32)).astype(jnp.bfloat16)
    projected_rows = jnp.einsum(
        "spd,de->spe", normalized_rows, input_weight, preferred_element_type=jnp.float32
    ).astype(jnp.bfloat16)
    length = hidden.shape[1]
    xbc_part = projected_rows[..., INNER : INNER + CONV_CH]
    border = shifted(xbc_part[:, length - KERNEL + 1 :, :], "fsdp", 1)
    widened = jnp.concatenate([border, xbc_part], axis=1)
    features = conv_features(
        widened.astype(jnp.float32),
        conv_weight.astype(jnp.float32),
        conv_bias.astype(jnp.float32),
        projected_rows[..., INNER + CONV_CH :].astype(jnp.float32),
        dt_bias.astype(jnp.float32),
        a_log.astype(jnp.float32),
    )
    decays, states = local_states(features[0], features[1], features[3], features[4])
    scanned = prefix(
        (decays, states), "fsdp", chain_rule, (jnp.ones_like(decays), jnp.zeros_like(states))
    )
    prior_state = scanned[1]
    gated_result = gated_output(
        features[0],
        features[1],
        features[2],
        features[3],
        features[4],
        prior_state,
        projected_rows[..., :INNER].astype(jnp.float32),
        skip_gain.astype(jnp.float32),
        gate_gain.astype(jnp.float32),
    )
    gated_low = gated_result.astype(jnp.bfloat16)
    final_result = hidden + jnp.einsum(
        "spi,id->spd", gated_low, output_weight, preferred_element_type=jnp.float32
    )
    return (
        final_result,
        (hidden, normalized_rows, projected_rows, widened, prior_state, gated_low),
    )


def layer_backward(gradient, kept_state, weights):
    hidden, normalized_rows, projected_rows, widened, prior_state, gated_low = kept_state
    (
        norm_gain,
        input_weight,
        conv_weight,
        conv_bias,
        dt_bias,
        a_log,
        skip_gain,
        gate_gain,
        output_weight,
    ) = weights
    grad_low = gradient.astype(jnp.bfloat16)
    grad_out_weight = jnp.einsum(
        "spi,spd->id", gated_low, grad_low, preferred_element_type=jnp.float32
    )
    grad_gated = jnp.einsum(
        "spd,id->spi", grad_low, output_weight, preferred_element_type=jnp.float32
    )
    features, pull_features = jax.vjp(
        conv_features,
        widened.astype(jnp.float32),
        conv_weight.astype(jnp.float32),
        conv_bias.astype(jnp.float32),
        projected_rows[..., INNER + CONV_CH :].astype(jnp.float32),
        dt_bias.astype(jnp.float32),
        a_log.astype(jnp.float32),
    )
    _, pull_gated = jax.vjp(
        gated_output,
        features[0],
        features[1],
        features[2],
        features[3],
        features[4],
        prior_state,
        projected_rows[..., :INNER].astype(jnp.float32),
        skip_gain.astype(jnp.float32),
        gate_gain.astype(jnp.float32),
    )
    grads_gated = pull_gated(grad_gated)
    decay_states, pull_states = jax.vjp(
        local_states, features[0], features[1], features[3], features[4]
    )
    decays = decay_states[0]
    later_state = prefix_2(
        (decays, grads_gated[5]),
        "fsdp",
        chain_rule,
        (jnp.ones_like(decays), jnp.zeros_like(grads_gated[5])),
    )
    grad_end = later_state[1]
    state_parts = pull_states((jnp.sum(grad_end * prior_state, axis=(2, 3)), grad_end))
    feature_grads = (
        grads_gated[0] + state_parts[0],
        grads_gated[1] + state_parts[1],
        grads_gated[2],
        grads_gated[3] + state_parts[2],
        grads_gated[4] + state_parts[3],
    )
    grad_wide, grad_conv_w, grad_conv_b, grad_dt_raw, grad_dt_bias, grad_a_log = pull_features(
        feature_grads
    )
    margin = KERNEL - 1
    returned = shifted(grad_wide[:, :margin, :].astype(jnp.bfloat16), "fsdp", -1).astype(
        jnp.float32
    )
    own_rows = grad_wide[:, margin:, :]
    length = own_rows.shape[1]
    grad_xbc = jnp.concatenate(
        [own_rows[:, : length - margin], own_rows[:, length - margin :] + returned], axis=1
    )
    grad_proj = jnp.concatenate([grads_gated[6], grad_xbc, grad_dt_raw], axis=-1).astype(
        jnp.bfloat16
    )
    grad_in_weight = jnp.einsum(
        "spd,spe->de", normalized_rows, grad_proj, preferred_element_type=jnp.float32
    )
    grad_normed = jnp.einsum(
        "spe,de->spd", grad_proj, input_weight, preferred_element_type=jnp.float32
    )
    _, pull_norm = jax.vjp(rms_scale, hidden, norm_gain.astype(jnp.float32))
    grad_hidden, grad_norm_gain = pull_norm(grad_normed)
    return (
        gradient + grad_hidden,
        (
            grad_norm_gain,
            grad_in_weight,
            grad_conv_w,
            grad_conv_b,
            grad_dt_bias,
            grad_a_log,
            grads_gated[7],
            grads_gated[8],
            grad_out_weight,
        ),
    )


def shards(
    ends,
    norm_gain,
    input_weight,
    conv_weight,
    conv_bias,
    dt_bias,
    a_log,
    skip_gain,
    gate_gain,
    output_weight,
):
    gathered = (
        lax.all_gather(norm_gain, "fsdp", axis=1, tiled=True),
        lax.all_gather(input_weight, "fsdp", axis=1, tiled=True),
        lax.all_gather(conv_weight, "fsdp", axis=1, tiled=True),
        lax.all_gather(conv_bias, "fsdp", axis=1, tiled=True),
        lax.all_gather(dt_bias, "fsdp", axis=1, tiled=True),
        lax.all_gather(a_log, "fsdp", axis=1, tiled=True),
        lax.all_gather(skip_gain, "fsdp", axis=1, tiled=True),
        lax.all_gather(gate_gain, "fsdp", axis=1, tiled=True),
        lax.all_gather(output_weight, "fsdp", axis=1, tiled=True),
    )
    layer_weights = tuple((member[0] for member in gathered))
    leading = lax.axis_index("section") == 0
    local_data = ends[0].astype(jnp.float32)
    batches = local_data.shape[0]
    arrived = jnp.zeros(local_data.shape[1:], jnp.float32)
    stored = []
    produced = []
    for moment in range(batches + 1):
        source = jnp.where(leading, local_data[min(moment, batches - 1)], arrived)
        final_result, kept_state = layer_forward(source, layer_weights)
        stored.append(kept_state)
        produced.append(final_result)
        if moment < batches:
            arrived = shifted(final_result.astype(jnp.bfloat16), "section", 1).astype(jnp.float32)
    totals = None
    coming = jnp.zeros(local_data.shape[1:], jnp.float32)
    returned_grads = []
    for moment in range(batches + 1):
        gradient = jnp.where(leading, coming, local_data[min(moment, batches - 1)])
        kept_state = jax.tree.map(
            lambda upper_part, lower_part: jnp.where(leading, upper_part, lower_part),
            stored[max(moment - 1, 0)],
            stored[min(moment + 1, batches)],
        )
        grad_input, gradients = layer_backward(gradient, kept_state, layer_weights)
        active = jnp.where(leading, moment >= 1, moment < batches)
        masked = tuple((jnp.where(active, member, 0.0) for member in gradients))
        if totals is None:
            totals = masked
        else:
            totals = tuple((earlier_sum + member for earlier_sum, member in zip(totals, masked)))
        returned_grads.append(grad_input)
        if moment < batches:
            coming = shifted(grad_input.astype(jnp.bfloat16), "section", -1).astype(jnp.float32)
    boundary = jnp.stack(
        [
            jnp.where(leading, returned_grads[number + 1], produced[number + 1])
            for number in range(batches)
        ]
    )
    owned_parts = (
        lax.psum_scatter(
            totals[0][None].astype(jnp.bfloat16), "fsdp", scatter_dimension=1, tiled=True
        ).astype(jnp.float32),
        lax.psum_scatter(
            totals[1][None].astype(jnp.bfloat16), "fsdp", scatter_dimension=1, tiled=True
        ).astype(jnp.float32),
        lax.psum_scatter(
            totals[2][None].astype(jnp.bfloat16), "fsdp", scatter_dimension=1, tiled=True
        ).astype(jnp.float32),
        lax.psum_scatter(
            totals[3][None].astype(jnp.bfloat16), "fsdp", scatter_dimension=1, tiled=True
        ).astype(jnp.float32),
        lax.psum_scatter(
            totals[4][None].astype(jnp.bfloat16), "fsdp", scatter_dimension=1, tiled=True
        ).astype(jnp.float32),
        lax.psum_scatter(
            totals[5][None].astype(jnp.bfloat16), "fsdp", scatter_dimension=1, tiled=True
        ).astype(jnp.float32),
        lax.psum_scatter(
            totals[6][None].astype(jnp.bfloat16), "fsdp", scatter_dimension=1, tiled=True
        ).astype(jnp.float32),
        lax.psum_scatter(
            totals[7][None].astype(jnp.bfloat16), "fsdp", scatter_dimension=1, tiled=True
        ).astype(jnp.float32),
        lax.psum_scatter(
            totals[8][None].astype(jnp.bfloat16), "fsdp", scatter_dimension=1, tiled=True
        ).astype(jnp.float32),
    )
    summed = (
        lax.psum(owned_parts[0].astype(jnp.bfloat16), "rep").astype(jnp.float32),
        lax.psum(owned_parts[1].astype(jnp.bfloat16), "rep").astype(jnp.float32),
        lax.psum(owned_parts[2].astype(jnp.bfloat16), "rep").astype(jnp.float32),
        lax.psum(owned_parts[3].astype(jnp.bfloat16), "rep").astype(jnp.float32),
        lax.psum(owned_parts[4].astype(jnp.bfloat16), "rep").astype(jnp.float32),
        lax.psum(owned_parts[5].astype(jnp.bfloat16), "rep").astype(jnp.float32),
        lax.psum(owned_parts[6].astype(jnp.bfloat16), "rep").astype(jnp.float32),
        lax.psum(owned_parts[7].astype(jnp.bfloat16), "rep").astype(jnp.float32),
        lax.psum(owned_parts[8].astype(jnp.bfloat16), "rep").astype(jnp.float32),
    )
    return (
        boundary.astype(jnp.bfloat16)[None],
        summed[0],
        summed[1],
        summed[2],
        summed[3],
        summed[4],
        summed[5],
        summed[6],
        summed[7],
        summed[8],
    )


def solution(mesh):
    shape = mesh.shape
    relay = shape["section"] == 2 and shape["rep"] == 4 and shape["fsdp"] == 4
    if relay:
        devices = mesh.devices.reshape(2, 2, 2, 4)
        mesh = Mesh(devices, ("section", "y", "core", "fsdp"))
    rep = ("y", "core") if relay else "rep"
    data = P("section", None, rep, "fsdp", None)
    vector, matrix = P("section", "fsdp"), P("section", "fsdp", None)
    params = (vector, matrix, matrix, vector, vector, vector, vector, vector, matrix)
    return jax.shard_map(
        relay_shards if relay else shards,
        mesh=mesh,
        in_specs=(data, *params),
        out_specs=(data, *params),
        check_vma=False,
    )
```

```python
import functools

import jax
import jax.numpy as jnp
from jax import lax
from jax.experimental import pallas as pl
from jax.experimental.pallas import tpu as pltpu
from jax.sharding import Mesh
from jax.sharding import PartitionSpec as P

D = 1536
HEADS = 48
HEAD_DIM = 64
STATE = 128
KERNEL = 4
INNER = 3072
CONV_CH = 3328
LANES = 128

OWN = INNER // 2
OWN_HEADS = HEADS // 2
OWN_CONV = OWN + 2 * STATE
X_AT = OWN
BC_AT = 2 * OWN
DT_AT = 2 * OWN + 2 * STATE
OWN_PROJ = DT_AT + 2 * LANES
PAIRS = OWN // LANES

EPSILON = 1e-05
EXACT_MATMUL = lax.Precision.HIGHEST
F32 = jnp.float32
BF16 = jnp.bfloat16
FORWARD_VMEM = 24
BACKWARD_VMEM = 30
JOIN_VMEM = 12


def dot(a, b):
    return lax.dot_general(a, b, (((1,), (0,)), ((), ())), preferred_element_type=F32)


def dot_nt(a, b):
    return lax.dot_general(a, b, (((1,), (1,)), ((), ())), preferred_element_type=F32)


def dot_tn(a, b):
    return lax.dot_general(a, b, (((0,), (0,)), ((), ())), preferred_element_type=F32)


def split(v, parts):
    pieces = []
    for _ in range(parts):
        piece = v.astype(BF16)
        pieces.append(piece)
        v = v - piece.astype(F32)
    return pieces


def sigmoid(v):
    return 0.5 * jnp.tanh(0.5 * v) + 0.5


def softplus(v):
    return jnp.maximum(v, 0.0) + jnp.log1p(jnp.exp(-jnp.abs(v)))


def step_sizes(dt_raw, headp):
    t = dt_raw.shape[0]
    biased = dt_raw + headp[0:1]
    dt = softplus(biased)
    rows = lax.broadcasted_iota(jnp.int32, (t, t), 0)
    cols = lax.broadcasted_iota(jnp.int32, (t, t), 1)
    tri = jnp.where(rows >= cols, 1.0, 0.0).astype(BF16)
    ld = sum(dot(tri, part) for part in split(dt * headp[1:2], 3))
    return dt, ld, biased


def at_head(v, pair):
    turned = pltpu.roll(v, lax.rem(LANES - 2 * pair, LANES), 1)
    return [jnp.broadcast_to(turned[:, i : i + 1], v.shape) for i in range(2)]


def decay_blocks(col, row, swapped):
    n = col.shape[0] // 2
    rows = lax.broadcasted_iota(jnp.int32, (n, n), 0)
    cols = lax.broadcasted_iota(jnp.int32, (n, n), 1)
    keep = rows <= cols if swapped else rows >= cols

    def block(i, j):
        down, along = col[i * n : (i + 1) * n], row[:, j * n : (j + 1) * n]
        differ = along - down if swapped else down - along
        return jnp.exp(jnp.where(keep, differ, -1e30) if i == j else differ)

    return block(0, 0), block(0, 1) if swapped else block(1, 0), block(1, 1)


def convolve(xw, sl, convp, t):
    out = convp[4:5, sl] + xw[5 : 5 + t, sl] * convp[0:1, sl]
    for k in range(1, KERNEL):
        out = out + xw[5 + k : 5 + k + t, sl] * convp[k : k + 1, sl]
    return out


def pair_loop(step):
    def two(turn, _):
        step(2 * turn)
        step(2 * turn + 1)
        return 0

    lax.fori_loop(0, PAIRS // 2, two, 0)


def aligned(value):
    return pl.multiple_of(value, LANES)


def fetch(source, target, sem):
    copy = pltpu.make_async_copy(source, target, sem)
    copy.start()
    return copy


def fetch_one_of(first, one, other, target, sem):
    @pl.when(first)
    def _():
        pltpu.make_async_copy(one, target, sem).start()

    @pl.when(jnp.logical_not(first))
    def _():
        pltpu.make_async_copy(other, target, sem).start()

    return pltpu.make_async_copy(other, target, sem)


def forward_kernel(row, sc, *refs):
    @pl.when(sc[row, VALID] == 1)
    def _():
        forward_chunk(row, sc, *refs)


def forward_chunk(
    row, sc, got_hbm, other_hbm, x_hbm, ng_ref, convp, headp, chanp, st_ref, tail_ref, win, wout, *rest
):
    p, h, st_out, tail_out = rest[-22:-18]
    h_hbm, n_hbm, pr_hbm, mx_hbm, q_hbm, st_hbm, tl_hbm = rest[-18:-11]
    normed, pr, mx, q, sti, tl, xw, ldt, ss, g_ref, sem = rest[-11:]
    t = h.shape[0]
    half = t // 2
    slot = sc[row, SLOT]
    first = sc[row, FIRST] == 1
    leading = sc[row, LEADING] == 1
    core = sc[row, CORE]

    @pl.when(leading)
    def _():
        fetch(x_hbm, h, sem.at[0]).wait()

    @pl.when(jnp.logical_not(leading))
    def _():
        mine = h.at[pl.ds(aligned(core * half), half)]
        theirs = h.at[pl.ds(aligned((1 - core) * half), half)]
        copies = fetch(got_hbm, mine, sem.at[0]), fetch(other_hbm, theirs, sem.at[1])
        for copy in copies:
            copy.wait()

    stores = [fetch(h, h_hbm.at[slot], sem.at[0])]
    hf = h[...].astype(F32)
    r = lax.rsqrt(jnp.mean(hf * hf, axis=1, keepdims=True) + EPSILON)
    normed[...] = (hf * r * ng_ref[...]).astype(BF16)
    stores.append(fetch(normed, n_hbm.at[slot], sem.at[1]))

    sti[...] = jnp.where(first, 0.0, st_ref[...])
    tl[...] = jnp.where(first, 0.0, tail_ref[...])
    stores.append(fetch(sti, st_hbm.at[slot], sem.at[2]))
    stores.append(fetch(tl, tl_hbm.at[slot], sem.at[3]))
    xw[0:8, :] = tl[...]

    for at in range(0, OWN_PROJ, 512):
        cols = slice(at, min(at + 512, OWN_PROJ))
        pr[:, cols] = dot_nt(normed[...], win[cols, :]).astype(BF16)
    stores.append(fetch(pr, pr_hbm.at[slot], sem.at[4]))
    tail_out[...] = pr[t - 8 : t, X_AT : X_AT + OWN_CONV].astype(F32)

    bc = pl.ds(OWN, 2 * STATE)
    xw[8 : 8 + t, OWN:OWN_CONV] = pr[:, BC_AT:DT_AT].astype(F32)
    conv_bc = convolve(xw, bc, convp, t)
    act = (conv_bc * sigmoid(conv_bc)).astype(BF16)
    b, c = act[:, :STATE], act[:, STATE:]
    g_ref[...] = dot_nt(c, b)
    b_turned = act[:, :STATE].astype(F32).T.astype(BF16)
    dt, ld, _ = step_sizes(pr[:, DT_AT : DT_AT + LANES].astype(F32), headp[...])
    ldt[...] = ld.T
    left = lax.broadcasted_iota(jnp.int32, (t, LANES), 1) < HEAD_DIM
    ss[...] = jnp.zeros_like(ss)

    def pair_step(pair):
        at = pl.multiple_of(pair * LANES, LANES)
        sl = pl.ds(at, LANES)
        xw[8 : 8 + t, sl] = pr[:, pl.ds(X_AT + at, LANES)].astype(F32)
        conv = convolve(xw, sl, convp, t)
        x = conv * sigmoid(conv)
        cols = at_head(ld, pair)
        u = jnp.where(left, *at_head(dt, pair)) * x
        ld_p = jnp.where(left, *cols)
        tops, bottoms, sides = [], [], []
        for i in range(2):
            u_i = jnp.where(left if i == 0 else jnp.logical_not(left), u, 0.0).astype(BF16)
            d00, d10, d11 = decay_blocks(cols[i], ldt[pl.ds(2 * pair + i, 1), :], False)
            m00 = (g_ref[:half, :half] * d00).astype(BF16)
            m10 = (g_ref[half:, :half] * d10).astype(BF16)
            m11 = (g_ref[half:, half:] * d11).astype(BF16)
            tops.append(m00)
            bottoms += [m10, m11]
            sides.append(u_i)
        top = dot(jnp.concatenate(tops, axis=1), jnp.concatenate([v[:half] for v in sides], axis=0))
        bottom = dot(jnp.concatenate(bottoms, axis=1), jnp.concatenate(sides, axis=0))
        eld = jnp.exp(ld_p)
        st = sti[:, sl]
        y = jnp.concatenate([top, bottom], axis=0) + eld * dot(c, st.astype(BF16))
        weighted = (u * jnp.exp(ld_p[t - 1 : t] - ld_p)).astype(BF16)
        st_out[:, sl] = eld[t - 1 : t] * st + dot(b_turned, weighted)
        mixed = y + chanp[0:1, sl] * x
        mx[:, sl] = mixed
        z = pr[:, sl].astype(F32)
        gated = mixed * (z * sigmoid(z))
        ss[...] += gated * gated
        q[:, sl] = (gated * chanp[1:2, sl]).astype(BF16)

    pair_loop(pair_step)
    stores.append(fetch(mx, mx_hbm.at[slot], sem.at[5]))
    stores.append(fetch(q, q_hbm.at[slot], sem.at[6]))
    total = jnp.sum(ss[...], axis=1, keepdims=True)
    high = total.astype(BF16).astype(F32)
    lane = lax.broadcasted_iota(jnp.int32, (t, LANES), 1)
    p[:, D:] = jnp.where(lane == 0, high, jnp.where(lane == 1, total - high, 0.0)).astype(BF16)
    for at in range(0, D, 512):
        p[:, at : at + 512] = dot(q[...], wout[:, at : at + 512]).astype(BF16)
    for store in stores:
        store.wait()


def backward_kernel(row, sc, *refs):
    acc_ref, acc_out = refs[17], refs[-21]

    @pl.when(sc[row, VALID] == 1)
    def _():
        backward_chunk(row, sc, *refs)

    @pl.when(sc[row, VALID] == 0)
    def _():
        acc_out[...] = acc_ref[...]


def backward_chunk(
    row,
    sc,
    arrived_hbm,
    other_hbm,
    cot_hbm,
    h_hbm,
    n_hbm,
    pr_hbm,
    mx_hbm,
    st_hbm,
    tl_hbm,
    y_hbm,
    ri_hbm,
    convp,
    headp,
    chanp,
    dst_ref,
    dc_ref,
    val_ref,
    acc_ref,
    win,
    wout,
    *rest,
):
    gn, g_ref, h_out, dst_out, dc_out, val_out, acc_out, gp_hbm, gs_hbm = rest[-27:-18]
    pr, mx, st_ref, tl, y_ref, ri, gp, gs, normed = rest[-18:-9]
    xw, dw, ldt, gw, gt, dgt, dci, dbi, sem = rest[-9:]
    t = g_ref.shape[0]
    half = t // 2
    slot = sc[row, SLOT]
    last = sc[row, FIRST] == 1
    leading = sc[row, LEADING] == 1
    core = sc[row, CORE]
    mine = g_ref.at[pl.ds(aligned(core * half), half)]
    theirs = g_ref.at[pl.ds(aligned((1 - core) * half), half)]

    @pl.when(leading)
    def _():
        copies = fetch(arrived_hbm, mine, sem.at[0]), fetch(other_hbm, theirs, sem.at[10])
        for copy in copies:
            copy.wait()

    @pl.when(jnp.logical_not(leading))
    def _():
        fetch(cot_hbm, g_ref, sem.at[0]).wait()

    y_copy = fetch(y_hbm.at[slot], y_ref, sem.at[1])
    ri_copy = fetch(ri_hbm.at[slot], ri, sem.at[2])
    pr_copy = fetch(pr_hbm.at[slot], pr, sem.at[3])
    tl_copy = fetch(tl_hbm.at[slot], tl, sem.at[4])
    mx_copy = fetch(mx_hbm.at[slot], mx, sem.at[5])
    st_copy = fetch(st_hbm.at[slot], st_ref, sem.at[6])
    h_copy = fetch(h_hbm.at[slot], h_out, sem.at[8])
    n_copy = fetch(n_hbm.at[slot], normed, sem.at[9])

    acc_out[...] = acc_ref[...]
    dw[t : t + 8, :] = jnp.where(last, 0.0, dc_ref[...])
    dgt[...] = jnp.zeros_like(dgt)
    dci[...] = jnp.zeros_like(dci)
    dbi[...] = jnp.zeros_like(dbi)
    for at in range(0, OWN, 512):
        gw[:, at : at + 512] = dot_nt(g_ref[...], wout[at : at + 512, :])
    y_copy.wait()
    ri_copy.wait()
    rinv = ri[:, 0:1]
    mean = jnp.sum(g_ref[...].astype(F32) * y_ref[...].astype(F32), axis=1, keepdims=True)
    lean = rinv * rinv * (mean * (1.0 / INNER))
    gs[...] = (g_ref[...].astype(F32) * rinv).astype(BF16)
    gs_store = fetch(gs, gs_hbm.at[sc[row, WRITE]], sem.at[7])
    pr_copy.wait()
    tl_copy.wait()
    xw[0:8, :] = tl[...]

    bc = pl.ds(OWN, 2 * STATE)
    xw[8 : 8 + t, OWN:OWN_CONV] = pr[:, BC_AT:DT_AT].astype(F32)
    conv_bc = convolve(xw, bc, convp, t)
    sig_bc = sigmoid(conv_bc)
    act = (conv_bc * sig_bc).astype(BF16)
    b, c = act[:, :STATE], act[:, STATE:]
    c_turned = c.astype(F32).T.astype(BF16)
    gt[...] = dot_nt(b, c)
    dt, ld, biased = step_sizes(pr[:, DT_AT : DT_AT + LANES].astype(F32), headp[...])
    ldt[...] = ld.T
    left = lax.broadcasted_iota(jnp.int32, (t, LANES), 1) < HEAD_DIM

    def add(line, sl, v):
        acc_out[line : line + 1, sl] += v

    def conv_back(dact, conv, sig, sl):
        dconv = dact * (sig * (1.0 + conv * (1.0 - sig)))
        dw[0:t, sl] = dconv
        add(4, sl, jnp.sum(dconv, axis=0, keepdims=True))
        for k in range(KERNEL):
            add(k, sl, jnp.sum(dconv * xw[5 + k : 5 + k + t, sl], axis=0, keepdims=True))
        dx = dconv * convp[KERNEL - 1 : KERNEL, sl]
        for k in range(KERNEL - 1):
            ahead = KERNEL - 1 - k
            dx = dx + dw[ahead : ahead + t, sl] * convp[k : k + 1, sl]
        return dx.astype(BF16)

    lane_head = lax.rem(lax.broadcasted_iota(jnp.int32, (2 * LANES, LANES), 0), LANES) // HEAD_DIM
    head_lane = lax.broadcasted_iota(jnp.int32, (2 * LANES, LANES), 1)
    mx_copy.wait()
    st_copy.wait()

    def pair_step(pair, carry):
        ddt, dld, dval = carry
        at = pl.multiple_of(pair * LANES, LANES)
        sl = pl.ds(at, LANES)
        xsl = pl.ds(X_AT + at, LANES)
        xw[8 : 8 + t, sl] = pr[:, xsl].astype(F32)
        conv = convolve(xw, sl, convp, t)
        sig = sigmoid(conv)
        x = conv * sig
        z = pr[:, sl].astype(F32)
        sig_z = sigmoid(z)
        s = z * sig_z
        mixed = mx[:, sl]
        gated = mixed * s
        scaled = gw[:, sl] * rinv
        add(6, sl, jnp.sum(scaled * gated, axis=0, keepdims=True))
        dgated = chanp[1:2, sl] * scaled - gated * lean
        dy = dgated * s
        gp[:, sl] = (dgated * mixed * (sig_z * (1.0 + z * (1.0 - sig_z)))).astype(BF16)
        skip = chanp[0:1, sl]
        add(5, sl, jnp.sum(dy * x, axis=0, keepdims=True))
        y = mixed - skip * x

        cols = at_head(ld, pair)
        ld_p = jnp.where(left, *cols)
        eld = jnp.exp(ld_p)
        wend = jnp.exp(ld_p[t - 1 : t] - ld_p)
        dt_p = jnp.where(left, *at_head(dt, pair))
        u = dt_p * x
        u_low = u.astype(BF16)
        dy_low = dy.astype(BF16)
        dst = jnp.where(last, 0.0, dst_ref[:, sl])
        dst_low = dst.astype(BF16)
        top = jnp.zeros((half, LANES), F32)
        bottom = top
        for i in range(2):
            side = left if i == 0 else jnp.logical_not(left)
            d00, d01, d11 = decay_blocks(cols[i], ldt[pl.ds(2 * pair + i, 1), :], True)
            m00 = (gt[:half, :half] * d00).astype(BF16)
            m01 = (gt[:half, half:] * d01).astype(BF16)
            m11 = (gt[half:, half:] * d11).astype(BF16)
            dy_i = jnp.where(side, dy, 0.0).astype(BF16)
            top = top + dot(jnp.concatenate([m00, m01], axis=1), dy_i)
            bottom = bottom + dot(m11, dy_i[half:])
            u_i = jnp.where(side, u, 0.0).astype(BF16)
            dm = dot_nt(u_i[:half], dy_low)
            dgt[:half, :half] += dm[:, :half] * d00
            dgt[:half, half:] += dm[:, half:] * d01
            dgt[half:, half:] += dot_nt(u_i[half:], dy_low[half:]) * d11
        du = jnp.concatenate([top, bottom], axis=0) + wend * dot(b, dst_low)
        st = st_ref[:, sl]
        dyl = (eld * dy).astype(BF16)
        dst_new = eld[t - 1 : t] * dst + dot(c_turned, dyl)
        dst_out[:, sl] = dst_new
        val_out[:, sl] = jnp.broadcast_to(
            jnp.sum(dst_new * st, axis=0, keepdims=True), (8, LANES)
        )
        dci[...] += dot_nt(dyl, st.astype(BF16))
        dbi[...] += dot_nt((wend * u).astype(BF16), dst_low)

        pick = jnp.where(lane_head + 2 * pair == head_lane, 1.0, 0.0).astype(BF16)


        def by_head(v):
            return dot(jnp.concatenate(split(v, 2), axis=1), pick)

        ddt = ddt + by_head(du * x)
        dld = dld + by_head(dy_low.astype(F32) * y - u_low.astype(F32) * du)
        dval = dval + by_head(jnp.where(last, 0.0, val_ref[:, sl]))
        gp[:, xsl] = conv_back(dt_p * du + skip * dy, conv, sig, sl)
        return ddt, dld, dval

    zero = jnp.zeros((t, LANES), F32)
    ddt, dld, dval = lax.fori_loop(
        0,
        PAIRS // 2,
        lambda turn, carry: pair_step(2 * turn + 1, pair_step(2 * turn, carry)),
        (zero, zero, jnp.zeros((8, LANES), F32)),
    )

    dgt_low = dgt[...].astype(BF16)
    db = dbi[...] + dot(dgt_low, c)
    dc = dci[...] + dot_tn(dgt_low, b)
    gp[:, BC_AT:DT_AT] = conv_back(jnp.concatenate([db, dc], axis=1), conv_bc, sig_bc, bc)

    rows = lax.broadcasted_iota(jnp.int32, (t, t), 0)
    cols = lax.broadcasted_iota(jnp.int32, (t, t), 1)
    upper = jnp.where(rows <= cols, 1.0, 0.0).astype(BF16)
    da = sum(dot(upper, part) for part in split(dld, 3)) + dval[0:1]
    rate = headp[1:2]
    head = pl.ds(0, LANES)
    add(8, head, jnp.sum(da * rate * dt, axis=0, keepdims=True))
    ddt_raw = (ddt + rate * da) * sigmoid(biased)
    add(7, head, jnp.sum(ddt_raw, axis=0, keepdims=True))
    gp[:, DT_AT : DT_AT + LANES] = ddt_raw.astype(BF16)
    gp[:, DT_AT + LANES :] = jnp.zeros((t, LANES), BF16)
    gp_store = fetch(gp, gp_hbm.at[sc[row, WRITE]], sem.at[0])
    dc_out[...] = dw[0:8, :]
    n_copy.wait()
    for at in range(0, D, 512):
        cols = slice(at, at + 512)
        values = dot(gp[...], win[:, cols])
        gn[:, cols] = values.astype(BF16)
        add(9, cols, jnp.sum(values * normed[:, cols].astype(F32), axis=0, keepdims=True))
    gp_store.wait()
    gs_store.wait()
    h_copy.wait()


def forward_join_kernel(row, sc, own_ref, other_ref, h_ref, *rest):
    out, y_hbm, ri_hbm, e_hbm, y_v, ri_v, low_v, sem = rest[-8:]
    half = out.shape[0]

    @pl.when(sc[row, VALID] == 1)
    def _():
        copies = []
        for k in range(2):
            rows = slice(k * half, (k + 1) * half)
            total = own_ref[rows].astype(F32) + other_ref[rows].astype(F32)
            square = total[:, D : D + 1] + total[:, D + 1 : D + 2]
            rinv = lax.rsqrt(square * (1.0 / INNER) + EPSILON)
            y = total[:, :D] * rinv
            y_v[rows] = y.astype(BF16)
            ri_v[rows] = jnp.broadcast_to(rinv, (half, LANES))
            low_v[rows] = (h_ref[rows].astype(F32) + y).astype(BF16)
            pieces = ((y_v, y_hbm, SLOT), (ri_v, ri_hbm, SLOT), (low_v, e_hbm, EDGE))
            for near_ref, far_ref, which in pieces:
                target = far_ref.at[sc[row, which], pl.ds(k * half, half)]
                copies.append(fetch(near_ref.at[pl.ds(k * half, half)], target, sem.at[len(copies)]))
        out[...] = low_v[pl.ds(aligned(sc[row, CORE] * half), half), :]
        for copy in copies:
            copy.wait()


def backward_join_kernel(row, sc, own_ref, other_ref, h_ref, g_ref, ng_ref, *rest):
    out, e_hbm, low_v, sem = rest[-4:]
    half = out.shape[0]

    @pl.when(sc[row, VALID] == 1)
    def _():
        copies = []
        for k in range(2):
            rows = slice(k * half, (k + 1) * half)
            gn = own_ref[rows].astype(F32) + other_ref[rows].astype(F32)
            h = h_ref[rows].astype(F32)
            r = lax.rsqrt(jnp.mean(h * h, axis=1, keepdims=True) + EPSILON)
            t = gn * ng_ref[...]
            m = jnp.mean(h * t, axis=1, keepdims=True)
            low_v[rows] = (g_ref[rows].astype(F32) + r * (t - h * (r * r * m))).astype(BF16)
            target = e_hbm.at[sc[row, EDGE], pl.ds(k * half, half)]
            copies.append(fetch(low_v.at[pl.ds(k * half, half)], target, sem.at[k]))
        out[...] = low_v[pl.ds(aligned(sc[row, CORE] * half), half), :]
        for copy in copies:
            copy.wait()


def pick_kernel(first, sc, stack_hbm, out, sem):
    fetch(stack_hbm.at[first + sc[0, CORE]], out, sem.at[0]).wait()


ANY = pl.BlockSpec(memory_space=pl.ANY)
NEAR = pl.BlockSpec(memory_space=pltpu.VMEM)
SLOT, LEADING, FIRST, VALID, WRITE, EDGE, CORE = range(7)
LITTLE = pl.CostEstimate(flops=1 << 20, bytes_accessed=1 << 16, transcendentals=0)


def near(value):
    return pltpu.with_memory_space_constraint(value, pltpu.VMEM)


def away(value):
    return pltpu.with_memory_space_constraint(value, pltpu.HBM)


def chunk_call(kernel, table, free, far, close, close_outs, buffers, scratch, limit, name):
    inputs = [table, *free, *(away(v) for v in far), *(near(v) for v in close)]
    in_specs = [pl.BlockSpec(memory_space=pltpu.SMEM)]
    in_specs += [ANY] * (len(free) + len(far)) + [NEAR] * len(close)
    outs = [pltpu.VMEM(*o) for o in close_outs]
    out_specs = [NEAR] * len(close_outs)
    aliases = {}
    for held, shape, dtype in buffers:
        if held is not None:
            aliases[len(inputs)] = len(outs)
            inputs.append(away(held))
            in_specs.append(ANY)
        outs.append(pltpu.HBM(shape, dtype))
        out_specs.append(ANY)
    results = pl.pallas_call(
        kernel,
        in_specs=in_specs,
        out_specs=out_specs,
        out_shape=outs,
        scratch_shapes=scratch,
        input_output_aliases=aliases,
        compiler_params=pltpu.CompilerParams(vmem_limit_bytes=limit << 20),
        cost_estimate=LITTLE,
        name=name,
    )(*inputs)
    return tuple(results[: len(close_outs)]), tuple(results[len(close_outs) :])


def forward_call(table, row, slots, x, arrived, params, carry, held):
    t = x.shape[0]
    held = held or (None,) * 7
    kinds = (
        ((t, D), BF16),
        ((t, D), BF16),
        ((t, OWN_PROJ), BF16),
        ((t, OWN), F32),
        ((t, OWN), BF16),
        ((STATE, OWN), F32),
        ((8, OWN_CONV), F32),
    )
    gain, convp, headp, chanp, win, wout = params
    outs, held = chunk_call(
        functools.partial(forward_kernel, row),
        table,
        (*arrived, x),
        (),
        (gain, convp, headp, chanp, *carry, win, wout),
        (((t, D + LANES), BF16), kinds[0], kinds[5], kinds[6]),
        [(b, (slots,) + k, d) for b, (k, d) in zip(held, kinds)],
        [pltpu.VMEM(*k) for k in kinds[1:]]
        + [
            pltpu.VMEM((t + 8, OWN_CONV), F32),
            pltpu.VMEM((LANES, t), F32),
            pltpu.VMEM((t, LANES), F32),
            pltpu.VMEM((t, t), F32),
            pltpu.SemaphoreType.DMA((8,)),
        ],
        FORWARD_VMEM,
        "forward_chunk",
    )
    return outs[0], outs[1], outs[2:], held


def backward_call(table, row, slots, cot, arrived, saved, params, carry, held):
    t = cot.shape[0]
    held = held or (None, None)
    _, convp, headp, chanp, win, wout = params
    wide, projected = ((t, D), BF16), ((t, OWN_PROJ), BF16)
    outs, held = chunk_call(
        functools.partial(backward_kernel, row),
        table,
        (*arrived, cot),
        saved,
        (convp, headp, chanp, *carry, win, wout),
        [wide] * 3 + [(v.shape, v.dtype) for v in carry],
        [(held[0], (slots, t, OWN_PROJ), BF16), (held[1], (slots, t, D), BF16)],
        [
            pltpu.VMEM(*projected),
            pltpu.VMEM((t, OWN), F32),
            pltpu.VMEM((STATE, OWN), F32),
            pltpu.VMEM((8, OWN_CONV), F32),
            pltpu.VMEM(*wide),
            pltpu.VMEM((t, LANES), F32),
            pltpu.VMEM(*projected),
            pltpu.VMEM(*wide),
            pltpu.VMEM(*wide),
            pltpu.VMEM((t + 8, OWN_CONV), F32),
            pltpu.VMEM((t + 8, OWN_CONV), F32),
            pltpu.VMEM((LANES, t), F32),
            pltpu.VMEM((t, OWN), F32),
            pltpu.VMEM((t, t), F32),
            pltpu.VMEM((t, t), F32),
            pltpu.VMEM((t, STATE), F32),
            pltpu.VMEM((t, STATE), F32),
            pltpu.SemaphoreType.DMA((11,)),
        ],
        BACKWARD_VMEM,
        "backward_chunk",
    )
    return outs[:3], outs[3:], held


def forward_join(table, row, slots, own, other, h, held):
    t = h.shape[0]
    held = held or (None,) * 3
    wide, thin = ((t, D), BF16), ((t, LANES), F32)
    outs, held = chunk_call(
        functools.partial(forward_join_kernel, row),
        table,
        (),
        (),
        (own, other, h),
        [((t // 2, D), BF16)],
        [(b, (slots,) + k, d) for b, (k, d) in zip(held, (wide, thin, wide))],
        [pltpu.VMEM(*k) for k in (wide, thin, wide)] + [pltpu.SemaphoreType.DMA((6,))],
        JOIN_VMEM,
        "forward_join",
    )
    return outs[0], held


def backward_join(table, row, own, other, h, g, gain, edge_held):
    slots, t, _ = edge_held.shape
    outs, held = chunk_call(
        functools.partial(backward_join_kernel, row),
        table,
        (),
        (),
        (own, other, h, g, gain),
        [((t // 2, D), BF16)],
        [(edge_held, (slots, t, D), BF16)],
        [pltpu.VMEM((t, D), BF16), pltpu.SemaphoreType.DMA((2,))],
        JOIN_VMEM,
        "backward_join",
    )
    return outs[0], held[0]


def pick(table, stack, first):
    outs, _ = chunk_call(
        functools.partial(pick_kernel, first),
        table,
        (),
        (stack,),
        (),
        [(stack.shape[1:], stack.dtype)],
        [],
        [pltpu.SemaphoreType.DMA((1,))],
        JOIN_VMEM,
        "pick",
    )
    return outs[0]


def own_of(values, core):
    lead, width = values.shape[:-1], values.shape[-1]
    blocks = values.reshape(lead + (4, 2, width // 8))
    return lax.dynamic_index_in_dim(blocks, core, len(lead) + 1, False).reshape(
        lead + (width // 2,)
    )


def woven(halves):
    width = halves.shape[-1]
    lead = halves.shape[1:-1]
    blocks = halves.reshape((2,) + lead + (4, width // 4))
    return jnp.moveaxis(blocks, 0, -2).reshape(lead + (2 * width,))


def small_params(norm_gain, conv_weight, conv_bias, dt_bias, a_log, skip_gain, gate_gain, core):
    own = functools.partial(own_of, core=core)
    taps = jnp.concatenate([conv_weight.T, conv_bias[None]], axis=0).astype(F32)
    taps = jnp.concatenate([own(taps[:, :INNER]), taps[:, INNER:]], axis=1)
    convp = jnp.pad(taps, ((0, 3), (0, 0)))
    heads = jnp.stack([own(dt_bias.astype(F32)), -jnp.exp(own(a_log.astype(F32)))])
    headp = jnp.pad(heads, ((0, 6), (0, LANES - OWN_HEADS)))
    skip = jnp.repeat(own(skip_gain.astype(F32)), HEAD_DIM)
    chanp = jnp.pad(jnp.stack([skip, own(gate_gain.astype(F32))]), ((0, 6), (0, 0)))
    return norm_gain.astype(F32)[None], convp, headp, chanp


def own_steps(weight, core):
    own = own_of(weight[INNER + CONV_CH :].T, core).T
    return jnp.pad(own, ((0, 2 * LANES - OWN_HEADS), (0, 0)))


HALF = OWN // 2
BLOCK = HALF // 2
PACKED_ROWS = HALF + HALF + 2 * STATE + 2 * BLOCK
PARTS = (
    ("in", HALF, X_AT, HALF),
    ("in", HALF, 0, HALF),
    ("in", 2 * STATE, BC_AT, 2 * STATE),
    ("out", BLOCK, 0, HALF),
    ("out", BLOCK, BLOCK, HALF),
)


def ring_place(position, count):
    back = position >= count
    return jnp.where(back, 1, 0), jnp.where(back, 2 * count - 1 - position, position)


def ring_route(count, step):
    def index(position):
        return position if position < count else count + (2 * count - 1 - position)

    size = 2 * count
    return [(index(p), index((p + step) % size)) for p in range(size)]


def pack_kernel(sc, w, steps, o, own, rest, sem):
    core, side = sc[0], sc[1]
    copies = []
    for target, y in ((own, side), (rest, 1 - side)):
        at = 0

        def put(source, rows):
            span = target.at[pl.ds(at, rows)]
            copies.append(fetch(source, span, sem.at[len(copies)]))

        for base in (INNER, 0):
            for k in range(2):
                first = aligned(base + (2 * y + k) * HALF + core * BLOCK)
                put(w.at[pl.ds(first, BLOCK)], BLOCK)
                at += BLOCK
        bc = w.at[pl.ds(2 * INNER, 2 * STATE)]
        span = target.at[pl.ds(at, 2 * STATE)]
        copies.append(fetch_one_of(y == 0, bc, steps, span, sem.at[len(copies)]))
        at += 2 * STATE
        for k in range(2):
            cols = pl.ds(aligned(y * HALF + k * BLOCK), BLOCK)
            put(o.at[pl.ds(aligned(core * BLOCK), BLOCK), cols], BLOCK)
            at += BLOCK
    for copy in copies:
        copy.wait()


def pack_weights(scalars, w, steps, o):
    return pl.pallas_call(
        pack_kernel,
        in_specs=[pl.BlockSpec(memory_space=pltpu.SMEM), ANY, ANY, ANY],
        out_specs=[NEAR, NEAR],
        out_shape=[pltpu.VMEM((PACKED_ROWS, BLOCK), BF16)] * 2,
        scratch_shapes=[pltpu.SemaphoreType.DMA((14,))],
        compiler_params=pltpu.CompilerParams(vmem_limit_bytes=4 << 20),
        cost_estimate=LITTLE,
        name="pack_weights",
    )(scalars, away(w), steps, away(o))


def place_kernel(sc, own, rest, *refs):
    (near_z, inner_2, outer_2, inner_3, outer_3), (win, wout, sem) = (
        [refs[2 * i : 2 * i + 2] for i in range(5)],
        refs[-3:],
    )
    side, place = sc[1], sc[2]
    inner = jnp.logical_and(place > 0, place < 3)
    second = jnp.where(inner, 3 - place, jnp.where(place == 0, 2, 1))
    third = jnp.where(place < 2, 3, 0)
    used = []

    def put(source, z, y, start):
        lanes = pl.ds(aligned(z * BLOCK), BLOCK)
        at = 0
        for k, (matrix, rows, first, step) in enumerate(PARTS):
            if matrix == "in":
                target = win.at[pl.ds(aligned(first + y * step), rows), lanes]
            else:
                target = wout.at[lanes, pl.ds(aligned(first + y * step), BLOCK)]
            copy = pltpu.make_async_copy(source.at[pl.ds(at, rows)], target, sem.at[start + k])
            copy.start()
            used.append(copy)
            at += rows

    put(own, place, side, 0)
    put(rest, place, 1 - side, 5)
    put(near_z[0], place + 1 - 2 * lax.rem(place, 2), side, 10)
    put(near_z[1], place + 1 - 2 * lax.rem(place, 2), 1 - side, 15)
    waits = list(used)

    @pl.when(inner)
    def _():
        put(inner_2[0], second, side, 20)
        put(inner_2[1], second, 1 - side, 25)
        put(inner_3[0], third, side, 30)
        put(inner_3[1], third, 1 - side, 35)
        for copy in used[20:]:
            copy.wait()
        del used[20:]

    @pl.when(jnp.logical_not(inner))
    def _():
        put(outer_2[0], second, side, 20)
        put(outer_2[1], second, 1 - side, 25)
        put(outer_3[0], third, side, 30)
        put(outer_3[1], third, 1 - side, 35)
        for copy in used[20:]:
            copy.wait()

    for copy in waits:
        copy.wait()


def place_weights(here, own, rest, pairs):
    inputs = [own, rest, *sum(pairs, ())]
    return pl.pallas_call(
        place_kernel,
        in_specs=[pl.BlockSpec(memory_space=pltpu.SMEM)] + [ANY] * len(inputs),
        out_specs=[NEAR, NEAR],
        out_shape=[pltpu.VMEM((OWN_PROJ, D), BF16), pltpu.VMEM((OWN, D), BF16)],
        scratch_shapes=[pltpu.SemaphoreType.DMA((40,))],
        compiler_params=pltpu.CompilerParams(vmem_limit_bytes=4 << 20),
        cost_estimate=LITTLE,
        name="place_weights",
    )(here, *inputs)


def line_gather(own, beside):
    def along(value, hops):
        route = [(y * 4 + a, y * 4 + b) for y in range(2) for a, b in hops]
        return lax.ppermute(value, ("y", "fsdp"), route)

    def across(value, places):
        route = [(y * 4 + z, (1 - y) * 4 + z) for y in range(2) for z in places]
        return lax.ppermute(value, ("y", "fsdp"), route)

    outward, middle = [(1, 0), (2, 3)], [(1, 2), (2, 1)]
    near_z = along(own, [(0, 1), (1, 0), (2, 3), (3, 2)])
    inner_2 = along(own, middle)
    near_z, inner_2, *beside = lax.optimization_barrier((near_z, inner_2, *beside))
    outer_2 = along(inner_2, outward)
    inner_3 = along(near_z, middle)
    near_y = across(near_z, range(4))
    outer_2, inner_3, near_y = lax.optimization_barrier((outer_2, inner_3, near_y))
    outer_3 = along(inner_3, outward)
    outer_2_y = across(outer_2, (0, 3))
    inner_2_y = across(inner_2, (1, 2))
    outer_3, outer_2_y, inner_2_y = lax.optimization_barrier((outer_3, outer_2_y, inner_2_y))
    ready = inner_2_y
    outer_3_y = across(outer_3, (0, 3))
    inner_3_y = across(inner_3, (1, 2))
    return [
        (near_z, near_y),
        (inner_2, inner_2_y),
        (outer_2, outer_2_y),
        (inner_3, inner_3_y),
        (outer_3, outer_3_y),
    ], ready, beside


GROUPS = (
    (1, (HALF, X_AT, HALF), (LANES, BC_AT, 2 * STATE)),
    (-1, (HALF, 0, HALF), (LANES, BC_AT + LANES, 2 * STATE)),
)


SMALL_ROWS = 16
IN_ROWS = HALF + LANES
GROUP_ROWS = IN_ROWS + BLOCK


def block_grad_kernel(row, sc, normed_ref, q_ref, gs_ref, *refs):
    out = refs[-1]
    chunks = normed_ref.shape[0]
    at = 0
    for ref in refs[:2]:
        width = ref.shape[2]
        value = sum(dot_tn(ref[k], normed_ref[k]) for k in range(chunks))
        out[at : at + width, :] = value.astype(BF16)
        at += width
    out[at:, :] = sum(dot_tn(q_ref[k], gs_ref[k]) for k in range(chunks)).astype(BF16)
    if len(refs) > 3:

        @pl.when(sc[row, 0] == 1)
        def _():
            out[HALF : HALF + SMALL_ROWS, :] = refs[2][0].astype(BF16)


def block_grad(table, row, group, normed_held, grads_held, q_held, gs_held, small):
    slots, t, _ = normed_held.shape
    number, (_, *parts) = group, GROUPS[group]

    def block(width, index):
        return pl.BlockSpec((slots - 1, t, width), lambda i, s: (0, 0, index(s)))

    in_specs = [
        block(BLOCK, lambda s: s[row, 1]),
        block(BLOCK, lambda s: s[row, 1]),
        block(BLOCK, lambda s: 2 * s[row, 0] + number),
    ]
    for width, first, step in parts:

        def index(s, width=width, first=first, step=step):
            return first // width + s[row, 0] * (step // width)

        in_specs.append(block(width, index))
    extra = []
    if number == 1:
        extra = [small]
        in_specs.append(pl.BlockSpec((1, SMALL_ROWS, BLOCK), lambda i, s: (s[row, 1], 0, 0)))
    return pl.pallas_call(
        functools.partial(block_grad_kernel, row),
        grid_spec=pltpu.PrefetchScalarGridSpec(
            num_scalar_prefetch=1,
            grid=(1,),
            in_specs=in_specs,
            out_specs=pl.BlockSpec((GROUP_ROWS, BLOCK), lambda i, s: (0, 0)),
        ),
        out_shape=jax.ShapeDtypeStruct((GROUP_ROWS, BLOCK), BF16),
        compiler_params=pltpu.CompilerParams(vmem_limit_bytes=24 << 20),
        cost_estimate=LITTLE,
        name="block_grad",
    )(
        table,
        away(normed_held),
        away(q_held),
        away(gs_held),
        *([away(grads_held)] * len(parts)),
        *extra,
    )


def grads_kernel(sc, *refs):
    in_hbm, out_hbm, small_out, in_v, out_v, sem = refs[-6:]
    core, side = sc[0], sc[1]

    def block(i, c, y, rows):
        own, across, other, far = refs[4 * i : 4 * i + 4]
        here = jnp.where(side == y, own[rows], across[rows])
        there = jnp.where(side == y, other[rows], far[rows])
        return jnp.where(core == c, here, there).astype(F32)

    copies = []

    def store(values, near_ref, far_ref, at):
        near_ref[at : at + values.shape[0]] = values
        span = pl.ds(at, values.shape[0])
        copies.append(fetch(near_ref.at[span], far_ref.at[span], sem.at[len(copies)]))

    for i, base in ((0, INNER), (1, 0)):
        for c in range(2):
            for y in range(2):
                for k in range(2):
                    rows = slice(k * BLOCK, (k + 1) * BLOCK)
                    store(block(i, c, y, rows), in_v, in_hbm, base + (2 * y + k) * HALF + c * BLOCK)
    rows = slice(HALF, HALF + STATE)
    for i in range(2):
        store(block(i, 0, 0, rows) + block(i, 1, 0, rows), in_v, in_hbm, 2 * INNER + i * STATE)
    steps = [block(0, c, 1, slice(HALF, HALF + 32)) for c in range(2)]
    steps = [steps[c][z * 6 : z * 6 + 6] for z in range(4) for c in range(2)]
    store(jnp.concatenate(steps, axis=0), in_v, in_hbm, INNER + CONV_CH)
    rows = slice(HALF, HALF + SMALL_ROWS)
    small_out[...] = block(1, 0, 1, rows) + block(1, 1, 1, rows)
    rows = slice(IN_ROWS, GROUP_ROWS)
    for c in range(2):
        values = [block(i, c, y, rows) for y in range(2) for i in range(2)]
        store(jnp.concatenate(values, axis=1), out_v, out_hbm, c * BLOCK)
    for copy in copies:
        copy.wait()


def join_grads(scalars, parts):
    arrays = [near(a) for part in parts for a in part]
    height = INNER + CONV_CH + HEADS
    shapes = ((height, BLOCK), F32), ((2 * BLOCK, D), F32)
    return pl.pallas_call(
        grads_kernel,
        in_specs=[pl.BlockSpec(memory_space=pltpu.SMEM)] + [NEAR] * len(arrays),
        out_specs=[ANY, ANY, NEAR],
        out_shape=[pltpu.HBM(*k) for k in shapes] + [pltpu.VMEM((SMALL_ROWS, BLOCK), F32)],
        scratch_shapes=[pltpu.VMEM(*k) for k in shapes] + [pltpu.SemaphoreType.DMA((24,))],
        compiler_params=pltpu.CompilerParams(vmem_limit_bytes=28 << 20),
        cost_estimate=LITTLE,
        name="join_grads",
    )(scalars, *arrays)


def swap(value, axis):
    return lax.ppermute(value, axis, [(0, 1), (1, 0)])


def sent_along(value, axis):
    size = lax.axis_size(axis)
    routes = [[(i, (i + k) % size) for i in range(size)] for k in range(1, size)]
    return [lax.ppermute(value, axis, path) for path in routes]


def in_order(value, others, axis):
    size, place = len(others) + 1, lax.axis_index(axis)
    ring = jnp.stack([*others[::-1], value] * 2)
    return lax.dynamic_slice_in_dim(ring, (size - 1 - place) % size, size, 0)


LAG = 2


def relay_shards(
    ends,
    norm_gain,
    input_weight,
    conv_weight,
    conv_bias,
    dt_bias,
    a_log,
    skip_gain,
    gate_gain,
    output_weight,
):
    core = lax.axis_index("core")
    place = lax.axis_index("fsdp")
    side = lax.axis_index("y")
    section = lax.axis_index("section")
    leading = (section == 0).astype(jnp.int32)
    local = ends[0][:, 0]
    t = local.shape[1]
    chunks = lax.axis_size("fsdp")
    micro = place // 2

    small = [norm_gain[0], conv_weight[0].reshape(-1), conv_bias[0], dt_bias[0], a_log[0]]
    small += [skip_gain[0], gate_gain[0]]
    packed = jnp.concatenate(small)
    others = sent_along(packed, "fsdp")
    w = input_weight[0].T
    steps = own_steps(w, core)
    here = jnp.stack([core, side, place]).astype(jnp.int32)
    own, rest = pack_weights(here, w, steps, output_weight[0])
    pairs, ready, others = line_gather(own, others)
    packed = in_order(packed, others, "fsdp")
    pieces, at = [], 0
    for member in small:
        pieces.append(packed[:, at : at + member.shape[0]].reshape(-1))
        at += member.shape[0]
    pieces[1] = pieces[1].reshape(CONV_CH, KERNEL)
    gain, convp, headp, chanp = small_params(*pieces, core)
    local, _ = lax.optimization_barrier((local, ready))

    def route(first, m):
        return [
            (c * chunks + z, (z % 2) * chunks + 2 * m + c)
            for c in range(2)
            for z in (first, first + 1)
        ]

    def bring(first):
        return [lax.ppermute(local[m], ("core", "fsdp"), route(first, m)) for m in range(2)]

    def shared(got):
        got = jnp.where(micro == 0, got[0], got[1])
        other = swap(got, "core")
        return [jnp.where(core == 0, got, other), jnp.where(core == 0, other, got)]

    def give(piece, first):
        return [
            lax.ppermute(piece, ("core", "fsdp"), [(b, a) for a, b in route(first, m)])
            for m in range(2)
        ]

    last = (*pairs[3], *pairs[4])
    here, *got = lax.optimization_barrier((here, *bring(0), *bring(2), *last))
    got, pairs[3:] = got[:4], [tuple(got[4:6]), tuple(got[6:8])]
    pieces = shared(got[:2]) + shared(got[2:])
    win, wout = place_weights(here, own, rest, pairs)
    params = (gain, convp, headp, chanp, win, wout)

    def scalars(moment, lag, reverse):
        begin = jnp.where(leading == 1, lag if reverse else 0, 0 if reverse else lag)
        step = moment - begin
        valid = jnp.logical_and(step >= 0, step < chunks)
        inside = jnp.clip(step, 0, chunks - 1)
        chunk = chunks - 1 - inside if reverse else inside
        write = jnp.where(valid, chunk, chunks)
        edge_here = leading == 1 if reverse else leading == 0
        edge = jnp.where(jnp.logical_and(valid, edge_here), chunk, chunks)
        values = [chunk if reverse else write, leading, step == 0, valid, write, edge, core]
        return [jnp.asarray(v, jnp.int32) for v in values]

    moments = chunks + LAG
    table = [scalars(moment, LAG, False) for moment in range(moments)]
    table += [scalars(moment, LAG, True) for moment in range(moments)]
    table = jnp.stack(sum(table, [])).reshape(len(table), -1)
    size = 2 * chunks
    position = jnp.where(side == 0, place, size - 1 - place).astype(jnp.int32)
    owners = []
    for direction in (1, -1):
        for hop in range(size):
            owners += ring_place((position - direction * (1 + hop)) % size, chunks)
    owners = jnp.stack(owners).reshape(2 * size, 2).astype(jnp.int32)
    table, owners = lax.optimization_barrier((table, owners))

    state, tail = jnp.zeros((STATE, OWN), F32), jnp.zeros((8, OWN_CONV), F32)
    blank = jnp.zeros((t, D), BF16)
    held, joined, result = None, None, None
    moved, incoming = {}, {}
    for moment in range(moments):
        if moment > 0:
            tail, result = lax.optimization_barrier((tail, result))
            if moment - 1 < chunks:
                moved[moment - 1] = lax.ppermute(result, "section", [(0, 1)])
        arrived = incoming.get(moment - LAG, (blank[: t // 2],) * 2)
        partial, h, (state, tail), held = forward_call(
            table,
            moment,
            chunks + 1,
            pieces[min(moment, chunks - 1)],
            arrived,
            params,
            (state, tail),
            held,
        )
        if moment - 1 in moved:
            partial, got = lax.optimization_barrier((partial, moved[moment - 1]))
            incoming[moment - 1] = (got, swap(got, "core"))
        other = swap(partial, "core")
        result, joined = forward_join(table, moment, chunks + 1, partial, other, h, joined)
    h_held, normed_held, pr_held, mx_held, q_held, st_held, tl_held = held
    y_held, ri_held, edge_held = joined
    saved = (h_held, normed_held, pr_held, mx_held, st_held, tl_held, y_held, ri_held)

    def tokens(buffer):
        return buffer[:chunks].reshape(chunks * t, buffer.shape[-1])

    carry = (
        jnp.zeros((STATE, OWN), F32),
        jnp.zeros((8, OWN_CONV), F32),
        jnp.zeros((8, OWN), F32),
        jnp.zeros((16, OWN_CONV), F32),
    )
    grads_held = None
    moved, incoming = {}, {}
    for moment in range(moments):
        if moment > 0:
            *carry, acc = carry
            acc, result = lax.optimization_barrier((acc, result))
            carry = (*carry, acc)
            if moment - 1 < chunks:
                moved[moment - 1] = lax.ppermute(result, "section", [(1, 0)])
        arrived = incoming.get(moment - LAG, (blank[: t // 2],) * 2)
        cot = pieces[max(chunks - 1 - moment, 0)]
        (partial, g, h), carry, grads_held = backward_call(
            table, moments + moment, chunks + 1, cot, arrived, saved, params, carry, grads_held
        )
        if moment - 1 in moved:
            partial, got = lax.optimization_barrier((partial, moved[moment - 1]))
            incoming[moment - 1] = (got, swap(got, "core"))
        other = swap(partial, "core")
        result, edge_held = backward_join(
            table, moments + moment, partial, other, h, g, gain, edge_held
        )

    def both(own, other, index):
        return jnp.where(index == 0, jnp.stack([own, other]), jnp.stack([other, own]))

    acc = carry[3]

    def placed(own):
        zero = jnp.zeros_like(own)
        return woven(both(own, zero, core))

    taps = jnp.concatenate([placed(acc[:5, :OWN]), acc[:5, OWN:]], axis=1)
    taps = jnp.moveaxis(taps.reshape(KERNEL + 1, chunks, -1), 1, 0)
    skip = acc[5, :OWN].reshape(OWN_HEADS, HEAD_DIM).sum(axis=1)
    vectors = [
        acc[9, :D] / gain[0],
        taps,
        placed(acc[7, :OWN_HEADS]),
        placed(acc[8, :OWN_HEADS]),
        placed(skip),
        placed(acc[6, :OWN]),
    ]
    vectors = [v.reshape(chunks, -1) for v in vectors]
    small = jnp.concatenate(vectors, axis=1)
    small = jnp.pad(small, ((0, 0), (0, SMALL_ROWS * BLOCK - small.shape[1])))
    small = small.reshape(chunks, SMALL_ROWS, BLOCK)

    onward, back = ring_route(chunks, 1), ring_route(chunks, -1)
    grads_held, gs_held = grads_held
    sums = [None] * len(GROUPS)
    for hop in range(size):
        if hop > 0:
            owners, *sums = lax.optimization_barrier((owners, *sums))
        for i, (direction, *_) in enumerate(GROUPS):
            row = hop + (0 if direction == 1 else size)
            block = block_grad(owners, row, i, normed_held, grads_held, q_held, gs_held, small)
            if hop > 0:
                path = onward if direction == 1 else back
                came = lax.ppermute(sums[i], ("y", "fsdp"), path).astype(F32)
                block = (block.astype(F32) + came).astype(BF16)
            sums[i] = block
        if hop == 3:
            finished = pick(table, edge_held, 0), pick(table, edge_held, 2)
            owners, *finished = lax.optimization_barrier((owners, *finished))
    *sums, early, late = lax.optimization_barrier((*sums, *finished))

    edges = jnp.where(place < 2, jnp.stack(give(early, 0)), jnp.stack(give(late, 2)))
    edges = edges[None, :, None]
    parts = []
    for own in sums:
        across = swap(own, "y")
        parts.append((own, across, swap(own, "core"), swap(across, "core")))
    here = jnp.stack([core, side]).astype(jnp.int32)
    here, edges = lax.optimization_barrier((here, edges))
    in_grad, out_grad, summed = join_grads(here, parts)
    in_grad = in_grad.T
    summed = summed.reshape(-1)
    grads, at = [], 0
    for v in vectors:
        grads.append(summed[at : at + v.shape[1]][None])
        at += v.shape[1]
    taps = grads[1].reshape(KERNEL + 1, -1)
    grads[1:2] = taps[:KERNEL].T[None], taps[KERNEL:]
    return (
        edges,
        grads[0],
        in_grad[None],
        grads[1],
        grads[2],
        grads[3],
        grads[4],
        grads[5],
        grads[6],
        out_grad[None],
    )


def shifted(block, axis, distance):
    devices = range(lax.axis_size(axis))
    route = [(i - distance, i) for i in devices if i - distance in devices]
    return lax.ppermute(block, axis, route)


def prefix(value, axis, join, neutral):
    place = lax.axis_index(axis)
    gathered = jax.tree.map(
        lambda a, kind: lax.all_gather(a.astype(kind), axis), value, (jnp.bfloat16, jnp.bfloat16)
    )
    state = jax.tree.map(lambda a, e: jnp.zeros_like(a) + jnp.asarray(e, a.dtype), value, neutral)

    def one(turn, state):
        return join(
            state,
            jax.tree.map(
                lambda a, own: lax.dynamic_index_in_dim(a, turn, 0, False).astype(own.dtype),
                gathered,
                value,
            ),
        )

    return lax.fori_loop(0, place, one, state)


def prefix_2(value, axis, join, neutral):
    count = lax.axis_size(axis)
    place = lax.axis_index(axis)
    ahead = count - 1 - place
    gathered = jax.tree.map(
        lambda a, kind: lax.all_gather(a.astype(kind), axis),
        value,
        jax.tree.map(lambda a: jnp.bfloat16 if a.dtype == jnp.float32 else a.dtype, value),
    )
    state = jax.tree.map(lambda a, e: jnp.zeros_like(a) + jnp.asarray(e, a.dtype), value, neutral)

    def one(turn, state):
        source = count - 1 - turn
        return join(
            state,
            jax.tree.map(
                lambda a, own: lax.dynamic_index_in_dim(a, source, 0, False).astype(own.dtype),
                gathered,
                value,
            ),
        )

    return lax.fori_loop(0, ahead, one, state)


def rms_scale(values, scale_gain):
    return (
        values * lax.rsqrt(jnp.mean(values * values, axis=-1, keepdims=True) + EPSILON) * scale_gain
    )


def chain_rule(earlier, later_part):
    return (
        earlier[0] * later_part[0],
        later_part[1] + later_part[0][:, :, None, None] * earlier[1],
    )


def conv_features(widened, conv_weight, conv_bias, dt_raw, dt_bias, a_log):
    tap_count = conv_weight.shape[1]
    step_count = widened.shape[1] - tap_count + 1
    convolved = conv_bias
    for offset in range(tap_count):
        convolved = convolved + widened[:, offset : offset + step_count, :] * conv_weight[:, offset]
    activated = jax.nn.silu(convolved)
    x_heads = activated[..., :INNER]
    b_rows = activated[..., INNER : INNER + STATE]
    c_rows = activated[..., INNER + STATE :]
    dt_step = jax.nn.softplus(dt_raw + dt_bias)
    log_decay = jnp.cumsum(-jnp.exp(a_log) * dt_step, axis=1)
    return (x_heads, b_rows, c_rows, dt_step, log_decay)


def local_states(x_heads, b_rows, dt_step, log_decay):
    seq_count, length = (x_heads.shape[0], x_heads.shape[1])
    spread = x_heads.reshape(seq_count, length, HEADS, HEAD_DIM)
    weights = jnp.exp(log_decay[:, -1:, :] - log_decay) * dt_step
    weighted = spread * weights[..., None]
    states = jnp.einsum("sqhd,sqn->shdn", weighted, b_rows, precision=EXACT_MATMUL)
    return (jnp.exp(log_decay[:, -1]), states)


def gated_output(
    x_heads, b_rows, c_rows, dt_step, log_decay, prior_state, gate_z, skip_gain, gate_gain
):
    seq_count, length = (x_heads.shape[0], x_heads.shape[1])
    spread = x_heads.reshape(seq_count, length, HEADS, HEAD_DIM)
    scaled = spread * dt_step[..., None]
    by_head = jnp.transpose(log_decay, (0, 2, 1))
    differ = by_head[:, :, :, None] - by_head[:, :, None, :]
    causal = jnp.arange(length)[:, None] >= jnp.arange(length)[None, :]
    mixing = jnp.where(causal, jnp.exp(jnp.where(causal, differ, 0.0)), 0.0)
    intersections = jnp.einsum("sqn,skn->sqk", c_rows, b_rows, precision=EXACT_MATMUL)
    mixed_out = jnp.einsum(
        "shqk,skhd->sqhd", mixing * intersections[:, None], scaled, precision=EXACT_MATMUL
    )
    mixed_out = mixed_out + jnp.exp(log_decay)[..., None] * jnp.einsum(
        "sqn,shdn->sqhd", c_rows, prior_state, precision=EXACT_MATMUL
    )
    mixed_out = (mixed_out + skip_gain[:, None] * spread).reshape(seq_count, length, INNER)
    return rms_scale(mixed_out * jax.nn.silu(gate_z), gate_gain)


def layer_forward(hidden, weights):
    (
        norm_gain,
        input_weight,
        conv_weight,
        conv_bias,
        dt_bias,
        a_log,
        skip_gain,
        gate_gain,
        output_weight,
    ) = weights
    normalized_rows = rms_scale(hidden, norm_gain.astype(jnp.float32)).astype(jnp.bfloat16)
    projected_rows = jnp.einsum(
        "spd,de->spe", normalized_rows, input_weight, preferred_element_type=jnp.float32
    ).astype(jnp.bfloat16)
    length = hidden.shape[1]
    xbc_part = projected_rows[..., INNER : INNER + CONV_CH]
    border = shifted(xbc_part[:, length - KERNEL + 1 :, :], "fsdp", 1)
    widened = jnp.concatenate([border, xbc_part], axis=1)
    features = conv_features(
        widened.astype(jnp.float32),
        conv_weight.astype(jnp.float32),
        conv_bias.astype(jnp.float32),
        projected_rows[..., INNER + CONV_CH :].astype(jnp.float32),
        dt_bias.astype(jnp.float32),
        a_log.astype(jnp.float32),
    )
    decays, states = local_states(features[0], features[1], features[3], features[4])
    scanned = prefix(
        (decays, states), "fsdp", chain_rule, (jnp.ones_like(decays), jnp.zeros_like(states))
    )
    prior_state = scanned[1]
    gated_result = gated_output(
        features[0],
        features[1],
        features[2],
        features[3],
        features[4],
        prior_state,
        projected_rows[..., :INNER].astype(jnp.float32),
        skip_gain.astype(jnp.float32),
        gate_gain.astype(jnp.float32),
    )
    gated_low = gated_result.astype(jnp.bfloat16)
    final_result = hidden + jnp.einsum(
        "spi,id->spd", gated_low, output_weight, preferred_element_type=jnp.float32
    )
    return (
        final_result,
        (hidden, normalized_rows, projected_rows, widened, prior_state, gated_low),
    )


def layer_backward(gradient, kept_state, weights):
    hidden, normalized_rows, projected_rows, widened, prior_state, gated_low = kept_state
    (
        norm_gain,
        input_weight,
        conv_weight,
        conv_bias,
        dt_bias,
        a_log,
        skip_gain,
        gate_gain,
        output_weight,
    ) = weights
    grad_low = gradient.astype(jnp.bfloat16)
    grad_out_weight = jnp.einsum(
        "spi,spd->id", gated_low, grad_low, preferred_element_type=jnp.float32
    )
    grad_gated = jnp.einsum(
        "spd,id->spi", grad_low, output_weight, preferred_element_type=jnp.float32
    )
    features, pull_features = jax.vjp(
        conv_features,
        widened.astype(jnp.float32),
        conv_weight.astype(jnp.float32),
        conv_bias.astype(jnp.float32),
        projected_rows[..., INNER + CONV_CH :].astype(jnp.float32),
        dt_bias.astype(jnp.float32),
        a_log.astype(jnp.float32),
    )
    _, pull_gated = jax.vjp(
        gated_output,
        features[0],
        features[1],
        features[2],
        features[3],
        features[4],
        prior_state,
        projected_rows[..., :INNER].astype(jnp.float32),
        skip_gain.astype(jnp.float32),
        gate_gain.astype(jnp.float32),
    )
    grads_gated = pull_gated(grad_gated)
    decay_states, pull_states = jax.vjp(
        local_states, features[0], features[1], features[3], features[4]
    )
    decays = decay_states[0]
    later_state = prefix_2(
        (decays, grads_gated[5]),
        "fsdp",
        chain_rule,
        (jnp.ones_like(decays), jnp.zeros_like(grads_gated[5])),
    )
    grad_end = later_state[1]
    state_parts = pull_states((jnp.sum(grad_end * prior_state, axis=(2, 3)), grad_end))
    feature_grads = (
        grads_gated[0] + state_parts[0],
        grads_gated[1] + state_parts[1],
        grads_gated[2],
        grads_gated[3] + state_parts[2],
        grads_gated[4] + state_parts[3],
    )
    grad_wide, grad_conv_w, grad_conv_b, grad_dt_raw, grad_dt_bias, grad_a_log = pull_features(
        feature_grads
    )
    margin = KERNEL - 1
    returned = shifted(grad_wide[:, :margin, :].astype(jnp.bfloat16), "fsdp", -1).astype(
        jnp.float32
    )
    own_rows = grad_wide[:, margin:, :]
    length = own_rows.shape[1]
    grad_xbc = jnp.concatenate(
        [own_rows[:, : length - margin], own_rows[:, length - margin :] + returned], axis=1
    )
    grad_proj = jnp.concatenate([grads_gated[6], grad_xbc, grad_dt_raw], axis=-1).astype(
        jnp.bfloat16
    )
    grad_in_weight = jnp.einsum(
        "spd,spe->de", normalized_rows, grad_proj, preferred_element_type=jnp.float32
    )
    grad_normed = jnp.einsum(
        "spe,de->spd", grad_proj, input_weight, preferred_element_type=jnp.float32
    )
    _, pull_norm = jax.vjp(rms_scale, hidden, norm_gain.astype(jnp.float32))
    grad_hidden, grad_norm_gain = pull_norm(grad_normed)
    return (
        gradient + grad_hidden,
        (
            grad_norm_gain,
            grad_in_weight,
            grad_conv_w,
            grad_conv_b,
            grad_dt_bias,
            grad_a_log,
            grads_gated[7],
            grads_gated[8],
            grad_out_weight,
        ),
    )


def shards(
    ends,
    norm_gain,
    input_weight,
    conv_weight,
    conv_bias,
    dt_bias,
    a_log,
    skip_gain,
    gate_gain,
    output_weight,
):
    gathered = (
        lax.all_gather(norm_gain, "fsdp", axis=1, tiled=True),
        lax.all_gather(input_weight, "fsdp", axis=1, tiled=True),
        lax.all_gather(conv_weight, "fsdp", axis=1, tiled=True),
        lax.all_gather(conv_bias, "fsdp", axis=1, tiled=True),
        lax.all_gather(dt_bias, "fsdp", axis=1, tiled=True),
        lax.all_gather(a_log, "fsdp", axis=1, tiled=True),
        lax.all_gather(skip_gain, "fsdp", axis=1, tiled=True),
        lax.all_gather(gate_gain, "fsdp", axis=1, tiled=True),
        lax.all_gather(output_weight, "fsdp", axis=1, tiled=True),
    )
    layer_weights = tuple((member[0] for member in gathered))
    leading = lax.axis_index("section") == 0
    local_data = ends[0].astype(jnp.float32)
    batches = local_data.shape[0]
    arrived = jnp.zeros(local_data.shape[1:], jnp.float32)
    stored = []
    produced = []
    for moment in range(batches + 1):
        source = jnp.where(leading, local_data[min(moment, batches - 1)], arrived)
        final_result, kept_state = layer_forward(source, layer_weights)
        stored.append(kept_state)
        produced.append(final_result)
        if moment < batches:
            arrived = shifted(final_result.astype(jnp.bfloat16), "section", 1).astype(jnp.float32)
    totals = None
    coming = jnp.zeros(local_data.shape[1:], jnp.float32)
    returned_grads = []
    for moment in range(batches + 1):
        gradient = jnp.where(leading, coming, local_data[min(moment, batches - 1)])
        kept_state = jax.tree.map(
            lambda upper_part, lower_part: jnp.where(leading, upper_part, lower_part),
            stored[max(moment - 1, 0)],
            stored[min(moment + 1, batches)],
        )
        grad_input, gradients = layer_backward(gradient, kept_state, layer_weights)
        active = jnp.where(leading, moment >= 1, moment < batches)
        masked = tuple((jnp.where(active, member, 0.0) for member in gradients))
        if totals is None:
            totals = masked
        else:
            totals = tuple((earlier_sum + member for earlier_sum, member in zip(totals, masked)))
        returned_grads.append(grad_input)
        if moment < batches:
            coming = shifted(grad_input.astype(jnp.bfloat16), "section", -1).astype(jnp.float32)
    boundary = jnp.stack(
        [
            jnp.where(leading, returned_grads[number + 1], produced[number + 1])
            for number in range(batches)
        ]
    )
    owned_parts = (
        lax.psum_scatter(
            totals[0][None].astype(jnp.bfloat16), "fsdp", scatter_dimension=1, tiled=True
        ).astype(jnp.float32),
        lax.psum_scatter(
            totals[1][None].astype(jnp.bfloat16), "fsdp", scatter_dimension=1, tiled=True
        ).astype(jnp.float32),
        lax.psum_scatter(
            totals[2][None].astype(jnp.bfloat16), "fsdp", scatter_dimension=1, tiled=True
        ).astype(jnp.float32),
        lax.psum_scatter(
            totals[3][None].astype(jnp.bfloat16), "fsdp", scatter_dimension=1, tiled=True
        ).astype(jnp.float32),
        lax.psum_scatter(
            totals[4][None].astype(jnp.bfloat16), "fsdp", scatter_dimension=1, tiled=True
        ).astype(jnp.float32),
        lax.psum_scatter(
            totals[5][None].astype(jnp.bfloat16), "fsdp", scatter_dimension=1, tiled=True
        ).astype(jnp.float32),
        lax.psum_scatter(
            totals[6][None].astype(jnp.bfloat16), "fsdp", scatter_dimension=1, tiled=True
        ).astype(jnp.float32),
        lax.psum_scatter(
            totals[7][None].astype(jnp.bfloat16), "fsdp", scatter_dimension=1, tiled=True
        ).astype(jnp.float32),
        lax.psum_scatter(
            totals[8][None].astype(jnp.bfloat16), "fsdp", scatter_dimension=1, tiled=True
        ).astype(jnp.float32),
    )
    summed = (
        lax.psum(owned_parts[0].astype(jnp.bfloat16), "rep").astype(jnp.float32),
        lax.psum(owned_parts[1].astype(jnp.bfloat16), "rep").astype(jnp.float32),
        lax.psum(owned_parts[2].astype(jnp.bfloat16), "rep").astype(jnp.float32),
        lax.psum(owned_parts[3].astype(jnp.bfloat16), "rep").astype(jnp.float32),
        lax.psum(owned_parts[4].astype(jnp.bfloat16), "rep").astype(jnp.float32),
        lax.psum(owned_parts[5].astype(jnp.bfloat16), "rep").astype(jnp.float32),
        lax.psum(owned_parts[6].astype(jnp.bfloat16), "rep").astype(jnp.float32),
        lax.psum(owned_parts[7].astype(jnp.bfloat16), "rep").astype(jnp.float32),
        lax.psum(owned_parts[8].astype(jnp.bfloat16), "rep").astype(jnp.float32),
    )
    return (
        boundary.astype(jnp.bfloat16)[None],
        summed[0],
        summed[1],
        summed[2],
        summed[3],
        summed[4],
        summed[5],
        summed[6],
        summed[7],
        summed[8],
    )


def solution(mesh):
    shape = mesh.shape
    relay = shape["section"] == 2 and shape["rep"] == 4 and shape["fsdp"] == 4
    if relay:
        devices = mesh.devices.reshape(2, 2, 2, 4)
        mesh = Mesh(devices, ("section", "y", "core", "fsdp"))
    rep = ("y", "core") if relay else "rep"
    data = P("section", None, rep, "fsdp", None)
    vector, matrix = P("section", "fsdp"), P("section", "fsdp", None)
    params = (vector, matrix, matrix, vector, vector, vector, vector, vector, matrix)
    return jax.shard_map(
        relay_shards if relay else shards,
        mesh=mesh,
        in_specs=(data, *params),
        out_specs=(data, *params),
        check_vma=False,
    )
```

```python
import functools

import jax
import jax.numpy as jnp
from jax import lax
from jax.experimental import pallas as pl
from jax.experimental.pallas import tpu as pltpu
from jax.sharding import Mesh
from jax.sharding import PartitionSpec as P

D = 1536
HEADS = 48
HEAD_DIM = 64
STATE = 128
KERNEL = 4
INNER = 3072
CONV_CH = 3328
LANES = 128

OWN = INNER // 2
OWN_HEADS = HEADS // 2
OWN_CONV = OWN + 2 * STATE
X_AT = OWN
BC_AT = 2 * OWN
DT_AT = 2 * OWN + 2 * STATE
OWN_PROJ = DT_AT + 2 * LANES
PAIRS = OWN // LANES

EPSILON = 1e-05
EXACT_MATMUL = lax.Precision.HIGHEST
F32 = jnp.float32
BF16 = jnp.bfloat16
FORWARD_VMEM = 24
BACKWARD_VMEM = 30
JOIN_VMEM = 12


def dot(a, b):
    return lax.dot_general(a, b, (((1,), (0,)), ((), ())), preferred_element_type=F32)


def dot_nt(a, b):
    return lax.dot_general(a, b, (((1,), (1,)), ((), ())), preferred_element_type=F32)


def dot_tn(a, b):
    return lax.dot_general(a, b, (((0,), (0,)), ((), ())), preferred_element_type=F32)


def split(v, parts):
    pieces = []
    for _ in range(parts):
        piece = v.astype(BF16)
        pieces.append(piece)
        v = v - piece.astype(F32)
    return pieces


def sigmoid(v):
    return 0.5 * jnp.tanh(0.5 * v) + 0.5


def softplus(v):
    return jnp.maximum(v, 0.0) + jnp.log1p(jnp.exp(-jnp.abs(v)))


def step_sizes(dt_raw, headp):
    t = dt_raw.shape[0]
    biased = dt_raw + headp[0:1]
    dt = softplus(biased)
    rows = lax.broadcasted_iota(jnp.int32, (t, t), 0)
    cols = lax.broadcasted_iota(jnp.int32, (t, t), 1)
    tri = jnp.where(rows >= cols, 1.0, 0.0).astype(BF16)
    ld = sum(dot(tri, part) for part in split(dt * headp[1:2], 3))
    return dt, ld, biased


def at_head(v, pair):
    turned = pltpu.roll(v, lax.rem(LANES - 2 * pair, LANES), 1)
    return [jnp.broadcast_to(turned[:, i : i + 1], v.shape) for i in range(2)]


def decay_blocks(col, row, swapped):
    n = col.shape[0] // 2
    rows = lax.broadcasted_iota(jnp.int32, (n, n), 0)
    cols = lax.broadcasted_iota(jnp.int32, (n, n), 1)
    keep = rows <= cols if swapped else rows >= cols

    def block(i, j):
        down, along = col[i * n : (i + 1) * n], row[:, j * n : (j + 1) * n]
        differ = along - down if swapped else down - along
        return jnp.exp(jnp.where(keep, differ, -1e30) if i == j else differ)

    return block(0, 0), block(0, 1) if swapped else block(1, 0), block(1, 1)


def convolve(xw, sl, convp, t):
    out = convp[4:5, sl] + xw[5 : 5 + t, sl] * convp[0:1, sl]
    for k in range(1, KERNEL):
        out = out + xw[5 + k : 5 + k + t, sl] * convp[k : k + 1, sl]
    return out


def pair_loop(step):
    def two(turn, _):
        step(2 * turn)
        step(2 * turn + 1)
        return 0

    lax.fori_loop(0, PAIRS // 2, two, 0)


def aligned(value):
    return pl.multiple_of(value, LANES)


def fetch(source, target, sem):
    copy = pltpu.make_async_copy(source, target, sem)
    copy.start()
    return copy


def fetch_one_of(first, one, other, target, sem):
    @pl.when(first)
    def _():
        pltpu.make_async_copy(one, target, sem).start()

    @pl.when(jnp.logical_not(first))
    def _():
        pltpu.make_async_copy(other, target, sem).start()

    return pltpu.make_async_copy(other, target, sem)


def forward_kernel(row, sc, *refs):
    @pl.when(sc[row, VALID] == 1)
    def _():
        forward_chunk(row, sc, *refs)


def forward_chunk(
    row, sc, got_hbm, other_hbm, x_hbm, ng_ref, convp, headp, chanp, st_ref, tail_ref, win, wout, *rest
):
    p, h, st_out, tail_out = rest[-22:-18]
    h_hbm, n_hbm, pr_hbm, mx_hbm, q_hbm, st_hbm, tl_hbm = rest[-18:-11]
    normed, pr, mx, q, sti, tl, xw, ldt, ss, g_ref, sem = rest[-11:]
    t = h.shape[0]
    half = t // 2
    slot = sc[row, SLOT]
    first = sc[row, FIRST] == 1
    leading = sc[row, LEADING] == 1
    core = sc[row, CORE]

    @pl.when(leading)
    def _():
        fetch(x_hbm, h, sem.at[0]).wait()

    @pl.when(jnp.logical_not(leading))
    def _():
        mine = h.at[pl.ds(aligned(core * half), half)]
        theirs = h.at[pl.ds(aligned((1 - core) * half), half)]
        copies = fetch(got_hbm, mine, sem.at[0]), fetch(other_hbm, theirs, sem.at[1])
        for copy in copies:
            copy.wait()

    stores = [fetch(h, h_hbm.at[slot], sem.at[0])]
    hf = h[...].astype(F32)
    r = lax.rsqrt(jnp.mean(hf * hf, axis=1, keepdims=True) + EPSILON)
    normed[...] = (hf * r * ng_ref[...]).astype(BF16)
    stores.append(fetch(normed, n_hbm.at[slot], sem.at[1]))

    sti[...] = jnp.where(first, 0.0, st_ref[...])
    tl[...] = jnp.where(first, 0.0, tail_ref[...])
    stores.append(fetch(sti, st_hbm.at[slot], sem.at[2]))
    stores.append(fetch(tl, tl_hbm.at[slot], sem.at[3]))
    xw[0:8, :] = tl[...]

    for at in range(0, OWN_PROJ, 512):
        cols = slice(at, min(at + 512, OWN_PROJ))
        pr[:, cols] = dot_nt(normed[...], win[cols, :]).astype(BF16)
    stores.append(fetch(pr, pr_hbm.at[slot], sem.at[4]))
    tail_out[...] = pr[t - 8 : t, X_AT : X_AT + OWN_CONV].astype(F32)

    bc = pl.ds(OWN, 2 * STATE)
    xw[8 : 8 + t, OWN:OWN_CONV] = pr[:, BC_AT:DT_AT].astype(F32)
    conv_bc = convolve(xw, bc, convp, t)
    act = (conv_bc * sigmoid(conv_bc)).astype(BF16)
    b, c = act[:, :STATE], act[:, STATE:]
    g_ref[...] = dot_nt(c, b)
    b_turned = act[:, :STATE].astype(F32).T.astype(BF16)
    dt, ld, _ = step_sizes(pr[:, DT_AT : DT_AT + LANES].astype(F32), headp[...])
    ldt[...] = ld.T
    left = lax.broadcasted_iota(jnp.int32, (t, LANES), 1) < HEAD_DIM
    ss[...] = jnp.zeros_like(ss)

    def pair_step(pair):
        at = pl.multiple_of(pair * LANES, LANES)
        sl = pl.ds(at, LANES)
        xw[8 : 8 + t, sl] = pr[:, pl.ds(X_AT + at, LANES)].astype(F32)
        conv = convolve(xw, sl, convp, t)
        x = conv * sigmoid(conv)
        cols = at_head(ld, pair)
        u = jnp.where(left, *at_head(dt, pair)) * x
        ld_p = jnp.where(left, *cols)
        tops, bottoms, sides = [], [], []
        for i in range(2):
            u_i = jnp.where(left if i == 0 else jnp.logical_not(left), u, 0.0).astype(BF16)
            d00, d10, d11 = decay_blocks(cols[i], ldt[pl.ds(2 * pair + i, 1), :], False)
            m00 = (g_ref[:half, :half] * d00).astype(BF16)
            m10 = (g_ref[half:, :half] * d10).astype(BF16)
            m11 = (g_ref[half:, half:] * d11).astype(BF16)
            tops.append(m00)
            bottoms += [m10, m11]
            sides.append(u_i)
        top = dot(jnp.concatenate(tops, axis=1), jnp.concatenate([v[:half] for v in sides], axis=0))
        bottom = dot(jnp.concatenate(bottoms, axis=1), jnp.concatenate(sides, axis=0))
        eld = jnp.exp(ld_p)
        st = sti[:, sl]
        y = jnp.concatenate([top, bottom], axis=0) + eld * dot(c, st.astype(BF16))
        weighted = (u * jnp.exp(ld_p[t - 1 : t] - ld_p)).astype(BF16)
        st_out[:, sl] = eld[t - 1 : t] * st + dot(b_turned, weighted)
        mixed = y + chanp[0:1, sl] * x
        mx[:, sl] = mixed
        z = pr[:, sl].astype(F32)
        gated = mixed * (z * sigmoid(z))
        ss[...] += gated * gated
        q[:, sl] = (gated * chanp[1:2, sl]).astype(BF16)

    pair_loop(pair_step)
    stores.append(fetch(mx, mx_hbm.at[slot], sem.at[5]))
    stores.append(fetch(q, q_hbm.at[slot], sem.at[6]))
    total = jnp.sum(ss[...], axis=1, keepdims=True)
    high = total.astype(BF16).astype(F32)
    lane = lax.broadcasted_iota(jnp.int32, (t, LANES), 1)
    p[:, D:] = jnp.where(lane == 0, high, jnp.where(lane == 1, total - high, 0.0)).astype(BF16)
    for at in range(0, D, 512):
        p[:, at : at + 512] = dot(q[...], wout[:, at : at + 512]).astype(BF16)
    for store in stores:
        store.wait()


def backward_kernel(row, sc, *refs):
    acc_ref, acc_out = refs[17], refs[-21]

    @pl.when(sc[row, VALID] == 1)
    def _():
        backward_chunk(row, sc, *refs)

    @pl.when(sc[row, VALID] == 0)
    def _():
        acc_out[...] = acc_ref[...]


def backward_chunk(
    row,
    sc,
    arrived_hbm,
    other_hbm,
    cot_hbm,
    h_hbm,
    n_hbm,
    pr_hbm,
    mx_hbm,
    st_hbm,
    tl_hbm,
    y_hbm,
    ri_hbm,
    convp,
    headp,
    chanp,
    dst_ref,
    dc_ref,
    val_ref,
    acc_ref,
    win,
    wout,
    *rest,
):
    gn, g_ref, h_out, dst_out, dc_out, val_out, acc_out, gp_hbm, gs_hbm = rest[-27:-18]
    pr, mx, st_ref, tl, y_ref, ri, gp, gs, normed = rest[-18:-9]
    xw, dw, ldt, gw, gt, dgt, dci, dbi, sem = rest[-9:]
    t = g_ref.shape[0]
    half = t // 2
    slot = sc[row, SLOT]
    last = sc[row, FIRST] == 1
    leading = sc[row, LEADING] == 1
    core = sc[row, CORE]
    mine = g_ref.at[pl.ds(aligned(core * half), half)]
    theirs = g_ref.at[pl.ds(aligned((1 - core) * half), half)]

    @pl.when(leading)
    def _():
        pltpu.make_async_copy(arrived_hbm, mine, sem.at[0]).start()
        pltpu.make_async_copy(other_hbm, theirs, sem.at[10]).start()

    @pl.when(jnp.logical_not(leading))
    def _():
        pltpu.make_async_copy(cot_hbm, g_ref, sem.at[0]).start()

    y_copy = fetch(y_hbm.at[slot], y_ref, sem.at[1])
    ri_copy = fetch(ri_hbm.at[slot], ri, sem.at[2])
    pr_copy = fetch(pr_hbm.at[slot], pr, sem.at[3])
    tl_copy = fetch(tl_hbm.at[slot], tl, sem.at[4])
    mx_copy = fetch(mx_hbm.at[slot], mx, sem.at[5])
    st_copy = fetch(st_hbm.at[slot], st_ref, sem.at[6])

    acc_out[...] = acc_ref[...]
    dw[t : t + 8, :] = jnp.where(last, 0.0, dc_ref[...])
    dgt[...] = jnp.zeros_like(dgt)
    dci[...] = jnp.zeros_like(dci)
    dbi[...] = jnp.zeros_like(dbi)

    @pl.when(leading)
    def _():
        pltpu.make_async_copy(arrived_hbm, mine, sem.at[0]).wait()
        pltpu.make_async_copy(other_hbm, theirs, sem.at[10]).wait()

    @pl.when(jnp.logical_not(leading))
    def _():
        pltpu.make_async_copy(cot_hbm, g_ref, sem.at[0]).wait()

    for at in range(0, OWN, 512):
        gw[:, at : at + 512] = dot_nt(g_ref[...], wout[at : at + 512, :])
    y_copy.wait()
    ri_copy.wait()
    rinv = ri[:, 0:1]
    mean = jnp.sum(g_ref[...].astype(F32) * y_ref[...].astype(F32), axis=1, keepdims=True)
    lean = rinv * rinv * (mean * (1.0 / INNER))
    gs[...] = (g_ref[...].astype(F32) * rinv).astype(BF16)
    gs_store = fetch(gs, gs_hbm.at[sc[row, WRITE]], sem.at[7])
    pr_copy.wait()
    tl_copy.wait()
    xw[0:8, :] = tl[...]

    bc = pl.ds(OWN, 2 * STATE)
    xw[8 : 8 + t, OWN:OWN_CONV] = pr[:, BC_AT:DT_AT].astype(F32)
    conv_bc = convolve(xw, bc, convp, t)
    sig_bc = sigmoid(conv_bc)
    act = (conv_bc * sig_bc).astype(BF16)
    b, c = act[:, :STATE], act[:, STATE:]
    c_turned = c.astype(F32).T.astype(BF16)
    gt[...] = dot_nt(b, c)
    dt, ld, biased = step_sizes(pr[:, DT_AT : DT_AT + LANES].astype(F32), headp[...])
    ldt[...] = ld.T
    left = lax.broadcasted_iota(jnp.int32, (t, LANES), 1) < HEAD_DIM

    def add(line, sl, v):
        acc_out[line : line + 1, sl] += v

    def conv_back(dact, conv, sig, sl):
        dconv = dact * (sig * (1.0 + conv * (1.0 - sig)))
        dw[0:t, sl] = dconv
        add(4, sl, jnp.sum(dconv, axis=0, keepdims=True))
        for k in range(KERNEL):
            add(k, sl, jnp.sum(dconv * xw[5 + k : 5 + k + t, sl], axis=0, keepdims=True))
        dx = dconv * convp[KERNEL - 1 : KERNEL, sl]
        for k in range(KERNEL - 1):
            ahead = KERNEL - 1 - k
            dx = dx + dw[ahead : ahead + t, sl] * convp[k : k + 1, sl]
        return dx.astype(BF16)

    lane_head = lax.rem(lax.broadcasted_iota(jnp.int32, (2 * LANES, LANES), 0), LANES) // HEAD_DIM
    head_lane = lax.broadcasted_iota(jnp.int32, (2 * LANES, LANES), 1)
    mx_copy.wait()
    st_copy.wait()
    h_copy = fetch(h_hbm.at[slot], h_out, sem.at[8])
    n_copy = fetch(n_hbm.at[slot], normed, sem.at[9])

    def pair_step(pair, carry):
        ddt, dld, dval = carry
        at = pl.multiple_of(pair * LANES, LANES)
        sl = pl.ds(at, LANES)
        xsl = pl.ds(X_AT + at, LANES)
        xw[8 : 8 + t, sl] = pr[:, xsl].astype(F32)
        conv = convolve(xw, sl, convp, t)
        sig = sigmoid(conv)
        x = conv * sig
        z = pr[:, sl].astype(F32)
        sig_z = sigmoid(z)
        s = z * sig_z
        mixed = mx[:, sl]
        gated = mixed * s
        scaled = gw[:, sl] * rinv
        add(6, sl, jnp.sum(scaled * gated, axis=0, keepdims=True))
        dgated = chanp[1:2, sl] * scaled - gated * lean
        dy = dgated * s
        gp[:, sl] = (dgated * mixed * (sig_z * (1.0 + z * (1.0 - sig_z)))).astype(BF16)
        skip = chanp[0:1, sl]
        add(5, sl, jnp.sum(dy * x, axis=0, keepdims=True))
        y = mixed - skip * x

        cols = at_head(ld, pair)
        ld_p = jnp.where(left, *cols)
        eld = jnp.exp(ld_p)
        wend = jnp.exp(ld_p[t - 1 : t] - ld_p)
        dt_p = jnp.where(left, *at_head(dt, pair))
        u = dt_p * x
        u_low = u.astype(BF16)
        dy_low = dy.astype(BF16)
        dst = jnp.where(last, 0.0, dst_ref[:, sl])
        dst_low = dst.astype(BF16)
        top = jnp.zeros((half, LANES), F32)
        bottom = top
        for i in range(2):
            side = left if i == 0 else jnp.logical_not(left)
            d00, d01, d11 = decay_blocks(cols[i], ldt[pl.ds(2 * pair + i, 1), :], True)
            m00 = (gt[:half, :half] * d00).astype(BF16)
            m01 = (gt[:half, half:] * d01).astype(BF16)
            m11 = (gt[half:, half:] * d11).astype(BF16)
            dy_i = jnp.where(side, dy, 0.0).astype(BF16)
            top = top + dot(jnp.concatenate([m00, m01], axis=1), dy_i)
            bottom = bottom + dot(m11, dy_i[half:])
            u_i = jnp.where(side, u, 0.0).astype(BF16)
            dm = dot_nt(u_i[:half], dy_low)
            dgt[:half, :half] += dm[:, :half] * d00
            dgt[:half, half:] += dm[:, half:] * d01
            dgt[half:, half:] += dot_nt(u_i[half:], dy_low[half:]) * d11
        du = jnp.concatenate([top, bottom], axis=0) + wend * dot(b, dst_low)
        st = st_ref[:, sl]
        dyl = (eld * dy).astype(BF16)
        dst_new = eld[t - 1 : t] * dst + dot(c_turned, dyl)
        dst_out[:, sl] = dst_new
        val_out[:, sl] = jnp.broadcast_to(
            jnp.sum(dst_new * st, axis=0, keepdims=True), (8, LANES)
        )
        dci[...] += dot_nt(dyl, st.astype(BF16))
        dbi[...] += dot_nt((wend * u).astype(BF16), dst_low)

        pick = jnp.where(lane_head + 2 * pair == head_lane, 1.0, 0.0).astype(BF16)


        def by_head(v):
            return dot(jnp.concatenate(split(v, 2), axis=1), pick)

        ddt = ddt + by_head(du * x)
        dld = dld + by_head(dy_low.astype(F32) * y - u_low.astype(F32) * du)
        dval = dval + by_head(jnp.where(last, 0.0, val_ref[:, sl]))
        gp[:, xsl] = conv_back(dt_p * du + skip * dy, conv, sig, sl)
        return ddt, dld, dval

    zero = jnp.zeros((t, LANES), F32)
    ddt, dld, dval = lax.fori_loop(
        0,
        PAIRS // 2,
        lambda turn, carry: pair_step(2 * turn + 1, pair_step(2 * turn, carry)),
        (zero, zero, jnp.zeros((8, LANES), F32)),
    )

    dgt_low = dgt[...].astype(BF16)
    db = dbi[...] + dot(dgt_low, c)
    dc = dci[...] + dot_tn(dgt_low, b)
    gp[:, BC_AT:DT_AT] = conv_back(jnp.concatenate([db, dc], axis=1), conv_bc, sig_bc, bc)

    rows = lax.broadcasted_iota(jnp.int32, (t, t), 0)
    cols = lax.broadcasted_iota(jnp.int32, (t, t), 1)
    upper = jnp.where(rows <= cols, 1.0, 0.0).astype(BF16)
    da = sum(dot(upper, part) for part in split(dld, 3)) + dval[0:1]
    rate = headp[1:2]
    head = pl.ds(0, LANES)
    add(8, head, jnp.sum(da * rate * dt, axis=0, keepdims=True))
    ddt_raw = (ddt + rate * da) * sigmoid(biased)
    add(7, head, jnp.sum(ddt_raw, axis=0, keepdims=True))
    gp[:, DT_AT : DT_AT + LANES] = ddt_raw.astype(BF16)
    gp[:, DT_AT + LANES :] = jnp.zeros((t, LANES), BF16)
    gp_store = fetch(gp, gp_hbm.at[sc[row, WRITE]], sem.at[0])
    dc_out[...] = dw[0:8, :]
    n_copy.wait()
    for at in range(0, D, 512):
        cols = slice(at, at + 512)
        values = dot(gp[...], win[:, cols])
        gn[:, cols] = values.astype(BF16)
        add(9, cols, jnp.sum(values * normed[:, cols].astype(F32), axis=0, keepdims=True))
    gp_store.wait()
    gs_store.wait()
    h_copy.wait()


def forward_join_kernel(row, sc, own_ref, other_ref, h_ref, *rest):
    out, y_hbm, ri_hbm, e_hbm, y_v, ri_v, low_v, sem = rest[-8:]
    half = out.shape[0]

    @pl.when(sc[row, VALID] == 1)
    def _():
        copies = []
        for k in range(2):
            rows = slice(k * half, (k + 1) * half)
            total = own_ref[rows].astype(F32) + other_ref[rows].astype(F32)
            square = total[:, D : D + 1] + total[:, D + 1 : D + 2]
            rinv = lax.rsqrt(square * (1.0 / INNER) + EPSILON)
            y = total[:, :D] * rinv
            y_v[rows] = y.astype(BF16)
            ri_v[rows] = jnp.broadcast_to(rinv, (half, LANES))
            low_v[rows] = (h_ref[rows].astype(F32) + y).astype(BF16)
            pieces = ((y_v, y_hbm, SLOT), (ri_v, ri_hbm, SLOT), (low_v, e_hbm, EDGE))
            for near_ref, far_ref, which in pieces:
                target = far_ref.at[sc[row, which], pl.ds(k * half, half)]
                copies.append(fetch(near_ref.at[pl.ds(k * half, half)], target, sem.at[len(copies)]))
        out[...] = low_v[pl.ds(aligned(sc[row, CORE] * half), half), :]
        for copy in copies:
            copy.wait()


def backward_join_kernel(row, sc, own_ref, other_ref, h_ref, g_ref, ng_ref, *rest):
    out, e_hbm, low_v, sem = rest[-4:]
    half = out.shape[0]

    @pl.when(sc[row, VALID] == 1)
    def _():
        copies = []
        for k in range(2):
            rows = slice(k * half, (k + 1) * half)
            gn = own_ref[rows].astype(F32) + other_ref[rows].astype(F32)
            h = h_ref[rows].astype(F32)
            r = lax.rsqrt(jnp.mean(h * h, axis=1, keepdims=True) + EPSILON)
            t = gn * ng_ref[...]
            m = jnp.mean(h * t, axis=1, keepdims=True)
            low_v[rows] = (g_ref[rows].astype(F32) + r * (t - h * (r * r * m))).astype(BF16)
            target = e_hbm.at[sc[row, EDGE], pl.ds(k * half, half)]
            copies.append(fetch(low_v.at[pl.ds(k * half, half)], target, sem.at[k]))
        out[...] = low_v[pl.ds(aligned(sc[row, CORE] * half), half), :]
        for copy in copies:
            copy.wait()


def pick_kernel(first, sc, stack_hbm, out, sem):
    fetch(stack_hbm.at[first + sc[0, CORE]], out, sem.at[0]).wait()


ANY = pl.BlockSpec(memory_space=pl.ANY)
NEAR = pl.BlockSpec(memory_space=pltpu.VMEM)
SLOT, LEADING, FIRST, VALID, WRITE, EDGE, CORE = range(7)
LITTLE = pl.CostEstimate(flops=1 << 20, bytes_accessed=1 << 16, transcendentals=0)


def near(value):
    return pltpu.with_memory_space_constraint(value, pltpu.VMEM)


def away(value):
    return pltpu.with_memory_space_constraint(value, pltpu.HBM)


def chunk_call(kernel, table, free, far, close, close_outs, buffers, scratch, limit, name):
    inputs = [table, *free, *(away(v) for v in far), *(near(v) for v in close)]
    in_specs = [pl.BlockSpec(memory_space=pltpu.SMEM)]
    in_specs += [ANY] * (len(free) + len(far)) + [NEAR] * len(close)
    outs = [pltpu.VMEM(*o) for o in close_outs]
    out_specs = [NEAR] * len(close_outs)
    aliases = {}
    for held, shape, dtype in buffers:
        if held is not None:
            aliases[len(inputs)] = len(outs)
            inputs.append(away(held))
            in_specs.append(ANY)
        outs.append(pltpu.HBM(shape, dtype))
        out_specs.append(ANY)
    results = pl.pallas_call(
        kernel,
        in_specs=in_specs,
        out_specs=out_specs,
        out_shape=outs,
        scratch_shapes=scratch,
        input_output_aliases=aliases,
        compiler_params=pltpu.CompilerParams(vmem_limit_bytes=limit << 20),
        cost_estimate=LITTLE,
        name=name,
    )(*inputs)
    return tuple(results[: len(close_outs)]), tuple(results[len(close_outs) :])


def forward_call(table, row, slots, x, arrived, params, carry, held):
    t = x.shape[0]
    held = held or (None,) * 7
    kinds = (
        ((t, D), BF16),
        ((t, D), BF16),
        ((t, OWN_PROJ), BF16),
        ((t, OWN), F32),
        ((t, OWN), BF16),
        ((STATE, OWN), F32),
        ((8, OWN_CONV), F32),
    )
    gain, convp, headp, chanp, win, wout = params
    outs, held = chunk_call(
        functools.partial(forward_kernel, row),
        table,
        (*arrived, x),
        (),
        (gain, convp, headp, chanp, *carry, win, wout),
        (((t, D + LANES), BF16), kinds[0], kinds[5], kinds[6]),
        [(b, (slots,) + k, d) for b, (k, d) in zip(held, kinds)],
        [pltpu.VMEM(*k) for k in kinds[1:]]
        + [
            pltpu.VMEM((t + 8, OWN_CONV), F32),
            pltpu.VMEM((LANES, t), F32),
            pltpu.VMEM((t, LANES), F32),
            pltpu.VMEM((t, t), F32),
            pltpu.SemaphoreType.DMA((8,)),
        ],
        FORWARD_VMEM,
        "forward_chunk",
    )
    return outs[0], outs[1], outs[2:], held


def backward_call(table, row, slots, cot, arrived, saved, params, carry, held):
    t = cot.shape[0]
    held = held or (None, None)
    _, convp, headp, chanp, win, wout = params
    wide, projected = ((t, D), BF16), ((t, OWN_PROJ), BF16)
    outs, held = chunk_call(
        functools.partial(backward_kernel, row),
        table,
        (*arrived, cot),
        saved,
        (convp, headp, chanp, *carry, win, wout),
        [wide] * 3 + [(v.shape, v.dtype) for v in carry],
        [(held[0], (slots, t, OWN_PROJ), BF16), (held[1], (slots, t, D), BF16)],
        [
            pltpu.VMEM(*projected),
            pltpu.VMEM((t, OWN), F32),
            pltpu.VMEM((STATE, OWN), F32),
            pltpu.VMEM((8, OWN_CONV), F32),
            pltpu.VMEM(*wide),
            pltpu.VMEM((t, LANES), F32),
            pltpu.VMEM(*projected),
            pltpu.VMEM(*wide),
            pltpu.VMEM(*wide),
            pltpu.VMEM((t + 8, OWN_CONV), F32),
            pltpu.VMEM((t + 8, OWN_CONV), F32),
            pltpu.VMEM((LANES, t), F32),
            pltpu.VMEM((t, OWN), F32),
            pltpu.VMEM((t, t), F32),
            pltpu.VMEM((t, t), F32),
            pltpu.VMEM((t, STATE), F32),
            pltpu.VMEM((t, STATE), F32),
            pltpu.SemaphoreType.DMA((11,)),
        ],
        BACKWARD_VMEM,
        "backward_chunk",
    )
    return outs[:3], outs[3:], held


def forward_join(table, row, slots, own, other, h, held):
    t = h.shape[0]
    held = held or (None,) * 3
    wide, thin = ((t, D), BF16), ((t, LANES), F32)
    outs, held = chunk_call(
        functools.partial(forward_join_kernel, row),
        table,
        (),
        (),
        (own, other, h),
        [((t // 2, D), BF16)],
        [(b, (slots,) + k, d) for b, (k, d) in zip(held, (wide, thin, wide))],
        [pltpu.VMEM(*k) for k in (wide, thin, wide)] + [pltpu.SemaphoreType.DMA((6,))],
        JOIN_VMEM,
        "forward_join",
    )
    return outs[0], held


def backward_join(table, row, own, other, h, g, gain, edge_held):
    slots, t, _ = edge_held.shape
    outs, held = chunk_call(
        functools.partial(backward_join_kernel, row),
        table,
        (),
        (),
        (own, other, h, g, gain),
        [((t // 2, D), BF16)],
        [(edge_held, (slots, t, D), BF16)],
        [pltpu.VMEM((t, D), BF16), pltpu.SemaphoreType.DMA((2,))],
        JOIN_VMEM,
        "backward_join",
    )
    return outs[0], held[0]


def pick(table, stack, first):
    outs, _ = chunk_call(
        functools.partial(pick_kernel, first),
        table,
        (),
        (stack,),
        (),
        [(stack.shape[1:], stack.dtype)],
        [],
        [pltpu.SemaphoreType.DMA((1,))],
        JOIN_VMEM,
        "pick",
    )
    return outs[0]


def own_of(values, core):
    lead, width = values.shape[:-1], values.shape[-1]
    blocks = values.reshape(lead + (4, 2, width // 8))
    return lax.dynamic_index_in_dim(blocks, core, len(lead) + 1, False).reshape(
        lead + (width // 2,)
    )


def woven(halves):
    width = halves.shape[-1]
    lead = halves.shape[1:-1]
    blocks = halves.reshape((2,) + lead + (4, width // 4))
    return jnp.moveaxis(blocks, 0, -2).reshape(lead + (2 * width,))


def small_params(norm_gain, conv_weight, conv_bias, dt_bias, a_log, skip_gain, gate_gain, core):
    own = functools.partial(own_of, core=core)
    taps = jnp.concatenate([conv_weight.T, conv_bias[None]], axis=0).astype(F32)
    taps = jnp.concatenate([own(taps[:, :INNER]), taps[:, INNER:]], axis=1)
    convp = jnp.pad(taps, ((0, 3), (0, 0)))
    heads = jnp.stack([own(dt_bias.astype(F32)), -jnp.exp(own(a_log.astype(F32)))])
    headp = jnp.pad(heads, ((0, 6), (0, LANES - OWN_HEADS)))
    skip = jnp.repeat(own(skip_gain.astype(F32)), HEAD_DIM)
    chanp = jnp.pad(jnp.stack([skip, own(gate_gain.astype(F32))]), ((0, 6), (0, 0)))
    return norm_gain.astype(F32)[None], convp, headp, chanp


def own_steps(weight, core):
    own = own_of(weight[INNER + CONV_CH :].T, core).T
    return jnp.pad(own, ((0, 2 * LANES - OWN_HEADS), (0, 0)))


HALF = OWN // 2
BLOCK = HALF // 2
PACKED_ROWS = HALF + HALF + 2 * STATE + 2 * BLOCK
PARTS = (
    ("in", HALF, X_AT, HALF),
    ("in", HALF, 0, HALF),
    ("in", 2 * STATE, BC_AT, 2 * STATE),
    ("out", BLOCK, 0, HALF),
    ("out", BLOCK, BLOCK, HALF),
)


def ring_place(position, count):
    back = position >= count
    return jnp.where(back, 1, 0), jnp.where(back, 2 * count - 1 - position, position)


def ring_route(count, step):
    def index(position):
        return position if position < count else count + (2 * count - 1 - position)

    size = 2 * count
    return [(index(p), index((p + step) % size)) for p in range(size)]


HALF_ROWS = PACKED_ROWS // 2


def cut(at, rows):
    spans = []
    for i in range(2):
        a, b = max(at, i * HALF_ROWS), min(at + rows, (i + 1) * HALF_ROWS)
        if a < b:
            spans.append((i, a - i * HALF_ROWS, a - at, b - a))
    return spans


def pack_kernel(sc, w, steps, o, own_a, own_b, rest_a, rest_b, sem):
    core, side = sc[0], sc[1]
    copies = []
    for targets, y in (((own_a, own_b), side), ((rest_a, rest_b), 1 - side)):
        at = 0
        for base in (INNER, 0):
            for k in range(2):
                first = base + (2 * y + k) * HALF + core * BLOCK
                for i, to, off, rows in cut(at, BLOCK):
                    source = w.at[pl.ds(aligned(first + off), rows)]
                    copies.append(fetch(source, targets[i].at[pl.ds(to, rows)], sem.at[len(copies)]))
                at += BLOCK
        bc = w.at[pl.ds(2 * INNER, 2 * STATE)]
        ((i, to, _, rows),) = cut(at, 2 * STATE)
        span = targets[i].at[pl.ds(to, rows)]
        copies.append(fetch_one_of(y == 0, bc, steps, span, sem.at[len(copies)]))
        at += 2 * STATE
        for k in range(2):
            ((i, to, _, rows),) = cut(at, BLOCK)
            cols = pl.ds(aligned(y * HALF + k * BLOCK), BLOCK)
            source = o.at[pl.ds(aligned(core * BLOCK), BLOCK), cols]
            copies.append(fetch(source, targets[i].at[pl.ds(to, rows)], sem.at[len(copies)]))
            at += BLOCK
    for copy in copies:
        copy.wait()


def pack_weights(scalars, w, steps, o):
    return pl.pallas_call(
        pack_kernel,
        in_specs=[pl.BlockSpec(memory_space=pltpu.SMEM), ANY, ANY, ANY],
        out_specs=[NEAR, NEAR, NEAR, NEAR],
        out_shape=[pltpu.VMEM((HALF_ROWS, BLOCK), BF16)] * 4,
        scratch_shapes=[pltpu.SemaphoreType.DMA((16,))],
        compiler_params=pltpu.CompilerParams(vmem_limit_bytes=4 << 20),
        cost_estimate=LITTLE,
        name="pack_weights",
    )(scalars, away(w), steps, away(o))


def place_kernel(sc, *refs):
    blocks, (win, wout, sem) = [refs[2 * i : 2 * i + 2] for i in range(12)], refs[-3:]
    side, place = sc[1], sc[2]
    inner = jnp.logical_and(place > 0, place < 3)
    second = jnp.where(inner, 3 - place, jnp.where(place == 0, 2, 1))
    third = jnp.where(place < 2, 3, 0)

    def put(number, block, z, y):
        lanes = pl.ds(aligned(z * BLOCK), BLOCK)
        copies, at = [], 0
        for matrix, rows, first, step in PARTS:
            for i, to, off, count in cut(at, rows):
                if matrix == "in":
                    span = pl.ds(aligned(first + y * step + off), count)
                    target = win.at[span, lanes]
                else:
                    target = wout.at[lanes, pl.ds(aligned(first + y * step), BLOCK)]
                source = blocks[block][i].at[pl.ds(to, count)]
                copies.append(fetch(source, target, sem.at[8 * number + len(copies)]))
            at += rows
        return copies

    beside = place + 1 - 2 * lax.rem(place, 2)
    always = put(0, 0, place, side) + put(1, 1, place, 1 - side)
    always += put(2, 2, beside, side) + put(3, 3, beside, 1 - side)

    def rest(first):
        copies = put(4, first, second, side) + put(5, first + 1, second, 1 - side)
        copies += put(6, first + 4, third, side) + put(7, first + 5, third, 1 - side)
        for copy in copies:
            copy.wait()

    @pl.when(inner)
    def _():
        rest(4)

    @pl.when(jnp.logical_not(inner))
    def _():
        rest(6)

    for copy in always:
        copy.wait()


def place_weights(here, blocks):
    inputs = [away(half) for block in blocks for half in block]
    return pl.pallas_call(
        place_kernel,
        in_specs=[pl.BlockSpec(memory_space=pltpu.SMEM)] + [ANY] * len(inputs),
        out_specs=[NEAR, NEAR],
        out_shape=[pltpu.VMEM((OWN_PROJ, D), BF16), pltpu.VMEM((OWN, D), BF16)],
        scratch_shapes=[pltpu.SemaphoreType.DMA((64,))],
        compiler_params=pltpu.CompilerParams(vmem_limit_bytes=4 << 20),
        cost_estimate=LITTLE,
        name="place_weights",
    )(here, *inputs)


def line_gather(own, beside):
    def along(value, hops):
        path = [(y * 4 + a, y * 4 + b) for y in range(2) for a, b in hops]
        return lax.ppermute(value, ("y", "fsdp"), path)

    def across(value, places):
        path = [(y * 4 + z, (1 - y) * 4 + z) for y in range(2) for z in places]
        return lax.ppermute(value, ("y", "fsdp"), path)

    pair, middle, outward = [(0, 1), (1, 0), (2, 3), (3, 2)], [(1, 2), (2, 1)], [(1, 0), (2, 3)]
    inner, outer = (1, 2), (0, 3)
    barrier = lax.optimization_barrier
    a, b = own
    near_a, in2_a = along(a, pair), along(a, middle)
    near_a, in2_a, b, *beside = barrier((near_a, in2_a, b, *beside))
    near_b, in2_b, near_ya = along(b, pair), along(b, middle), across(near_a, range(4))
    near_a, in2_a, near_b, in2_b, near_ya = barrier((near_a, in2_a, near_b, in2_b, near_ya))
    out2_a, in3_a, near_yb = along(in2_a, outward), along(near_a, middle), across(near_b, range(4))
    out2_a, in3_a, near_yb, in2_a, near_b, in2_b = barrier(
        (out2_a, in3_a, near_yb, in2_a, near_b, in2_b)
    )
    out2_b, in3_b = along(in2_b, outward), along(near_b, middle)
    out2_ya, in2_ya = across(out2_a, outer), across(in2_a, inner)
    out2_b, in3_b, out2_ya, in2_ya, in3_a, in2_b = barrier(
        (out2_b, in3_b, out2_ya, in2_ya, in3_a, in2_b)
    )
    out3_a = along(in3_a, outward)
    out2_yb, in2_yb = across(out2_b, outer), across(in2_b, inner)
    out3_a, out2_yb, in2_yb, in3_a, in3_b = barrier((out3_a, out2_yb, in2_yb, in3_a, in3_b))
    out3_b = along(in3_b, outward)
    out3_ya, in3_ya = across(out3_a, outer), across(in3_a, inner)
    ready = out2_yb
    out3_b, out3_ya, in3_ya, in3_b = barrier((out3_b, out3_ya, in3_ya, in3_b))
    out3_yb, in3_yb = across(out3_b, outer), across(in3_b, inner)
    blocks = [
        (near_a, near_b),
        (near_ya, near_yb),
        (in2_a, in2_b),
        (in2_ya, in2_yb),
        (out2_a, out2_b),
        (out2_ya, out2_yb),
        (in3_a, in3_b),
        (in3_ya, in3_yb),
        (out3_a, out3_b),
        (out3_ya, out3_yb),
    ]
    return blocks, beside, ready


GROUPS = (
    (1, (HALF, X_AT, HALF), (LANES, BC_AT, 2 * STATE)),
    (-1, (HALF, 0, HALF), (LANES, BC_AT + LANES, 2 * STATE)),
)


SMALL_ROWS = 16
IN_ROWS = HALF + LANES
GROUP_ROWS = IN_ROWS + BLOCK


def block_grad_kernel(row, sc, normed_ref, q_ref, gs_ref, *refs):
    out = refs[-1]
    chunks = normed_ref.shape[0]
    at = 0
    for ref in refs[:2]:
        width = ref.shape[2]
        value = sum(dot_tn(ref[k], normed_ref[k]) for k in range(chunks))
        out[at : at + width, :] = value.astype(BF16)
        at += width
    out[at:, :] = sum(dot_tn(q_ref[k], gs_ref[k]) for k in range(chunks)).astype(BF16)
    if len(refs) > 3:

        @pl.when(sc[row, 0] == 1)
        def _():
            out[HALF : HALF + SMALL_ROWS, :] = refs[2][0].astype(BF16)


def block_grad(table, row, group, normed_held, grads_held, q_held, gs_held, small):
    slots, t, _ = normed_held.shape
    number, (_, *parts) = group, GROUPS[group]

    def block(width, index):
        return pl.BlockSpec((slots - 1, t, width), lambda i, s: (0, 0, index(s)))

    in_specs = [
        block(BLOCK, lambda s: s[row, 1]),
        block(BLOCK, lambda s: s[row, 1]),
        block(BLOCK, lambda s: 2 * s[row, 0] + number),
    ]
    for width, first, step in parts:

        def index(s, width=width, first=first, step=step):
            return first // width + s[row, 0] * (step // width)

        in_specs.append(block(width, index))
    extra = []
    if number == 1:
        extra = [small]
        in_specs.append(pl.BlockSpec((1, SMALL_ROWS, BLOCK), lambda i, s: (s[row, 1], 0, 0)))
    return pl.pallas_call(
        functools.partial(block_grad_kernel, row),
        grid_spec=pltpu.PrefetchScalarGridSpec(
            num_scalar_prefetch=1,
            grid=(1,),
            in_specs=in_specs,
            out_specs=pl.BlockSpec((GROUP_ROWS, BLOCK), lambda i, s: (0, 0)),
        ),
        out_shape=jax.ShapeDtypeStruct((GROUP_ROWS, BLOCK), BF16),
        compiler_params=pltpu.CompilerParams(vmem_limit_bytes=24 << 20),
        cost_estimate=LITTLE,
        name="block_grad",
    )(
        table,
        away(normed_held),
        away(q_held),
        away(gs_held),
        *([away(grads_held)] * len(parts)),
        *extra,
    )


def grads_kernel(sc, *refs):
    in_hbm, out_hbm, small_out, in_v, out_v, sem = refs[-6:]
    core, side = sc[0], sc[1]

    def block(i, c, y, rows):
        own, across, other, far = refs[4 * i : 4 * i + 4]
        here = jnp.where(side == y, own[rows], across[rows])
        there = jnp.where(side == y, other[rows], far[rows])
        return jnp.where(core == c, here, there).astype(F32)

    copies = []

    def store(values, near_ref, far_ref, at):
        near_ref[at : at + values.shape[0]] = values
        span = pl.ds(at, values.shape[0])
        copies.append(fetch(near_ref.at[span], far_ref.at[span], sem.at[len(copies)]))

    for i, base in ((0, INNER), (1, 0)):
        for c in range(2):
            for y in range(2):
                for k in range(2):
                    rows = slice(k * BLOCK, (k + 1) * BLOCK)
                    store(block(i, c, y, rows), in_v, in_hbm, base + (2 * y + k) * HALF + c * BLOCK)
    rows = slice(HALF, HALF + STATE)
    for i in range(2):
        store(block(i, 0, 0, rows) + block(i, 1, 0, rows), in_v, in_hbm, 2 * INNER + i * STATE)
    steps = [block(0, c, 1, slice(HALF, HALF + 32)) for c in range(2)]
    steps = [steps[c][z * 6 : z * 6 + 6] for z in range(4) for c in range(2)]
    store(jnp.concatenate(steps, axis=0), in_v, in_hbm, INNER + CONV_CH)
    rows = slice(HALF, HALF + SMALL_ROWS)
    small_out[...] = block(1, 0, 1, rows) + block(1, 1, 1, rows)
    rows = slice(IN_ROWS, GROUP_ROWS)
    for c in range(2):
        values = [block(i, c, y, rows) for y in range(2) for i in range(2)]
        store(jnp.concatenate(values, axis=1), out_v, out_hbm, c * BLOCK)
    for copy in copies:
        copy.wait()


def join_grads(scalars, parts):
    arrays = [near(a) for part in parts for a in part]
    height = INNER + CONV_CH + HEADS
    shapes = ((height, BLOCK), F32), ((2 * BLOCK, D), F32)
    return pl.pallas_call(
        grads_kernel,
        in_specs=[pl.BlockSpec(memory_space=pltpu.SMEM)] + [NEAR] * len(arrays),
        out_specs=[ANY, ANY, NEAR],
        out_shape=[pltpu.HBM(*k) for k in shapes] + [pltpu.VMEM((SMALL_ROWS, BLOCK), F32)],
        scratch_shapes=[pltpu.VMEM(*k) for k in shapes] + [pltpu.SemaphoreType.DMA((24,))],
        compiler_params=pltpu.CompilerParams(vmem_limit_bytes=28 << 20),
        cost_estimate=LITTLE,
        name="join_grads",
    )(scalars, *arrays)


def swap(value, axis):
    return lax.ppermute(value, axis, [(0, 1), (1, 0)])


def sent_along(value, axis):
    size = lax.axis_size(axis)
    routes = [[(i, (i + k) % size) for i in range(size)] for k in range(1, size)]
    return [lax.ppermute(value, axis, path) for path in routes]


def in_order(value, others, axis):
    size, place = len(others) + 1, lax.axis_index(axis)
    ring = jnp.stack([*others[::-1], value] * 2)
    return lax.dynamic_slice_in_dim(ring, (size - 1 - place) % size, size, 0)


LAG = 2


def relay_shards(
    ends,
    norm_gain,
    input_weight,
    conv_weight,
    conv_bias,
    dt_bias,
    a_log,
    skip_gain,
    gate_gain,
    output_weight,
):
    core = lax.axis_index("core")
    place = lax.axis_index("fsdp")
    side = lax.axis_index("y")
    section = lax.axis_index("section")
    leading = (section == 0).astype(jnp.int32)
    local = ends[0][:, 0]
    t = local.shape[1]
    chunks = lax.axis_size("fsdp")
    micro = place // 2

    small = [norm_gain[0], conv_weight[0].reshape(-1), conv_bias[0], dt_bias[0], a_log[0]]
    small += [skip_gain[0], gate_gain[0]]
    packed = jnp.concatenate(small)
    others = sent_along(packed, "fsdp")
    w = input_weight[0].T
    steps = own_steps(w, core)
    here = jnp.stack([core, side, place]).astype(jnp.int32)
    packed_halves = pack_weights(here, w, steps, output_weight[0])
    blocks, others, ready = line_gather(packed_halves[:2], others)
    packed = in_order(packed, others, "fsdp")
    pieces, at = [], 0
    for member in small:
        pieces.append(packed[:, at : at + member.shape[0]].reshape(-1))
        at += member.shape[0]
    pieces[1] = pieces[1].reshape(CONV_CH, KERNEL)
    gain, convp, headp, chanp = small_params(*pieces, core)
    local, _ = lax.optimization_barrier((local, ready))

    def route(first, m):
        return [
            (c * chunks + z, (z % 2) * chunks + 2 * m + c)
            for c in range(2)
            for z in (first, first + 1)
        ]

    def bring(first):
        return [lax.ppermute(local[m], ("core", "fsdp"), route(first, m)) for m in range(2)]

    def shared(got):
        got = jnp.where(micro == 0, got[0], got[1])
        other = swap(got, "core")
        return [jnp.where(core == 0, got, other), jnp.where(core == 0, other, got)]

    def give(piece, first):
        return [
            lax.ppermute(piece, ("core", "fsdp"), [(b, a) for a, b in route(first, m)])
            for m in range(2)
        ]

    last = (blocks[7][1], blocks[9][1])
    here, *got = lax.optimization_barrier((here, *bring(0), *bring(2), *last))
    blocks[7], blocks[9] = (blocks[7][0], got[4]), (blocks[9][0], got[5])
    pieces = shared(got[:2]) + shared(got[2:4])
    blocks = [packed_halves[:2], packed_halves[2:], *blocks]
    win, wout = place_weights(here, blocks)
    params = (gain, convp, headp, chanp, win, wout)

    def scalars(moment, lag, reverse):
        begin = jnp.where(leading == 1, lag if reverse else 0, 0 if reverse else lag)
        step = moment - begin
        valid = jnp.logical_and(step >= 0, step < chunks)
        inside = jnp.clip(step, 0, chunks - 1)
        chunk = chunks - 1 - inside if reverse else inside
        write = jnp.where(valid, chunk, chunks)
        edge_here = leading == 1 if reverse else leading == 0
        edge = jnp.where(jnp.logical_and(valid, edge_here), chunk, chunks)
        values = [chunk if reverse else write, leading, step == 0, valid, write, edge, core]
        return [jnp.asarray(v, jnp.int32) for v in values]

    moments = chunks + LAG
    table = [scalars(moment, LAG, False) for moment in range(moments)]
    table += [scalars(moment, LAG, True) for moment in range(moments)]
    table = jnp.stack(sum(table, [])).reshape(len(table), -1)
    size = 2 * chunks
    position = jnp.where(side == 0, place, size - 1 - place).astype(jnp.int32)
    owners = []
    for direction in (1, -1):
        for hop in range(size):
            owners += ring_place((position - direction * (1 + hop)) % size, chunks)
    owners = jnp.stack(owners).reshape(2 * size, 2).astype(jnp.int32)
    table, owners = lax.optimization_barrier((table, owners))

    state, tail = jnp.zeros((STATE, OWN), F32), jnp.zeros((8, OWN_CONV), F32)
    blank = jnp.zeros((t, D), BF16)
    held, joined, result = None, None, None
    moved, incoming = {}, {}
    for moment in range(moments):
        if moment > 0:
            tail, result = lax.optimization_barrier((tail, result))
            if moment - 1 < chunks:
                moved[moment - 1] = lax.ppermute(result, "section", [(0, 1)])
        arrived = incoming.get(moment - LAG, (blank[: t // 2],) * 2)
        partial, h, (state, tail), held = forward_call(
            table,
            moment,
            chunks + 1,
            pieces[min(moment, chunks - 1)],
            arrived,
            params,
            (state, tail),
            held,
        )
        if moment - 1 in moved:
            partial, got = lax.optimization_barrier((partial, moved[moment - 1]))
            incoming[moment - 1] = (got, swap(got, "core"))
        other = swap(partial, "core")
        result, joined = forward_join(table, moment, chunks + 1, partial, other, h, joined)
    h_held, normed_held, pr_held, mx_held, q_held, st_held, tl_held = held
    y_held, ri_held, edge_held = joined
    saved = (h_held, normed_held, pr_held, mx_held, st_held, tl_held, y_held, ri_held)

    def tokens(buffer):
        return buffer[:chunks].reshape(chunks * t, buffer.shape[-1])

    carry = (
        jnp.zeros((STATE, OWN), F32),
        jnp.zeros((8, OWN_CONV), F32),
        jnp.zeros((8, OWN), F32),
        jnp.zeros((16, OWN_CONV), F32),
    )
    grads_held = None
    moved, incoming = {}, {}
    for moment in range(moments):
        if moment > 0:
            *carry, acc = carry
            acc, result = lax.optimization_barrier((acc, result))
            carry = (*carry, acc)
            if moment - 1 < chunks:
                moved[moment - 1] = lax.ppermute(result, "section", [(1, 0)])
        arrived = incoming.get(moment - LAG, (blank[: t // 2],) * 2)
        cot = pieces[max(chunks - 1 - moment, 0)]
        (partial, g, h), carry, grads_held = backward_call(
            table, moments + moment, chunks + 1, cot, arrived, saved, params, carry, grads_held
        )
        if moment - 1 in moved:
            partial, got = lax.optimization_barrier((partial, moved[moment - 1]))
            incoming[moment - 1] = (got, swap(got, "core"))
        other = swap(partial, "core")
        result, edge_held = backward_join(
            table, moments + moment, partial, other, h, g, gain, edge_held
        )

    def both(own, other, index):
        return jnp.where(index == 0, jnp.stack([own, other]), jnp.stack([other, own]))

    acc = carry[3]

    def placed(own):
        zero = jnp.zeros_like(own)
        return woven(both(own, zero, core))

    taps = jnp.concatenate([placed(acc[:5, :OWN]), acc[:5, OWN:]], axis=1)
    taps = jnp.moveaxis(taps.reshape(KERNEL + 1, chunks, -1), 1, 0)
    skip = acc[5, :OWN].reshape(OWN_HEADS, HEAD_DIM).sum(axis=1)
    vectors = [
        acc[9, :D] / gain[0],
        taps,
        placed(acc[7, :OWN_HEADS]),
        placed(acc[8, :OWN_HEADS]),
        placed(skip),
        placed(acc[6, :OWN]),
    ]
    vectors = [v.reshape(chunks, -1) for v in vectors]
    small = jnp.concatenate(vectors, axis=1)
    small = jnp.pad(small, ((0, 0), (0, SMALL_ROWS * BLOCK - small.shape[1])))
    small = small.reshape(chunks, SMALL_ROWS, BLOCK)

    onward, back = ring_route(chunks, 1), ring_route(chunks, -1)
    grads_held, gs_held = grads_held
    sums = [None] * len(GROUPS)
    for hop in range(size):
        if hop > 0:
            owners, *sums = lax.optimization_barrier((owners, *sums))
        for i, (direction, *_) in enumerate(GROUPS):
            row = hop + (0 if direction == 1 else size)
            block = block_grad(owners, row, i, normed_held, grads_held, q_held, gs_held, small)
            if hop > 0:
                path = onward if direction == 1 else back
                came = lax.ppermute(sums[i], ("y", "fsdp"), path).astype(F32)
                block = (block.astype(F32) + came).astype(BF16)
            sums[i] = block
        if hop == 3:
            finished = pick(table, edge_held, 0), pick(table, edge_held, 2)
            owners, *finished = lax.optimization_barrier((owners, *finished))
    *sums, early, late = lax.optimization_barrier((*sums, *finished))

    edges = jnp.where(place < 2, jnp.stack(give(early, 0)), jnp.stack(give(late, 2)))
    edges = edges[None, :, None]
    parts = []
    for own in sums:
        across = swap(own, "y")
        parts.append((own, across, swap(own, "core"), swap(across, "core")))
    here = jnp.stack([core, side]).astype(jnp.int32)
    here, edges = lax.optimization_barrier((here, edges))
    in_grad, out_grad, summed = join_grads(here, parts)
    in_grad = in_grad.T
    summed = summed.reshape(-1)
    grads, at = [], 0
    for v in vectors:
        grads.append(summed[at : at + v.shape[1]][None])
        at += v.shape[1]
    taps = grads[1].reshape(KERNEL + 1, -1)
    grads[1:2] = taps[:KERNEL].T[None], taps[KERNEL:]
    return (
        edges,
        grads[0],
        in_grad[None],
        grads[1],
        grads[2],
        grads[3],
        grads[4],
        grads[5],
        grads[6],
        out_grad[None],
    )


def shifted(block, axis, distance):
    devices = range(lax.axis_size(axis))
    route = [(i - distance, i) for i in devices if i - distance in devices]
    return lax.ppermute(block, axis, route)


def prefix(value, axis, join, neutral):
    place = lax.axis_index(axis)
    gathered = jax.tree.map(
        lambda a, kind: lax.all_gather(a.astype(kind), axis), value, (jnp.bfloat16, jnp.bfloat16)
    )
    state = jax.tree.map(lambda a, e: jnp.zeros_like(a) + jnp.asarray(e, a.dtype), value, neutral)

    def one(turn, state):
        return join(
            state,
            jax.tree.map(
                lambda a, own: lax.dynamic_index_in_dim(a, turn, 0, False).astype(own.dtype),
                gathered,
                value,
            ),
        )

    return lax.fori_loop(0, place, one, state)


def prefix_2(value, axis, join, neutral):
    count = lax.axis_size(axis)
    place = lax.axis_index(axis)
    ahead = count - 1 - place
    gathered = jax.tree.map(
        lambda a, kind: lax.all_gather(a.astype(kind), axis),
        value,
        jax.tree.map(lambda a: jnp.bfloat16 if a.dtype == jnp.float32 else a.dtype, value),
    )
    state = jax.tree.map(lambda a, e: jnp.zeros_like(a) + jnp.asarray(e, a.dtype), value, neutral)

    def one(turn, state):
        source = count - 1 - turn
        return join(
            state,
            jax.tree.map(
                lambda a, own: lax.dynamic_index_in_dim(a, source, 0, False).astype(own.dtype),
                gathered,
                value,
            ),
        )

    return lax.fori_loop(0, ahead, one, state)


def rms_scale(values, scale_gain):
    return (
        values * lax.rsqrt(jnp.mean(values * values, axis=-1, keepdims=True) + EPSILON) * scale_gain
    )


def chain_rule(earlier, later_part):
    return (
        earlier[0] * later_part[0],
        later_part[1] + later_part[0][:, :, None, None] * earlier[1],
    )


def conv_features(widened, conv_weight, conv_bias, dt_raw, dt_bias, a_log):
    tap_count = conv_weight.shape[1]
    step_count = widened.shape[1] - tap_count + 1
    convolved = conv_bias
    for offset in range(tap_count):
        convolved = convolved + widened[:, offset : offset + step_count, :] * conv_weight[:, offset]
    activated = jax.nn.silu(convolved)
    x_heads = activated[..., :INNER]
    b_rows = activated[..., INNER : INNER + STATE]
    c_rows = activated[..., INNER + STATE :]
    dt_step = jax.nn.softplus(dt_raw + dt_bias)
    log_decay = jnp.cumsum(-jnp.exp(a_log) * dt_step, axis=1)
    return (x_heads, b_rows, c_rows, dt_step, log_decay)


def local_states(x_heads, b_rows, dt_step, log_decay):
    seq_count, length = (x_heads.shape[0], x_heads.shape[1])
    spread = x_heads.reshape(seq_count, length, HEADS, HEAD_DIM)
    weights = jnp.exp(log_decay[:, -1:, :] - log_decay) * dt_step
    weighted = spread * weights[..., None]
    states = jnp.einsum("sqhd,sqn->shdn", weighted, b_rows, precision=EXACT_MATMUL)
    return (jnp.exp(log_decay[:, -1]), states)


def gated_output(
    x_heads, b_rows, c_rows, dt_step, log_decay, prior_state, gate_z, skip_gain, gate_gain
):
    seq_count, length = (x_heads.shape[0], x_heads.shape[1])
    spread = x_heads.reshape(seq_count, length, HEADS, HEAD_DIM)
    scaled = spread * dt_step[..., None]
    by_head = jnp.transpose(log_decay, (0, 2, 1))
    differ = by_head[:, :, :, None] - by_head[:, :, None, :]
    causal = jnp.arange(length)[:, None] >= jnp.arange(length)[None, :]
    mixing = jnp.where(causal, jnp.exp(jnp.where(causal, differ, 0.0)), 0.0)
    intersections = jnp.einsum("sqn,skn->sqk", c_rows, b_rows, precision=EXACT_MATMUL)
    mixed_out = jnp.einsum(
        "shqk,skhd->sqhd", mixing * intersections[:, None], scaled, precision=EXACT_MATMUL
    )
    mixed_out = mixed_out + jnp.exp(log_decay)[..., None] * jnp.einsum(
        "sqn,shdn->sqhd", c_rows, prior_state, precision=EXACT_MATMUL
    )
    mixed_out = (mixed_out + skip_gain[:, None] * spread).reshape(seq_count, length, INNER)
    return rms_scale(mixed_out * jax.nn.silu(gate_z), gate_gain)


def layer_forward(hidden, weights):
    (
        norm_gain,
        input_weight,
        conv_weight,
        conv_bias,
        dt_bias,
        a_log,
        skip_gain,
        gate_gain,
        output_weight,
    ) = weights
    normalized_rows = rms_scale(hidden, norm_gain.astype(jnp.float32)).astype(jnp.bfloat16)
    projected_rows = jnp.einsum(
        "spd,de->spe", normalized_rows, input_weight, preferred_element_type=jnp.float32
    ).astype(jnp.bfloat16)
    length = hidden.shape[1]
    xbc_part = projected_rows[..., INNER : INNER + CONV_CH]
    border = shifted(xbc_part[:, length - KERNEL + 1 :, :], "fsdp", 1)
    widened = jnp.concatenate([border, xbc_part], axis=1)
    features = conv_features(
        widened.astype(jnp.float32),
        conv_weight.astype(jnp.float32),
        conv_bias.astype(jnp.float32),
        projected_rows[..., INNER + CONV_CH :].astype(jnp.float32),
        dt_bias.astype(jnp.float32),
        a_log.astype(jnp.float32),
    )
    decays, states = local_states(features[0], features[1], features[3], features[4])
    scanned = prefix(
        (decays, states), "fsdp", chain_rule, (jnp.ones_like(decays), jnp.zeros_like(states))
    )
    prior_state = scanned[1]
    gated_result = gated_output(
        features[0],
        features[1],
        features[2],
        features[3],
        features[4],
        prior_state,
        projected_rows[..., :INNER].astype(jnp.float32),
        skip_gain.astype(jnp.float32),
        gate_gain.astype(jnp.float32),
    )
    gated_low = gated_result.astype(jnp.bfloat16)
    final_result = hidden + jnp.einsum(
        "spi,id->spd", gated_low, output_weight, preferred_element_type=jnp.float32
    )
    return (
        final_result,
        (hidden, normalized_rows, projected_rows, widened, prior_state, gated_low),
    )


def layer_backward(gradient, kept_state, weights):
    hidden, normalized_rows, projected_rows, widened, prior_state, gated_low = kept_state
    (
        norm_gain,
        input_weight,
        conv_weight,
        conv_bias,
        dt_bias,
        a_log,
        skip_gain,
        gate_gain,
        output_weight,
    ) = weights
    grad_low = gradient.astype(jnp.bfloat16)
    grad_out_weight = jnp.einsum(
        "spi,spd->id", gated_low, grad_low, preferred_element_type=jnp.float32
    )
    grad_gated = jnp.einsum(
        "spd,id->spi", grad_low, output_weight, preferred_element_type=jnp.float32
    )
    features, pull_features = jax.vjp(
        conv_features,
        widened.astype(jnp.float32),
        conv_weight.astype(jnp.float32),
        conv_bias.astype(jnp.float32),
        projected_rows[..., INNER + CONV_CH :].astype(jnp.float32),
        dt_bias.astype(jnp.float32),
        a_log.astype(jnp.float32),
    )
    _, pull_gated = jax.vjp(
        gated_output,
        features[0],
        features[1],
        features[2],
        features[3],
        features[4],
        prior_state,
        projected_rows[..., :INNER].astype(jnp.float32),
        skip_gain.astype(jnp.float32),
        gate_gain.astype(jnp.float32),
    )
    grads_gated = pull_gated(grad_gated)
    decay_states, pull_states = jax.vjp(
        local_states, features[0], features[1], features[3], features[4]
    )
    decays = decay_states[0]
    later_state = prefix_2(
        (decays, grads_gated[5]),
        "fsdp",
        chain_rule,
        (jnp.ones_like(decays), jnp.zeros_like(grads_gated[5])),
    )
    grad_end = later_state[1]
    state_parts = pull_states((jnp.sum(grad_end * prior_state, axis=(2, 3)), grad_end))
    feature_grads = (
        grads_gated[0] + state_parts[0],
        grads_gated[1] + state_parts[1],
        grads_gated[2],
        grads_gated[3] + state_parts[2],
        grads_gated[4] + state_parts[3],
    )
    grad_wide, grad_conv_w, grad_conv_b, grad_dt_raw, grad_dt_bias, grad_a_log = pull_features(
        feature_grads
    )
    margin = KERNEL - 1
    returned = shifted(grad_wide[:, :margin, :].astype(jnp.bfloat16), "fsdp", -1).astype(
        jnp.float32
    )
    own_rows = grad_wide[:, margin:, :]
    length = own_rows.shape[1]
    grad_xbc = jnp.concatenate(
        [own_rows[:, : length - margin], own_rows[:, length - margin :] + returned], axis=1
    )
    grad_proj = jnp.concatenate([grads_gated[6], grad_xbc, grad_dt_raw], axis=-1).astype(
        jnp.bfloat16
    )
    grad_in_weight = jnp.einsum(
        "spd,spe->de", normalized_rows, grad_proj, preferred_element_type=jnp.float32
    )
    grad_normed = jnp.einsum(
        "spe,de->spd", grad_proj, input_weight, preferred_element_type=jnp.float32
    )
    _, pull_norm = jax.vjp(rms_scale, hidden, norm_gain.astype(jnp.float32))
    grad_hidden, grad_norm_gain = pull_norm(grad_normed)
    return (
        gradient + grad_hidden,
        (
            grad_norm_gain,
            grad_in_weight,
            grad_conv_w,
            grad_conv_b,
            grad_dt_bias,
            grad_a_log,
            grads_gated[7],
            grads_gated[8],
            grad_out_weight,
        ),
    )


def shards(
    ends,
    norm_gain,
    input_weight,
    conv_weight,
    conv_bias,
    dt_bias,
    a_log,
    skip_gain,
    gate_gain,
    output_weight,
):
    gathered = (
        lax.all_gather(norm_gain, "fsdp", axis=1, tiled=True),
        lax.all_gather(input_weight, "fsdp", axis=1, tiled=True),
        lax.all_gather(conv_weight, "fsdp", axis=1, tiled=True),
        lax.all_gather(conv_bias, "fsdp", axis=1, tiled=True),
        lax.all_gather(dt_bias, "fsdp", axis=1, tiled=True),
        lax.all_gather(a_log, "fsdp", axis=1, tiled=True),
        lax.all_gather(skip_gain, "fsdp", axis=1, tiled=True),
        lax.all_gather(gate_gain, "fsdp", axis=1, tiled=True),
        lax.all_gather(output_weight, "fsdp", axis=1, tiled=True),
    )
    layer_weights = tuple((member[0] for member in gathered))
    leading = lax.axis_index("section") == 0
    local_data = ends[0].astype(jnp.float32)
    batches = local_data.shape[0]
    arrived = jnp.zeros(local_data.shape[1:], jnp.float32)
    stored = []
    produced = []
    for moment in range(batches + 1):
        source = jnp.where(leading, local_data[min(moment, batches - 1)], arrived)
        final_result, kept_state = layer_forward(source, layer_weights)
        stored.append(kept_state)
        produced.append(final_result)
        if moment < batches:
            arrived = shifted(final_result.astype(jnp.bfloat16), "section", 1).astype(jnp.float32)
    totals = None
    coming = jnp.zeros(local_data.shape[1:], jnp.float32)
    returned_grads = []
    for moment in range(batches + 1):
        gradient = jnp.where(leading, coming, local_data[min(moment, batches - 1)])
        kept_state = jax.tree.map(
            lambda upper_part, lower_part: jnp.where(leading, upper_part, lower_part),
            stored[max(moment - 1, 0)],
            stored[min(moment + 1, batches)],
        )
        grad_input, gradients = layer_backward(gradient, kept_state, layer_weights)
        active = jnp.where(leading, moment >= 1, moment < batches)
        masked = tuple((jnp.where(active, member, 0.0) for member in gradients))
        if totals is None:
            totals = masked
        else:
            totals = tuple((earlier_sum + member for earlier_sum, member in zip(totals, masked)))
        returned_grads.append(grad_input)
        if moment < batches:
            coming = shifted(grad_input.astype(jnp.bfloat16), "section", -1).astype(jnp.float32)
    boundary = jnp.stack(
        [
            jnp.where(leading, returned_grads[number + 1], produced[number + 1])
            for number in range(batches)
        ]
    )
    owned_parts = (
        lax.psum_scatter(
            totals[0][None].astype(jnp.bfloat16), "fsdp", scatter_dimension=1, tiled=True
        ).astype(jnp.float32),
        lax.psum_scatter(
            totals[1][None].astype(jnp.bfloat16), "fsdp", scatter_dimension=1, tiled=True
        ).astype(jnp.float32),
        lax.psum_scatter(
            totals[2][None].astype(jnp.bfloat16), "fsdp", scatter_dimension=1, tiled=True
        ).astype(jnp.float32),
        lax.psum_scatter(
            totals[3][None].astype(jnp.bfloat16), "fsdp", scatter_dimension=1, tiled=True
        ).astype(jnp.float32),
        lax.psum_scatter(
            totals[4][None].astype(jnp.bfloat16), "fsdp", scatter_dimension=1, tiled=True
        ).astype(jnp.float32),
        lax.psum_scatter(
            totals[5][None].astype(jnp.bfloat16), "fsdp", scatter_dimension=1, tiled=True
        ).astype(jnp.float32),
        lax.psum_scatter(
            totals[6][None].astype(jnp.bfloat16), "fsdp", scatter_dimension=1, tiled=True
        ).astype(jnp.float32),
        lax.psum_scatter(
            totals[7][None].astype(jnp.bfloat16), "fsdp", scatter_dimension=1, tiled=True
        ).astype(jnp.float32),
        lax.psum_scatter(
            totals[8][None].astype(jnp.bfloat16), "fsdp", scatter_dimension=1, tiled=True
        ).astype(jnp.float32),
    )
    summed = (
        lax.psum(owned_parts[0].astype(jnp.bfloat16), "rep").astype(jnp.float32),
        lax.psum(owned_parts[1].astype(jnp.bfloat16), "rep").astype(jnp.float32),
        lax.psum(owned_parts[2].astype(jnp.bfloat16), "rep").astype(jnp.float32),
        lax.psum(owned_parts[3].astype(jnp.bfloat16), "rep").astype(jnp.float32),
        lax.psum(owned_parts[4].astype(jnp.bfloat16), "rep").astype(jnp.float32),
        lax.psum(owned_parts[5].astype(jnp.bfloat16), "rep").astype(jnp.float32),
        lax.psum(owned_parts[6].astype(jnp.bfloat16), "rep").astype(jnp.float32),
        lax.psum(owned_parts[7].astype(jnp.bfloat16), "rep").astype(jnp.float32),
        lax.psum(owned_parts[8].astype(jnp.bfloat16), "rep").astype(jnp.float32),
    )
    return (
        boundary.astype(jnp.bfloat16)[None],
        summed[0],
        summed[1],
        summed[2],
        summed[3],
        summed[4],
        summed[5],
        summed[6],
        summed[7],
        summed[8],
    )


def solution(mesh):
    shape = mesh.shape
    relay = shape["section"] == 2 and shape["rep"] == 4 and shape["fsdp"] == 4
    if relay:
        devices = mesh.devices.reshape(2, 2, 2, 4)
        mesh = Mesh(devices, ("section", "y", "core", "fsdp"))
    rep = ("y", "core") if relay else "rep"
    data = P("section", None, rep, "fsdp", None)
    vector, matrix = P("section", "fsdp"), P("section", "fsdp", None)
    params = (vector, matrix, matrix, vector, vector, vector, vector, vector, matrix)
    return jax.shard_map(
        relay_shards if relay else shards,
        mesh=mesh,
        in_specs=(data, *params),
        out_specs=(data, *params),
        check_vma=False,
    )
```

```python
import functools

import jax
import jax.numpy as jnp
from jax import lax
from jax.experimental import pallas as pl
from jax.experimental.pallas import tpu as pltpu
from jax.sharding import Mesh
from jax.sharding import PartitionSpec as P

D = 1536
HEADS = 48
HEAD_DIM = 64
STATE = 128
KERNEL = 4
INNER = 3072
CONV_CH = 3328
LANES = 128

OWN = INNER // 2
OWN_HEADS = HEADS // 2
OWN_CONV = OWN + 2 * STATE
X_AT = OWN
BC_AT = 2 * OWN
DT_AT = 2 * OWN + 2 * STATE
OWN_PROJ = DT_AT + 2 * LANES
PAIRS = OWN // LANES

EPSILON = 1e-05
EXACT_MATMUL = lax.Precision.HIGHEST
F32 = jnp.float32
BF16 = jnp.bfloat16
FORWARD_VMEM = 24
BACKWARD_VMEM = 30
JOIN_VMEM = 12


def dot(a, b):
    return lax.dot_general(a, b, (((1,), (0,)), ((), ())), preferred_element_type=F32)


def dot_nt(a, b):
    return lax.dot_general(a, b, (((1,), (1,)), ((), ())), preferred_element_type=F32)


def dot_tn(a, b):
    return lax.dot_general(a, b, (((0,), (0,)), ((), ())), preferred_element_type=F32)


def split(v, parts):
    pieces = []
    for _ in range(parts):
        piece = v.astype(BF16)
        pieces.append(piece)
        v = v - piece.astype(F32)
    return pieces


def sigmoid(v):
    return 0.5 * jnp.tanh(0.5 * v) + 0.5


def softplus(v):
    return jnp.maximum(v, 0.0) + jnp.log1p(jnp.exp(-jnp.abs(v)))


def step_sizes(dt_raw, headp):
    t = dt_raw.shape[0]
    biased = dt_raw + headp[0:1]
    dt = softplus(biased)
    rows = lax.broadcasted_iota(jnp.int32, (t, t), 0)
    cols = lax.broadcasted_iota(jnp.int32, (t, t), 1)
    tri = jnp.where(rows >= cols, 1.0, 0.0).astype(BF16)
    ld = sum(dot(tri, part) for part in split(dt * headp[1:2], 3))
    return dt, ld, biased


def at_head(v, pair):
    turned = pltpu.roll(v, lax.rem(LANES - 2 * pair, LANES), 1)
    return [jnp.broadcast_to(turned[:, i : i + 1], v.shape) for i in range(2)]


def decay_blocks(col, row, swapped):
    n = col.shape[0] // 2
    rows = lax.broadcasted_iota(jnp.int32, (n, n), 0)
    cols = lax.broadcasted_iota(jnp.int32, (n, n), 1)
    keep = rows <= cols if swapped else rows >= cols

    def block(i, j):
        down, along = col[i * n : (i + 1) * n], row[:, j * n : (j + 1) * n]
        differ = along - down if swapped else down - along
        return jnp.exp(jnp.where(keep, differ, -1e30) if i == j else differ)

    return block(0, 0), block(0, 1) if swapped else block(1, 0), block(1, 1)


def convolve(xw, sl, convp, t):
    out = convp[4:5, sl] + xw[5 : 5 + t, sl] * convp[0:1, sl]
    for k in range(1, KERNEL):
        out = out + xw[5 + k : 5 + k + t, sl] * convp[k : k + 1, sl]
    return out


def pair_loop(step):
    def two(turn, _):
        step(2 * turn)
        step(2 * turn + 1)
        return 0

    lax.fori_loop(0, PAIRS // 2, two, 0)


def aligned(value):
    return pl.multiple_of(value, LANES)


def fetch(source, target, sem):
    copy = pltpu.make_async_copy(source, target, sem)
    copy.start()
    return copy


def fetch_one_of(first, one, other, target, sem):
    @pl.when(first)
    def _():
        pltpu.make_async_copy(one, target, sem).start()

    @pl.when(jnp.logical_not(first))
    def _():
        pltpu.make_async_copy(other, target, sem).start()

    return pltpu.make_async_copy(other, target, sem)


def forward_kernel(row, sc, *refs):
    @pl.when(sc[row, VALID] == 1)
    def _():
        forward_chunk(row, sc, *refs)


def forward_chunk(
    row, sc, got_hbm, other_hbm, x_hbm, ng_ref, convp, headp, chanp, st_ref, tail_ref, win, wout, *rest
):
    p, h, st_out, tail_out = rest[-22:-18]
    h_hbm, n_hbm, pr_hbm, mx_hbm, q_hbm, st_hbm, tl_hbm = rest[-18:-11]
    normed, pr, mx, q, sti, tl, xw, ldt, ss, g_ref, sem = rest[-11:]
    t = h.shape[0]
    half = t // 2
    slot = sc[row, SLOT]
    first = sc[row, FIRST] == 1
    leading = sc[row, LEADING] == 1
    core = sc[row, CORE]

    @pl.when(leading)
    def _():
        fetch(x_hbm, h, sem.at[0]).wait()

    @pl.when(jnp.logical_not(leading))
    def _():
        mine = h.at[pl.ds(aligned(core * half), half)]
        theirs = h.at[pl.ds(aligned((1 - core) * half), half)]
        copies = fetch(got_hbm, mine, sem.at[0]), fetch(other_hbm, theirs, sem.at[1])
        for copy in copies:
            copy.wait()

    stores = [fetch(h, h_hbm.at[slot], sem.at[0])]
    hf = h[...].astype(F32)
    r = lax.rsqrt(jnp.mean(hf * hf, axis=1, keepdims=True) + EPSILON)
    normed[...] = (hf * r * ng_ref[...]).astype(BF16)
    stores.append(fetch(normed, n_hbm.at[slot], sem.at[1]))

    sti[...] = jnp.where(first, 0.0, st_ref[...])
    tl[...] = jnp.where(first, 0.0, tail_ref[...])
    stores.append(fetch(sti, st_hbm.at[slot], sem.at[2]))
    stores.append(fetch(tl, tl_hbm.at[slot], sem.at[3]))
    xw[0:8, :] = tl[...]

    for at in range(0, OWN_PROJ, 512):
        cols = slice(at, min(at + 512, OWN_PROJ))
        pr[:, cols] = dot_nt(normed[...], win[cols, :]).astype(BF16)
    stores.append(fetch(pr, pr_hbm.at[slot], sem.at[4]))
    tail_out[...] = pr[t - 8 : t, X_AT : X_AT + OWN_CONV].astype(F32)

    bc = pl.ds(OWN, 2 * STATE)
    xw[8 : 8 + t, OWN:OWN_CONV] = pr[:, BC_AT:DT_AT].astype(F32)
    conv_bc = convolve(xw, bc, convp, t)
    act = (conv_bc * sigmoid(conv_bc)).astype(BF16)
    b, c = act[:, :STATE], act[:, STATE:]
    g_ref[...] = dot_nt(c, b)
    b_turned = act[:, :STATE].astype(F32).T.astype(BF16)
    dt, ld, _ = step_sizes(pr[:, DT_AT : DT_AT + LANES].astype(F32), headp[...])
    ldt[...] = ld.T
    left = lax.broadcasted_iota(jnp.int32, (t, LANES), 1) < HEAD_DIM
    ss[...] = jnp.zeros_like(ss)

    def pair_step(pair):
        at = pl.multiple_of(pair * LANES, LANES)
        sl = pl.ds(at, LANES)
        xw[8 : 8 + t, sl] = pr[:, pl.ds(X_AT + at, LANES)].astype(F32)
        conv = convolve(xw, sl, convp, t)
        x = conv * sigmoid(conv)
        cols = at_head(ld, pair)
        u = jnp.where(left, *at_head(dt, pair)) * x
        ld_p = jnp.where(left, *cols)
        tops, bottoms, sides = [], [], []
        for i in range(2):
            u_i = jnp.where(left if i == 0 else jnp.logical_not(left), u, 0.0).astype(BF16)
            d00, d10, d11 = decay_blocks(cols[i], ldt[pl.ds(2 * pair + i, 1), :], False)
            m00 = (g_ref[:half, :half] * d00).astype(BF16)
            m10 = (g_ref[half:, :half] * d10).astype(BF16)
            m11 = (g_ref[half:, half:] * d11).astype(BF16)
            tops.append(m00)
            bottoms += [m10, m11]
            sides.append(u_i)
        top = dot(jnp.concatenate(tops, axis=1), jnp.concatenate([v[:half] for v in sides], axis=0))
        bottom = dot(jnp.concatenate(bottoms, axis=1), jnp.concatenate(sides, axis=0))
        eld = jnp.exp(ld_p)
        st = sti[:, sl]
        y = jnp.concatenate([top, bottom], axis=0) + eld * dot(c, st.astype(BF16))
        weighted = (u * jnp.exp(ld_p[t - 1 : t] - ld_p)).astype(BF16)
        st_out[:, sl] = eld[t - 1 : t] * st + dot(b_turned, weighted)
        mixed = y + chanp[0:1, sl] * x
        mx[:, sl] = mixed
        z = pr[:, sl].astype(F32)
        gated = mixed * (z * sigmoid(z))
        ss[...] += gated * gated
        q[:, sl] = (gated * chanp[1:2, sl]).astype(BF16)

    pair_loop(pair_step)
    stores.append(fetch(mx, mx_hbm.at[slot], sem.at[5]))
    stores.append(fetch(q, q_hbm.at[slot], sem.at[6]))
    total = jnp.sum(ss[...], axis=1, keepdims=True)
    high = total.astype(BF16).astype(F32)
    lane = lax.broadcasted_iota(jnp.int32, (t, LANES), 1)
    p[:, D:] = jnp.where(lane == 0, high, jnp.where(lane == 1, total - high, 0.0)).astype(BF16)
    for at in range(0, D, 512):
        p[:, at : at + 512] = dot(q[...], wout[:, at : at + 512]).astype(BF16)
    for store in stores:
        store.wait()


def backward_kernel(row, sc, *refs):
    acc_ref, acc_out = refs[17], refs[-21]

    @pl.when(sc[row, VALID] == 1)
    def _():
        backward_chunk(row, sc, *refs)

    @pl.when(sc[row, VALID] == 0)
    def _():
        acc_out[...] = acc_ref[...]


def backward_chunk(
    row,
    sc,
    arrived_hbm,
    other_hbm,
    cot_hbm,
    h_hbm,
    n_hbm,
    pr_hbm,
    mx_hbm,
    st_hbm,
    tl_hbm,
    y_hbm,
    ri_hbm,
    convp,
    headp,
    chanp,
    dst_ref,
    dc_ref,
    val_ref,
    acc_ref,
    win,
    wout,
    *rest,
):
    gn, g_ref, h_out, dst_out, dc_out, val_out, acc_out, gp_hbm, gs_hbm = rest[-27:-18]
    pr, mx, st_ref, tl, y_ref, ri, gp, gs, normed = rest[-18:-9]
    xw, dw, ldt, gw, gt, dgt, dci, dbi, sem = rest[-9:]
    t = g_ref.shape[0]
    half = t // 2
    slot = sc[row, SLOT]
    last = sc[row, FIRST] == 1
    leading = sc[row, LEADING] == 1
    core = sc[row, CORE]
    mine = g_ref.at[pl.ds(aligned(core * half), half)]
    theirs = g_ref.at[pl.ds(aligned((1 - core) * half), half)]

    @pl.when(leading)
    def _():
        pltpu.make_async_copy(arrived_hbm, mine, sem.at[0]).start()
        pltpu.make_async_copy(other_hbm, theirs, sem.at[10]).start()

    @pl.when(jnp.logical_not(leading))
    def _():
        pltpu.make_async_copy(cot_hbm, g_ref, sem.at[0]).start()

    y_copy = fetch(y_hbm.at[slot], y_ref, sem.at[1])
    ri_copy = fetch(ri_hbm.at[slot], ri, sem.at[2])
    pr_copy = fetch(pr_hbm.at[slot], pr, sem.at[3])
    tl_copy = fetch(tl_hbm.at[slot], tl, sem.at[4])
    mx_copy = fetch(mx_hbm.at[slot], mx, sem.at[5])
    st_copy = fetch(st_hbm.at[slot], st_ref, sem.at[6])

    acc_out[...] = acc_ref[...]
    dw[t : t + 8, :] = jnp.where(last, 0.0, dc_ref[...])
    dgt[...] = jnp.zeros_like(dgt)
    dci[...] = jnp.zeros_like(dci)
    dbi[...] = jnp.zeros_like(dbi)

    @pl.when(leading)
    def _():
        pltpu.make_async_copy(arrived_hbm, mine, sem.at[0]).wait()
        pltpu.make_async_copy(other_hbm, theirs, sem.at[10]).wait()

    @pl.when(jnp.logical_not(leading))
    def _():
        pltpu.make_async_copy(cot_hbm, g_ref, sem.at[0]).wait()

    for at in range(0, OWN, 512):
        gw[:, at : at + 512] = dot_nt(g_ref[...], wout[at : at + 512, :])
    y_copy.wait()
    ri_copy.wait()
    rinv = ri[:, 0:1]
    mean = jnp.sum(g_ref[...].astype(F32) * y_ref[...].astype(F32), axis=1, keepdims=True)
    lean = rinv * rinv * (mean * (1.0 / INNER))
    gs[...] = (g_ref[...].astype(F32) * rinv).astype(BF16)
    gs_store = fetch(gs, gs_hbm.at[sc[row, WRITE]], sem.at[7])
    pr_copy.wait()
    tl_copy.wait()
    xw[0:8, :] = tl[...]

    bc = pl.ds(OWN, 2 * STATE)
    xw[8 : 8 + t, OWN:OWN_CONV] = pr[:, BC_AT:DT_AT].astype(F32)
    conv_bc = convolve(xw, bc, convp, t)
    sig_bc = sigmoid(conv_bc)
    act = (conv_bc * sig_bc).astype(BF16)
    b, c = act[:, :STATE], act[:, STATE:]
    c_turned = c.astype(F32).T.astype(BF16)
    gt[...] = dot_nt(b, c)
    dt, ld, biased = step_sizes(pr[:, DT_AT : DT_AT + LANES].astype(F32), headp[...])
    ldt[...] = ld.T
    left = lax.broadcasted_iota(jnp.int32, (t, LANES), 1) < HEAD_DIM

    def add(line, sl, v):
        acc_out[line : line + 1, sl] += v

    def conv_back(dact, conv, sig, sl):
        dconv = dact * (sig * (1.0 + conv * (1.0 - sig)))
        dw[0:t, sl] = dconv
        add(4, sl, jnp.sum(dconv, axis=0, keepdims=True))
        for k in range(KERNEL):
            add(k, sl, jnp.sum(dconv * xw[5 + k : 5 + k + t, sl], axis=0, keepdims=True))
        dx = dconv * convp[KERNEL - 1 : KERNEL, sl]
        for k in range(KERNEL - 1):
            ahead = KERNEL - 1 - k
            dx = dx + dw[ahead : ahead + t, sl] * convp[k : k + 1, sl]
        return dx.astype(BF16)

    lane_head = lax.rem(lax.broadcasted_iota(jnp.int32, (2 * LANES, LANES), 0), LANES) // HEAD_DIM
    head_lane = lax.broadcasted_iota(jnp.int32, (2 * LANES, LANES), 1)
    mx_copy.wait()
    st_copy.wait()
    h_copy = fetch(h_hbm.at[slot], h_out, sem.at[8])
    n_copy = fetch(n_hbm.at[slot], normed, sem.at[9])

    def pair_step(pair, carry):
        ddt, dld, dval = carry
        at = pl.multiple_of(pair * LANES, LANES)
        sl = pl.ds(at, LANES)
        xsl = pl.ds(X_AT + at, LANES)
        xw[8 : 8 + t, sl] = pr[:, xsl].astype(F32)
        conv = convolve(xw, sl, convp, t)
        sig = sigmoid(conv)
        x = conv * sig
        z = pr[:, sl].astype(F32)
        sig_z = sigmoid(z)
        s = z * sig_z
        mixed = mx[:, sl]
        gated = mixed * s
        scaled = gw[:, sl] * rinv
        add(6, sl, jnp.sum(scaled * gated, axis=0, keepdims=True))
        dgated = chanp[1:2, sl] * scaled - gated * lean
        dy = dgated * s
        gp[:, sl] = (dgated * mixed * (sig_z * (1.0 + z * (1.0 - sig_z)))).astype(BF16)
        skip = chanp[0:1, sl]
        add(5, sl, jnp.sum(dy * x, axis=0, keepdims=True))
        y = mixed - skip * x

        cols = at_head(ld, pair)
        ld_p = jnp.where(left, *cols)
        eld = jnp.exp(ld_p)
        wend = jnp.exp(ld_p[t - 1 : t] - ld_p)
        dt_p = jnp.where(left, *at_head(dt, pair))
        u = dt_p * x
        u_low = u.astype(BF16)
        dy_low = dy.astype(BF16)
        dst = jnp.where(last, 0.0, dst_ref[:, sl])
        dst_low = dst.astype(BF16)
        top = jnp.zeros((half, LANES), F32)
        bottom = top
        for i in range(2):
            side = left if i == 0 else jnp.logical_not(left)
            d00, d01, d11 = decay_blocks(cols[i], ldt[pl.ds(2 * pair + i, 1), :], True)
            m00 = (gt[:half, :half] * d00).astype(BF16)
            m01 = (gt[:half, half:] * d01).astype(BF16)
            m11 = (gt[half:, half:] * d11).astype(BF16)
            dy_i = jnp.where(side, dy, 0.0).astype(BF16)
            top = top + dot(jnp.concatenate([m00, m01], axis=1), dy_i)
            bottom = bottom + dot(m11, dy_i[half:])
            u_i = jnp.where(side, u, 0.0).astype(BF16)
            dm = dot_nt(u_i[:half], dy_low)
            dgt[:half, :half] += dm[:, :half] * d00
            dgt[:half, half:] += dm[:, half:] * d01
            dgt[half:, half:] += dot_nt(u_i[half:], dy_low[half:]) * d11
        du = jnp.concatenate([top, bottom], axis=0) + wend * dot(b, dst_low)
        st = st_ref[:, sl]
        dyl = (eld * dy).astype(BF16)
        dst_new = eld[t - 1 : t] * dst + dot(c_turned, dyl)
        dst_out[:, sl] = dst_new
        val_out[:, sl] = jnp.broadcast_to(
            jnp.sum(dst_new * st, axis=0, keepdims=True), (8, LANES)
        )
        dci[...] += dot_nt(dyl, st.astype(BF16))
        dbi[...] += dot_nt((wend * u).astype(BF16), dst_low)

        pick = jnp.where(lane_head + 2 * pair == head_lane, 1.0, 0.0).astype(BF16)


        def by_head(v):
            return dot(jnp.concatenate(split(v, 2), axis=1), pick)

        ddt = ddt + by_head(du * x)
        dld = dld + by_head(dy_low.astype(F32) * y - u_low.astype(F32) * du)
        dval = dval + by_head(jnp.where(last, 0.0, val_ref[:, sl]))
        gp[:, xsl] = conv_back(dt_p * du + skip * dy, conv, sig, sl)
        return ddt, dld, dval

    zero = jnp.zeros((t, LANES), F32)
    ddt, dld, dval = lax.fori_loop(
        0,
        PAIRS // 2,
        lambda turn, carry: pair_step(2 * turn + 1, pair_step(2 * turn, carry)),
        (zero, zero, jnp.zeros((8, LANES), F32)),
    )

    dgt_low = dgt[...].astype(BF16)
    db = dbi[...] + dot(dgt_low, c)
    dc = dci[...] + dot_tn(dgt_low, b)
    gp[:, BC_AT:DT_AT] = conv_back(jnp.concatenate([db, dc], axis=1), conv_bc, sig_bc, bc)

    rows = lax.broadcasted_iota(jnp.int32, (t, t), 0)
    cols = lax.broadcasted_iota(jnp.int32, (t, t), 1)
    upper = jnp.where(rows <= cols, 1.0, 0.0).astype(BF16)
    da = sum(dot(upper, part) for part in split(dld, 3)) + dval[0:1]
    rate = headp[1:2]
    head = pl.ds(0, LANES)
    add(8, head, jnp.sum(da * rate * dt, axis=0, keepdims=True))
    ddt_raw = (ddt + rate * da) * sigmoid(biased)
    add(7, head, jnp.sum(ddt_raw, axis=0, keepdims=True))
    gp[:, DT_AT : DT_AT + LANES] = ddt_raw.astype(BF16)
    gp[:, DT_AT + LANES :] = jnp.zeros((t, LANES), BF16)
    gp_store = fetch(gp, gp_hbm.at[sc[row, WRITE]], sem.at[0])
    dc_out[...] = dw[0:8, :]
    n_copy.wait()
    for at in range(0, D, 512):
        cols = slice(at, at + 512)
        values = dot(gp[...], win[:, cols])
        gn[:, cols] = values.astype(BF16)
        add(9, cols, jnp.sum(values * normed[:, cols].astype(F32), axis=0, keepdims=True))
    gp_store.wait()
    gs_store.wait()
    h_copy.wait()


def forward_join_kernel(row, sc, own_ref, other_ref, h_ref, *rest):
    out, y_hbm, ri_hbm, e_hbm, y_v, ri_v, low_v, sem = rest[-8:]
    half = out.shape[0]

    @pl.when(sc[row, VALID] == 1)
    def _():
        copies = []
        for k in range(2):
            rows = slice(k * half, (k + 1) * half)
            total = own_ref[rows].astype(F32) + other_ref[rows].astype(F32)
            square = total[:, D : D + 1] + total[:, D + 1 : D + 2]
            rinv = lax.rsqrt(square * (1.0 / INNER) + EPSILON)
            y = total[:, :D] * rinv
            y_v[rows] = y.astype(BF16)
            ri_v[rows] = jnp.broadcast_to(rinv, (half, LANES))
            low_v[rows] = (h_ref[rows].astype(F32) + y).astype(BF16)
            pieces = ((y_v, y_hbm, SLOT), (ri_v, ri_hbm, SLOT), (low_v, e_hbm, EDGE))
            for near_ref, far_ref, which in pieces:
                target = far_ref.at[sc[row, which], pl.ds(k * half, half)]
                copies.append(fetch(near_ref.at[pl.ds(k * half, half)], target, sem.at[len(copies)]))
        out[...] = low_v[pl.ds(aligned(sc[row, CORE] * half), half), :]
        for copy in copies:
            copy.wait()


def backward_join_kernel(row, sc, own_ref, other_ref, h_ref, g_ref, ng_ref, *rest):
    out, e_hbm, low_v, sem = rest[-4:]
    half = out.shape[0]

    @pl.when(sc[row, VALID] == 1)
    def _():
        copies = []
        for k in range(2):
            rows = slice(k * half, (k + 1) * half)
            gn = own_ref[rows].astype(F32) + other_ref[rows].astype(F32)
            h = h_ref[rows].astype(F32)
            r = lax.rsqrt(jnp.mean(h * h, axis=1, keepdims=True) + EPSILON)
            t = gn * ng_ref[...]
            m = jnp.mean(h * t, axis=1, keepdims=True)
            low_v[rows] = (g_ref[rows].astype(F32) + r * (t - h * (r * r * m))).astype(BF16)
            target = e_hbm.at[sc[row, EDGE], pl.ds(k * half, half)]
            copies.append(fetch(low_v.at[pl.ds(k * half, half)], target, sem.at[k]))
        out[...] = low_v[pl.ds(aligned(sc[row, CORE] * half), half), :]
        for copy in copies:
            copy.wait()


def pick_kernel(first, sc, stack_hbm, out, sem):
    fetch(stack_hbm.at[first + sc[0, CORE]], out, sem.at[0]).wait()


ANY = pl.BlockSpec(memory_space=pl.ANY)
NEAR = pl.BlockSpec(memory_space=pltpu.VMEM)
SLOT, LEADING, FIRST, VALID, WRITE, EDGE, CORE = range(7)
LITTLE = pl.CostEstimate(flops=1 << 20, bytes_accessed=1 << 16, transcendentals=0)


def near(value):
    return pltpu.with_memory_space_constraint(value, pltpu.VMEM)


def away(value):
    return pltpu.with_memory_space_constraint(value, pltpu.HBM)


def chunk_call(kernel, table, free, far, close, close_outs, buffers, scratch, limit, name):
    inputs = [table, *free, *(away(v) for v in far), *(near(v) for v in close)]
    in_specs = [pl.BlockSpec(memory_space=pltpu.SMEM)]
    in_specs += [ANY] * (len(free) + len(far)) + [NEAR] * len(close)
    outs = [pltpu.VMEM(*o) for o in close_outs]
    out_specs = [NEAR] * len(close_outs)
    aliases = {}
    for held, shape, dtype in buffers:
        if held is not None:
            aliases[len(inputs)] = len(outs)
            inputs.append(away(held))
            in_specs.append(ANY)
        outs.append(pltpu.HBM(shape, dtype))
        out_specs.append(ANY)
    results = pl.pallas_call(
        kernel,
        in_specs=in_specs,
        out_specs=out_specs,
        out_shape=outs,
        scratch_shapes=scratch,
        input_output_aliases=aliases,
        compiler_params=pltpu.CompilerParams(vmem_limit_bytes=limit << 20),
        cost_estimate=LITTLE,
        name=name,
    )(*inputs)
    return tuple(results[: len(close_outs)]), tuple(results[len(close_outs) :])


def forward_call(table, row, slots, x, arrived, params, carry, held):
    t = x.shape[0]
    held = held or (None,) * 7
    kinds = (
        ((t, D), BF16),
        ((t, D), BF16),
        ((t, OWN_PROJ), BF16),
        ((t, OWN), F32),
        ((t, OWN), BF16),
        ((STATE, OWN), F32),
        ((8, OWN_CONV), F32),
    )
    gain, convp, headp, chanp, win, wout = params
    outs, held = chunk_call(
        functools.partial(forward_kernel, row),
        table,
        (*arrived, x),
        (),
        (gain, convp, headp, chanp, *carry, win, wout),
        (((t, D + LANES), BF16), kinds[0], kinds[5], kinds[6]),
        [(b, (slots,) + k, d) for b, (k, d) in zip(held, kinds)],
        [pltpu.VMEM(*k) for k in kinds[1:]]
        + [
            pltpu.VMEM((t + 8, OWN_CONV), F32),
            pltpu.VMEM((LANES, t), F32),
            pltpu.VMEM((t, LANES), F32),
            pltpu.VMEM((t, t), F32),
            pltpu.SemaphoreType.DMA((8,)),
        ],
        FORWARD_VMEM,
        "forward_chunk",
    )
    return outs[0], outs[1], outs[2:], held


def backward_call(table, row, slots, cot, arrived, saved, params, carry, held):
    t = cot.shape[0]
    held = held or (None, None)
    _, convp, headp, chanp, win, wout = params
    wide, projected = ((t, D), BF16), ((t, OWN_PROJ), BF16)
    outs, held = chunk_call(
        functools.partial(backward_kernel, row),
        table,
        (*arrived, cot),
        saved,
        (convp, headp, chanp, *carry, win, wout),
        [wide] * 3 + [(v.shape, v.dtype) for v in carry],
        [(held[0], (slots, t, OWN_PROJ), BF16), (held[1], (slots, t, D), BF16)],
        [
            pltpu.VMEM(*projected),
            pltpu.VMEM((t, OWN), F32),
            pltpu.VMEM((STATE, OWN), F32),
            pltpu.VMEM((8, OWN_CONV), F32),
            pltpu.VMEM(*wide),
            pltpu.VMEM((t, LANES), F32),
            pltpu.VMEM(*projected),
            pltpu.VMEM(*wide),
            pltpu.VMEM(*wide),
            pltpu.VMEM((t + 8, OWN_CONV), F32),
            pltpu.VMEM((t + 8, OWN_CONV), F32),
            pltpu.VMEM((LANES, t), F32),
            pltpu.VMEM((t, OWN), F32),
            pltpu.VMEM((t, t), F32),
            pltpu.VMEM((t, t), F32),
            pltpu.VMEM((t, STATE), F32),
            pltpu.VMEM((t, STATE), F32),
            pltpu.SemaphoreType.DMA((11,)),
        ],
        BACKWARD_VMEM,
        "backward_chunk",
    )
    return outs[:3], outs[3:], held


def forward_join(table, row, slots, own, other, h, held):
    t = h.shape[0]
    held = held or (None,) * 3
    wide, thin = ((t, D), BF16), ((t, LANES), F32)
    outs, held = chunk_call(
        functools.partial(forward_join_kernel, row),
        table,
        (),
        (),
        (own, other, h),
        [((t // 2, D), BF16)],
        [(b, (slots,) + k, d) for b, (k, d) in zip(held, (wide, thin, wide))],
        [pltpu.VMEM(*k) for k in (wide, thin, wide)] + [pltpu.SemaphoreType.DMA((6,))],
        JOIN_VMEM,
        "forward_join",
    )
    return outs[0], held


def backward_join(table, row, own, other, h, g, gain, edge_held):
    slots, t, _ = edge_held.shape
    outs, held = chunk_call(
        functools.partial(backward_join_kernel, row),
        table,
        (),
        (),
        (own, other, h, g, gain),
        [((t // 2, D), BF16)],
        [(edge_held, (slots, t, D), BF16)],
        [pltpu.VMEM((t, D), BF16), pltpu.SemaphoreType.DMA((2,))],
        JOIN_VMEM,
        "backward_join",
    )
    return outs[0], held[0]


def pick(table, stack, first):
    outs, _ = chunk_call(
        functools.partial(pick_kernel, first),
        table,
        (),
        (stack,),
        (),
        [(stack.shape[1:], stack.dtype)],
        [],
        [pltpu.SemaphoreType.DMA((1,))],
        JOIN_VMEM,
        "pick",
    )
    return outs[0]


def own_of(values, core):
    lead, width = values.shape[:-1], values.shape[-1]
    blocks = values.reshape(lead + (4, 2, width // 8))
    return lax.dynamic_index_in_dim(blocks, core, len(lead) + 1, False).reshape(
        lead + (width // 2,)
    )


def woven(halves):
    width = halves.shape[-1]
    lead = halves.shape[1:-1]
    blocks = halves.reshape((2,) + lead + (4, width // 4))
    return jnp.moveaxis(blocks, 0, -2).reshape(lead + (2 * width,))


def small_params(norm_gain, conv_weight, conv_bias, dt_bias, a_log, skip_gain, gate_gain, core):
    own = functools.partial(own_of, core=core)
    taps = jnp.concatenate([conv_weight.T, conv_bias[None]], axis=0).astype(F32)
    taps = jnp.concatenate([own(taps[:, :INNER]), taps[:, INNER:]], axis=1)
    convp = jnp.pad(taps, ((0, 3), (0, 0)))
    heads = jnp.stack([own(dt_bias.astype(F32)), -jnp.exp(own(a_log.astype(F32)))])
    headp = jnp.pad(heads, ((0, 6), (0, LANES - OWN_HEADS)))
    skip = jnp.repeat(own(skip_gain.astype(F32)), HEAD_DIM)
    chanp = jnp.pad(jnp.stack([skip, own(gate_gain.astype(F32))]), ((0, 6), (0, 0)))
    return norm_gain.astype(F32)[None], convp, headp, chanp


def own_steps(weight, core):
    own = own_of(weight[INNER + CONV_CH :].T, core).T
    return jnp.pad(own, ((0, 2 * LANES - OWN_HEADS), (0, 0)))


HALF = OWN // 2
BLOCK = HALF // 2
PACKED_ROWS = HALF + HALF + 2 * STATE + 2 * BLOCK
PARTS = (
    ("in", HALF, X_AT, HALF),
    ("in", HALF, 0, HALF),
    ("in", 2 * STATE, BC_AT, 2 * STATE),
    ("out", BLOCK, 0, HALF),
    ("out", BLOCK, BLOCK, HALF),
)


def ring_place(position, count):
    back = position >= count
    return jnp.where(back, 1, 0), jnp.where(back, 2 * count - 1 - position, position)


def ring_route(count, step):
    def index(position):
        return position if position < count else count + (2 * count - 1 - position)

    size = 2 * count
    return [(index(p), index((p + step) % size)) for p in range(size)]


HALF_ROWS = PACKED_ROWS // 2


def cut(at, rows):
    spans = []
    for i in range(2):
        a, b = max(at, i * HALF_ROWS), min(at + rows, (i + 1) * HALF_ROWS)
        if a < b:
            spans.append((i, a - i * HALF_ROWS, a - at, b - a))
    return spans


def pack_kernel(sc, w, steps, o, own_a, own_b, rest_a, rest_b, sem):
    core, side = sc[0], sc[1]
    copies = []
    for targets, y in (((own_a, own_b), side), ((rest_a, rest_b), 1 - side)):
        at = 0
        for base in (INNER, 0):
            for k in range(2):
                first = base + (2 * y + k) * HALF + core * BLOCK
                for i, to, off, rows in cut(at, BLOCK):
                    source = w.at[pl.ds(aligned(first + off), rows)]
                    copies.append(fetch(source, targets[i].at[pl.ds(to, rows)], sem.at[len(copies)]))
                at += BLOCK
        bc = w.at[pl.ds(2 * INNER, 2 * STATE)]
        ((i, to, _, rows),) = cut(at, 2 * STATE)
        span = targets[i].at[pl.ds(to, rows)]
        copies.append(fetch_one_of(y == 0, bc, steps, span, sem.at[len(copies)]))
        at += 2 * STATE
        for k in range(2):
            ((i, to, _, rows),) = cut(at, BLOCK)
            cols = pl.ds(aligned(y * HALF + k * BLOCK), BLOCK)
            source = o.at[pl.ds(aligned(core * BLOCK), BLOCK), cols]
            copies.append(fetch(source, targets[i].at[pl.ds(to, rows)], sem.at[len(copies)]))
            at += BLOCK
    for copy in copies:
        copy.wait()


def pack_weights(scalars, w, steps, o):
    return pl.pallas_call(
        pack_kernel,
        in_specs=[pl.BlockSpec(memory_space=pltpu.SMEM), ANY, ANY, ANY],
        out_specs=[NEAR, NEAR, NEAR, NEAR],
        out_shape=[pltpu.VMEM((HALF_ROWS, BLOCK), BF16)] * 4,
        scratch_shapes=[pltpu.SemaphoreType.DMA((16,))],
        compiler_params=pltpu.CompilerParams(vmem_limit_bytes=4 << 20),
        cost_estimate=LITTLE,
        name="pack_weights",
    )(scalars, away(w), steps, away(o))


def put_block(sc, halves, z, y, win, wout, sem, start):
    lanes = pl.ds(aligned(z * BLOCK), BLOCK)
    copies, at = [], 0
    for matrix, rows, first, step in PARTS:
        for i, to, off, count in cut(at, rows):
            if matrix == "in":
                target = win.at[pl.ds(aligned(first + y * step + off), count), lanes]
            else:
                target = wout.at[lanes, pl.ds(aligned(first + y * step), BLOCK)]
            source = halves[i].at[pl.ds(to, count)]
            copies.append(fetch(source, target, sem.at[start + len(copies)]))
        at += rows
    return copies


def place_kernel(which, sc, *refs):
    win, wout, sem = refs[-3:]
    blocks = [refs[2 * i : 2 * i + 2] for i in range(8 if which == 0 else 4)]
    side, place = sc[1], sc[2]
    inner = jnp.logical_and(place > 0, place < 3)

    def put(number, block, z, y):
        return put_block(sc, blocks[block], z, y, win, wout, sem, 8 * number)

    always = []
    if which == 0:
        beside = place + 1 - 2 * lax.rem(place, 2)
        always += put(0, 0, place, side) + put(1, 1, place, 1 - side)
        always += put(2, 2, beside, side) + put(3, 3, beside, 1 - side)
        from_z, first = jnp.where(inner, 3 - place, jnp.where(place == 0, 2, 1)), 4
    else:
        from_z, first = jnp.where(place < 2, 3, 0), 0

    def rest(block):
        copies = put(4, block, from_z, side) + put(5, block + 1, from_z, 1 - side)
        for copy in copies:
            copy.wait()

    @pl.when(inner)
    def _():
        rest(first)

    @pl.when(jnp.logical_not(inner))
    def _():
        rest(first + 2)

    for copy in always:
        copy.wait()


def place_weights(here, blocks, held):
    inputs = [here] + [away(half) for block in blocks for half in block]
    in_specs = [pl.BlockSpec(memory_space=pltpu.SMEM)] + [ANY] * (len(inputs) - 1)
    aliases = {}
    if held is not None:
        aliases = {len(inputs): 0, len(inputs) + 1: 1}
        inputs += [near(v) for v in held]
        in_specs += [NEAR, NEAR]
    return pl.pallas_call(
        functools.partial(place_kernel, 0 if held is None else 1),
        in_specs=in_specs,
        out_specs=[NEAR, NEAR],
        out_shape=[pltpu.VMEM((OWN_PROJ, D), BF16), pltpu.VMEM((OWN, D), BF16)],
        scratch_shapes=[pltpu.SemaphoreType.DMA((48,))],
        input_output_aliases=aliases,
        compiler_params=pltpu.CompilerParams(vmem_limit_bytes=4 << 20),
        cost_estimate=LITTLE,
        name="place_weights",
    )(*inputs)


def line_gather(own, beside):
    def along(value, hops):
        path = [(y * 4 + a, y * 4 + b) for y in range(2) for a, b in hops]
        return lax.ppermute(value, ("y", "fsdp"), path)

    def across(value, places):
        path = [(y * 4 + z, (1 - y) * 4 + z) for y in range(2) for z in places]
        return lax.ppermute(value, ("y", "fsdp"), path)

    pair, middle, outward = [(0, 1), (1, 0), (2, 3), (3, 2)], [(1, 2), (2, 1)], [(1, 0), (2, 3)]
    inner, outer = (1, 2), (0, 3)
    barrier = lax.optimization_barrier
    a, b = own
    near_a, in2_a = along(a, pair), along(a, middle)
    near_a, in2_a, b = barrier((near_a, in2_a, b))
    near_b, in2_b, near_ya = along(b, pair), along(b, middle), across(near_a, range(4))
    near_a, in2_a, near_b, in2_b, near_ya, *beside = barrier(
        (near_a, in2_a, near_b, in2_b, near_ya, *beside)
    )
    out2_a, in3_a, near_yb = along(in2_a, outward), along(near_a, middle), across(near_b, range(4))
    out2_a, in3_a, near_yb, in2_a, near_b, in2_b = barrier(
        (out2_a, in3_a, near_yb, in2_a, near_b, in2_b)
    )
    out2_b, in3_b = along(in2_b, outward), along(near_b, middle)
    out2_ya, in2_ya = across(out2_a, outer), across(in2_a, inner)
    out2_b, in3_b, out2_ya, in2_ya, in3_a, in2_b = barrier(
        (out2_b, in3_b, out2_ya, in2_ya, in3_a, in2_b)
    )
    ready = in2_ya
    out3_a = along(in3_a, outward)
    out2_yb, in2_yb = across(out2_b, outer), across(in2_b, inner)
    out3_a, out2_yb, in2_yb, in3_a, in3_b = barrier((out3_a, out2_yb, in2_yb, in3_a, in3_b))
    out3_b = along(in3_b, outward)
    out3_ya, in3_ya = across(out3_a, outer), across(in3_a, inner)
    out3_b, out3_ya, in3_ya, in3_b = barrier((out3_b, out3_ya, in3_ya, in3_b))
    out3_yb, in3_yb = across(out3_b, outer), across(in3_b, inner)
    blocks = [
        (near_a, near_b),
        (near_ya, near_yb),
        (in2_a, in2_b),
        (in2_ya, in2_yb),
        (out2_a, out2_b),
        (out2_ya, out2_yb),
        (in3_a, in3_b),
        (in3_ya, in3_yb),
        (out3_a, out3_b),
        (out3_ya, out3_yb),
    ]
    return blocks, beside, ready


GROUPS = (
    (1, (HALF, X_AT, HALF), (LANES, BC_AT, 2 * STATE)),
    (-1, (HALF, 0, HALF), (LANES, BC_AT + LANES, 2 * STATE)),
)


SMALL_ROWS = 16
IN_ROWS = HALF + LANES
GROUP_ROWS = IN_ROWS + BLOCK


def block_grad_kernel(row, sc, normed_ref, q_ref, gs_ref, *refs):
    out = refs[-1]
    chunks = normed_ref.shape[0]
    at = 0
    for ref in refs[:2]:
        width = ref.shape[2]
        value = sum(dot_tn(ref[k], normed_ref[k]) for k in range(chunks))
        out[at : at + width, :] = value.astype(BF16)
        at += width
    out[at:, :] = sum(dot_tn(q_ref[k], gs_ref[k]) for k in range(chunks)).astype(BF16)
    if len(refs) > 3:

        @pl.when(sc[row, 0] == 1)
        def _():
            out[HALF : HALF + SMALL_ROWS, :] = refs[2][0].astype(BF16)


def block_grad(table, row, group, normed_held, grads_held, q_held, gs_held, small):
    slots, t, _ = normed_held.shape
    number, (_, *parts) = group, GROUPS[group]

    def block(width, index):
        return pl.BlockSpec((slots - 1, t, width), lambda i, s: (0, 0, index(s)))

    in_specs = [
        block(BLOCK, lambda s: s[row, 1]),
        block(BLOCK, lambda s: s[row, 1]),
        block(BLOCK, lambda s: 2 * s[row, 0] + number),
    ]
    for width, first, step in parts:

        def index(s, width=width, first=first, step=step):
            return first // width + s[row, 0] * (step // width)

        in_specs.append(block(width, index))
    extra = []
    if number == 1:
        extra = [small]
        in_specs.append(pl.BlockSpec((1, SMALL_ROWS, BLOCK), lambda i, s: (s[row, 1], 0, 0)))
    return pl.pallas_call(
        functools.partial(block_grad_kernel, row),
        grid_spec=pltpu.PrefetchScalarGridSpec(
            num_scalar_prefetch=1,
            grid=(1,),
            in_specs=in_specs,
            out_specs=pl.BlockSpec((GROUP_ROWS, BLOCK), lambda i, s: (0, 0)),
        ),
        out_shape=jax.ShapeDtypeStruct((GROUP_ROWS, BLOCK), BF16),
        compiler_params=pltpu.CompilerParams(vmem_limit_bytes=24 << 20),
        cost_estimate=LITTLE,
        name="block_grad",
    )(
        table,
        away(normed_held),
        away(q_held),
        away(gs_held),
        *([away(grads_held)] * len(parts)),
        *extra,
    )


def grads_kernel(sc, *refs):
    in_hbm, out_hbm, small_out, in_v, out_v, sem = refs[-6:]
    core, side = sc[0], sc[1]

    def block(i, c, y, rows):
        own, across, other, far = refs[4 * i : 4 * i + 4]
        here = jnp.where(side == y, own[rows], across[rows])
        there = jnp.where(side == y, other[rows], far[rows])
        return jnp.where(core == c, here, there).astype(F32)

    copies = []

    def store(values, near_ref, far_ref, at):
        near_ref[at : at + values.shape[0]] = values
        span = pl.ds(at, values.shape[0])
        copies.append(fetch(near_ref.at[span], far_ref.at[span], sem.at[len(copies)]))

    for i, base in ((0, INNER), (1, 0)):
        for c in range(2):
            for y in range(2):
                for k in range(2):
                    rows = slice(k * BLOCK, (k + 1) * BLOCK)
                    store(block(i, c, y, rows), in_v, in_hbm, base + (2 * y + k) * HALF + c * BLOCK)
    rows = slice(HALF, HALF + STATE)
    for i in range(2):
        store(block(i, 0, 0, rows) + block(i, 1, 0, rows), in_v, in_hbm, 2 * INNER + i * STATE)
    steps = [block(0, c, 1, slice(HALF, HALF + 32)) for c in range(2)]
    steps = [steps[c][z * 6 : z * 6 + 6] for z in range(4) for c in range(2)]
    store(jnp.concatenate(steps, axis=0), in_v, in_hbm, INNER + CONV_CH)
    rows = slice(HALF, HALF + SMALL_ROWS)
    small_out[...] = block(1, 0, 1, rows) + block(1, 1, 1, rows)
    rows = slice(IN_ROWS, GROUP_ROWS)
    for c in range(2):
        values = [block(i, c, y, rows) for y in range(2) for i in range(2)]
        store(jnp.concatenate(values, axis=1), out_v, out_hbm, c * BLOCK)
    for copy in copies:
        copy.wait()


def join_grads(scalars, parts):
    arrays = [near(a) for part in parts for a in part]
    height = INNER + CONV_CH + HEADS
    shapes = ((height, BLOCK), F32), ((2 * BLOCK, D), F32)
    return pl.pallas_call(
        grads_kernel,
        in_specs=[pl.BlockSpec(memory_space=pltpu.SMEM)] + [NEAR] * len(arrays),
        out_specs=[ANY, ANY, NEAR],
        out_shape=[pltpu.HBM(*k) for k in shapes] + [pltpu.VMEM((SMALL_ROWS, BLOCK), F32)],
        scratch_shapes=[pltpu.VMEM(*k) for k in shapes] + [pltpu.SemaphoreType.DMA((24,))],
        compiler_params=pltpu.CompilerParams(vmem_limit_bytes=28 << 20),
        cost_estimate=LITTLE,
        name="join_grads",
    )(scalars, *arrays)


def swap(value, axis):
    return lax.ppermute(value, axis, [(0, 1), (1, 0)])


def sent_along(value, axis):
    size = lax.axis_size(axis)
    routes = [[(i, (i + k) % size) for i in range(size)] for k in range(1, size)]
    return [lax.ppermute(value, axis, path) for path in routes]


def in_order(value, others, axis):
    size, place = len(others) + 1, lax.axis_index(axis)
    ring = jnp.stack([*others[::-1], value] * 2)
    return lax.dynamic_slice_in_dim(ring, (size - 1 - place) % size, size, 0)


LAG = 2


def relay_shards(
    ends,
    norm_gain,
    input_weight,
    conv_weight,
    conv_bias,
    dt_bias,
    a_log,
    skip_gain,
    gate_gain,
    output_weight,
):
    core = lax.axis_index("core")
    place = lax.axis_index("fsdp")
    side = lax.axis_index("y")
    section = lax.axis_index("section")
    leading = (section == 0).astype(jnp.int32)
    local = ends[0][:, 0]
    t = local.shape[1]
    chunks = lax.axis_size("fsdp")
    micro = place // 2

    small = [norm_gain[0], conv_weight[0].reshape(-1), conv_bias[0], dt_bias[0], a_log[0]]
    small += [skip_gain[0], gate_gain[0]]
    packed = jnp.concatenate(small)
    others = sent_along(packed, "fsdp")
    w = input_weight[0].T
    steps = own_steps(w, core)
    here = jnp.stack([core, side, place]).astype(jnp.int32)
    packed_halves = pack_weights(here, w, steps, output_weight[0])
    blocks, others, ready = line_gather(packed_halves[:2], others)
    packed = in_order(packed, others, "fsdp")
    pieces, at = [], 0
    for member in small:
        pieces.append(packed[:, at : at + member.shape[0]].reshape(-1))
        at += member.shape[0]
    pieces[1] = pieces[1].reshape(CONV_CH, KERNEL)
    gain, convp, headp, chanp = small_params(*pieces, core)
    local, _ = lax.optimization_barrier((local, ready))

    def route(first, m):
        return [
            (c * chunks + z, (z % 2) * chunks + 2 * m + c)
            for c in range(2)
            for z in (first, first + 1)
        ]

    def bring(first):
        return [lax.ppermute(local[m], ("core", "fsdp"), route(first, m)) for m in range(2)]

    def shared(got):
        got = jnp.where(micro == 0, got[0], got[1])
        other = swap(got, "core")
        return [jnp.where(core == 0, got, other), jnp.where(core == 0, other, got)]

    def give(piece, first):
        return [
            lax.ppermute(piece, ("core", "fsdp"), [(b, a) for a, b in route(first, m)])
            for m in range(2)
        ]

    matrices = place_weights(here, [packed_halves[:2], packed_halves[2:], *blocks[:6]], None)
    last = (blocks[7][1], blocks[9][1])
    here, *got = lax.optimization_barrier((here, *bring(0), *bring(2), *last, *matrices))
    blocks[7], blocks[9] = (blocks[7][0], got[4]), (blocks[9][0], got[5])
    pieces = shared(got[:2]) + shared(got[2:4])
    win, wout = place_weights(here, blocks[6:], got[6:])
    params = (gain, convp, headp, chanp, win, wout)

    def scalars(moment, lag, reverse):
        begin = jnp.where(leading == 1, lag if reverse else 0, 0 if reverse else lag)
        step = moment - begin
        valid = jnp.logical_and(step >= 0, step < chunks)
        inside = jnp.clip(step, 0, chunks - 1)
        chunk = chunks - 1 - inside if reverse else inside
        write = jnp.where(valid, chunk, chunks)
        edge_here = leading == 1 if reverse else leading == 0
        edge = jnp.where(jnp.logical_and(valid, edge_here), chunk, chunks)
        values = [chunk if reverse else write, leading, step == 0, valid, write, edge, core]
        return [jnp.asarray(v, jnp.int32) for v in values]

    moments = chunks + LAG
    table = [scalars(moment, LAG, False) for moment in range(moments)]
    table += [scalars(moment, LAG, True) for moment in range(moments)]
    table = jnp.stack(sum(table, [])).reshape(len(table), -1)
    size = 2 * chunks
    position = jnp.where(side == 0, place, size - 1 - place).astype(jnp.int32)
    owners = []
    for direction in (1, -1):
        for hop in range(size):
            owners += ring_place((position - direction * (1 + hop)) % size, chunks)
    owners = jnp.stack(owners).reshape(2 * size, 2).astype(jnp.int32)
    table, owners = lax.optimization_barrier((table, owners))

    state, tail = jnp.zeros((STATE, OWN), F32), jnp.zeros((8, OWN_CONV), F32)
    blank = jnp.zeros((t, D), BF16)
    held, joined, result = None, None, None
    moved, incoming = {}, {}
    for moment in range(moments):
        if moment > 0:
            tail, result = lax.optimization_barrier((tail, result))
            if moment - 1 < chunks:
                moved[moment - 1] = lax.ppermute(result, "section", [(0, 1)])
        arrived = incoming.get(moment - LAG, (blank[: t // 2],) * 2)
        partial, h, (state, tail), held = forward_call(
            table,
            moment,
            chunks + 1,
            pieces[min(moment, chunks - 1)],
            arrived,
            params,
            (state, tail),
            held,
        )
        if moment - 1 in moved:
            partial, got = lax.optimization_barrier((partial, moved[moment - 1]))
            incoming[moment - 1] = (got, swap(got, "core"))
        other = swap(partial, "core")
        result, joined = forward_join(table, moment, chunks + 1, partial, other, h, joined)
    h_held, normed_held, pr_held, mx_held, q_held, st_held, tl_held = held
    y_held, ri_held, edge_held = joined
    saved = (h_held, normed_held, pr_held, mx_held, st_held, tl_held, y_held, ri_held)

    def tokens(buffer):
        return buffer[:chunks].reshape(chunks * t, buffer.shape[-1])

    carry = (
        jnp.zeros((STATE, OWN), F32),
        jnp.zeros((8, OWN_CONV), F32),
        jnp.zeros((8, OWN), F32),
        jnp.zeros((16, OWN_CONV), F32),
    )
    grads_held = None
    moved, incoming = {}, {}
    for moment in range(moments):
        if moment > 0:
            *carry, acc = carry
            acc, result = lax.optimization_barrier((acc, result))
            carry = (*carry, acc)
            if moment - 1 < chunks:
                moved[moment - 1] = lax.ppermute(result, "section", [(1, 0)])
        arrived = incoming.get(moment - LAG, (blank[: t // 2],) * 2)
        cot = pieces[max(chunks - 1 - moment, 0)]
        (partial, g, h), carry, grads_held = backward_call(
            table, moments + moment, chunks + 1, cot, arrived, saved, params, carry, grads_held
        )
        if moment - 1 in moved:
            partial, got = lax.optimization_barrier((partial, moved[moment - 1]))
            incoming[moment - 1] = (got, swap(got, "core"))
        other = swap(partial, "core")
        result, edge_held = backward_join(
            table, moments + moment, partial, other, h, g, gain, edge_held
        )

    def both(own, other, index):
        return jnp.where(index == 0, jnp.stack([own, other]), jnp.stack([other, own]))

    acc = carry[3]

    def placed(own):
        zero = jnp.zeros_like(own)
        return woven(both(own, zero, core))

    taps = jnp.concatenate([placed(acc[:5, :OWN]), acc[:5, OWN:]], axis=1)
    taps = jnp.moveaxis(taps.reshape(KERNEL + 1, chunks, -1), 1, 0)
    skip = acc[5, :OWN].reshape(OWN_HEADS, HEAD_DIM).sum(axis=1)
    vectors = [
        acc[9, :D] / gain[0],
        taps,
        placed(acc[7, :OWN_HEADS]),
        placed(acc[8, :OWN_HEADS]),
        placed(skip),
        placed(acc[6, :OWN]),
    ]
    vectors = [v.reshape(chunks, -1) for v in vectors]
    small = jnp.concatenate(vectors, axis=1)
    small = jnp.pad(small, ((0, 0), (0, SMALL_ROWS * BLOCK - small.shape[1])))
    small = small.reshape(chunks, SMALL_ROWS, BLOCK)

    onward, back = ring_route(chunks, 1), ring_route(chunks, -1)
    grads_held, gs_held = grads_held
    sums = [None] * len(GROUPS)
    for hop in range(size):
        if hop > 0:
            owners, *sums = lax.optimization_barrier((owners, *sums))
        for i, (direction, *_) in enumerate(GROUPS):
            row = hop + (0 if direction == 1 else size)
            block = block_grad(owners, row, i, normed_held, grads_held, q_held, gs_held, small)
            if hop > 0:
                path = onward if direction == 1 else back
                came = lax.ppermute(sums[i], ("y", "fsdp"), path).astype(F32)
                block = (block.astype(F32) + came).astype(BF16)
            sums[i] = block
        if hop == 3:
            finished = pick(table, edge_held, 0), pick(table, edge_held, 2)
            owners, *finished = lax.optimization_barrier((owners, *finished))
    *sums, early, late = lax.optimization_barrier((*sums, *finished))

    edges = jnp.where(place < 2, jnp.stack(give(early, 0)), jnp.stack(give(late, 2)))
    edges = edges[None, :, None]
    parts = []
    for own in sums:
        across = swap(own, "y")
        parts.append((own, across, swap(own, "core"), swap(across, "core")))
    here = jnp.stack([core, side]).astype(jnp.int32)
    here, edges = lax.optimization_barrier((here, edges))
    in_grad, out_grad, summed = join_grads(here, parts)
    in_grad = in_grad.T
    summed = summed.reshape(-1)
    grads, at = [], 0
    for v in vectors:
        grads.append(summed[at : at + v.shape[1]][None])
        at += v.shape[1]
    taps = grads[1].reshape(KERNEL + 1, -1)
    grads[1:2] = taps[:KERNEL].T[None], taps[KERNEL:]
    return (
        edges,
        grads[0],
        in_grad[None],
        grads[1],
        grads[2],
        grads[3],
        grads[4],
        grads[5],
        grads[6],
        out_grad[None],
    )


def shifted(block, axis, distance):
    devices = range(lax.axis_size(axis))
    route = [(i - distance, i) for i in devices if i - distance in devices]
    return lax.ppermute(block, axis, route)


def prefix(value, axis, join, neutral):
    place = lax.axis_index(axis)
    gathered = jax.tree.map(
        lambda a, kind: lax.all_gather(a.astype(kind), axis), value, (jnp.bfloat16, jnp.bfloat16)
    )
    state = jax.tree.map(lambda a, e: jnp.zeros_like(a) + jnp.asarray(e, a.dtype), value, neutral)

    def one(turn, state):
        return join(
            state,
            jax.tree.map(
                lambda a, own: lax.dynamic_index_in_dim(a, turn, 0, False).astype(own.dtype),
                gathered,
                value,
            ),
        )

    return lax.fori_loop(0, place, one, state)


def prefix_2(value, axis, join, neutral):
    count = lax.axis_size(axis)
    place = lax.axis_index(axis)
    ahead = count - 1 - place
    gathered = jax.tree.map(
        lambda a, kind: lax.all_gather(a.astype(kind), axis),
        value,
        jax.tree.map(lambda a: jnp.bfloat16 if a.dtype == jnp.float32 else a.dtype, value),
    )
    state = jax.tree.map(lambda a, e: jnp.zeros_like(a) + jnp.asarray(e, a.dtype), value, neutral)

    def one(turn, state):
        source = count - 1 - turn
        return join(
            state,
            jax.tree.map(
                lambda a, own: lax.dynamic_index_in_dim(a, source, 0, False).astype(own.dtype),
                gathered,
                value,
            ),
        )

    return lax.fori_loop(0, ahead, one, state)


def rms_scale(values, scale_gain):
    return (
        values * lax.rsqrt(jnp.mean(values * values, axis=-1, keepdims=True) + EPSILON) * scale_gain
    )


def chain_rule(earlier, later_part):
    return (
        earlier[0] * later_part[0],
        later_part[1] + later_part[0][:, :, None, None] * earlier[1],
    )


def conv_features(widened, conv_weight, conv_bias, dt_raw, dt_bias, a_log):
    tap_count = conv_weight.shape[1]
    step_count = widened.shape[1] - tap_count + 1
    convolved = conv_bias
    for offset in range(tap_count):
        convolved = convolved + widened[:, offset : offset + step_count, :] * conv_weight[:, offset]
    activated = jax.nn.silu(convolved)
    x_heads = activated[..., :INNER]
    b_rows = activated[..., INNER : INNER + STATE]
    c_rows = activated[..., INNER + STATE :]
    dt_step = jax.nn.softplus(dt_raw + dt_bias)
    log_decay = jnp.cumsum(-jnp.exp(a_log) * dt_step, axis=1)
    return (x_heads, b_rows, c_rows, dt_step, log_decay)


def local_states(x_heads, b_rows, dt_step, log_decay):
    seq_count, length = (x_heads.shape[0], x_heads.shape[1])
    spread = x_heads.reshape(seq_count, length, HEADS, HEAD_DIM)
    weights = jnp.exp(log_decay[:, -1:, :] - log_decay) * dt_step
    weighted = spread * weights[..., None]
    states = jnp.einsum("sqhd,sqn->shdn", weighted, b_rows, precision=EXACT_MATMUL)
    return (jnp.exp(log_decay[:, -1]), states)


def gated_output(
    x_heads, b_rows, c_rows, dt_step, log_decay, prior_state, gate_z, skip_gain, gate_gain
):
    seq_count, length = (x_heads.shape[0], x_heads.shape[1])
    spread = x_heads.reshape(seq_count, length, HEADS, HEAD_DIM)
    scaled = spread * dt_step[..., None]
    by_head = jnp.transpose(log_decay, (0, 2, 1))
    differ = by_head[:, :, :, None] - by_head[:, :, None, :]
    causal = jnp.arange(length)[:, None] >= jnp.arange(length)[None, :]
    mixing = jnp.where(causal, jnp.exp(jnp.where(causal, differ, 0.0)), 0.0)
    intersections = jnp.einsum("sqn,skn->sqk", c_rows, b_rows, precision=EXACT_MATMUL)
    mixed_out = jnp.einsum(
        "shqk,skhd->sqhd", mixing * intersections[:, None], scaled, precision=EXACT_MATMUL
    )
    mixed_out = mixed_out + jnp.exp(log_decay)[..., None] * jnp.einsum(
        "sqn,shdn->sqhd", c_rows, prior_state, precision=EXACT_MATMUL
    )
    mixed_out = (mixed_out + skip_gain[:, None] * spread).reshape(seq_count, length, INNER)
    return rms_scale(mixed_out * jax.nn.silu(gate_z), gate_gain)


def layer_forward(hidden, weights):
    (
        norm_gain,
        input_weight,
        conv_weight,
        conv_bias,
        dt_bias,
        a_log,
        skip_gain,
        gate_gain,
        output_weight,
    ) = weights
    normalized_rows = rms_scale(hidden, norm_gain.astype(jnp.float32)).astype(jnp.bfloat16)
    projected_rows = jnp.einsum(
        "spd,de->spe", normalized_rows, input_weight, preferred_element_type=jnp.float32
    ).astype(jnp.bfloat16)
    length = hidden.shape[1]
    xbc_part = projected_rows[..., INNER : INNER + CONV_CH]
    border = shifted(xbc_part[:, length - KERNEL + 1 :, :], "fsdp", 1)
    widened = jnp.concatenate([border, xbc_part], axis=1)
    features = conv_features(
        widened.astype(jnp.float32),
        conv_weight.astype(jnp.float32),
        conv_bias.astype(jnp.float32),
        projected_rows[..., INNER + CONV_CH :].astype(jnp.float32),
        dt_bias.astype(jnp.float32),
        a_log.astype(jnp.float32),
    )
    decays, states = local_states(features[0], features[1], features[3], features[4])
    scanned = prefix(
        (decays, states), "fsdp", chain_rule, (jnp.ones_like(decays), jnp.zeros_like(states))
    )
    prior_state = scanned[1]
    gated_result = gated_output(
        features[0],
        features[1],
        features[2],
        features[3],
        features[4],
        prior_state,
        projected_rows[..., :INNER].astype(jnp.float32),
        skip_gain.astype(jnp.float32),
        gate_gain.astype(jnp.float32),
    )
    gated_low = gated_result.astype(jnp.bfloat16)
    final_result = hidden + jnp.einsum(
        "spi,id->spd", gated_low, output_weight, preferred_element_type=jnp.float32
    )
    return (
        final_result,
        (hidden, normalized_rows, projected_rows, widened, prior_state, gated_low),
    )


def layer_backward(gradient, kept_state, weights):
    hidden, normalized_rows, projected_rows, widened, prior_state, gated_low = kept_state
    (
        norm_gain,
        input_weight,
        conv_weight,
        conv_bias,
        dt_bias,
        a_log,
        skip_gain,
        gate_gain,
        output_weight,
    ) = weights
    grad_low = gradient.astype(jnp.bfloat16)
    grad_out_weight = jnp.einsum(
        "spi,spd->id", gated_low, grad_low, preferred_element_type=jnp.float32
    )
    grad_gated = jnp.einsum(
        "spd,id->spi", grad_low, output_weight, preferred_element_type=jnp.float32
    )
    features, pull_features = jax.vjp(
        conv_features,
        widened.astype(jnp.float32),
        conv_weight.astype(jnp.float32),
        conv_bias.astype(jnp.float32),
        projected_rows[..., INNER + CONV_CH :].astype(jnp.float32),
        dt_bias.astype(jnp.float32),
        a_log.astype(jnp.float32),
    )
    _, pull_gated = jax.vjp(
        gated_output,
        features[0],
        features[1],
        features[2],
        features[3],
        features[4],
        prior_state,
        projected_rows[..., :INNER].astype(jnp.float32),
        skip_gain.astype(jnp.float32),
        gate_gain.astype(jnp.float32),
    )
    grads_gated = pull_gated(grad_gated)
    decay_states, pull_states = jax.vjp(
        local_states, features[0], features[1], features[3], features[4]
    )
    decays = decay_states[0]
    later_state = prefix_2(
        (decays, grads_gated[5]),
        "fsdp",
        chain_rule,
        (jnp.ones_like(decays), jnp.zeros_like(grads_gated[5])),
    )
    grad_end = later_state[1]
    state_parts = pull_states((jnp.sum(grad_end * prior_state, axis=(2, 3)), grad_end))
    feature_grads = (
        grads_gated[0] + state_parts[0],
        grads_gated[1] + state_parts[1],
        grads_gated[2],
        grads_gated[3] + state_parts[2],
        grads_gated[4] + state_parts[3],
    )
    grad_wide, grad_conv_w, grad_conv_b, grad_dt_raw, grad_dt_bias, grad_a_log = pull_features(
        feature_grads
    )
    margin = KERNEL - 1
    returned = shifted(grad_wide[:, :margin, :].astype(jnp.bfloat16), "fsdp", -1).astype(
        jnp.float32
    )
    own_rows = grad_wide[:, margin:, :]
    length = own_rows.shape[1]
    grad_xbc = jnp.concatenate(
        [own_rows[:, : length - margin], own_rows[:, length - margin :] + returned], axis=1
    )
    grad_proj = jnp.concatenate([grads_gated[6], grad_xbc, grad_dt_raw], axis=-1).astype(
        jnp.bfloat16
    )
    grad_in_weight = jnp.einsum(
        "spd,spe->de", normalized_rows, grad_proj, preferred_element_type=jnp.float32
    )
    grad_normed = jnp.einsum(
        "spe,de->spd", grad_proj, input_weight, preferred_element_type=jnp.float32
    )
    _, pull_norm = jax.vjp(rms_scale, hidden, norm_gain.astype(jnp.float32))
    grad_hidden, grad_norm_gain = pull_norm(grad_normed)
    return (
        gradient + grad_hidden,
        (
            grad_norm_gain,
            grad_in_weight,
            grad_conv_w,
            grad_conv_b,
            grad_dt_bias,
            grad_a_log,
            grads_gated[7],
            grads_gated[8],
            grad_out_weight,
        ),
    )


def shards(
    ends,
    norm_gain,
    input_weight,
    conv_weight,
    conv_bias,
    dt_bias,
    a_log,
    skip_gain,
    gate_gain,
    output_weight,
):
    gathered = (
        lax.all_gather(norm_gain, "fsdp", axis=1, tiled=True),
        lax.all_gather(input_weight, "fsdp", axis=1, tiled=True),
        lax.all_gather(conv_weight, "fsdp", axis=1, tiled=True),
        lax.all_gather(conv_bias, "fsdp", axis=1, tiled=True),
        lax.all_gather(dt_bias, "fsdp", axis=1, tiled=True),
        lax.all_gather(a_log, "fsdp", axis=1, tiled=True),
        lax.all_gather(skip_gain, "fsdp", axis=1, tiled=True),
        lax.all_gather(gate_gain, "fsdp", axis=1, tiled=True),
        lax.all_gather(output_weight, "fsdp", axis=1, tiled=True),
    )
    layer_weights = tuple((member[0] for member in gathered))
    leading = lax.axis_index("section") == 0
    local_data = ends[0].astype(jnp.float32)
    batches = local_data.shape[0]
    arrived = jnp.zeros(local_data.shape[1:], jnp.float32)
    stored = []
    produced = []
    for moment in range(batches + 1):
        source = jnp.where(leading, local_data[min(moment, batches - 1)], arrived)
        final_result, kept_state = layer_forward(source, layer_weights)
        stored.append(kept_state)
        produced.append(final_result)
        if moment < batches:
            arrived = shifted(final_result.astype(jnp.bfloat16), "section", 1).astype(jnp.float32)
    totals = None
    coming = jnp.zeros(local_data.shape[1:], jnp.float32)
    returned_grads = []
    for moment in range(batches + 1):
        gradient = jnp.where(leading, coming, local_data[min(moment, batches - 1)])
        kept_state = jax.tree.map(
            lambda upper_part, lower_part: jnp.where(leading, upper_part, lower_part),
            stored[max(moment - 1, 0)],
            stored[min(moment + 1, batches)],
        )
        grad_input, gradients = layer_backward(gradient, kept_state, layer_weights)
        active = jnp.where(leading, moment >= 1, moment < batches)
        masked = tuple((jnp.where(active, member, 0.0) for member in gradients))
        if totals is None:
            totals = masked
        else:
            totals = tuple((earlier_sum + member for earlier_sum, member in zip(totals, masked)))
        returned_grads.append(grad_input)
        if moment < batches:
            coming = shifted(grad_input.astype(jnp.bfloat16), "section", -1).astype(jnp.float32)
    boundary = jnp.stack(
        [
            jnp.where(leading, returned_grads[number + 1], produced[number + 1])
            for number in range(batches)
        ]
    )
    owned_parts = (
        lax.psum_scatter(
            totals[0][None].astype(jnp.bfloat16), "fsdp", scatter_dimension=1, tiled=True
        ).astype(jnp.float32),
        lax.psum_scatter(
            totals[1][None].astype(jnp.bfloat16), "fsdp", scatter_dimension=1, tiled=True
        ).astype(jnp.float32),
        lax.psum_scatter(
            totals[2][None].astype(jnp.bfloat16), "fsdp", scatter_dimension=1, tiled=True
        ).astype(jnp.float32),
        lax.psum_scatter(
            totals[3][None].astype(jnp.bfloat16), "fsdp", scatter_dimension=1, tiled=True
        ).astype(jnp.float32),
        lax.psum_scatter(
            totals[4][None].astype(jnp.bfloat16), "fsdp", scatter_dimension=1, tiled=True
        ).astype(jnp.float32),
        lax.psum_scatter(
            totals[5][None].astype(jnp.bfloat16), "fsdp", scatter_dimension=1, tiled=True
        ).astype(jnp.float32),
        lax.psum_scatter(
            totals[6][None].astype(jnp.bfloat16), "fsdp", scatter_dimension=1, tiled=True
        ).astype(jnp.float32),
        lax.psum_scatter(
            totals[7][None].astype(jnp.bfloat16), "fsdp", scatter_dimension=1, tiled=True
        ).astype(jnp.float32),
        lax.psum_scatter(
            totals[8][None].astype(jnp.bfloat16), "fsdp", scatter_dimension=1, tiled=True
        ).astype(jnp.float32),
    )
    summed = (
        lax.psum(owned_parts[0].astype(jnp.bfloat16), "rep").astype(jnp.float32),
        lax.psum(owned_parts[1].astype(jnp.bfloat16), "rep").astype(jnp.float32),
        lax.psum(owned_parts[2].astype(jnp.bfloat16), "rep").astype(jnp.float32),
        lax.psum(owned_parts[3].astype(jnp.bfloat16), "rep").astype(jnp.float32),
        lax.psum(owned_parts[4].astype(jnp.bfloat16), "rep").astype(jnp.float32),
        lax.psum(owned_parts[5].astype(jnp.bfloat16), "rep").astype(jnp.float32),
        lax.psum(owned_parts[6].astype(jnp.bfloat16), "rep").astype(jnp.float32),
        lax.psum(owned_parts[7].astype(jnp.bfloat16), "rep").astype(jnp.float32),
        lax.psum(owned_parts[8].astype(jnp.bfloat16), "rep").astype(jnp.float32),
    )
    return (
        boundary.astype(jnp.bfloat16)[None],
        summed[0],
        summed[1],
        summed[2],
        summed[3],
        summed[4],
        summed[5],
        summed[6],
        summed[7],
        summed[8],
    )


def solution(mesh):
    shape = mesh.shape
    relay = shape["section"] == 2 and shape["rep"] == 4 and shape["fsdp"] == 4
    if relay:
        devices = mesh.devices.reshape(2, 2, 2, 4)
        mesh = Mesh(devices, ("section", "y", "core", "fsdp"))
    rep = ("y", "core") if relay else "rep"
    data = P("section", None, rep, "fsdp", None)
    vector, matrix = P("section", "fsdp"), P("section", "fsdp", None)
    params = (vector, matrix, matrix, vector, vector, vector, vector, vector, matrix)
    return jax.shard_map(
        relay_shards if relay else shards,
        mesh=mesh,
        in_specs=(data, *params),
        out_specs=(data, *params),
        check_vma=False,
    )
```

```python
import functools

import jax
import jax.numpy as jnp
from jax import lax
from jax.experimental import pallas as pl
from jax.experimental.pallas import tpu as pltpu
from jax.sharding import Mesh
from jax.sharding import PartitionSpec as P

D = 1536
HEADS = 48
HEAD_DIM = 64
STATE = 128
KERNEL = 4
INNER = 3072
CONV_CH = 3328
LANES = 128

OWN = INNER // 2
OWN_HEADS = HEADS // 2
OWN_CONV = OWN + 2 * STATE
X_AT = OWN
BC_AT = 2 * OWN
DT_AT = 2 * OWN + 2 * STATE
OWN_PROJ = DT_AT + 2 * LANES
PAIRS = OWN // LANES

EPSILON = 1e-05
EXACT_MATMUL = lax.Precision.HIGHEST
F32 = jnp.float32
BF16 = jnp.bfloat16
FORWARD_VMEM = 24
BACKWARD_VMEM = 30
JOIN_VMEM = 12


def dot(a, b):
    return lax.dot_general(a, b, (((1,), (0,)), ((), ())), preferred_element_type=F32)


def dot_nt(a, b):
    return lax.dot_general(a, b, (((1,), (1,)), ((), ())), preferred_element_type=F32)


def dot_tn(a, b):
    return lax.dot_general(a, b, (((0,), (0,)), ((), ())), preferred_element_type=F32)


def split(v, parts):
    pieces = []
    for _ in range(parts):
        piece = v.astype(BF16)
        pieces.append(piece)
        v = v - piece.astype(F32)
    return pieces


def sigmoid(v):
    return 0.5 * jnp.tanh(0.5 * v) + 0.5


def softplus(v):
    return jnp.maximum(v, 0.0) + jnp.log1p(jnp.exp(-jnp.abs(v)))


def step_sizes(dt_raw, headp):
    t = dt_raw.shape[0]
    biased = dt_raw + headp[0:1]
    dt = softplus(biased)
    rows = lax.broadcasted_iota(jnp.int32, (t, t), 0)
    cols = lax.broadcasted_iota(jnp.int32, (t, t), 1)
    tri = jnp.where(rows >= cols, 1.0, 0.0).astype(BF16)
    ld = sum(dot(tri, part) for part in split(dt * headp[1:2], 3))
    return dt, ld, biased


def at_head(v, pair):
    turned = pltpu.roll(v, lax.rem(LANES - 2 * pair, LANES), 1)
    return [jnp.broadcast_to(turned[:, i : i + 1], v.shape) for i in range(2)]


def decay_blocks(col, row, swapped):
    n = col.shape[0] // 2
    rows = lax.broadcasted_iota(jnp.int32, (n, n), 0)
    cols = lax.broadcasted_iota(jnp.int32, (n, n), 1)
    keep = rows <= cols if swapped else rows >= cols

    def block(i, j):
        down, along = col[i * n : (i + 1) * n], row[:, j * n : (j + 1) * n]
        differ = along - down if swapped else down - along
        return jnp.exp(jnp.where(keep, differ, -1e30) if i == j else differ)

    return block(0, 0), block(0, 1) if swapped else block(1, 0), block(1, 1)


def convolve(xw, sl, convp, t):
    out = convp[4:5, sl] + xw[5 : 5 + t, sl] * convp[0:1, sl]
    for k in range(1, KERNEL):
        out = out + xw[5 + k : 5 + k + t, sl] * convp[k : k + 1, sl]
    return out


def loop(count, step):
    def turn(i, _):
        step(i)
        return 0

    lax.fori_loop(0, count, turn, 0)


def by_blocks(total, step):
    loop(total // 512, lambda i: step(pl.ds(pl.multiple_of(i * 512, 512), 512)))


def aligned(value):
    return pl.multiple_of(value, LANES)


def fetch(source, target, sem):
    copy = pltpu.make_async_copy(source, target, sem)
    copy.start()
    return copy


def fetch_one_of(first, one, other, target, sem):
    @pl.when(first)
    def _():
        pltpu.make_async_copy(one, target, sem).start()

    @pl.when(jnp.logical_not(first))
    def _():
        pltpu.make_async_copy(other, target, sem).start()

    return pltpu.make_async_copy(other, target, sem)


def forward_kernel(row, sc, *refs):
    @pl.when(sc[row, VALID] == 1)
    def _():
        forward_chunk(row, sc, *refs)


def forward_chunk(
    row, sc, got_hbm, other_hbm, x_hbm, ng_ref, convp, headp, chanp, st_ref, tail_ref, win, wout, *rest
):
    p, h, st_out, tail_out = rest[-22:-18]
    h_hbm, n_hbm, pr_hbm, mx_hbm, q_hbm, st_hbm, tl_hbm = rest[-18:-11]
    normed, pr, mx, q, sti, tl, xw, ldt, ss, g_ref, sem = rest[-11:]
    t = h.shape[0]
    half = t // 2
    slot = sc[row, SLOT]
    first = sc[row, FIRST] == 1
    leading = sc[row, LEADING] == 1
    core = sc[row, CORE]

    @pl.when(leading)
    def _():
        fetch(x_hbm, h, sem.at[0]).wait()

    @pl.when(jnp.logical_not(leading))
    def _():
        mine = h.at[pl.ds(aligned(core * half), half)]
        theirs = h.at[pl.ds(aligned((1 - core) * half), half)]
        copies = fetch(got_hbm, mine, sem.at[0]), fetch(other_hbm, theirs, sem.at[1])
        for copy in copies:
            copy.wait()

    stores = [fetch(h, h_hbm.at[slot], sem.at[0])]
    hf = h[...].astype(F32)
    r = lax.rsqrt(jnp.mean(hf * hf, axis=1, keepdims=True) + EPSILON)
    normed[...] = (hf * r * ng_ref[...]).astype(BF16)
    stores.append(fetch(normed, n_hbm.at[slot], sem.at[1]))

    sti[...] = jnp.where(first, 0.0, st_ref[...])
    tl[...] = jnp.where(first, 0.0, tail_ref[...])
    stores.append(fetch(sti, st_hbm.at[slot], sem.at[2]))
    stores.append(fetch(tl, tl_hbm.at[slot], sem.at[3]))
    xw[0:8, :] = tl[...]

    def project(cols):
        pr[:, cols] = dot_nt(normed[...], win[cols, :]).astype(BF16)

    by_blocks(OWN_PROJ, project)
    stores.append(fetch(pr, pr_hbm.at[slot], sem.at[4]))
    tail_out[...] = pr[t - 8 : t, X_AT : X_AT + OWN_CONV].astype(F32)

    bc = pl.ds(OWN, 2 * STATE)
    xw[8 : 8 + t, OWN:OWN_CONV] = pr[:, BC_AT:DT_AT].astype(F32)
    conv_bc = convolve(xw, bc, convp, t)
    act = (conv_bc * sigmoid(conv_bc)).astype(BF16)
    b, c = act[:, :STATE], act[:, STATE:]
    g_ref[...] = dot_nt(c, b)
    b_turned = act[:, :STATE].astype(F32).T.astype(BF16)
    dt, ld, _ = step_sizes(pr[:, DT_AT : DT_AT + LANES].astype(F32), headp[...])
    ldt[...] = ld.T
    left = lax.broadcasted_iota(jnp.int32, (t, LANES), 1) < HEAD_DIM
    ss[...] = jnp.zeros_like(ss)

    def pair_step(pair):
        at = pl.multiple_of(pair * LANES, LANES)
        sl = pl.ds(at, LANES)
        xw[8 : 8 + t, sl] = pr[:, pl.ds(X_AT + at, LANES)].astype(F32)
        conv = convolve(xw, sl, convp, t)
        x = conv * sigmoid(conv)
        cols = at_head(ld, pair)
        u = jnp.where(left, *at_head(dt, pair)) * x
        ld_p = jnp.where(left, *cols)
        tops, bottoms, sides = [], [], []
        for i in range(2):
            u_i = jnp.where(left if i == 0 else jnp.logical_not(left), u, 0.0).astype(BF16)
            d00, d10, d11 = decay_blocks(cols[i], ldt[pl.ds(2 * pair + i, 1), :], False)
            m00 = (g_ref[:half, :half] * d00).astype(BF16)
            m10 = (g_ref[half:, :half] * d10).astype(BF16)
            m11 = (g_ref[half:, half:] * d11).astype(BF16)
            tops.append(m00)
            bottoms += [m10, m11]
            sides.append(u_i)
        top = dot(jnp.concatenate(tops, axis=1), jnp.concatenate([v[:half] for v in sides], axis=0))
        bottom = dot(jnp.concatenate(bottoms, axis=1), jnp.concatenate(sides, axis=0))
        eld = jnp.exp(ld_p)
        st = sti[:, sl]
        y = jnp.concatenate([top, bottom], axis=0) + eld * dot(c, st.astype(BF16))
        weighted = (u * jnp.exp(ld_p[t - 1 : t] - ld_p)).astype(BF16)
        st_out[:, sl] = eld[t - 1 : t] * st + dot(b_turned, weighted)
        mixed = y + chanp[0:1, sl] * x
        mx[:, sl] = mixed
        z = pr[:, sl].astype(F32)
        gated = mixed * (z * sigmoid(z))
        ss[...] += gated * gated
        q[:, sl] = (gated * chanp[1:2, sl]).astype(BF16)

    loop(PAIRS, pair_step)
    stores.append(fetch(mx, mx_hbm.at[slot], sem.at[5]))
    stores.append(fetch(q, q_hbm.at[slot], sem.at[6]))
    total = jnp.sum(ss[...], axis=1, keepdims=True)
    high = total.astype(BF16).astype(F32)
    lane = lax.broadcasted_iota(jnp.int32, (t, LANES), 1)
    p[:, D:] = jnp.where(lane == 0, high, jnp.where(lane == 1, total - high, 0.0)).astype(BF16)
    def output(cols):
        p[:, cols] = dot(q[...], wout[:, cols]).astype(BF16)

    by_blocks(D, output)
    for store in stores:
        store.wait()


def backward_kernel(row, sc, *refs):
    acc_ref, acc_out = refs[17], refs[-21]

    @pl.when(sc[row, VALID] == 1)
    def _():
        backward_chunk(row, sc, *refs)

    @pl.when(sc[row, VALID] == 0)
    def _():
        acc_out[...] = acc_ref[...]


def backward_chunk(
    row,
    sc,
    arrived_hbm,
    other_hbm,
    cot_hbm,
    h_hbm,
    n_hbm,
    pr_hbm,
    mx_hbm,
    st_hbm,
    tl_hbm,
    y_hbm,
    ri_hbm,
    convp,
    headp,
    chanp,
    dst_ref,
    dc_ref,
    val_ref,
    acc_ref,
    win,
    wout,
    *rest,
):
    gn, g_ref, h_out, dst_out, dc_out, val_out, acc_out, gp_hbm, gs_hbm = rest[-27:-18]
    pr, mx, st_ref, tl, y_ref, ri, gp, gs, normed = rest[-18:-9]
    xw, dw, ldt, gw, gt, dgt, dci, dbi, sem = rest[-9:]
    t = g_ref.shape[0]
    half = t // 2
    slot = sc[row, SLOT]
    last = sc[row, FIRST] == 1
    leading = sc[row, LEADING] == 1
    core = sc[row, CORE]
    mine = g_ref.at[pl.ds(aligned(core * half), half)]
    theirs = g_ref.at[pl.ds(aligned((1 - core) * half), half)]

    @pl.when(leading)
    def _():
        pltpu.make_async_copy(arrived_hbm, mine, sem.at[0]).start()
        pltpu.make_async_copy(other_hbm, theirs, sem.at[10]).start()

    @pl.when(jnp.logical_not(leading))
    def _():
        pltpu.make_async_copy(cot_hbm, g_ref, sem.at[0]).start()

    y_copy = fetch(y_hbm.at[slot], y_ref, sem.at[1])
    ri_copy = fetch(ri_hbm.at[slot], ri, sem.at[2])
    pr_copy = fetch(pr_hbm.at[slot], pr, sem.at[3])
    tl_copy = fetch(tl_hbm.at[slot], tl, sem.at[4])
    mx_copy = fetch(mx_hbm.at[slot], mx, sem.at[5])
    st_copy = fetch(st_hbm.at[slot], st_ref, sem.at[6])

    acc_out[...] = acc_ref[...]
    dw[t : t + 8, :] = jnp.where(last, 0.0, dc_ref[...])
    dgt[...] = jnp.zeros_like(dgt)
    dci[...] = jnp.zeros_like(dci)
    dbi[...] = jnp.zeros_like(dbi)

    @pl.when(leading)
    def _():
        pltpu.make_async_copy(arrived_hbm, mine, sem.at[0]).wait()
        pltpu.make_async_copy(other_hbm, theirs, sem.at[10]).wait()

    @pl.when(jnp.logical_not(leading))
    def _():
        pltpu.make_async_copy(cot_hbm, g_ref, sem.at[0]).wait()

    def output_back(cols):
        gw[:, cols] = dot_nt(g_ref[...], wout[cols, :])

    by_blocks(OWN, output_back)
    y_copy.wait()
    ri_copy.wait()
    rinv = ri[:, 0:1]
    mean = jnp.sum(g_ref[...].astype(F32) * y_ref[...].astype(F32), axis=1, keepdims=True)
    lean = rinv * rinv * (mean * (1.0 / INNER))
    gs[...] = (g_ref[...].astype(F32) * rinv).astype(BF16)
    gs_store = fetch(gs, gs_hbm.at[sc[row, WRITE]], sem.at[7])
    pr_copy.wait()
    tl_copy.wait()
    xw[0:8, :] = tl[...]

    bc = pl.ds(OWN, 2 * STATE)
    xw[8 : 8 + t, OWN:OWN_CONV] = pr[:, BC_AT:DT_AT].astype(F32)
    conv_bc = convolve(xw, bc, convp, t)
    sig_bc = sigmoid(conv_bc)
    act = (conv_bc * sig_bc).astype(BF16)
    b, c = act[:, :STATE], act[:, STATE:]
    c_turned = c.astype(F32).T.astype(BF16)
    gt[...] = dot_nt(b, c)
    dt, ld, biased = step_sizes(pr[:, DT_AT : DT_AT + LANES].astype(F32), headp[...])
    ldt[...] = ld.T
    left = lax.broadcasted_iota(jnp.int32, (t, LANES), 1) < HEAD_DIM

    def add(line, sl, v):
        acc_out[line : line + 1, sl] += v

    def conv_back(dact, conv, sig, sl):
        dconv = dact * (sig * (1.0 + conv * (1.0 - sig)))
        dw[0:t, sl] = dconv
        add(4, sl, jnp.sum(dconv, axis=0, keepdims=True))
        for k in range(KERNEL):
            add(k, sl, jnp.sum(dconv * xw[5 + k : 5 + k + t, sl], axis=0, keepdims=True))
        dx = dconv * convp[KERNEL - 1 : KERNEL, sl]
        for k in range(KERNEL - 1):
            ahead = KERNEL - 1 - k
            dx = dx + dw[ahead : ahead + t, sl] * convp[k : k + 1, sl]
        return dx.astype(BF16)

    lane_head = lax.rem(lax.broadcasted_iota(jnp.int32, (2 * LANES, LANES), 0), LANES) // HEAD_DIM
    head_lane = lax.broadcasted_iota(jnp.int32, (2 * LANES, LANES), 1)
    mx_copy.wait()
    st_copy.wait()
    h_copy = fetch(h_hbm.at[slot], h_out, sem.at[8])
    n_copy = fetch(n_hbm.at[slot], normed, sem.at[9])

    def pair_step(pair, carry):
        ddt, dld, dval = carry
        at = pl.multiple_of(pair * LANES, LANES)
        sl = pl.ds(at, LANES)
        xsl = pl.ds(X_AT + at, LANES)
        xw[8 : 8 + t, sl] = pr[:, xsl].astype(F32)
        conv = convolve(xw, sl, convp, t)
        sig = sigmoid(conv)
        x = conv * sig
        z = pr[:, sl].astype(F32)
        sig_z = sigmoid(z)
        s = z * sig_z
        mixed = mx[:, sl]
        gated = mixed * s
        scaled = gw[:, sl] * rinv
        add(6, sl, jnp.sum(scaled * gated, axis=0, keepdims=True))
        dgated = chanp[1:2, sl] * scaled - gated * lean
        dy = dgated * s
        gp[:, sl] = (dgated * mixed * (sig_z * (1.0 + z * (1.0 - sig_z)))).astype(BF16)
        skip = chanp[0:1, sl]
        add(5, sl, jnp.sum(dy * x, axis=0, keepdims=True))
        y = mixed - skip * x

        cols = at_head(ld, pair)
        ld_p = jnp.where(left, *cols)
        eld = jnp.exp(ld_p)
        wend = jnp.exp(ld_p[t - 1 : t] - ld_p)
        dt_p = jnp.where(left, *at_head(dt, pair))
        u = dt_p * x
        u_low = u.astype(BF16)
        dy_low = dy.astype(BF16)
        dst = jnp.where(last, 0.0, dst_ref[:, sl])
        dst_low = dst.astype(BF16)
        top = jnp.zeros((half, LANES), F32)
        bottom = top
        for i in range(2):
            side = left if i == 0 else jnp.logical_not(left)
            d00, d01, d11 = decay_blocks(cols[i], ldt[pl.ds(2 * pair + i, 1), :], True)
            m00 = (gt[:half, :half] * d00).astype(BF16)
            m01 = (gt[:half, half:] * d01).astype(BF16)
            m11 = (gt[half:, half:] * d11).astype(BF16)
            dy_i = jnp.where(side, dy, 0.0).astype(BF16)
            top = top + dot(jnp.concatenate([m00, m01], axis=1), dy_i)
            bottom = bottom + dot(m11, dy_i[half:])
            u_i = jnp.where(side, u, 0.0).astype(BF16)
            dm = dot_nt(u_i[:half], dy_low)
            dgt[:half, :half] += dm[:, :half] * d00
            dgt[:half, half:] += dm[:, half:] * d01
            dgt[half:, half:] += dot_nt(u_i[half:], dy_low[half:]) * d11
        du = jnp.concatenate([top, bottom], axis=0) + wend * dot(b, dst_low)
        st = st_ref[:, sl]
        dyl = (eld * dy).astype(BF16)
        dst_new = eld[t - 1 : t] * dst + dot(c_turned, dyl)
        dst_out[:, sl] = dst_new
        val_out[:, sl] = jnp.broadcast_to(
            jnp.sum(dst_new * st, axis=0, keepdims=True), (8, LANES)
        )
        dci[...] += dot_nt(dyl, st.astype(BF16))
        dbi[...] += dot_nt((wend * u).astype(BF16), dst_low)

        pick = jnp.where(lane_head + 2 * pair == head_lane, 1.0, 0.0).astype(BF16)


        def by_head(v):
            return dot(jnp.concatenate(split(v, 2), axis=1), pick)

        ddt = ddt + by_head(du * x)
        dld = dld + by_head(dy_low.astype(F32) * y - u_low.astype(F32) * du)
        dval = dval + by_head(jnp.where(last, 0.0, val_ref[:, sl]))
        gp[:, xsl] = conv_back(dt_p * du + skip * dy, conv, sig, sl)
        return ddt, dld, dval

    zero = jnp.zeros((t, LANES), F32)
    ddt, dld, dval = lax.fori_loop(
        0,
        PAIRS,
        pair_step,
        (zero, zero, jnp.zeros((8, LANES), F32)),
    )

    dgt_low = dgt[...].astype(BF16)
    db = dbi[...] + dot(dgt_low, c)
    dc = dci[...] + dot_tn(dgt_low, b)
    gp[:, BC_AT:DT_AT] = conv_back(jnp.concatenate([db, dc], axis=1), conv_bc, sig_bc, bc)

    rows = lax.broadcasted_iota(jnp.int32, (t, t), 0)
    cols = lax.broadcasted_iota(jnp.int32, (t, t), 1)
    upper = jnp.where(rows <= cols, 1.0, 0.0).astype(BF16)
    da = sum(dot(upper, part) for part in split(dld, 3)) + dval[0:1]
    rate = headp[1:2]
    head = pl.ds(0, LANES)
    add(8, head, jnp.sum(da * rate * dt, axis=0, keepdims=True))
    ddt_raw = (ddt + rate * da) * sigmoid(biased)
    add(7, head, jnp.sum(ddt_raw, axis=0, keepdims=True))
    gp[:, DT_AT : DT_AT + LANES] = ddt_raw.astype(BF16)
    gp[:, DT_AT + LANES :] = jnp.zeros((t, LANES), BF16)
    gp_store = fetch(gp, gp_hbm.at[sc[row, WRITE]], sem.at[0])
    dc_out[...] = dw[0:8, :]
    n_copy.wait()

    def project_back(cols):
        values = dot(gp[...], win[:, cols])
        gn[:, cols] = values.astype(BF16)
        add(9, cols, jnp.sum(values * normed[:, cols].astype(F32), axis=0, keepdims=True))

    by_blocks(D, project_back)
    gp_store.wait()
    gs_store.wait()
    h_copy.wait()


def forward_join_kernel(row, sc, own_ref, other_ref, h_ref, *rest):
    out, y_hbm, ri_hbm, e_hbm, y_v, ri_v, low_v, sem = rest[-8:]
    half = out.shape[0]

    @pl.when(sc[row, VALID] == 1)
    def _():
        copies = []
        for k in range(2):
            rows = slice(k * half, (k + 1) * half)
            total = own_ref[rows].astype(F32) + other_ref[rows].astype(F32)
            square = total[:, D : D + 1] + total[:, D + 1 : D + 2]
            rinv = lax.rsqrt(square * (1.0 / INNER) + EPSILON)
            y = total[:, :D] * rinv
            y_v[rows] = y.astype(BF16)
            ri_v[rows] = jnp.broadcast_to(rinv, (half, LANES))
            low_v[rows] = (h_ref[rows].astype(F32) + y).astype(BF16)
            pieces = ((y_v, y_hbm, SLOT), (ri_v, ri_hbm, SLOT), (low_v, e_hbm, EDGE))
            for near_ref, far_ref, which in pieces:
                target = far_ref.at[sc[row, which], pl.ds(k * half, half)]
                copies.append(fetch(near_ref.at[pl.ds(k * half, half)], target, sem.at[len(copies)]))
        out[...] = low_v[pl.ds(aligned(sc[row, CORE] * half), half), :]
        for copy in copies:
            copy.wait()


def backward_join_kernel(row, sc, own_ref, other_ref, h_ref, g_ref, ng_ref, *rest):
    out, e_hbm, low_v, sem = rest[-4:]
    half = out.shape[0]

    @pl.when(sc[row, VALID] == 1)
    def _():
        copies = []
        for k in range(2):
            rows = slice(k * half, (k + 1) * half)
            gn = own_ref[rows].astype(F32) + other_ref[rows].astype(F32)
            h = h_ref[rows].astype(F32)
            r = lax.rsqrt(jnp.mean(h * h, axis=1, keepdims=True) + EPSILON)
            t = gn * ng_ref[...]
            m = jnp.mean(h * t, axis=1, keepdims=True)
            low_v[rows] = (g_ref[rows].astype(F32) + r * (t - h * (r * r * m))).astype(BF16)
            target = e_hbm.at[sc[row, EDGE], pl.ds(k * half, half)]
            copies.append(fetch(low_v.at[pl.ds(k * half, half)], target, sem.at[k]))
        out[...] = low_v[pl.ds(aligned(sc[row, CORE] * half), half), :]
        for copy in copies:
            copy.wait()


def pick_kernel(first, sc, stack_hbm, out, sem):
    fetch(stack_hbm.at[first + sc[0, CORE]], out, sem.at[0]).wait()


ANY = pl.BlockSpec(memory_space=pl.ANY)
NEAR = pl.BlockSpec(memory_space=pltpu.VMEM)
SLOT, LEADING, FIRST, VALID, WRITE, EDGE, CORE = range(7)
LITTLE = pl.CostEstimate(flops=1 << 20, bytes_accessed=1 << 16, transcendentals=0)


def near(value):
    return pltpu.with_memory_space_constraint(value, pltpu.VMEM)


def away(value):
    return pltpu.with_memory_space_constraint(value, pltpu.HBM)


def chunk_call(kernel, table, free, far, close, close_outs, buffers, scratch, limit, name):
    inputs = [table, *free, *(away(v) for v in far), *(near(v) for v in close)]
    in_specs = [pl.BlockSpec(memory_space=pltpu.SMEM)]
    in_specs += [ANY] * (len(free) + len(far)) + [NEAR] * len(close)
    outs = [pltpu.VMEM(*o) for o in close_outs]
    out_specs = [NEAR] * len(close_outs)
    aliases = {}
    for held, shape, dtype in buffers:
        if held is not None:
            aliases[len(inputs)] = len(outs)
            inputs.append(away(held))
            in_specs.append(ANY)
        outs.append(pltpu.HBM(shape, dtype))
        out_specs.append(ANY)
    results = pl.pallas_call(
        kernel,
        in_specs=in_specs,
        out_specs=out_specs,
        out_shape=outs,
        scratch_shapes=scratch,
        input_output_aliases=aliases,
        compiler_params=pltpu.CompilerParams(vmem_limit_bytes=limit << 20),
        cost_estimate=LITTLE,
        name=name,
    )(*inputs)
    return tuple(results[: len(close_outs)]), tuple(results[len(close_outs) :])


def forward_call(table, row, slots, x, arrived, params, carry, held):
    t = x.shape[0]
    held = held or (None,) * 7
    kinds = (
        ((t, D), BF16),
        ((t, D), BF16),
        ((t, OWN_PROJ), BF16),
        ((t, OWN), F32),
        ((t, OWN), BF16),
        ((STATE, OWN), F32),
        ((8, OWN_CONV), F32),
    )
    gain, convp, headp, chanp, win, wout = params
    outs, held = chunk_call(
        functools.partial(forward_kernel, row),
        table,
        (*arrived, x),
        (),
        (gain, convp, headp, chanp, *carry, win, wout),
        (((t, D + LANES), BF16), kinds[0], kinds[5], kinds[6]),
        [(b, (slots,) + k, d) for b, (k, d) in zip(held, kinds)],
        [pltpu.VMEM(*k) for k in kinds[1:]]
        + [
            pltpu.VMEM((t + 8, OWN_CONV), F32),
            pltpu.VMEM((LANES, t), F32),
            pltpu.VMEM((t, LANES), F32),
            pltpu.VMEM((t, t), F32),
            pltpu.SemaphoreType.DMA((8,)),
        ],
        FORWARD_VMEM,
        "forward_chunk",
    )
    return outs[0], outs[1], outs[2:], held


def backward_call(table, row, slots, cot, arrived, saved, params, carry, held):
    t = cot.shape[0]
    held = held or (None, None)
    _, convp, headp, chanp, win, wout = params
    wide, projected = ((t, D), BF16), ((t, OWN_PROJ), BF16)
    outs, held = chunk_call(
        functools.partial(backward_kernel, row),
        table,
        (*arrived, cot),
        saved,
        (convp, headp, chanp, *carry, win, wout),
        [wide] * 3 + [(v.shape, v.dtype) for v in carry],
        [(held[0], (slots, t, OWN_PROJ), BF16), (held[1], (slots, t, D), BF16)],
        [
            pltpu.VMEM(*projected),
            pltpu.VMEM((t, OWN), F32),
            pltpu.VMEM((STATE, OWN), F32),
            pltpu.VMEM((8, OWN_CONV), F32),
            pltpu.VMEM(*wide),
            pltpu.VMEM((t, LANES), F32),
            pltpu.VMEM(*projected),
            pltpu.VMEM(*wide),
            pltpu.VMEM(*wide),
            pltpu.VMEM((t + 8, OWN_CONV), F32),
            pltpu.VMEM((t + 8, OWN_CONV), F32),
            pltpu.VMEM((LANES, t), F32),
            pltpu.VMEM((t, OWN), F32),
            pltpu.VMEM((t, t), F32),
            pltpu.VMEM((t, t), F32),
            pltpu.VMEM((t, STATE), F32),
            pltpu.VMEM((t, STATE), F32),
            pltpu.SemaphoreType.DMA((11,)),
        ],
        BACKWARD_VMEM,
        "backward_chunk",
    )
    return outs[:3], outs[3:], held


def forward_join(table, row, slots, own, other, h, held):
    t = h.shape[0]
    held = held or (None,) * 3
    wide, thin = ((t, D), BF16), ((t, LANES), F32)
    outs, held = chunk_call(
        functools.partial(forward_join_kernel, row),
        table,
        (),
        (),
        (own, other, h),
        [((t // 2, D), BF16)],
        [(b, (slots,) + k, d) for b, (k, d) in zip(held, (wide, thin, wide))],
        [pltpu.VMEM(*k) for k in (wide, thin, wide)] + [pltpu.SemaphoreType.DMA((6,))],
        JOIN_VMEM,
        "forward_join",
    )
    return outs[0], held


def backward_join(table, row, own, other, h, g, gain, edge_held):
    slots, t, _ = edge_held.shape
    outs, held = chunk_call(
        functools.partial(backward_join_kernel, row),
        table,
        (),
        (),
        (own, other, h, g, gain),
        [((t // 2, D), BF16)],
        [(edge_held, (slots, t, D), BF16)],
        [pltpu.VMEM((t, D), BF16), pltpu.SemaphoreType.DMA((2,))],
        JOIN_VMEM,
        "backward_join",
    )
    return outs[0], held[0]


def pick(table, stack, first):
    outs, _ = chunk_call(
        functools.partial(pick_kernel, first),
        table,
        (),
        (stack,),
        (),
        [(stack.shape[1:], stack.dtype)],
        [],
        [pltpu.SemaphoreType.DMA((1,))],
        JOIN_VMEM,
        "pick",
    )
    return outs[0]


def own_of(values, core):
    lead, width = values.shape[:-1], values.shape[-1]
    blocks = values.reshape(lead + (4, 2, width // 8))
    return lax.dynamic_index_in_dim(blocks, core, len(lead) + 1, False).reshape(
        lead + (width // 2,)
    )


def woven(halves):
    width = halves.shape[-1]
    lead = halves.shape[1:-1]
    blocks = halves.reshape((2,) + lead + (4, width // 4))
    return jnp.moveaxis(blocks, 0, -2).reshape(lead + (2 * width,))


def small_params(norm_gain, conv_weight, conv_bias, dt_bias, a_log, skip_gain, gate_gain, core):
    own = functools.partial(own_of, core=core)
    taps = jnp.concatenate([conv_weight.T, conv_bias[None]], axis=0).astype(F32)
    taps = jnp.concatenate([own(taps[:, :INNER]), taps[:, INNER:]], axis=1)
    convp = jnp.pad(taps, ((0, 3), (0, 0)))
    heads = jnp.stack([own(dt_bias.astype(F32)), -jnp.exp(own(a_log.astype(F32)))])
    headp = jnp.pad(heads, ((0, 6), (0, LANES - OWN_HEADS)))
    skip = jnp.repeat(own(skip_gain.astype(F32)), HEAD_DIM)
    chanp = jnp.pad(jnp.stack([skip, own(gate_gain.astype(F32))]), ((0, 6), (0, 0)))
    return norm_gain.astype(F32)[None], convp, headp, chanp


def own_steps(weight, core):
    own = own_of(weight[INNER + CONV_CH :].T, core).T
    return jnp.pad(own, ((0, 2 * LANES - OWN_HEADS), (0, 0)))


HALF = OWN // 2
BLOCK = HALF // 2
PACKED_ROWS = HALF + HALF + 2 * STATE + 2 * BLOCK
PARTS = (
    ("in", HALF, X_AT, HALF),
    ("in", HALF, 0, HALF),
    ("in", 2 * STATE, BC_AT, 2 * STATE),
    ("out", BLOCK, 0, HALF),
    ("out", BLOCK, BLOCK, HALF),
)


def ring_place(position, count):
    back = position >= count
    return jnp.where(back, 1, 0), jnp.where(back, 2 * count - 1 - position, position)


def ring_route(count, step):
    def index(position):
        return position if position < count else count + (2 * count - 1 - position)

    size = 2 * count
    return [(index(p), index((p + step) % size)) for p in range(size)]


HALF_ROWS = PACKED_ROWS // 2


def cut(at, rows):
    spans = []
    for i in range(2):
        a, b = max(at, i * HALF_ROWS), min(at + rows, (i + 1) * HALF_ROWS)
        if a < b:
            spans.append((i, a - i * HALF_ROWS, a - at, b - a))
    return spans


def pack_kernel(sc, w, steps, o, own_a, own_b, rest_a, rest_b, sem):
    core, side = sc[0], sc[1]
    copies = []
    for targets, y in (((own_a, own_b), side), ((rest_a, rest_b), 1 - side)):
        at = 0
        for base in (INNER, 0):
            for k in range(2):
                first = base + (2 * y + k) * HALF + core * BLOCK
                for i, to, off, rows in cut(at, BLOCK):
                    source = w.at[pl.ds(aligned(first + off), rows)]
                    copies.append(fetch(source, targets[i].at[pl.ds(to, rows)], sem.at[len(copies)]))
                at += BLOCK
        bc = w.at[pl.ds(2 * INNER, 2 * STATE)]
        ((i, to, _, rows),) = cut(at, 2 * STATE)
        span = targets[i].at[pl.ds(to, rows)]
        copies.append(fetch_one_of(y == 0, bc, steps, span, sem.at[len(copies)]))
        at += 2 * STATE
        for k in range(2):
            ((i, to, _, rows),) = cut(at, BLOCK)
            cols = pl.ds(aligned(y * HALF + k * BLOCK), BLOCK)
            source = o.at[pl.ds(aligned(core * BLOCK), BLOCK), cols]
            copies.append(fetch(source, targets[i].at[pl.ds(to, rows)], sem.at[len(copies)]))
            at += BLOCK
    for copy in copies:
        copy.wait()


def pack_weights(scalars, w, steps, o):
    return pl.pallas_call(
        pack_kernel,
        in_specs=[pl.BlockSpec(memory_space=pltpu.SMEM), ANY, ANY, ANY],
        out_specs=[NEAR, NEAR, NEAR, NEAR],
        out_shape=[pltpu.VMEM((HALF_ROWS, BLOCK), BF16)] * 4,
        scratch_shapes=[pltpu.SemaphoreType.DMA((16,))],
        compiler_params=pltpu.CompilerParams(vmem_limit_bytes=4 << 20),
        cost_estimate=LITTLE,
        name="pack_weights",
    )(scalars, away(w), steps, away(o))


def put_block(sc, halves, z, y, win, wout, sem, start):
    lanes = pl.ds(aligned(z * BLOCK), BLOCK)
    copies, at = [], 0
    for matrix, rows, first, step in PARTS:
        for i, to, off, count in cut(at, rows):
            if matrix == "in":
                target = win.at[pl.ds(aligned(first + y * step + off), count), lanes]
            else:
                target = wout.at[lanes, pl.ds(aligned(first + y * step), BLOCK)]
            source = halves[i].at[pl.ds(to, count)]
            copies.append(fetch(source, target, sem.at[start + len(copies)]))
        at += rows
    return copies


def place_kernel(which, sc, *refs):
    win, wout, sem = refs[-3:]
    blocks = [refs[2 * i : 2 * i + 2] for i in range(8 if which == 0 else 4)]
    side, place = sc[1], sc[2]
    inner = jnp.logical_and(place > 0, place < 3)

    def put(number, block, z, y):
        return put_block(sc, blocks[block], z, y, win, wout, sem, 8 * number)

    always = []
    if which == 0:
        beside = place + 1 - 2 * lax.rem(place, 2)
        always += put(0, 0, place, side) + put(1, 1, place, 1 - side)
        always += put(2, 2, beside, side) + put(3, 3, beside, 1 - side)
        from_z, first = jnp.where(inner, 3 - place, jnp.where(place == 0, 2, 1)), 4
    else:
        from_z, first = jnp.where(place < 2, 3, 0), 0

    def rest(block):
        copies = put(4, block, from_z, side) + put(5, block + 1, from_z, 1 - side)
        for copy in copies:
            copy.wait()

    @pl.when(inner)
    def _():
        rest(first)

    @pl.when(jnp.logical_not(inner))
    def _():
        rest(first + 2)

    for copy in always:
        copy.wait()


def place_weights(here, blocks, held):
    inputs = [here] + [away(half) for block in blocks for half in block]
    in_specs = [pl.BlockSpec(memory_space=pltpu.SMEM)] + [ANY] * (len(inputs) - 1)
    aliases = {}
    if held is not None:
        aliases = {len(inputs): 0, len(inputs) + 1: 1}
        inputs += [near(v) for v in held]
        in_specs += [NEAR, NEAR]
    return pl.pallas_call(
        functools.partial(place_kernel, 0 if held is None else 1),
        in_specs=in_specs,
        out_specs=[NEAR, NEAR],
        out_shape=[pltpu.VMEM((OWN_PROJ, D), BF16), pltpu.VMEM((OWN, D), BF16)],
        scratch_shapes=[pltpu.SemaphoreType.DMA((48,))],
        input_output_aliases=aliases,
        compiler_params=pltpu.CompilerParams(vmem_limit_bytes=4 << 20),
        cost_estimate=LITTLE,
        name="place_weights",
    )(*inputs)


def line_gather(own, beside):
    def along(value, hops):
        path = [(y * 4 + a, y * 4 + b) for y in range(2) for a, b in hops]
        return lax.ppermute(value, ("y", "fsdp"), path)

    def across(value, places):
        path = [(y * 4 + z, (1 - y) * 4 + z) for y in range(2) for z in places]
        return lax.ppermute(value, ("y", "fsdp"), path)

    pair, middle, outward = [(0, 1), (1, 0), (2, 3), (3, 2)], [(1, 2), (2, 1)], [(1, 0), (2, 3)]
    inner, outer = (1, 2), (0, 3)
    barrier = lax.optimization_barrier
    a, b = own
    near_a, in2_a = along(a, pair), along(a, middle)
    near_a, in2_a, b = barrier((near_a, in2_a, b))
    near_b, in2_b, near_ya = along(b, pair), along(b, middle), across(near_a, range(4))
    near_a, in2_a, near_b, in2_b, near_ya, *beside = barrier(
        (near_a, in2_a, near_b, in2_b, near_ya, *beside)
    )
    out2_a, in3_a, near_yb = along(in2_a, outward), along(near_a, middle), across(near_b, range(4))
    out2_a, in3_a, near_yb, in2_a, near_b, in2_b = barrier(
        (out2_a, in3_a, near_yb, in2_a, near_b, in2_b)
    )
    out2_b, in3_b = along(in2_b, outward), along(near_b, middle)
    out2_ya, in2_ya = across(out2_a, outer), across(in2_a, inner)
    out2_b, in3_b, out2_ya, in2_ya, in3_a, in2_b = barrier(
        (out2_b, in3_b, out2_ya, in2_ya, in3_a, in2_b)
    )
    ready = in2_ya
    out3_a = along(in3_a, outward)
    out2_yb, in2_yb = across(out2_b, outer), across(in2_b, inner)
    out3_a, out2_yb, in2_yb, in3_a, in3_b = barrier((out3_a, out2_yb, in2_yb, in3_a, in3_b))
    out3_b = along(in3_b, outward)
    out3_ya, in3_ya = across(out3_a, outer), across(in3_a, inner)
    out3_b, out3_ya, in3_ya, in3_b = barrier((out3_b, out3_ya, in3_ya, in3_b))
    out3_yb, in3_yb = across(out3_b, outer), across(in3_b, inner)
    blocks = [
        (near_a, near_b),
        (near_ya, near_yb),
        (in2_a, in2_b),
        (in2_ya, in2_yb),
        (out2_a, out2_b),
        (out2_ya, out2_yb),
        (in3_a, in3_b),
        (in3_ya, in3_yb),
        (out3_a, out3_b),
        (out3_ya, out3_yb),
    ]
    return blocks, beside, ready


GROUPS = (
    (1, (HALF, X_AT, HALF), (LANES, BC_AT, 2 * STATE)),
    (-1, (HALF, 0, HALF), (LANES, BC_AT + LANES, 2 * STATE)),
)


SMALL_ROWS = 16
IN_ROWS = HALF + LANES
GROUP_ROWS = IN_ROWS + BLOCK


def block_grad_kernel(row, sc, normed_ref, q_ref, gs_ref, *refs):
    out = refs[-1]
    chunks = normed_ref.shape[0]
    at = 0
    for ref in refs[:2]:
        width = ref.shape[2]
        value = sum(dot_tn(ref[k], normed_ref[k]) for k in range(chunks))
        out[at : at + width, :] = value.astype(BF16)
        at += width
    out[at:, :] = sum(dot_tn(q_ref[k], gs_ref[k]) for k in range(chunks)).astype(BF16)
    if len(refs) > 3:

        @pl.when(sc[row, 0] == 1)
        def _():
            out[HALF : HALF + SMALL_ROWS, :] = refs[2][0].astype(BF16)


def block_grad(table, row, group, normed_held, grads_held, q_held, gs_held, small):
    slots, t, _ = normed_held.shape
    number, (_, *parts) = group, GROUPS[group]

    def block(width, index):
        return pl.BlockSpec((slots - 1, t, width), lambda i, s: (0, 0, index(s)))

    in_specs = [
        block(BLOCK, lambda s: s[row, 1]),
        block(BLOCK, lambda s: s[row, 1]),
        block(BLOCK, lambda s: 2 * s[row, 0] + number),
    ]
    for width, first, step in parts:

        def index(s, width=width, first=first, step=step):
            return first // width + s[row, 0] * (step // width)

        in_specs.append(block(width, index))
    extra = []
    if number == 1:
        extra = [small]
        in_specs.append(pl.BlockSpec((1, SMALL_ROWS, BLOCK), lambda i, s: (s[row, 1], 0, 0)))
    return pl.pallas_call(
        functools.partial(block_grad_kernel, row),
        grid_spec=pltpu.PrefetchScalarGridSpec(
            num_scalar_prefetch=1,
            grid=(1,),
            in_specs=in_specs,
            out_specs=pl.BlockSpec((GROUP_ROWS, BLOCK), lambda i, s: (0, 0)),
        ),
        out_shape=jax.ShapeDtypeStruct((GROUP_ROWS, BLOCK), BF16),
        compiler_params=pltpu.CompilerParams(vmem_limit_bytes=24 << 20),
        cost_estimate=LITTLE,
        name="block_grad",
    )(
        table,
        away(normed_held),
        away(q_held),
        away(gs_held),
        *([away(grads_held)] * len(parts)),
        *extra,
    )


def grads_kernel(sc, *refs):
    in_hbm, out_hbm, small_out, in_v, out_v, sem = refs[-6:]
    core, side = sc[0], sc[1]

    def block(i, c, y, rows):
        own, across, other, far = refs[4 * i : 4 * i + 4]
        here = jnp.where(side == y, own[rows], across[rows])
        there = jnp.where(side == y, other[rows], far[rows])
        return jnp.where(core == c, here, there).astype(F32)

    copies = []

    def store(values, near_ref, far_ref, at):
        near_ref[at : at + values.shape[0]] = values
        span = pl.ds(at, values.shape[0])
        copies.append(fetch(near_ref.at[span], far_ref.at[span], sem.at[len(copies)]))

    for i, base in ((0, INNER), (1, 0)):
        for c in range(2):
            for y in range(2):
                for k in range(2):
                    rows = slice(k * BLOCK, (k + 1) * BLOCK)
                    store(block(i, c, y, rows), in_v, in_hbm, base + (2 * y + k) * HALF + c * BLOCK)
    rows = slice(HALF, HALF + STATE)
    for i in range(2):
        store(block(i, 0, 0, rows) + block(i, 1, 0, rows), in_v, in_hbm, 2 * INNER + i * STATE)
    steps = [block(0, c, 1, slice(HALF, HALF + 32)) for c in range(2)]
    steps = [steps[c][z * 6 : z * 6 + 6] for z in range(4) for c in range(2)]
    store(jnp.concatenate(steps, axis=0), in_v, in_hbm, INNER + CONV_CH)
    rows = slice(HALF, HALF + SMALL_ROWS)
    small_out[...] = block(1, 0, 1, rows) + block(1, 1, 1, rows)
    rows = slice(IN_ROWS, GROUP_ROWS)
    for c in range(2):
        values = [block(i, c, y, rows) for y in range(2) for i in range(2)]
        store(jnp.concatenate(values, axis=1), out_v, out_hbm, c * BLOCK)
    for copy in copies:
        copy.wait()


def join_grads(scalars, parts):
    arrays = [near(a) for part in parts for a in part]
    height = INNER + CONV_CH + HEADS
    shapes = ((height, BLOCK), F32), ((2 * BLOCK, D), F32)
    return pl.pallas_call(
        grads_kernel,
        in_specs=[pl.BlockSpec(memory_space=pltpu.SMEM)] + [NEAR] * len(arrays),
        out_specs=[ANY, ANY, NEAR],
        out_shape=[pltpu.HBM(*k) for k in shapes] + [pltpu.VMEM((SMALL_ROWS, BLOCK), F32)],
        scratch_shapes=[pltpu.VMEM(*k) for k in shapes] + [pltpu.SemaphoreType.DMA((24,))],
        compiler_params=pltpu.CompilerParams(vmem_limit_bytes=28 << 20),
        cost_estimate=LITTLE,
        name="join_grads",
    )(scalars, *arrays)


def swap(value, axis):
    return lax.ppermute(value, axis, [(0, 1), (1, 0)])


def sent_along(value, axis):
    size = lax.axis_size(axis)
    routes = [[(i, (i + k) % size) for i in range(size)] for k in range(1, size)]
    return [lax.ppermute(value, axis, path) for path in routes]


def in_order(value, others, axis):
    size, place = len(others) + 1, lax.axis_index(axis)
    ring = jnp.stack([*others[::-1], value] * 2)
    return lax.dynamic_slice_in_dim(ring, (size - 1 - place) % size, size, 0)


LAG = 2


def relay_shards(
    ends,
    norm_gain,
    input_weight,
    conv_weight,
    conv_bias,
    dt_bias,
    a_log,
    skip_gain,
    gate_gain,
    output_weight,
):
    core = lax.axis_index("core")
    place = lax.axis_index("fsdp")
    side = lax.axis_index("y")
    section = lax.axis_index("section")
    leading = (section == 0).astype(jnp.int32)
    local = ends[0][:, 0]
    t = local.shape[1]
    chunks = lax.axis_size("fsdp")
    micro = place // 2

    small = [norm_gain[0], conv_weight[0].reshape(-1), conv_bias[0], dt_bias[0], a_log[0]]
    small += [skip_gain[0], gate_gain[0]]
    packed = jnp.concatenate(small)
    others = sent_along(packed, "fsdp")
    w = input_weight[0].T
    steps = own_steps(w, core)
    here = jnp.stack([core, side, place]).astype(jnp.int32)
    packed_halves = pack_weights(here, w, steps, output_weight[0])
    blocks, others, ready = line_gather(packed_halves[:2], others)
    packed = in_order(packed, others, "fsdp")
    pieces, at = [], 0
    for member in small:
        pieces.append(packed[:, at : at + member.shape[0]].reshape(-1))
        at += member.shape[0]
    pieces[1] = pieces[1].reshape(CONV_CH, KERNEL)
    gain, convp, headp, chanp = small_params(*pieces, core)
    local, _ = lax.optimization_barrier((local, ready))

    def route(first, m):
        return [
            (c * chunks + z, (z % 2) * chunks + 2 * m + c)
            for c in range(2)
            for z in (first, first + 1)
        ]

    def bring(first):
        return [lax.ppermute(local[m], ("core", "fsdp"), route(first, m)) for m in range(2)]

    def shared(got):
        got = jnp.where(micro == 0, got[0], got[1])
        other = swap(got, "core")
        return [jnp.where(core == 0, got, other), jnp.where(core == 0, other, got)]

    def give(piece, first):
        return [
            lax.ppermute(piece, ("core", "fsdp"), [(b, a) for a, b in route(first, m)])
            for m in range(2)
        ]

    matrices = place_weights(here, [packed_halves[:2], packed_halves[2:], *blocks[:6]], None)
    last = (blocks[7][1], blocks[9][1])
    here, *got = lax.optimization_barrier((here, *bring(0), *bring(2), *last, *matrices))
    blocks[7], blocks[9] = (blocks[7][0], got[4]), (blocks[9][0], got[5])
    pieces = shared(got[:2]) + shared(got[2:4])
    win, wout = place_weights(here, blocks[6:], got[6:])
    params = (gain, convp, headp, chanp, win, wout)

    def scalars(moment, lag, reverse):
        begin = jnp.where(leading == 1, lag if reverse else 0, 0 if reverse else lag)
        step = moment - begin
        valid = jnp.logical_and(step >= 0, step < chunks)
        inside = jnp.clip(step, 0, chunks - 1)
        chunk = chunks - 1 - inside if reverse else inside
        write = jnp.where(valid, chunk, chunks)
        edge_here = leading == 1 if reverse else leading == 0
        edge = jnp.where(jnp.logical_and(valid, edge_here), chunk, chunks)
        values = [chunk if reverse else write, leading, step == 0, valid, write, edge, core]
        return [jnp.asarray(v, jnp.int32) for v in values]

    moments = chunks + LAG
    table = [scalars(moment, LAG, False) for moment in range(moments)]
    table += [scalars(moment, LAG, True) for moment in range(moments)]
    table = jnp.stack(sum(table, [])).reshape(len(table), -1)
    size = 2 * chunks
    position = jnp.where(side == 0, place, size - 1 - place).astype(jnp.int32)
    owners = []
    for direction in (1, -1):
        for hop in range(size):
            owners += ring_place((position - direction * (1 + hop)) % size, chunks)
    owners = jnp.stack(owners).reshape(2 * size, 2).astype(jnp.int32)
    table, owners = lax.optimization_barrier((table, owners))

    state, tail = jnp.zeros((STATE, OWN), F32), jnp.zeros((8, OWN_CONV), F32)
    blank = jnp.zeros((t, D), BF16)
    held, joined, result = None, None, None
    moved, incoming = {}, {}
    for moment in range(moments):
        if moment > 0:
            tail, result = lax.optimization_barrier((tail, result))
            if moment - 1 < chunks:
                moved[moment - 1] = lax.ppermute(result, "section", [(0, 1)])
        arrived = incoming.get(moment - LAG, (blank[: t // 2],) * 2)
        partial, h, (state, tail), held = forward_call(
            table,
            moment,
            chunks + 1,
            pieces[min(moment, chunks - 1)],
            arrived,
            params,
            (state, tail),
            held,
        )
        if moment - 1 in moved:
            partial, got = lax.optimization_barrier((partial, moved[moment - 1]))
            incoming[moment - 1] = (got, swap(got, "core"))
        other = swap(partial, "core")
        result, joined = forward_join(table, moment, chunks + 1, partial, other, h, joined)
    h_held, normed_held, pr_held, mx_held, q_held, st_held, tl_held = held
    y_held, ri_held, edge_held = joined
    saved = (h_held, normed_held, pr_held, mx_held, st_held, tl_held, y_held, ri_held)

    def tokens(buffer):
        return buffer[:chunks].reshape(chunks * t, buffer.shape[-1])

    carry = (
        jnp.zeros((STATE, OWN), F32),
        jnp.zeros((8, OWN_CONV), F32),
        jnp.zeros((8, OWN), F32),
        jnp.zeros((16, OWN_CONV), F32),
    )
    grads_held = None
    moved, incoming = {}, {}
    for moment in range(moments):
        if moment > 0:
            *carry, acc = carry
            acc, result = lax.optimization_barrier((acc, result))
            carry = (*carry, acc)
            if moment - 1 < chunks:
                moved[moment - 1] = lax.ppermute(result, "section", [(1, 0)])
        arrived = incoming.get(moment - LAG, (blank[: t // 2],) * 2)
        cot = pieces[max(chunks - 1 - moment, 0)]
        (partial, g, h), carry, grads_held = backward_call(
            table, moments + moment, chunks + 1, cot, arrived, saved, params, carry, grads_held
        )
        if moment - 1 in moved:
            partial, got = lax.optimization_barrier((partial, moved[moment - 1]))
            incoming[moment - 1] = (got, swap(got, "core"))
        other = swap(partial, "core")
        result, edge_held = backward_join(
            table, moments + moment, partial, other, h, g, gain, edge_held
        )

    def both(own, other, index):
        return jnp.where(index == 0, jnp.stack([own, other]), jnp.stack([other, own]))

    acc = carry[3]

    def placed(own):
        zero = jnp.zeros_like(own)
        return woven(both(own, zero, core))

    taps = jnp.concatenate([placed(acc[:5, :OWN]), acc[:5, OWN:]], axis=1)
    taps = jnp.moveaxis(taps.reshape(KERNEL + 1, chunks, -1), 1, 0)
    skip = acc[5, :OWN].reshape(OWN_HEADS, HEAD_DIM).sum(axis=1)
    vectors = [
        acc[9, :D] / gain[0],
        taps,
        placed(acc[7, :OWN_HEADS]),
        placed(acc[8, :OWN_HEADS]),
        placed(skip),
        placed(acc[6, :OWN]),
    ]
    vectors = [v.reshape(chunks, -1) for v in vectors]
    small = jnp.concatenate(vectors, axis=1)
    small = jnp.pad(small, ((0, 0), (0, SMALL_ROWS * BLOCK - small.shape[1])))
    small = small.reshape(chunks, SMALL_ROWS, BLOCK)

    onward, back = ring_route(chunks, 1), ring_route(chunks, -1)
    grads_held, gs_held = grads_held
    sums = [None] * len(GROUPS)
    for hop in range(size):
        if hop > 0:
            owners, *sums = lax.optimization_barrier((owners, *sums))
        for i, (direction, *_) in enumerate(GROUPS):
            row = hop + (0 if direction == 1 else size)
            block = block_grad(owners, row, i, normed_held, grads_held, q_held, gs_held, small)
            if hop > 0:
                path = onward if direction == 1 else back
                came = lax.ppermute(sums[i], ("y", "fsdp"), path).astype(F32)
                block = (block.astype(F32) + came).astype(BF16)
            sums[i] = block
        if hop == 3:
            owners, edge_held = lax.optimization_barrier((owners, edge_held))
        if hop == 5:
            finished = pick(table, edge_held, 0), pick(table, edge_held, 2)
            owners, *finished = lax.optimization_barrier((owners, *finished))
    *sums, early, late = lax.optimization_barrier((*sums, *finished))

    edges = jnp.where(place < 2, jnp.stack(give(early, 0)), jnp.stack(give(late, 2)))
    edges = edges[None, :, None]
    parts = []
    for own in sums:
        across = swap(own, "y")
        parts.append((own, across, swap(own, "core"), swap(across, "core")))
    here = jnp.stack([core, side]).astype(jnp.int32)
    here, edges = lax.optimization_barrier((here, edges))
    in_grad, out_grad, summed = join_grads(here, parts)
    in_grad = in_grad.T
    summed = summed.reshape(-1)
    grads, at = [], 0
    for v in vectors:
        grads.append(summed[at : at + v.shape[1]][None])
        at += v.shape[1]
    taps = grads[1].reshape(KERNEL + 1, -1)
    grads[1:2] = taps[:KERNEL].T[None], taps[KERNEL:]
    return (
        edges,
        grads[0],
        in_grad[None],
        grads[1],
        grads[2],
        grads[3],
        grads[4],
        grads[5],
        grads[6],
        out_grad[None],
    )


def shifted(block, axis, distance):
    devices = range(lax.axis_size(axis))
    route = [(i - distance, i) for i in devices if i - distance in devices]
    return lax.ppermute(block, axis, route)


def prefix(value, axis, join, neutral):
    place = lax.axis_index(axis)
    gathered = jax.tree.map(
        lambda a, kind: lax.all_gather(a.astype(kind), axis), value, (jnp.bfloat16, jnp.bfloat16)
    )
    state = jax.tree.map(lambda a, e: jnp.zeros_like(a) + jnp.asarray(e, a.dtype), value, neutral)

    def one(turn, state):
        return join(
            state,
            jax.tree.map(
                lambda a, own: lax.dynamic_index_in_dim(a, turn, 0, False).astype(own.dtype),
                gathered,
                value,
            ),
        )

    return lax.fori_loop(0, place, one, state)


def prefix_2(value, axis, join, neutral):
    count = lax.axis_size(axis)
    place = lax.axis_index(axis)
    ahead = count - 1 - place
    gathered = jax.tree.map(
        lambda a, kind: lax.all_gather(a.astype(kind), axis),
        value,
        jax.tree.map(lambda a: jnp.bfloat16 if a.dtype == jnp.float32 else a.dtype, value),
    )
    state = jax.tree.map(lambda a, e: jnp.zeros_like(a) + jnp.asarray(e, a.dtype), value, neutral)

    def one(turn, state):
        source = count - 1 - turn
        return join(
            state,
            jax.tree.map(
                lambda a, own: lax.dynamic_index_in_dim(a, source, 0, False).astype(own.dtype),
                gathered,
                value,
            ),
        )

    return lax.fori_loop(0, ahead, one, state)


def rms_scale(values, scale_gain):
    return (
        values * lax.rsqrt(jnp.mean(values * values, axis=-1, keepdims=True) + EPSILON) * scale_gain
    )


def chain_rule(earlier, later_part):
    return (
        earlier[0] * later_part[0],
        later_part[1] + later_part[0][:, :, None, None] * earlier[1],
    )


def conv_features(widened, conv_weight, conv_bias, dt_raw, dt_bias, a_log):
    tap_count = conv_weight.shape[1]
    step_count = widened.shape[1] - tap_count + 1
    convolved = conv_bias
    for offset in range(tap_count):
        convolved = convolved + widened[:, offset : offset + step_count, :] * conv_weight[:, offset]
    activated = jax.nn.silu(convolved)
    x_heads = activated[..., :INNER]
    b_rows = activated[..., INNER : INNER + STATE]
    c_rows = activated[..., INNER + STATE :]
    dt_step = jax.nn.softplus(dt_raw + dt_bias)
    log_decay = jnp.cumsum(-jnp.exp(a_log) * dt_step, axis=1)
    return (x_heads, b_rows, c_rows, dt_step, log_decay)


def local_states(x_heads, b_rows, dt_step, log_decay):
    seq_count, length = (x_heads.shape[0], x_heads.shape[1])
    spread = x_heads.reshape(seq_count, length, HEADS, HEAD_DIM)
    weights = jnp.exp(log_decay[:, -1:, :] - log_decay) * dt_step
    weighted = spread * weights[..., None]
    states = jnp.einsum("sqhd,sqn->shdn", weighted, b_rows, precision=EXACT_MATMUL)
    return (jnp.exp(log_decay[:, -1]), states)


def gated_output(
    x_heads, b_rows, c_rows, dt_step, log_decay, prior_state, gate_z, skip_gain, gate_gain
):
    seq_count, length = (x_heads.shape[0], x_heads.shape[1])
    spread = x_heads.reshape(seq_count, length, HEADS, HEAD_DIM)
    scaled = spread * dt_step[..., None]
    by_head = jnp.transpose(log_decay, (0, 2, 1))
    differ = by_head[:, :, :, None] - by_head[:, :, None, :]
    causal = jnp.arange(length)[:, None] >= jnp.arange(length)[None, :]
    mixing = jnp.where(causal, jnp.exp(jnp.where(causal, differ, 0.0)), 0.0)
    intersections = jnp.einsum("sqn,skn->sqk", c_rows, b_rows, precision=EXACT_MATMUL)
    mixed_out = jnp.einsum(
        "shqk,skhd->sqhd", mixing * intersections[:, None], scaled, precision=EXACT_MATMUL
    )
    mixed_out = mixed_out + jnp.exp(log_decay)[..., None] * jnp.einsum(
        "sqn,shdn->sqhd", c_rows, prior_state, precision=EXACT_MATMUL
    )
    mixed_out = (mixed_out + skip_gain[:, None] * spread).reshape(seq_count, length, INNER)
    return rms_scale(mixed_out * jax.nn.silu(gate_z), gate_gain)


def layer_forward(hidden, weights):
    (
        norm_gain,
        input_weight,
        conv_weight,
        conv_bias,
        dt_bias,
        a_log,
        skip_gain,
        gate_gain,
        output_weight,
    ) = weights
    normalized_rows = rms_scale(hidden, norm_gain.astype(jnp.float32)).astype(jnp.bfloat16)
    projected_rows = jnp.einsum(
        "spd,de->spe", normalized_rows, input_weight, preferred_element_type=jnp.float32
    ).astype(jnp.bfloat16)
    length = hidden.shape[1]
    xbc_part = projected_rows[..., INNER : INNER + CONV_CH]
    border = shifted(xbc_part[:, length - KERNEL + 1 :, :], "fsdp", 1)
    widened = jnp.concatenate([border, xbc_part], axis=1)
    features = conv_features(
        widened.astype(jnp.float32),
        conv_weight.astype(jnp.float32),
        conv_bias.astype(jnp.float32),
        projected_rows[..., INNER + CONV_CH :].astype(jnp.float32),
        dt_bias.astype(jnp.float32),
        a_log.astype(jnp.float32),
    )
    decays, states = local_states(features[0], features[1], features[3], features[4])
    scanned = prefix(
        (decays, states), "fsdp", chain_rule, (jnp.ones_like(decays), jnp.zeros_like(states))
    )
    prior_state = scanned[1]
    gated_result = gated_output(
        features[0],
        features[1],
        features[2],
        features[3],
        features[4],
        prior_state,
        projected_rows[..., :INNER].astype(jnp.float32),
        skip_gain.astype(jnp.float32),
        gate_gain.astype(jnp.float32),
    )
    gated_low = gated_result.astype(jnp.bfloat16)
    final_result = hidden + jnp.einsum(
        "spi,id->spd", gated_low, output_weight, preferred_element_type=jnp.float32
    )
    return (
        final_result,
        (hidden, normalized_rows, projected_rows, widened, prior_state, gated_low),
    )


def layer_backward(gradient, kept_state, weights):
    hidden, normalized_rows, projected_rows, widened, prior_state, gated_low = kept_state
    (
        norm_gain,
        input_weight,
        conv_weight,
        conv_bias,
        dt_bias,
        a_log,
        skip_gain,
        gate_gain,
        output_weight,
    ) = weights
    grad_low = gradient.astype(jnp.bfloat16)
    grad_out_weight = jnp.einsum(
        "spi,spd->id", gated_low, grad_low, preferred_element_type=jnp.float32
    )
    grad_gated = jnp.einsum(
        "spd,id->spi", grad_low, output_weight, preferred_element_type=jnp.float32
    )
    features, pull_features = jax.vjp(
        conv_features,
        widened.astype(jnp.float32),
        conv_weight.astype(jnp.float32),
        conv_bias.astype(jnp.float32),
        projected_rows[..., INNER + CONV_CH :].astype(jnp.float32),
        dt_bias.astype(jnp.float32),
        a_log.astype(jnp.float32),
    )
    _, pull_gated = jax.vjp(
        gated_output,
        features[0],
        features[1],
        features[2],
        features[3],
        features[4],
        prior_state,
        projected_rows[..., :INNER].astype(jnp.float32),
        skip_gain.astype(jnp.float32),
        gate_gain.astype(jnp.float32),
    )
    grads_gated = pull_gated(grad_gated)
    decay_states, pull_states = jax.vjp(
        local_states, features[0], features[1], features[3], features[4]
    )
    decays = decay_states[0]
    later_state = prefix_2(
        (decays, grads_gated[5]),
        "fsdp",
        chain_rule,
        (jnp.ones_like(decays), jnp.zeros_like(grads_gated[5])),
    )
    grad_end = later_state[1]
    state_parts = pull_states((jnp.sum(grad_end * prior_state, axis=(2, 3)), grad_end))
    feature_grads = (
        grads_gated[0] + state_parts[0],
        grads_gated[1] + state_parts[1],
        grads_gated[2],
        grads_gated[3] + state_parts[2],
        grads_gated[4] + state_parts[3],
    )
    grad_wide, grad_conv_w, grad_conv_b, grad_dt_raw, grad_dt_bias, grad_a_log = pull_features(
        feature_grads
    )
    margin = KERNEL - 1
    returned = shifted(grad_wide[:, :margin, :].astype(jnp.bfloat16), "fsdp", -1).astype(
        jnp.float32
    )
    own_rows = grad_wide[:, margin:, :]
    length = own_rows.shape[1]
    grad_xbc = jnp.concatenate(
        [own_rows[:, : length - margin], own_rows[:, length - margin :] + returned], axis=1
    )
    grad_proj = jnp.concatenate([grads_gated[6], grad_xbc, grad_dt_raw], axis=-1).astype(
        jnp.bfloat16
    )
    grad_in_weight = jnp.einsum(
        "spd,spe->de", normalized_rows, grad_proj, preferred_element_type=jnp.float32
    )
    grad_normed = jnp.einsum(
        "spe,de->spd", grad_proj, input_weight, preferred_element_type=jnp.float32
    )
    _, pull_norm = jax.vjp(rms_scale, hidden, norm_gain.astype(jnp.float32))
    grad_hidden, grad_norm_gain = pull_norm(grad_normed)
    return (
        gradient + grad_hidden,
        (
            grad_norm_gain,
            grad_in_weight,
            grad_conv_w,
            grad_conv_b,
            grad_dt_bias,
            grad_a_log,
            grads_gated[7],
            grads_gated[8],
            grad_out_weight,
        ),
    )


def shards(
    ends,
    norm_gain,
    input_weight,
    conv_weight,
    conv_bias,
    dt_bias,
    a_log,
    skip_gain,
    gate_gain,
    output_weight,
):
    gathered = (
        lax.all_gather(norm_gain, "fsdp", axis=1, tiled=True),
        lax.all_gather(input_weight, "fsdp", axis=1, tiled=True),
        lax.all_gather(conv_weight, "fsdp", axis=1, tiled=True),
        lax.all_gather(conv_bias, "fsdp", axis=1, tiled=True),
        lax.all_gather(dt_bias, "fsdp", axis=1, tiled=True),
        lax.all_gather(a_log, "fsdp", axis=1, tiled=True),
        lax.all_gather(skip_gain, "fsdp", axis=1, tiled=True),
        lax.all_gather(gate_gain, "fsdp", axis=1, tiled=True),
        lax.all_gather(output_weight, "fsdp", axis=1, tiled=True),
    )
    layer_weights = tuple((member[0] for member in gathered))
    leading = lax.axis_index("section") == 0
    local_data = ends[0].astype(jnp.float32)
    batches = local_data.shape[0]
    arrived = jnp.zeros(local_data.shape[1:], jnp.float32)
    stored = []
    produced = []
    for moment in range(batches + 1):
        source = jnp.where(leading, local_data[min(moment, batches - 1)], arrived)
        final_result, kept_state = layer_forward(source, layer_weights)
        stored.append(kept_state)
        produced.append(final_result)
        if moment < batches:
            arrived = shifted(final_result.astype(jnp.bfloat16), "section", 1).astype(jnp.float32)
    totals = None
    coming = jnp.zeros(local_data.shape[1:], jnp.float32)
    returned_grads = []
    for moment in range(batches + 1):
        gradient = jnp.where(leading, coming, local_data[min(moment, batches - 1)])
        kept_state = jax.tree.map(
            lambda upper_part, lower_part: jnp.where(leading, upper_part, lower_part),
            stored[max(moment - 1, 0)],
            stored[min(moment + 1, batches)],
        )
        grad_input, gradients = layer_backward(gradient, kept_state, layer_weights)
        active = jnp.where(leading, moment >= 1, moment < batches)
        masked = tuple((jnp.where(active, member, 0.0) for member in gradients))
        if totals is None:
            totals = masked
        else:
            totals = tuple((earlier_sum + member for earlier_sum, member in zip(totals, masked)))
        returned_grads.append(grad_input)
        if moment < batches:
            coming = shifted(grad_input.astype(jnp.bfloat16), "section", -1).astype(jnp.float32)
    boundary = jnp.stack(
        [
            jnp.where(leading, returned_grads[number + 1], produced[number + 1])
            for number in range(batches)
        ]
    )
    owned_parts = (
        lax.psum_scatter(
            totals[0][None].astype(jnp.bfloat16), "fsdp", scatter_dimension=1, tiled=True
        ).astype(jnp.float32),
        lax.psum_scatter(
            totals[1][None].astype(jnp.bfloat16), "fsdp", scatter_dimension=1, tiled=True
        ).astype(jnp.float32),
        lax.psum_scatter(
            totals[2][None].astype(jnp.bfloat16), "fsdp", scatter_dimension=1, tiled=True
        ).astype(jnp.float32),
        lax.psum_scatter(
            totals[3][None].astype(jnp.bfloat16), "fsdp", scatter_dimension=1, tiled=True
        ).astype(jnp.float32),
        lax.psum_scatter(
            totals[4][None].astype(jnp.bfloat16), "fsdp", scatter_dimension=1, tiled=True
        ).astype(jnp.float32),
        lax.psum_scatter(
            totals[5][None].astype(jnp.bfloat16), "fsdp", scatter_dimension=1, tiled=True
        ).astype(jnp.float32),
        lax.psum_scatter(
            totals[6][None].astype(jnp.bfloat16), "fsdp", scatter_dimension=1, tiled=True
        ).astype(jnp.float32),
        lax.psum_scatter(
            totals[7][None].astype(jnp.bfloat16), "fsdp", scatter_dimension=1, tiled=True
        ).astype(jnp.float32),
        lax.psum_scatter(
            totals[8][None].astype(jnp.bfloat16), "fsdp", scatter_dimension=1, tiled=True
        ).astype(jnp.float32),
    )
    summed = (
        lax.psum(owned_parts[0].astype(jnp.bfloat16), "rep").astype(jnp.float32),
        lax.psum(owned_parts[1].astype(jnp.bfloat16), "rep").astype(jnp.float32),
        lax.psum(owned_parts[2].astype(jnp.bfloat16), "rep").astype(jnp.float32),
        lax.psum(owned_parts[3].astype(jnp.bfloat16), "rep").astype(jnp.float32),
        lax.psum(owned_parts[4].astype(jnp.bfloat16), "rep").astype(jnp.float32),
        lax.psum(owned_parts[5].astype(jnp.bfloat16), "rep").astype(jnp.float32),
        lax.psum(owned_parts[6].astype(jnp.bfloat16), "rep").astype(jnp.float32),
        lax.psum(owned_parts[7].astype(jnp.bfloat16), "rep").astype(jnp.float32),
        lax.psum(owned_parts[8].astype(jnp.bfloat16), "rep").astype(jnp.float32),
    )
    return (
        boundary.astype(jnp.bfloat16)[None],
        summed[0],
        summed[1],
        summed[2],
        summed[3],
        summed[4],
        summed[5],
        summed[6],
        summed[7],
        summed[8],
    )


def solution(mesh):
    shape = mesh.shape
    relay = shape["section"] == 2 and shape["rep"] == 4 and shape["fsdp"] == 4
    if relay:
        devices = mesh.devices.reshape(2, 2, 2, 4)
        mesh = Mesh(devices, ("section", "y", "core", "fsdp"))
    rep = ("y", "core") if relay else "rep"
    data = P("section", None, rep, "fsdp", None)
    vector, matrix = P("section", "fsdp"), P("section", "fsdp", None)
    params = (vector, matrix, matrix, vector, vector, vector, vector, vector, matrix)
    return jax.shard_map(
        relay_shards if relay else shards,
        mesh=mesh,
        in_specs=(data, *params),
        out_specs=(data, *params),
        check_vma=False,
    )
```

```python
import functools

import jax
import jax.numpy as jnp
from jax import lax
from jax.experimental import pallas as pl
from jax.experimental.pallas import tpu as pltpu
from jax.sharding import Mesh
from jax.sharding import PartitionSpec as P

D = 1536
HEADS = 48
HEAD_DIM = 64
STATE = 128
KERNEL = 4
INNER = 3072
CONV_CH = 3328
LANES = 128

OWN = INNER // 2
OWN_HEADS = HEADS // 2
OWN_CONV = OWN + 2 * STATE
X_AT = OWN
BC_AT = 2 * OWN
DT_AT = 2 * OWN + 2 * STATE
OWN_PROJ = DT_AT + 2 * LANES
PAIRS = OWN // LANES

EPSILON = 1e-05
EXACT_MATMUL = lax.Precision.HIGHEST
F32 = jnp.float32
BF16 = jnp.bfloat16
FORWARD_VMEM = 24
BACKWARD_VMEM = 30
JOIN_VMEM = 12


def dot(a, b):
    return lax.dot_general(a, b, (((1,), (0,)), ((), ())), preferred_element_type=F32)


def dot_nt(a, b):
    return lax.dot_general(a, b, (((1,), (1,)), ((), ())), preferred_element_type=F32)


def dot_tn(a, b):
    return lax.dot_general(a, b, (((0,), (0,)), ((), ())), preferred_element_type=F32)


def split(v, parts):
    pieces = []
    for _ in range(parts):
        piece = v.astype(BF16)
        pieces.append(piece)
        v = v - piece.astype(F32)
    return pieces


def sigmoid(v):
    return 0.5 * jnp.tanh(0.5 * v) + 0.5


def softplus(v):
    return jnp.maximum(v, 0.0) + jnp.log1p(jnp.exp(-jnp.abs(v)))


def step_sizes(dt_raw, headp):
    t = dt_raw.shape[0]
    biased = dt_raw + headp[0:1]
    dt = softplus(biased)
    rows = lax.broadcasted_iota(jnp.int32, (t, t), 0)
    cols = lax.broadcasted_iota(jnp.int32, (t, t), 1)
    tri = jnp.where(rows >= cols, 1.0, 0.0).astype(BF16)
    ld = sum(dot(tri, part) for part in split(dt * headp[1:2], 3))
    return dt, ld, biased


def at_head(v, pair):
    turned = pltpu.roll(v, lax.rem(LANES - 2 * pair, LANES), 1)
    return [jnp.broadcast_to(turned[:, i : i + 1], v.shape) for i in range(2)]


def decay_blocks(col, row, swapped):
    n = col.shape[0] // 2
    rows = lax.broadcasted_iota(jnp.int32, (n, n), 0)
    cols = lax.broadcasted_iota(jnp.int32, (n, n), 1)
    keep = rows <= cols if swapped else rows >= cols

    def block(i, j):
        down, along = col[i * n : (i + 1) * n], row[:, j * n : (j + 1) * n]
        differ = along - down if swapped else down - along
        return jnp.exp(jnp.where(keep, differ, -1e30) if i == j else differ)

    return block(0, 0), block(0, 1) if swapped else block(1, 0), block(1, 1)


def convolve(xw, sl, convp, t):
    out = convp[4:5, sl] + xw[5 : 5 + t, sl] * convp[0:1, sl]
    for k in range(1, KERNEL):
        out = out + xw[5 + k : 5 + k + t, sl] * convp[k : k + 1, sl]
    return out


def pair_loop(step):
    def three(turn, _):
        for i in range(3):
            step(3 * turn + i)
        return 0

    lax.fori_loop(0, PAIRS // 3, three, 0)


def aligned(value):
    return pl.multiple_of(value, LANES)


def fetch(source, target, sem):
    copy = pltpu.make_async_copy(source, target, sem)
    copy.start()
    return copy


def fetch_one_of(first, one, other, target, sem):
    @pl.when(first)
    def _():
        pltpu.make_async_copy(one, target, sem).start()

    @pl.when(jnp.logical_not(first))
    def _():
        pltpu.make_async_copy(other, target, sem).start()

    return pltpu.make_async_copy(other, target, sem)


def forward_kernel(row, sc, *refs):
    @pl.when(sc[row, VALID] == 1)
    def _():
        forward_chunk(row, sc, *refs)


def forward_chunk(
    row, sc, got_hbm, other_hbm, x_hbm, ng_ref, convp, headp, chanp, st_ref, tail_ref, win, wout, *rest
):
    p, h, st_out, tail_out = rest[-22:-18]
    h_hbm, n_hbm, pr_hbm, mx_hbm, q_hbm, st_hbm, tl_hbm = rest[-18:-11]
    normed, pr, mx, q, sti, tl, xw, ldt, ss, g_ref, sem = rest[-11:]
    t = h.shape[0]
    half = t // 2
    slot = sc[row, SLOT]
    first = sc[row, FIRST] == 1
    leading = sc[row, LEADING] == 1
    core = sc[row, CORE]

    @pl.when(leading)
    def _():
        fetch(x_hbm, h, sem.at[0]).wait()

    @pl.when(jnp.logical_not(leading))
    def _():
        mine = h.at[pl.ds(aligned(core * half), half)]
        theirs = h.at[pl.ds(aligned((1 - core) * half), half)]
        copies = fetch(got_hbm, mine, sem.at[0]), fetch(other_hbm, theirs, sem.at[1])
        for copy in copies:
            copy.wait()

    stores = [fetch(h, h_hbm.at[slot], sem.at[0])]
    hf = h[...].astype(F32)
    r = lax.rsqrt(jnp.mean(hf * hf, axis=1, keepdims=True) + EPSILON)
    normed[...] = (hf * r * ng_ref[...]).astype(BF16)
    stores.append(fetch(normed, n_hbm.at[slot], sem.at[1]))

    sti[...] = jnp.where(first, 0.0, st_ref[...])
    tl[...] = jnp.where(first, 0.0, tail_ref[...])
    stores.append(fetch(sti, st_hbm.at[slot], sem.at[2]))
    stores.append(fetch(tl, tl_hbm.at[slot], sem.at[3]))
    xw[0:8, :] = tl[...]

    for at in range(0, OWN_PROJ, 512):
        cols = slice(at, min(at + 512, OWN_PROJ))
        pr[:, cols] = dot_nt(normed[...], win[cols, :]).astype(BF16)
    stores.append(fetch(pr, pr_hbm.at[slot], sem.at[4]))
    tail_out[...] = pr[t - 8 : t, X_AT : X_AT + OWN_CONV].astype(F32)

    bc = pl.ds(OWN, 2 * STATE)
    xw[8 : 8 + t, OWN:OWN_CONV] = pr[:, BC_AT:DT_AT].astype(F32)
    conv_bc = convolve(xw, bc, convp, t)
    act = (conv_bc * sigmoid(conv_bc)).astype(BF16)
    b, c = act[:, :STATE], act[:, STATE:]
    g_ref[...] = dot_nt(c, b)
    b_turned = act[:, :STATE].astype(F32).T.astype(BF16)
    dt, ld, _ = step_sizes(pr[:, DT_AT : DT_AT + LANES].astype(F32), headp[...])
    ldt[...] = ld.T
    left = lax.broadcasted_iota(jnp.int32, (t, LANES), 1) < HEAD_DIM
    ss[...] = jnp.zeros_like(ss)

    def pair_step(pair):
        at = pl.multiple_of(pair * LANES, LANES)
        sl = pl.ds(at, LANES)
        xw[8 : 8 + t, sl] = pr[:, pl.ds(X_AT + at, LANES)].astype(F32)
        conv = convolve(xw, sl, convp, t)
        x = conv * sigmoid(conv)
        cols = at_head(ld, pair)
        u = jnp.where(left, *at_head(dt, pair)) * x
        ld_p = jnp.where(left, *cols)
        tops, bottoms, sides = [], [], []
        for i in range(2):
            u_i = jnp.where(left if i == 0 else jnp.logical_not(left), u, 0.0).astype(BF16)
            d00, d10, d11 = decay_blocks(cols[i], ldt[pl.ds(2 * pair + i, 1), :], False)
            m00 = (g_ref[:half, :half] * d00).astype(BF16)
            m10 = (g_ref[half:, :half] * d10).astype(BF16)
            m11 = (g_ref[half:, half:] * d11).astype(BF16)
            tops.append(m00)
            bottoms += [m10, m11]
            sides.append(u_i)
        top = dot(jnp.concatenate(tops, axis=1), jnp.concatenate([v[:half] for v in sides], axis=0))
        bottom = dot(jnp.concatenate(bottoms, axis=1), jnp.concatenate(sides, axis=0))
        eld = jnp.exp(ld_p)
        st = sti[:, sl]
        y = jnp.concatenate([top, bottom], axis=0) + eld * dot(c, st.astype(BF16))
        weighted = (u * jnp.exp(ld_p[t - 1 : t] - ld_p)).astype(BF16)
        st_out[:, sl] = eld[t - 1 : t] * st + dot(b_turned, weighted)
        mixed = y + chanp[0:1, sl] * x
        mx[:, sl] = mixed
        z = pr[:, sl].astype(F32)
        gated = mixed * (z * sigmoid(z))
        ss[...] += gated * gated
        q[:, sl] = (gated * chanp[1:2, sl]).astype(BF16)

    pair_loop(pair_step)
    stores.append(fetch(mx, mx_hbm.at[slot], sem.at[5]))
    stores.append(fetch(q, q_hbm.at[slot], sem.at[6]))
    total = jnp.sum(ss[...], axis=1, keepdims=True)
    high = total.astype(BF16).astype(F32)
    lane = lax.broadcasted_iota(jnp.int32, (t, LANES), 1)
    p[:, D:] = jnp.where(lane == 0, high, jnp.where(lane == 1, total - high, 0.0)).astype(BF16)
    for at in range(0, D, 512):
        p[:, at : at + 512] = dot(q[...], wout[:, at : at + 512]).astype(BF16)
    for store in stores:
        store.wait()


def backward_kernel(row, sc, *refs):
    acc_ref, acc_out = refs[17], refs[-21]

    @pl.when(sc[row, VALID] == 1)
    def _():
        backward_chunk(row, sc, *refs)

    @pl.when(sc[row, VALID] == 0)
    def _():
        acc_out[...] = acc_ref[...]


def backward_chunk(
    row,
    sc,
    arrived_hbm,
    other_hbm,
    cot_hbm,
    h_hbm,
    n_hbm,
    pr_hbm,
    mx_hbm,
    st_hbm,
    tl_hbm,
    y_hbm,
    ri_hbm,
    convp,
    headp,
    chanp,
    dst_ref,
    dc_ref,
    val_ref,
    acc_ref,
    win,
    wout,
    *rest,
):
    gn, g_ref, h_out, dst_out, dc_out, val_out, acc_out, gp_hbm, gs_hbm = rest[-27:-18]
    pr, mx, st_ref, tl, y_ref, ri, gp, gs, normed = rest[-18:-9]
    xw, dw, ldt, gw, gt, dgt, dci, dbi, sem = rest[-9:]
    t = g_ref.shape[0]
    half = t // 2
    slot = sc[row, SLOT]
    last = sc[row, FIRST] == 1
    leading = sc[row, LEADING] == 1
    core = sc[row, CORE]
    mine = g_ref.at[pl.ds(aligned(core * half), half)]
    theirs = g_ref.at[pl.ds(aligned((1 - core) * half), half)]

    @pl.when(leading)
    def _():
        pltpu.make_async_copy(arrived_hbm, mine, sem.at[0]).start()
        pltpu.make_async_copy(other_hbm, theirs, sem.at[10]).start()

    @pl.when(jnp.logical_not(leading))
    def _():
        pltpu.make_async_copy(cot_hbm, g_ref, sem.at[0]).start()

    y_copy = fetch(y_hbm.at[slot], y_ref, sem.at[1])
    ri_copy = fetch(ri_hbm.at[slot], ri, sem.at[2])
    pr_copy = fetch(pr_hbm.at[slot], pr, sem.at[3])
    tl_copy = fetch(tl_hbm.at[slot], tl, sem.at[4])
    mx_copy = fetch(mx_hbm.at[slot], mx, sem.at[5])
    st_copy = fetch(st_hbm.at[slot], st_ref, sem.at[6])

    acc_out[...] = acc_ref[...]
    dw[t : t + 8, :] = jnp.where(last, 0.0, dc_ref[...])
    dgt[...] = jnp.zeros_like(dgt)
    dci[...] = jnp.zeros_like(dci)
    dbi[...] = jnp.zeros_like(dbi)

    @pl.when(leading)
    def _():
        pltpu.make_async_copy(arrived_hbm, mine, sem.at[0]).wait()
        pltpu.make_async_copy(other_hbm, theirs, sem.at[10]).wait()

    @pl.when(jnp.logical_not(leading))
    def _():
        pltpu.make_async_copy(cot_hbm, g_ref, sem.at[0]).wait()

    for at in range(0, OWN, 512):
        gw[:, at : at + 512] = dot_nt(g_ref[...], wout[at : at + 512, :])
    y_copy.wait()
    ri_copy.wait()
    rinv = ri[:, 0:1]
    mean = jnp.sum(g_ref[...].astype(F32) * y_ref[...].astype(F32), axis=1, keepdims=True)
    lean = rinv * rinv * (mean * (1.0 / INNER))
    gs[...] = (g_ref[...].astype(F32) * rinv).astype(BF16)
    gs_store = fetch(gs, gs_hbm.at[sc[row, WRITE]], sem.at[7])
    pr_copy.wait()
    tl_copy.wait()
    xw[0:8, :] = tl[...]

    bc = pl.ds(OWN, 2 * STATE)
    xw[8 : 8 + t, OWN:OWN_CONV] = pr[:, BC_AT:DT_AT].astype(F32)
    conv_bc = convolve(xw, bc, convp, t)
    sig_bc = sigmoid(conv_bc)
    act = (conv_bc * sig_bc).astype(BF16)
    b, c = act[:, :STATE], act[:, STATE:]
    c_turned = c.astype(F32).T.astype(BF16)
    gt[...] = dot_nt(b, c)
    dt, ld, biased = step_sizes(pr[:, DT_AT : DT_AT + LANES].astype(F32), headp[...])
    ldt[...] = ld.T
    left = lax.broadcasted_iota(jnp.int32, (t, LANES), 1) < HEAD_DIM

    def add(line, sl, v):
        acc_out[line : line + 1, sl] += v

    def conv_back(dact, conv, sig, sl):
        dconv = dact * (sig * (1.0 + conv * (1.0 - sig)))
        dw[0:t, sl] = dconv
        add(4, sl, jnp.sum(dconv, axis=0, keepdims=True))
        for k in range(KERNEL):
            add(k, sl, jnp.sum(dconv * xw[5 + k : 5 + k + t, sl], axis=0, keepdims=True))
        dx = dconv * convp[KERNEL - 1 : KERNEL, sl]
        for k in range(KERNEL - 1):
            ahead = KERNEL - 1 - k
            dx = dx + dw[ahead : ahead + t, sl] * convp[k : k + 1, sl]
        return dx.astype(BF16)

    lane_head = lax.rem(lax.broadcasted_iota(jnp.int32, (2 * LANES, LANES), 0), LANES) // HEAD_DIM
    head_lane = lax.broadcasted_iota(jnp.int32, (2 * LANES, LANES), 1)
    mx_copy.wait()
    st_copy.wait()
    h_copy = fetch(h_hbm.at[slot], h_out, sem.at[8])
    n_copy = fetch(n_hbm.at[slot], normed, sem.at[9])

    def pair_step(pair, carry):
        ddt, dld, dval = carry
        at = pl.multiple_of(pair * LANES, LANES)
        sl = pl.ds(at, LANES)
        xsl = pl.ds(X_AT + at, LANES)
        xw[8 : 8 + t, sl] = pr[:, xsl].astype(F32)
        conv = convolve(xw, sl, convp, t)
        sig = sigmoid(conv)
        x = conv * sig
        z = pr[:, sl].astype(F32)
        sig_z = sigmoid(z)
        s = z * sig_z
        mixed = mx[:, sl]
        gated = mixed * s
        scaled = gw[:, sl] * rinv
        add(6, sl, jnp.sum(scaled * gated, axis=0, keepdims=True))
        dgated = chanp[1:2, sl] * scaled - gated * lean
        dy = dgated * s
        gp[:, sl] = (dgated * mixed * (sig_z * (1.0 + z * (1.0 - sig_z)))).astype(BF16)
        skip = chanp[0:1, sl]
        add(5, sl, jnp.sum(dy * x, axis=0, keepdims=True))
        y = mixed - skip * x

        cols = at_head(ld, pair)
        ld_p = jnp.where(left, *cols)
        eld = jnp.exp(ld_p)
        wend = jnp.exp(ld_p[t - 1 : t] - ld_p)
        dt_p = jnp.where(left, *at_head(dt, pair))
        u = dt_p * x
        u_low = u.astype(BF16)
        dy_low = dy.astype(BF16)
        dst = jnp.where(last, 0.0, dst_ref[:, sl])
        dst_low = dst.astype(BF16)
        top = jnp.zeros((half, LANES), F32)
        bottom = top
        for i in range(2):
            side = left if i == 0 else jnp.logical_not(left)
            d00, d01, d11 = decay_blocks(cols[i], ldt[pl.ds(2 * pair + i, 1), :], True)
            m00 = (gt[:half, :half] * d00).astype(BF16)
            m01 = (gt[:half, half:] * d01).astype(BF16)
            m11 = (gt[half:, half:] * d11).astype(BF16)
            dy_i = jnp.where(side, dy, 0.0).astype(BF16)
            top = top + dot(jnp.concatenate([m00, m01], axis=1), dy_i)
            bottom = bottom + dot(m11, dy_i[half:])
            u_i = jnp.where(side, u, 0.0).astype(BF16)
            dm = dot_nt(u_i[:half], dy_low)
            dgt[:half, :half] += dm[:, :half] * d00
            dgt[:half, half:] += dm[:, half:] * d01
            dgt[half:, half:] += dot_nt(u_i[half:], dy_low[half:]) * d11
        du = jnp.concatenate([top, bottom], axis=0) + wend * dot(b, dst_low)
        st = st_ref[:, sl]
        dyl = (eld * dy).astype(BF16)
        dst_new = eld[t - 1 : t] * dst + dot(c_turned, dyl)
        dst_out[:, sl] = dst_new
        val_out[:, sl] = jnp.broadcast_to(
            jnp.sum(dst_new * st, axis=0, keepdims=True), (8, LANES)
        )
        dci[...] += dot_nt(dyl, st.astype(BF16))
        dbi[...] += dot_nt((wend * u).astype(BF16), dst_low)

        pick = jnp.where(lane_head + 2 * pair == head_lane, 1.0, 0.0).astype(BF16)


        def by_head(v):
            return dot(jnp.concatenate(split(v, 2), axis=1), pick)

        ddt = ddt + by_head(du * x)
        dld = dld + by_head(dy_low.astype(F32) * y - u_low.astype(F32) * du)
        dval = dval + by_head(jnp.where(last, 0.0, val_ref[:, sl]))
        gp[:, xsl] = conv_back(dt_p * du + skip * dy, conv, sig, sl)
        return ddt, dld, dval

    zero = jnp.zeros((t, LANES), F32)
    ddt, dld, dval = lax.fori_loop(
        0,
        PAIRS // 3,
        lambda turn, carry: functools.reduce(
            lambda held, i: pair_step(3 * turn + i, held), range(3), carry
        ),
        (zero, zero, jnp.zeros((8, LANES), F32)),
    )

    dgt_low = dgt[...].astype(BF16)
    db = dbi[...] + dot(dgt_low, c)
    dc = dci[...] + dot_tn(dgt_low, b)
    gp[:, BC_AT:DT_AT] = conv_back(jnp.concatenate([db, dc], axis=1), conv_bc, sig_bc, bc)

    rows = lax.broadcasted_iota(jnp.int32, (t, t), 0)
    cols = lax.broadcasted_iota(jnp.int32, (t, t), 1)
    upper = jnp.where(rows <= cols, 1.0, 0.0).astype(BF16)
    da = sum(dot(upper, part) for part in split(dld, 3)) + dval[0:1]
    rate = headp[1:2]
    head = pl.ds(0, LANES)
    add(8, head, jnp.sum(da * rate * dt, axis=0, keepdims=True))
    ddt_raw = (ddt + rate * da) * sigmoid(biased)
    add(7, head, jnp.sum(ddt_raw, axis=0, keepdims=True))
    gp[:, DT_AT : DT_AT + LANES] = ddt_raw.astype(BF16)
    gp[:, DT_AT + LANES :] = jnp.zeros((t, LANES), BF16)
    gp_store = fetch(gp, gp_hbm.at[sc[row, WRITE]], sem.at[0])
    dc_out[...] = dw[0:8, :]
    n_copy.wait()
    for at in range(0, D, 512):
        cols = slice(at, at + 512)
        values = dot(gp[...], win[:, cols])
        gn[:, cols] = values.astype(BF16)
        add(9, cols, jnp.sum(values * normed[:, cols].astype(F32), axis=0, keepdims=True))
    gp_store.wait()
    gs_store.wait()
    h_copy.wait()


def forward_join_kernel(row, sc, own_ref, other_ref, h_ref, *rest):
    out, y_hbm, ri_hbm, e_hbm, y_v, ri_v, low_v, sem = rest[-8:]
    half = out.shape[0]

    @pl.when(sc[row, VALID] == 1)
    def _():
        copies = []
        for k in range(2):
            rows = slice(k * half, (k + 1) * half)
            total = own_ref[rows].astype(F32) + other_ref[rows].astype(F32)
            square = total[:, D : D + 1] + total[:, D + 1 : D + 2]
            rinv = lax.rsqrt(square * (1.0 / INNER) + EPSILON)
            y = total[:, :D] * rinv
            y_v[rows] = y.astype(BF16)
            ri_v[rows] = jnp.broadcast_to(rinv, (half, LANES))
            low_v[rows] = (h_ref[rows].astype(F32) + y).astype(BF16)
            pieces = ((y_v, y_hbm, SLOT), (ri_v, ri_hbm, SLOT), (low_v, e_hbm, EDGE))
            for near_ref, far_ref, which in pieces:
                target = far_ref.at[sc[row, which], pl.ds(k * half, half)]
                copies.append(fetch(near_ref.at[pl.ds(k * half, half)], target, sem.at[len(copies)]))
        out[...] = low_v[pl.ds(aligned(sc[row, CORE] * half), half), :]
        for copy in copies:
            copy.wait()


def backward_join_kernel(row, sc, own_ref, other_ref, h_ref, g_ref, ng_ref, *rest):
    out, e_hbm, low_v, sem = rest[-4:]
    half = out.shape[0]

    @pl.when(sc[row, VALID] == 1)
    def _():
        copies = []
        for k in range(2):
            rows = slice(k * half, (k + 1) * half)
            gn = own_ref[rows].astype(F32) + other_ref[rows].astype(F32)
            h = h_ref[rows].astype(F32)
            r = lax.rsqrt(jnp.mean(h * h, axis=1, keepdims=True) + EPSILON)
            t = gn * ng_ref[...]
            m = jnp.mean(h * t, axis=1, keepdims=True)
            low_v[rows] = (g_ref[rows].astype(F32) + r * (t - h * (r * r * m))).astype(BF16)
            target = e_hbm.at[sc[row, EDGE], pl.ds(k * half, half)]
            copies.append(fetch(low_v.at[pl.ds(k * half, half)], target, sem.at[k]))
        out[...] = low_v[pl.ds(aligned(sc[row, CORE] * half), half), :]
        for copy in copies:
            copy.wait()


def pick_kernel(first, sc, stack_hbm, out, sem):
    fetch(stack_hbm.at[first + sc[0, CORE]], out, sem.at[0]).wait()


ANY = pl.BlockSpec(memory_space=pl.ANY)
NEAR = pl.BlockSpec(memory_space=pltpu.VMEM)
SLOT, LEADING, FIRST, VALID, WRITE, EDGE, CORE = range(7)
LITTLE = pl.CostEstimate(flops=1 << 20, bytes_accessed=1 << 16, transcendentals=0)


def near(value):
    return pltpu.with_memory_space_constraint(value, pltpu.VMEM)


def away(value):
    return pltpu.with_memory_space_constraint(value, pltpu.HBM)


def chunk_call(kernel, table, free, far, close, close_outs, buffers, scratch, limit, name):
    inputs = [table, *free, *(away(v) for v in far), *(near(v) for v in close)]
    in_specs = [pl.BlockSpec(memory_space=pltpu.SMEM)]
    in_specs += [ANY] * (len(free) + len(far)) + [NEAR] * len(close)
    outs = [pltpu.VMEM(*o) for o in close_outs]
    out_specs = [NEAR] * len(close_outs)
    aliases = {}
    for held, shape, dtype in buffers:
        if held is not None:
            aliases[len(inputs)] = len(outs)
            inputs.append(away(held))
            in_specs.append(ANY)
        outs.append(pltpu.HBM(shape, dtype))
        out_specs.append(ANY)
    results = pl.pallas_call(
        kernel,
        in_specs=in_specs,
        out_specs=out_specs,
        out_shape=outs,
        scratch_shapes=scratch,
        input_output_aliases=aliases,
        compiler_params=pltpu.CompilerParams(vmem_limit_bytes=limit << 20),
        cost_estimate=LITTLE,
        name=name,
    )(*inputs)
    return tuple(results[: len(close_outs)]), tuple(results[len(close_outs) :])


def forward_call(table, row, slots, x, arrived, params, carry, held):
    t = x.shape[0]
    held = held or (None,) * 7
    kinds = (
        ((t, D), BF16),
        ((t, D), BF16),
        ((t, OWN_PROJ), BF16),
        ((t, OWN), F32),
        ((t, OWN), BF16),
        ((STATE, OWN), F32),
        ((8, OWN_CONV), F32),
    )
    gain, convp, headp, chanp, win, wout = params
    outs, held = chunk_call(
        functools.partial(forward_kernel, row),
        table,
        (*arrived, x),
        (),
        (gain, convp, headp, chanp, *carry, win, wout),
        (((t, D + LANES), BF16), kinds[0], kinds[5], kinds[6]),
        [(b, (slots,) + k, d) for b, (k, d) in zip(held, kinds)],
        [pltpu.VMEM(*k) for k in kinds[1:]]
        + [
            pltpu.VMEM((t + 8, OWN_CONV), F32),
            pltpu.VMEM((LANES, t), F32),
            pltpu.VMEM((t, LANES), F32),
            pltpu.VMEM((t, t), F32),
            pltpu.SemaphoreType.DMA((8,)),
        ],
        FORWARD_VMEM,
        "forward_chunk",
    )
    return outs[0], outs[1], outs[2:], held


def backward_call(table, row, slots, cot, arrived, saved, params, carry, held):
    t = cot.shape[0]
    held = held or (None, None)
    _, convp, headp, chanp, win, wout = params
    wide, projected = ((t, D), BF16), ((t, OWN_PROJ), BF16)
    outs, held = chunk_call(
        functools.partial(backward_kernel, row),
        table,
        (*arrived, cot),
        saved,
        (convp, headp, chanp, *carry, win, wout),
        [wide] * 3 + [(v.shape, v.dtype) for v in carry],
        [(held[0], (slots, t, OWN_PROJ), BF16), (held[1], (slots, t, D), BF16)],
        [
            pltpu.VMEM(*projected),
            pltpu.VMEM((t, OWN), F32),
            pltpu.VMEM((STATE, OWN), F32),
            pltpu.VMEM((8, OWN_CONV), F32),
            pltpu.VMEM(*wide),
            pltpu.VMEM((t, LANES), F32),
            pltpu.VMEM(*projected),
            pltpu.VMEM(*wide),
            pltpu.VMEM(*wide),
            pltpu.VMEM((t + 8, OWN_CONV), F32),
            pltpu.VMEM((t + 8, OWN_CONV), F32),
            pltpu.VMEM((LANES, t), F32),
            pltpu.VMEM((t, OWN), F32),
            pltpu.VMEM((t, t), F32),
            pltpu.VMEM((t, t), F32),
            pltpu.VMEM((t, STATE), F32),
            pltpu.VMEM((t, STATE), F32),
            pltpu.SemaphoreType.DMA((11,)),
        ],
        BACKWARD_VMEM,
        "backward_chunk",
    )
    return outs[:3], outs[3:], held


def forward_join(table, row, slots, own, other, h, held):
    t = h.shape[0]
    held = held or (None,) * 3
    wide, thin = ((t, D), BF16), ((t, LANES), F32)
    outs, held = chunk_call(
        functools.partial(forward_join_kernel, row),
        table,
        (),
        (),
        (own, other, h),
        [((t // 2, D), BF16)],
        [(b, (slots,) + k, d) for b, (k, d) in zip(held, (wide, thin, wide))],
        [pltpu.VMEM(*k) for k in (wide, thin, wide)] + [pltpu.SemaphoreType.DMA((6,))],
        JOIN_VMEM,
        "forward_join",
    )
    return outs[0], held


def backward_join(table, row, own, other, h, g, gain, edge_held):
    slots, t, _ = edge_held.shape
    outs, held = chunk_call(
        functools.partial(backward_join_kernel, row),
        table,
        (),
        (),
        (own, other, h, g, gain),
        [((t // 2, D), BF16)],
        [(edge_held, (slots, t, D), BF16)],
        [pltpu.VMEM((t, D), BF16), pltpu.SemaphoreType.DMA((2,))],
        JOIN_VMEM,
        "backward_join",
    )
    return outs[0], held[0]


def pick(table, stack, first):
    outs, _ = chunk_call(
        functools.partial(pick_kernel, first),
        table,
        (),
        (stack,),
        (),
        [(stack.shape[1:], stack.dtype)],
        [],
        [pltpu.SemaphoreType.DMA((1,))],
        JOIN_VMEM,
        "pick",
    )
    return outs[0]


def own_of(values, core):
    lead, width = values.shape[:-1], values.shape[-1]
    blocks = values.reshape(lead + (4, 2, width // 8))
    return lax.dynamic_index_in_dim(blocks, core, len(lead) + 1, False).reshape(
        lead + (width // 2,)
    )


def woven(halves):
    width = halves.shape[-1]
    lead = halves.shape[1:-1]
    blocks = halves.reshape((2,) + lead + (4, width // 4))
    return jnp.moveaxis(blocks, 0, -2).reshape(lead + (2 * width,))


def small_params(norm_gain, conv_weight, conv_bias, dt_bias, a_log, skip_gain, gate_gain, core):
    own = functools.partial(own_of, core=core)
    taps = jnp.concatenate([conv_weight.T, conv_bias[None]], axis=0).astype(F32)
    taps = jnp.concatenate([own(taps[:, :INNER]), taps[:, INNER:]], axis=1)
    convp = jnp.pad(taps, ((0, 3), (0, 0)))
    heads = jnp.stack([own(dt_bias.astype(F32)), -jnp.exp(own(a_log.astype(F32)))])
    headp = jnp.pad(heads, ((0, 6), (0, LANES - OWN_HEADS)))
    skip = jnp.repeat(own(skip_gain.astype(F32)), HEAD_DIM)
    chanp = jnp.pad(jnp.stack([skip, own(gate_gain.astype(F32))]), ((0, 6), (0, 0)))
    return norm_gain.astype(F32)[None], convp, headp, chanp


def own_steps(weight, core):
    own = own_of(weight[INNER + CONV_CH :].T, core).T
    return jnp.pad(own, ((0, 2 * LANES - OWN_HEADS), (0, 0)))


HALF = OWN // 2
BLOCK = HALF // 2
PACKED_ROWS = HALF + HALF + 2 * STATE + 2 * BLOCK
PARTS = (
    ("in", HALF, X_AT, HALF),
    ("in", HALF, 0, HALF),
    ("in", 2 * STATE, BC_AT, 2 * STATE),
    ("out", BLOCK, 0, HALF),
    ("out", BLOCK, BLOCK, HALF),
)


def ring_place(position, count):
    back = position >= count
    return jnp.where(back, 1, 0), jnp.where(back, 2 * count - 1 - position, position)


def ring_route(count, step):
    def index(position):
        return position if position < count else count + (2 * count - 1 - position)

    size = 2 * count
    return [(index(p), index((p + step) % size)) for p in range(size)]


HALF_ROWS = PACKED_ROWS // 2


def cut(at, rows):
    spans = []
    for i in range(2):
        a, b = max(at, i * HALF_ROWS), min(at + rows, (i + 1) * HALF_ROWS)
        if a < b:
            spans.append((i, a - i * HALF_ROWS, a - at, b - a))
    return spans


def pack_kernel(sc, w, steps, o, own_a, own_b, rest_a, rest_b, sem):
    core, side = sc[0], sc[1]
    copies = []
    for targets, y in (((own_a, own_b), side), ((rest_a, rest_b), 1 - side)):
        at = 0
        for base in (INNER, 0):
            for k in range(2):
                first = base + (2 * y + k) * HALF + core * BLOCK
                for i, to, off, rows in cut(at, BLOCK):
                    source = w.at[pl.ds(aligned(first + off), rows)]
                    copies.append(fetch(source, targets[i].at[pl.ds(to, rows)], sem.at[len(copies)]))
                at += BLOCK
        bc = w.at[pl.ds(2 * INNER, 2 * STATE)]
        ((i, to, _, rows),) = cut(at, 2 * STATE)
        span = targets[i].at[pl.ds(to, rows)]
        copies.append(fetch_one_of(y == 0, bc, steps, span, sem.at[len(copies)]))
        at += 2 * STATE
        for k in range(2):
            ((i, to, _, rows),) = cut(at, BLOCK)
            cols = pl.ds(aligned(y * HALF + k * BLOCK), BLOCK)
            source = o.at[pl.ds(aligned(core * BLOCK), BLOCK), cols]
            copies.append(fetch(source, targets[i].at[pl.ds(to, rows)], sem.at[len(copies)]))
            at += BLOCK
    for copy in copies:
        copy.wait()


def pack_weights(scalars, w, steps, o):
    return pl.pallas_call(
        pack_kernel,
        in_specs=[pl.BlockSpec(memory_space=pltpu.SMEM), ANY, ANY, ANY],
        out_specs=[NEAR, NEAR, NEAR, NEAR],
        out_shape=[pltpu.VMEM((HALF_ROWS, BLOCK), BF16)] * 4,
        scratch_shapes=[pltpu.SemaphoreType.DMA((16,))],
        compiler_params=pltpu.CompilerParams(vmem_limit_bytes=4 << 20),
        cost_estimate=LITTLE,
        name="pack_weights",
    )(scalars, away(w), steps, away(o))


def put_block(sc, halves, z, y, win, wout, sem, start):
    lanes = pl.ds(aligned(z * BLOCK), BLOCK)
    copies, at = [], 0
    for matrix, rows, first, step in PARTS:
        for i, to, off, count in cut(at, rows):
            if matrix == "in":
                target = win.at[pl.ds(aligned(first + y * step + off), count), lanes]
            else:
                target = wout.at[lanes, pl.ds(aligned(first + y * step), BLOCK)]
            source = halves[i].at[pl.ds(to, count)]
            copies.append(fetch(source, target, sem.at[start + len(copies)]))
        at += rows
    return copies


def place_kernel(which, sc, *refs):
    win, wout, sem = refs[-3:]
    blocks = [refs[2 * i : 2 * i + 2] for i in range(8 if which == 0 else 4)]
    side, place = sc[1], sc[2]
    inner = jnp.logical_and(place > 0, place < 3)

    def put(number, block, z, y):
        return put_block(sc, blocks[block], z, y, win, wout, sem, 8 * number)

    always = []
    if which == 0:
        beside = place + 1 - 2 * lax.rem(place, 2)
        always += put(0, 0, place, side) + put(1, 1, place, 1 - side)
        always += put(2, 2, beside, side) + put(3, 3, beside, 1 - side)
        from_z, first = jnp.where(inner, 3 - place, jnp.where(place == 0, 2, 1)), 4
    else:
        from_z, first = jnp.where(place < 2, 3, 0), 0

    def rest(block):
        copies = put(4, block, from_z, side) + put(5, block + 1, from_z, 1 - side)
        for copy in copies:
            copy.wait()

    @pl.when(inner)
    def _():
        rest(first)

    @pl.when(jnp.logical_not(inner))
    def _():
        rest(first + 2)

    for copy in always:
        copy.wait()


def place_weights(here, blocks, held):
    inputs = [here] + [away(half) for block in blocks for half in block]
    in_specs = [pl.BlockSpec(memory_space=pltpu.SMEM)] + [ANY] * (len(inputs) - 1)
    aliases = {}
    if held is not None:
        aliases = {len(inputs): 0, len(inputs) + 1: 1}
        inputs += [near(v) for v in held]
        in_specs += [NEAR, NEAR]
    return pl.pallas_call(
        functools.partial(place_kernel, 0 if held is None else 1),
        in_specs=in_specs,
        out_specs=[NEAR, NEAR],
        out_shape=[pltpu.VMEM((OWN_PROJ, D), BF16), pltpu.VMEM((OWN, D), BF16)],
        scratch_shapes=[pltpu.SemaphoreType.DMA((48,))],
        input_output_aliases=aliases,
        compiler_params=pltpu.CompilerParams(vmem_limit_bytes=4 << 20),
        cost_estimate=LITTLE,
        name="place_weights",
    )(*inputs)


def line_gather(own, beside):
    def along(value, hops):
        path = [(y * 4 + a, y * 4 + b) for y in range(2) for a, b in hops]
        return lax.ppermute(value, ("y", "fsdp"), path)

    def across(value, places):
        path = [(y * 4 + z, (1 - y) * 4 + z) for y in range(2) for z in places]
        return lax.ppermute(value, ("y", "fsdp"), path)

    pair, middle, outward = [(0, 1), (1, 0), (2, 3), (3, 2)], [(1, 2), (2, 1)], [(1, 0), (2, 3)]
    inner, outer = (1, 2), (0, 3)
    barrier = lax.optimization_barrier
    a, b = own
    near_a, in2_a = along(a, pair), along(a, middle)
    near_a, in2_a, b = barrier((near_a, in2_a, b))
    near_b, in2_b, near_ya = along(b, pair), along(b, middle), across(near_a, range(4))
    near_a, in2_a, near_b, in2_b, near_ya, *beside = barrier(
        (near_a, in2_a, near_b, in2_b, near_ya, *beside)
    )
    out2_a, in3_a, near_yb = along(in2_a, outward), along(near_a, middle), across(near_b, range(4))
    out2_a, in3_a, near_yb, in2_a, near_b, in2_b = barrier(
        (out2_a, in3_a, near_yb, in2_a, near_b, in2_b)
    )
    out2_b, in3_b = along(in2_b, outward), along(near_b, middle)
    out2_ya, in2_ya = across(out2_a, outer), across(in2_a, inner)
    out2_b, in3_b, out2_ya, in2_ya, in3_a, in2_b = barrier(
        (out2_b, in3_b, out2_ya, in2_ya, in3_a, in2_b)
    )
    ready = in2_ya
    out3_a = along(in3_a, outward)
    out2_yb, in2_yb = across(out2_b, outer), across(in2_b, inner)
    out3_a, out2_yb, in2_yb, in3_a, in3_b = barrier((out3_a, out2_yb, in2_yb, in3_a, in3_b))
    out3_b = along(in3_b, outward)
    out3_ya, in3_ya = across(out3_a, outer), across(in3_a, inner)
    out3_b, out3_ya, in3_ya, in3_b = barrier((out3_b, out3_ya, in3_ya, in3_b))
    out3_yb, in3_yb = across(out3_b, outer), across(in3_b, inner)
    blocks = [
        (near_a, near_b),
        (near_ya, near_yb),
        (in2_a, in2_b),
        (in2_ya, in2_yb),
        (out2_a, out2_b),
        (out2_ya, out2_yb),
        (in3_a, in3_b),
        (in3_ya, in3_yb),
        (out3_a, out3_b),
        (out3_ya, out3_yb),
    ]
    return blocks, beside, ready


GROUPS = (
    (1, (HALF, X_AT, HALF), (LANES, BC_AT, 2 * STATE)),
    (-1, (HALF, 0, HALF), (LANES, BC_AT + LANES, 2 * STATE)),
)


SMALL_ROWS = 16
IN_ROWS = HALF + LANES
GROUP_ROWS = IN_ROWS + BLOCK


def block_grad_kernel(row, sc, normed_ref, q_ref, gs_ref, *refs):
    out = refs[-1]
    chunks = normed_ref.shape[0]
    at = 0
    for ref in refs[:2]:
        width = ref.shape[2]
        value = sum(dot_tn(ref[k], normed_ref[k]) for k in range(chunks))
        out[at : at + width, :] = value.astype(BF16)
        at += width
    out[at:, :] = sum(dot_tn(q_ref[k], gs_ref[k]) for k in range(chunks)).astype(BF16)
    if len(refs) > 3:

        @pl.when(sc[row, 0] == 1)
        def _():
            out[HALF : HALF + SMALL_ROWS, :] = refs[2][0].astype(BF16)


def block_grad(table, row, group, normed_held, grads_held, q_held, gs_held, small):
    slots, t, _ = normed_held.shape
    number, (_, *parts) = group, GROUPS[group]

    def block(width, index):
        return pl.BlockSpec((slots - 1, t, width), lambda i, s: (0, 0, index(s)))

    in_specs = [
        block(BLOCK, lambda s: s[row, 1]),
        block(BLOCK, lambda s: s[row, 1]),
        block(BLOCK, lambda s: 2 * s[row, 0] + number),
    ]
    for width, first, step in parts:

        def index(s, width=width, first=first, step=step):
            return first // width + s[row, 0] * (step // width)

        in_specs.append(block(width, index))
    extra = []
    if number == 1:
        extra = [small]
        in_specs.append(pl.BlockSpec((1, SMALL_ROWS, BLOCK), lambda i, s: (s[row, 1], 0, 0)))
    return pl.pallas_call(
        functools.partial(block_grad_kernel, row),
        grid_spec=pltpu.PrefetchScalarGridSpec(
            num_scalar_prefetch=1,
            grid=(1,),
            in_specs=in_specs,
            out_specs=pl.BlockSpec((GROUP_ROWS, BLOCK), lambda i, s: (0, 0)),
        ),
        out_shape=jax.ShapeDtypeStruct((GROUP_ROWS, BLOCK), BF16),
        compiler_params=pltpu.CompilerParams(vmem_limit_bytes=24 << 20),
        cost_estimate=LITTLE,
        name="block_grad",
    )(
        table,
        away(normed_held),
        away(q_held),
        away(gs_held),
        *([away(grads_held)] * len(parts)),
        *extra,
    )


def grads_kernel(sc, *refs):
    in_hbm, out_hbm, small_out, in_v, out_v, sem = refs[-6:]
    core, side = sc[0], sc[1]

    def block(i, c, y, rows):
        own, across, other, far = refs[4 * i : 4 * i + 4]
        here = jnp.where(side == y, own[rows], across[rows])
        there = jnp.where(side == y, other[rows], far[rows])
        return jnp.where(core == c, here, there).astype(F32)

    copies = []

    def store(values, near_ref, far_ref, at):
        near_ref[at : at + values.shape[0]] = values
        span = pl.ds(at, values.shape[0])
        copies.append(fetch(near_ref.at[span], far_ref.at[span], sem.at[len(copies)]))

    for i, base in ((0, INNER), (1, 0)):
        for c in range(2):
            for y in range(2):
                for k in range(2):
                    rows = slice(k * BLOCK, (k + 1) * BLOCK)
                    store(block(i, c, y, rows), in_v, in_hbm, base + (2 * y + k) * HALF + c * BLOCK)
    rows = slice(HALF, HALF + STATE)
    for i in range(2):
        store(block(i, 0, 0, rows) + block(i, 1, 0, rows), in_v, in_hbm, 2 * INNER + i * STATE)
    steps = [block(0, c, 1, slice(HALF, HALF + 32)) for c in range(2)]
    steps = [steps[c][z * 6 : z * 6 + 6] for z in range(4) for c in range(2)]
    store(jnp.concatenate(steps, axis=0), in_v, in_hbm, INNER + CONV_CH)
    rows = slice(HALF, HALF + SMALL_ROWS)
    small_out[...] = block(1, 0, 1, rows) + block(1, 1, 1, rows)
    rows = slice(IN_ROWS, GROUP_ROWS)
    for c in range(2):
        values = [block(i, c, y, rows) for y in range(2) for i in range(2)]
        store(jnp.concatenate(values, axis=1), out_v, out_hbm, c * BLOCK)
    for copy in copies:
        copy.wait()


def join_grads(scalars, parts):
    arrays = [near(a) for part in parts for a in part]
    height = INNER + CONV_CH + HEADS
    shapes = ((height, BLOCK), F32), ((2 * BLOCK, D), F32)
    return pl.pallas_call(
        grads_kernel,
        in_specs=[pl.BlockSpec(memory_space=pltpu.SMEM)] + [NEAR] * len(arrays),
        out_specs=[ANY, ANY, NEAR],
        out_shape=[pltpu.HBM(*k) for k in shapes] + [pltpu.VMEM((SMALL_ROWS, BLOCK), F32)],
        scratch_shapes=[pltpu.VMEM(*k) for k in shapes] + [pltpu.SemaphoreType.DMA((24,))],
        compiler_params=pltpu.CompilerParams(vmem_limit_bytes=28 << 20),
        cost_estimate=LITTLE,
        name="join_grads",
    )(scalars, *arrays)


def swap(value, axis):
    return lax.ppermute(value, axis, [(0, 1), (1, 0)])


def sent_along(value, axis):
    size = lax.axis_size(axis)
    routes = [[(i, (i + k) % size) for i in range(size)] for k in range(1, size)]
    return [lax.ppermute(value, axis, path) for path in routes]


def in_order(value, others, axis):
    size, place = len(others) + 1, lax.axis_index(axis)
    ring = jnp.stack([*others[::-1], value] * 2)
    return lax.dynamic_slice_in_dim(ring, (size - 1 - place) % size, size, 0)


LAG = 2


def relay_shards(
    ends,
    norm_gain,
    input_weight,
    conv_weight,
    conv_bias,
    dt_bias,
    a_log,
    skip_gain,
    gate_gain,
    output_weight,
):
    core = lax.axis_index("core")
    place = lax.axis_index("fsdp")
    side = lax.axis_index("y")
    section = lax.axis_index("section")
    leading = (section == 0).astype(jnp.int32)
    local = ends[0][:, 0]
    t = local.shape[1]
    chunks = lax.axis_size("fsdp")
    micro = place // 2

    small = [norm_gain[0], conv_weight[0].reshape(-1), conv_bias[0], dt_bias[0], a_log[0]]
    small += [skip_gain[0], gate_gain[0]]
    packed = jnp.concatenate(small)
    others = sent_along(packed, "fsdp")
    w = input_weight[0].T
    steps = own_steps(w, core)
    here = jnp.stack([core, side, place]).astype(jnp.int32)
    packed_halves = pack_weights(here, w, steps, output_weight[0])
    blocks, others, ready = line_gather(packed_halves[:2], others)
    packed = in_order(packed, others, "fsdp")
    pieces, at = [], 0
    for member in small:
        pieces.append(packed[:, at : at + member.shape[0]].reshape(-1))
        at += member.shape[0]
    pieces[1] = pieces[1].reshape(CONV_CH, KERNEL)
    gain, convp, headp, chanp = small_params(*pieces, core)
    local, _ = lax.optimization_barrier((local, ready))

    def route(first, m):
        return [
            (c * chunks + z, (z % 2) * chunks + 2 * m + c)
            for c in range(2)
            for z in (first, first + 1)
        ]

    def bring(first):
        return [lax.ppermute(local[m], ("core", "fsdp"), route(first, m)) for m in range(2)]

    def shared(got):
        got = jnp.where(micro == 0, got[0], got[1])
        other = swap(got, "core")
        return [jnp.where(core == 0, got, other), jnp.where(core == 0, other, got)]

    def give(piece, first):
        return [
            lax.ppermute(piece, ("core", "fsdp"), [(b, a) for a, b in route(first, m)])
            for m in range(2)
        ]

    matrices = place_weights(here, [packed_halves[:2], packed_halves[2:], *blocks[:6]], None)
    last = (blocks[7][1], blocks[9][1])
    here, *got = lax.optimization_barrier((here, *bring(0), *bring(2), *last, *matrices))
    blocks[7], blocks[9] = (blocks[7][0], got[4]), (blocks[9][0], got[5])
    pieces = shared(got[:2]) + shared(got[2:4])
    win, wout = place_weights(here, blocks[6:], got[6:])
    params = (gain, convp, headp, chanp, win, wout)

    def scalars(moment, lag, reverse):
        begin = jnp.where(leading == 1, lag if reverse else 0, 0 if reverse else lag)
        step = moment - begin
        valid = jnp.logical_and(step >= 0, step < chunks)
        inside = jnp.clip(step, 0, chunks - 1)
        chunk = chunks - 1 - inside if reverse else inside
        write = jnp.where(valid, chunk, chunks)
        edge_here = leading == 1 if reverse else leading == 0
        edge = jnp.where(jnp.logical_and(valid, edge_here), chunk, chunks)
        values = [chunk if reverse else write, leading, step == 0, valid, write, edge, core]
        return [jnp.asarray(v, jnp.int32) for v in values]

    moments = chunks + LAG
    table = [scalars(moment, LAG, False) for moment in range(moments)]
    table += [scalars(moment, LAG, True) for moment in range(moments)]
    table = jnp.stack(sum(table, [])).reshape(len(table), -1)
    size = 2 * chunks
    position = jnp.where(side == 0, place, size - 1 - place).astype(jnp.int32)
    owners = []
    for direction in (1, -1):
        for hop in range(size):
            owners += ring_place((position - direction * (1 + hop)) % size, chunks)
    owners = jnp.stack(owners).reshape(2 * size, 2).astype(jnp.int32)
    table, owners = lax.optimization_barrier((table, owners))

    state, tail = jnp.zeros((STATE, OWN), F32), jnp.zeros((8, OWN_CONV), F32)
    blank = jnp.zeros((t, D), BF16)
    held, joined, result = None, None, None
    moved, incoming = {}, {}
    for moment in range(moments):
        if moment > 0:
            tail, result = lax.optimization_barrier((tail, result))
            if moment - 1 < chunks:
                moved[moment - 1] = lax.ppermute(result, "section", [(0, 1)])
        arrived = incoming.get(moment - LAG, (blank[: t // 2],) * 2)
        partial, h, (state, tail), held = forward_call(
            table,
            moment,
            chunks + 1,
            pieces[min(moment, chunks - 1)],
            arrived,
            params,
            (state, tail),
            held,
        )
        if moment - 1 in moved:
            partial, got = lax.optimization_barrier((partial, moved[moment - 1]))
            incoming[moment - 1] = (got, swap(got, "core"))
        other = swap(partial, "core")
        result, joined = forward_join(table, moment, chunks + 1, partial, other, h, joined)
    h_held, normed_held, pr_held, mx_held, q_held, st_held, tl_held = held
    y_held, ri_held, edge_held = joined
    saved = (h_held, normed_held, pr_held, mx_held, st_held, tl_held, y_held, ri_held)

    def tokens(buffer):
        return buffer[:chunks].reshape(chunks * t, buffer.shape[-1])

    carry = (
        jnp.zeros((STATE, OWN), F32),
        jnp.zeros((8, OWN_CONV), F32),
        jnp.zeros((8, OWN), F32),
        jnp.zeros((16, OWN_CONV), F32),
    )
    grads_held = None
    moved, incoming = {}, {}
    for moment in range(moments):
        if moment > 0:
            *carry, acc = carry
            acc, result = lax.optimization_barrier((acc, result))
            carry = (*carry, acc)
            if moment - 1 < chunks:
                moved[moment - 1] = lax.ppermute(result, "section", [(1, 0)])
        arrived = incoming.get(moment - LAG, (blank[: t // 2],) * 2)
        cot = pieces[max(chunks - 1 - moment, 0)]
        (partial, g, h), carry, grads_held = backward_call(
            table, moments + moment, chunks + 1, cot, arrived, saved, params, carry, grads_held
        )
        if moment - 1 in moved:
            partial, got = lax.optimization_barrier((partial, moved[moment - 1]))
            incoming[moment - 1] = (got, swap(got, "core"))
        other = swap(partial, "core")
        result, edge_held = backward_join(
            table, moments + moment, partial, other, h, g, gain, edge_held
        )

    def both(own, other, index):
        return jnp.where(index == 0, jnp.stack([own, other]), jnp.stack([other, own]))

    acc = carry[3]

    def placed(own):
        zero = jnp.zeros_like(own)
        return woven(both(own, zero, core))

    taps = jnp.concatenate([placed(acc[:5, :OWN]), acc[:5, OWN:]], axis=1)
    taps = jnp.moveaxis(taps.reshape(KERNEL + 1, chunks, -1), 1, 0)
    skip = acc[5, :OWN].reshape(OWN_HEADS, HEAD_DIM).sum(axis=1)
    vectors = [
        acc[9, :D] / gain[0],
        taps,
        placed(acc[7, :OWN_HEADS]),
        placed(acc[8, :OWN_HEADS]),
        placed(skip),
        placed(acc[6, :OWN]),
    ]
    vectors = [v.reshape(chunks, -1) for v in vectors]
    small = jnp.concatenate(vectors, axis=1)
    small = jnp.pad(small, ((0, 0), (0, SMALL_ROWS * BLOCK - small.shape[1])))
    small = small.reshape(chunks, SMALL_ROWS, BLOCK)

    onward, back = ring_route(chunks, 1), ring_route(chunks, -1)
    grads_held, gs_held = grads_held
    sums = [None] * len(GROUPS)
    for hop in range(size):
        if hop > 0:
            owners, *sums = lax.optimization_barrier((owners, *sums))
        for i, (direction, *_) in enumerate(GROUPS):
            row = hop + (0 if direction == 1 else size)
            block = block_grad(owners, row, i, normed_held, grads_held, q_held, gs_held, small)
            if hop > 0:
                path = onward if direction == 1 else back
                came = lax.ppermute(sums[i], ("y", "fsdp"), path).astype(F32)
                block = (block.astype(F32) + came).astype(BF16)
            sums[i] = block
        if hop == 3:
            owners, edge_held = lax.optimization_barrier((owners, edge_held))
        if hop == 5:
            finished = pick(table, edge_held, 0), pick(table, edge_held, 2)
            owners, *finished = lax.optimization_barrier((owners, *finished))
    *sums, early, late = lax.optimization_barrier((*sums, *finished))

    edges = jnp.where(place < 2, jnp.stack(give(early, 0)), jnp.stack(give(late, 2)))
    edges = edges[None, :, None]
    parts = []
    for own in sums:
        across = swap(own, "y")
        parts.append((own, across, swap(own, "core"), swap(across, "core")))
    here = jnp.stack([core, side]).astype(jnp.int32)
    here, edges = lax.optimization_barrier((here, edges))
    in_grad, out_grad, summed = join_grads(here, parts)
    in_grad = in_grad.T
    summed = summed.reshape(-1)
    grads, at = [], 0
    for v in vectors:
        grads.append(summed[at : at + v.shape[1]][None])
        at += v.shape[1]
    taps = grads[1].reshape(KERNEL + 1, -1)
    grads[1:2] = taps[:KERNEL].T[None], taps[KERNEL:]
    return (
        edges,
        grads[0],
        in_grad[None],
        grads[1],
        grads[2],
        grads[3],
        grads[4],
        grads[5],
        grads[6],
        out_grad[None],
    )


def shifted(block, axis, distance):
    devices = range(lax.axis_size(axis))
    route = [(i - distance, i) for i in devices if i - distance in devices]
    return lax.ppermute(block, axis, route)


def prefix(value, axis, join, neutral):
    place = lax.axis_index(axis)
    gathered = jax.tree.map(
        lambda a, kind: lax.all_gather(a.astype(kind), axis), value, (jnp.bfloat16, jnp.bfloat16)
    )
    state = jax.tree.map(lambda a, e: jnp.zeros_like(a) + jnp.asarray(e, a.dtype), value, neutral)

    def one(turn, state):
        return join(
            state,
            jax.tree.map(
                lambda a, own: lax.dynamic_index_in_dim(a, turn, 0, False).astype(own.dtype),
                gathered,
                value,
            ),
        )

    return lax.fori_loop(0, place, one, state)


def prefix_2(value, axis, join, neutral):
    count = lax.axis_size(axis)
    place = lax.axis_index(axis)
    ahead = count - 1 - place
    gathered = jax.tree.map(
        lambda a, kind: lax.all_gather(a.astype(kind), axis),
        value,
        jax.tree.map(lambda a: jnp.bfloat16 if a.dtype == jnp.float32 else a.dtype, value),
    )
    state = jax.tree.map(lambda a, e: jnp.zeros_like(a) + jnp.asarray(e, a.dtype), value, neutral)

    def one(turn, state):
        source = count - 1 - turn
        return join(
            state,
            jax.tree.map(
                lambda a, own: lax.dynamic_index_in_dim(a, source, 0, False).astype(own.dtype),
                gathered,
                value,
            ),
        )

    return lax.fori_loop(0, ahead, one, state)


def rms_scale(values, scale_gain):
    return (
        values * lax.rsqrt(jnp.mean(values * values, axis=-1, keepdims=True) + EPSILON) * scale_gain
    )


def chain_rule(earlier, later_part):
    return (
        earlier[0] * later_part[0],
        later_part[1] + later_part[0][:, :, None, None] * earlier[1],
    )


def conv_features(widened, conv_weight, conv_bias, dt_raw, dt_bias, a_log):
    tap_count = conv_weight.shape[1]
    step_count = widened.shape[1] - tap_count + 1
    convolved = conv_bias
    for offset in range(tap_count):
        convolved = convolved + widened[:, offset : offset + step_count, :] * conv_weight[:, offset]
    activated = jax.nn.silu(convolved)
    x_heads = activated[..., :INNER]
    b_rows = activated[..., INNER : INNER + STATE]
    c_rows = activated[..., INNER + STATE :]
    dt_step = jax.nn.softplus(dt_raw + dt_bias)
    log_decay = jnp.cumsum(-jnp.exp(a_log) * dt_step, axis=1)
    return (x_heads, b_rows, c_rows, dt_step, log_decay)


def local_states(x_heads, b_rows, dt_step, log_decay):
    seq_count, length = (x_heads.shape[0], x_heads.shape[1])
    spread = x_heads.reshape(seq_count, length, HEADS, HEAD_DIM)
    weights = jnp.exp(log_decay[:, -1:, :] - log_decay) * dt_step
    weighted = spread * weights[..., None]
    states = jnp.einsum("sqhd,sqn->shdn", weighted, b_rows, precision=EXACT_MATMUL)
    return (jnp.exp(log_decay[:, -1]), states)


def gated_output(
    x_heads, b_rows, c_rows, dt_step, log_decay, prior_state, gate_z, skip_gain, gate_gain
):
    seq_count, length = (x_heads.shape[0], x_heads.shape[1])
    spread = x_heads.reshape(seq_count, length, HEADS, HEAD_DIM)
    scaled = spread * dt_step[..., None]
    by_head = jnp.transpose(log_decay, (0, 2, 1))
    differ = by_head[:, :, :, None] - by_head[:, :, None, :]
    causal = jnp.arange(length)[:, None] >= jnp.arange(length)[None, :]
    mixing = jnp.where(causal, jnp.exp(jnp.where(causal, differ, 0.0)), 0.0)
    intersections = jnp.einsum("sqn,skn->sqk", c_rows, b_rows, precision=EXACT_MATMUL)
    mixed_out = jnp.einsum(
        "shqk,skhd->sqhd", mixing * intersections[:, None], scaled, precision=EXACT_MATMUL
    )
    mixed_out = mixed_out + jnp.exp(log_decay)[..., None] * jnp.einsum(
        "sqn,shdn->sqhd", c_rows, prior_state, precision=EXACT_MATMUL
    )
    mixed_out = (mixed_out + skip_gain[:, None] * spread).reshape(seq_count, length, INNER)
    return rms_scale(mixed_out * jax.nn.silu(gate_z), gate_gain)


def layer_forward(hidden, weights):
    (
        norm_gain,
        input_weight,
        conv_weight,
        conv_bias,
        dt_bias,
        a_log,
        skip_gain,
        gate_gain,
        output_weight,
    ) = weights
    normalized_rows = rms_scale(hidden, norm_gain.astype(jnp.float32)).astype(jnp.bfloat16)
    projected_rows = jnp.einsum(
        "spd,de->spe", normalized_rows, input_weight, preferred_element_type=jnp.float32
    ).astype(jnp.bfloat16)
    length = hidden.shape[1]
    xbc_part = projected_rows[..., INNER : INNER + CONV_CH]
    border = shifted(xbc_part[:, length - KERNEL + 1 :, :], "fsdp", 1)
    widened = jnp.concatenate([border, xbc_part], axis=1)
    features = conv_features(
        widened.astype(jnp.float32),
        conv_weight.astype(jnp.float32),
        conv_bias.astype(jnp.float32),
        projected_rows[..., INNER + CONV_CH :].astype(jnp.float32),
        dt_bias.astype(jnp.float32),
        a_log.astype(jnp.float32),
    )
    decays, states = local_states(features[0], features[1], features[3], features[4])
    scanned = prefix(
        (decays, states), "fsdp", chain_rule, (jnp.ones_like(decays), jnp.zeros_like(states))
    )
    prior_state = scanned[1]
    gated_result = gated_output(
        features[0],
        features[1],
        features[2],
        features[3],
        features[4],
        prior_state,
        projected_rows[..., :INNER].astype(jnp.float32),
        skip_gain.astype(jnp.float32),
        gate_gain.astype(jnp.float32),
    )
    gated_low = gated_result.astype(jnp.bfloat16)
    final_result = hidden + jnp.einsum(
        "spi,id->spd", gated_low, output_weight, preferred_element_type=jnp.float32
    )
    return (
        final_result,
        (hidden, normalized_rows, projected_rows, widened, prior_state, gated_low),
    )


def layer_backward(gradient, kept_state, weights):
    hidden, normalized_rows, projected_rows, widened, prior_state, gated_low = kept_state
    (
        norm_gain,
        input_weight,
        conv_weight,
        conv_bias,
        dt_bias,
        a_log,
        skip_gain,
        gate_gain,
        output_weight,
    ) = weights
    grad_low = gradient.astype(jnp.bfloat16)
    grad_out_weight = jnp.einsum(
        "spi,spd->id", gated_low, grad_low, preferred_element_type=jnp.float32
    )
    grad_gated = jnp.einsum(
        "spd,id->spi", grad_low, output_weight, preferred_element_type=jnp.float32
    )
    features, pull_features = jax.vjp(
        conv_features,
        widened.astype(jnp.float32),
        conv_weight.astype(jnp.float32),
        conv_bias.astype(jnp.float32),
        projected_rows[..., INNER + CONV_CH :].astype(jnp.float32),
        dt_bias.astype(jnp.float32),
        a_log.astype(jnp.float32),
    )
    _, pull_gated = jax.vjp(
        gated_output,
        features[0],
        features[1],
        features[2],
        features[3],
        features[4],
        prior_state,
        projected_rows[..., :INNER].astype(jnp.float32),
        skip_gain.astype(jnp.float32),
        gate_gain.astype(jnp.float32),
    )
    grads_gated = pull_gated(grad_gated)
    decay_states, pull_states = jax.vjp(
        local_states, features[0], features[1], features[3], features[4]
    )
    decays = decay_states[0]
    later_state = prefix_2(
        (decays, grads_gated[5]),
        "fsdp",
        chain_rule,
        (jnp.ones_like(decays), jnp.zeros_like(grads_gated[5])),
    )
    grad_end = later_state[1]
    state_parts = pull_states((jnp.sum(grad_end * prior_state, axis=(2, 3)), grad_end))
    feature_grads = (
        grads_gated[0] + state_parts[0],
        grads_gated[1] + state_parts[1],
        grads_gated[2],
        grads_gated[3] + state_parts[2],
        grads_gated[4] + state_parts[3],
    )
    grad_wide, grad_conv_w, grad_conv_b, grad_dt_raw, grad_dt_bias, grad_a_log = pull_features(
        feature_grads
    )
    margin = KERNEL - 1
    returned = shifted(grad_wide[:, :margin, :].astype(jnp.bfloat16), "fsdp", -1).astype(
        jnp.float32
    )
    own_rows = grad_wide[:, margin:, :]
    length = own_rows.shape[1]
    grad_xbc = jnp.concatenate(
        [own_rows[:, : length - margin], own_rows[:, length - margin :] + returned], axis=1
    )
    grad_proj = jnp.concatenate([grads_gated[6], grad_xbc, grad_dt_raw], axis=-1).astype(
        jnp.bfloat16
    )
    grad_in_weight = jnp.einsum(
        "spd,spe->de", normalized_rows, grad_proj, preferred_element_type=jnp.float32
    )
    grad_normed = jnp.einsum(
        "spe,de->spd", grad_proj, input_weight, preferred_element_type=jnp.float32
    )
    _, pull_norm = jax.vjp(rms_scale, hidden, norm_gain.astype(jnp.float32))
    grad_hidden, grad_norm_gain = pull_norm(grad_normed)
    return (
        gradient + grad_hidden,
        (
            grad_norm_gain,
            grad_in_weight,
            grad_conv_w,
            grad_conv_b,
            grad_dt_bias,
            grad_a_log,
            grads_gated[7],
            grads_gated[8],
            grad_out_weight,
        ),
    )


def shards(
    ends,
    norm_gain,
    input_weight,
    conv_weight,
    conv_bias,
    dt_bias,
    a_log,
    skip_gain,
    gate_gain,
    output_weight,
):
    gathered = (
        lax.all_gather(norm_gain, "fsdp", axis=1, tiled=True),
        lax.all_gather(input_weight, "fsdp", axis=1, tiled=True),
        lax.all_gather(conv_weight, "fsdp", axis=1, tiled=True),
        lax.all_gather(conv_bias, "fsdp", axis=1, tiled=True),
        lax.all_gather(dt_bias, "fsdp", axis=1, tiled=True),
        lax.all_gather(a_log, "fsdp", axis=1, tiled=True),
        lax.all_gather(skip_gain, "fsdp", axis=1, tiled=True),
        lax.all_gather(gate_gain, "fsdp", axis=1, tiled=True),
        lax.all_gather(output_weight, "fsdp", axis=1, tiled=True),
    )
    layer_weights = tuple((member[0] for member in gathered))
    leading = lax.axis_index("section") == 0
    local_data = ends[0].astype(jnp.float32)
    batches = local_data.shape[0]
    arrived = jnp.zeros(local_data.shape[1:], jnp.float32)
    stored = []
    produced = []
    for moment in range(batches + 1):
        source = jnp.where(leading, local_data[min(moment, batches - 1)], arrived)
        final_result, kept_state = layer_forward(source, layer_weights)
        stored.append(kept_state)
        produced.append(final_result)
        if moment < batches:
            arrived = shifted(final_result.astype(jnp.bfloat16), "section", 1).astype(jnp.float32)
    totals = None
    coming = jnp.zeros(local_data.shape[1:], jnp.float32)
    returned_grads = []
    for moment in range(batches + 1):
        gradient = jnp.where(leading, coming, local_data[min(moment, batches - 1)])
        kept_state = jax.tree.map(
            lambda upper_part, lower_part: jnp.where(leading, upper_part, lower_part),
            stored[max(moment - 1, 0)],
            stored[min(moment + 1, batches)],
        )
        grad_input, gradients = layer_backward(gradient, kept_state, layer_weights)
        active = jnp.where(leading, moment >= 1, moment < batches)
        masked = tuple((jnp.where(active, member, 0.0) for member in gradients))
        if totals is None:
            totals = masked
        else:
            totals = tuple((earlier_sum + member for earlier_sum, member in zip(totals, masked)))
        returned_grads.append(grad_input)
        if moment < batches:
            coming = shifted(grad_input.astype(jnp.bfloat16), "section", -1).astype(jnp.float32)
    boundary = jnp.stack(
        [
            jnp.where(leading, returned_grads[number + 1], produced[number + 1])
            for number in range(batches)
        ]
    )
    owned_parts = (
        lax.psum_scatter(
            totals[0][None].astype(jnp.bfloat16), "fsdp", scatter_dimension=1, tiled=True
        ).astype(jnp.float32),
        lax.psum_scatter(
            totals[1][None].astype(jnp.bfloat16), "fsdp", scatter_dimension=1, tiled=True
        ).astype(jnp.float32),
        lax.psum_scatter(
            totals[2][None].astype(jnp.bfloat16), "fsdp", scatter_dimension=1, tiled=True
        ).astype(jnp.float32),
        lax.psum_scatter(
            totals[3][None].astype(jnp.bfloat16), "fsdp", scatter_dimension=1, tiled=True
        ).astype(jnp.float32),
        lax.psum_scatter(
            totals[4][None].astype(jnp.bfloat16), "fsdp", scatter_dimension=1, tiled=True
        ).astype(jnp.float32),
        lax.psum_scatter(
            totals[5][None].astype(jnp.bfloat16), "fsdp", scatter_dimension=1, tiled=True
        ).astype(jnp.float32),
        lax.psum_scatter(
            totals[6][None].astype(jnp.bfloat16), "fsdp", scatter_dimension=1, tiled=True
        ).astype(jnp.float32),
        lax.psum_scatter(
            totals[7][None].astype(jnp.bfloat16), "fsdp", scatter_dimension=1, tiled=True
        ).astype(jnp.float32),
        lax.psum_scatter(
            totals[8][None].astype(jnp.bfloat16), "fsdp", scatter_dimension=1, tiled=True
        ).astype(jnp.float32),
    )
    summed = (
        lax.psum(owned_parts[0].astype(jnp.bfloat16), "rep").astype(jnp.float32),
        lax.psum(owned_parts[1].astype(jnp.bfloat16), "rep").astype(jnp.float32),
        lax.psum(owned_parts[2].astype(jnp.bfloat16), "rep").astype(jnp.float32),
        lax.psum(owned_parts[3].astype(jnp.bfloat16), "rep").astype(jnp.float32),
        lax.psum(owned_parts[4].astype(jnp.bfloat16), "rep").astype(jnp.float32),
        lax.psum(owned_parts[5].astype(jnp.bfloat16), "rep").astype(jnp.float32),
        lax.psum(owned_parts[6].astype(jnp.bfloat16), "rep").astype(jnp.float32),
        lax.psum(owned_parts[7].astype(jnp.bfloat16), "rep").astype(jnp.float32),
        lax.psum(owned_parts[8].astype(jnp.bfloat16), "rep").astype(jnp.float32),
    )
    return (
        boundary.astype(jnp.bfloat16)[None],
        summed[0],
        summed[1],
        summed[2],
        summed[3],
        summed[4],
        summed[5],
        summed[6],
        summed[7],
        summed[8],
    )


def solution(mesh):
    shape = mesh.shape
    relay = shape["section"] == 2 and shape["rep"] == 4 and shape["fsdp"] == 4
    if relay:
        devices = mesh.devices.reshape(2, 2, 2, 4)
        mesh = Mesh(devices, ("section", "y", "core", "fsdp"))
    rep = ("y", "core") if relay else "rep"
    data = P("section", None, rep, "fsdp", None)
    vector, matrix = P("section", "fsdp"), P("section", "fsdp", None)
    params = (vector, matrix, matrix, vector, vector, vector, vector, vector, matrix)
    return jax.shard_map(
        relay_shards if relay else shards,
        mesh=mesh,
        in_specs=(data, *params),
        out_specs=(data, *params),
        check_vma=False,
    )
```
